32 devices in a mesh: gx: 4 (over x, core), gy: 4 (over z), gz: 2 (over y).
Axes of the slice: x: 2, y: 2, z: 4, core: 2. Of those that a mesh axis runs over, the one named last changes fastest.
Arguments:
- features: bfloat16 [4, 4, 2, 64, 3200], P('gx', 'gy', 'gz'), may hold values from -6 to 6
- positions: float32 [4, 4, 2, 3, 64], P('gx', 'gy', 'gz'), as said below
- neighbours: int32 [4, 4, 2, 64, 32], P('gx', 'gy', 'gz'), may hold values from 0 to 575, as said below
- counts: int32 [4, 4, 2, 64], P('gx', 'gy', 'gz'), may hold values from 8 to 32, as said below
- cell_atoms: int32 [4, 4, 2, 64], P('gx', 'gy', 'gz'), may hold values from 0 to 63, as said below
- rbf_weight: bfloat16 [512, 128], replicated, may hold values from -3 to 3
- radial_weight: bfloat16 [128, 640], replicated, may hold values from -0.5 to 0.5
- mix_weight: bfloat16 [5, 128, 128], replicated, may hold values from -0.5 to 0.5
- out_weight: bfloat16 [5, 128, 128], replicated, may hold values from -1 to 1
- energy_weight: float32 [128], replicated, may hold values from -0.5 to 0.5
- norm_weight: float32 [4, 128], replicated, may hold values from -0.5 to 0.5
Outputs:
- new_features: bfloat16 [4, 4, 2, 64, 3200], P('gx', 'gy', 'gz')
- energies: float32 [4, 4, 2, 64], P('gx', 'gy', 'gz')
- forces: float32 [4, 4, 2, 3, 64], P('gx', 'gy', 'gz')
The draws below stay inside these ranges and needn't reach their ends.
Inputs may be any that keep to these rules, and one draw needn't show every extreme that they name: `positions`: the atom cell_atoms[q] of cell slot q = 8 c + r lies within 0.2 of the lattice site (2 cx + rx + 0.5, 2 cy + ry + 0.5, 2 cz + rz + 0.5) of its box. `neighbours`: the first 16 slots of atom i name other atoms of its domain (rows 0 to 63, never i); the rest name rows 64 + 8 e + r of extended cells e = ((ex 4 + ey) (4) + ez) that touch atom i's cell and lie outside the domain. `counts`: atom 0 of every domain has all 32 slots live. `cell_atoms`: A permutation of the domain's atoms.
All inputs are finite; a program needn't handle non-finite values.
Results may differ from the reference program's by a relative error of at most 0.012.
Values may be sent and summed in bfloat16 or wider, within the bound.
No kernel may reach another device: no remote copies, remote signals or barrier semaphores. Data moves between devices by JAX's collectives and lax.ppermute only.
A program may use at most 64 MiB of HBM per device.

```python
import math
from functools import partial
import jax
import jax.numpy as jnp
import numpy as np
from jax import lax

C = 128
LMAX = 4
FEAT = 3200
RBF = 512
HID = 128
NB = 32
ZCELLS = 2
ATOM_DEV = 64
N_GX = 4
N_GY = 4
N_GZ = 2


def cell_order(key):
    atom_total = 32 * ZCELLS
    scores = jax.random.randint(jax.random.fold_in(key, 51), (N_GX, N_GY, N_GZ, atom_total), 0, 1 << 20) * atom_total + jnp.arange(atom_total, dtype=jnp.int32)
    return jnp.argsort(scores, axis=-1).astype(jnp.int32)


def slot_coords(slot_of):
    cell = slot_of // 8
    within = slot_of % 8
    cell_x = cell // (2 * ZCELLS)
    cell_y = cell // ZCELLS % 2
    cell_z = cell % ZCELLS
    return (cell_x, cell_y, cell_z, within)


def draw_cell_atoms(key, part):
    return cell_order(key)


def draw_positions(key, part):
    atom_total = 32 * ZCELLS
    slot_of = jnp.argsort(cell_order(key), axis=-1).astype(jnp.int32)
    cell_x, cell_y, cell_z, within = slot_coords(slot_of)
    lattice = jnp.stack([2 * cell_x + within // 4, 2 * cell_y + within // 2 % 2, 2 * cell_z + within % 2], axis=3).astype(jnp.float32) + 0.5
    shape = (N_GX, N_GY, N_GZ, 3, atom_total)
    noise_key = jax.random.fold_in(key, 11)
    jitter = jnp.clip(0.07 * jax.random.normal(noise_key, shape, jnp.float32), -0.2, 0.2)
    return lattice + jitter


def draw_neighbours(key, part):
    atom_total = 32 * ZCELLS
    half_slots = NB // 2
    shape = (N_GX, N_GY, N_GZ, atom_total)
    own_pick = jax.random.randint(jax.random.fold_in(key, 21), shape + (half_slots,), 0, atom_total - 1)
    own_rows = (jnp.arange(atom_total, dtype=jnp.int32)[:, None] + 1 + own_pick) % atom_total
    slot_of = jnp.argsort(cell_order(key), axis=-1).astype(jnp.int32)
    cell_x, cell_y, cell_z, within = slot_coords(slot_of)
    cell_x = cell_x[..., None]
    cell_y = cell_y[..., None]
    cell_z = cell_z[..., None]
    ghost_shape = shape + (NB - half_slots,)
    axis_pick = jax.random.randint(jax.random.fold_in(key, 22), ghost_shape, 0, 3)
    step_x = jax.random.randint(jax.random.fold_in(key, 23), ghost_shape, -1, 2)
    step_y = jax.random.randint(jax.random.fold_in(key, 24), ghost_shape, -1, 2)
    step_z = jax.random.randint(jax.random.fold_in(key, 25), ghost_shape, -1, 2)
    sign_pick = jax.random.randint(jax.random.fold_in(key, 26), ghost_shape, 0, 2) * 2 - 1
    row_pick = jax.random.randint(jax.random.fold_in(key, 27), ghost_shape, 0, 8)
    out_x = jnp.where(cell_x == 0, -1, 1)
    out_y = jnp.where(cell_y == 0, -1, 1)
    low_z = cell_z == 0
    high_z = cell_z == ZCELLS - 1
    out_z = jnp.where(jnp.logical_and(low_z, high_z), sign_pick, jnp.where(low_z, -1, 1))
    edge_z = jnp.logical_or(low_z, high_z)
    axis_used = jnp.where(jnp.logical_and(axis_pick == 2, jnp.logical_not(edge_z)), 0, axis_pick)
    move_x = jnp.where(axis_used == 0, out_x, step_x)
    move_y = jnp.where(axis_used == 1, out_y, step_y)
    move_z = jnp.where(axis_used == 2, out_z, step_z)
    extended = ((cell_x + 1 + move_x) * 4 + (cell_y + 1 + move_y)) * (ZCELLS + 2) + (cell_z + 1 + move_z)
    ghost_rows = atom_total + extended * 8 + row_pick
    return jnp.concatenate([own_rows, ghost_rows], axis=-1).astype(jnp.int32)


def draw_counts(key, part):
    atom_total = 32 * ZCELLS
    drawn = jax.random.randint(jax.random.fold_in(key, 31), (N_GX, N_GY, N_GZ, atom_total), NB // 4, NB + 1)
    return drawn.at[:, :, :, 0].set(NB).astype(jnp.int32)


def level_of(key, dims, pieces, low, high):
    loudness = 1.0
    for position, blocks in pieces:
        steps = jax.random.uniform(jax.random.fold_in(jax.random.fold_in(key, 6), position), (blocks,), jnp.float32, low / len(pieces), high / len(pieces))
        loudness = loudness * jnp.repeat(jnp.exp(steps), dims[position] // blocks).reshape((-1,) + (1,) * (len(dims) - 1 - position))
    return loudness


def noise(rng, shape, deviation, limit, pieces=(), kind=jnp.bfloat16):
    values = jax.random.normal(rng, shape, jnp.float32) * deviation
    if len(pieces) > 0:
        values = level_of(rng, shape, pieces, -0.22, 0.18) * values
    return jnp.clip(values, min=-limit, max=limit).astype(kind)


def setup_inputs(seed: int = 0) -> dict:
    streams_of = jax.random.split(jax.random.key(seed), 12)
    features = noise(streams_of[0], (N_GX, N_GY, N_GZ, ATOM_DEV, FEAT), 1.0, 6.0, ((0, 4), (1, 4), (2, 2)))
    positions = draw_positions(jax.random.fold_in(streams_of[11], 71), 0)
    neighbours = draw_neighbours(jax.random.fold_in(streams_of[11], 71), 0)
    counts = draw_counts(jax.random.fold_in(streams_of[11], 71), 0)
    cell_atoms = draw_cell_atoms(jax.random.fold_in(streams_of[11], 71), 0)
    rbf_weight = noise(streams_of[5], (RBF, HID), 4 ** -0.5, 3.0)
    radial_weight = noise(streams_of[6], (HID, (LMAX + 1) * C), HID ** -0.5, 0.5)
    mix_weight = noise(streams_of[7], (LMAX + 1, C, C), C ** -0.5, 0.5)
    out_weight = noise(streams_of[8], (LMAX + 1, C, C), (C // 4) ** -0.5, 1.0)
    energy_weight = noise(streams_of[9], (C,), C ** -0.5, 0.5, (), jnp.float32)
    norm_weight = noise(streams_of[10], (LMAX, C), C ** -0.5, 0.5, (), jnp.float32)
    return dict(features=features, positions=positions, neighbours=neighbours, counts=counts, cell_atoms=cell_atoms, rbf_weight=rbf_weight, radial_weight=radial_weight, mix_weight=mix_weight, out_weight=out_weight, energy_weight=energy_weight, norm_weight=norm_weight)


def degree_of(coeff_total):
    top_degree = int(math.isqrt(coeff_total)) - 1
    return np.array([degree for degree in range(top_degree + 1) for _ in range(2 * degree + 1)], dtype=np.int32)

def product(pattern, first_op, second_op):
    return jnp.einsum(pattern, first_op.astype(jnp.float32), second_op.astype(jnp.float32), preferred_element_type=jnp.float32)

def image_shifts(zcells):
    depth = 2 * zcells
    side_x = [-4.0, 0.0, 0.0, 4.0]
    side_z = [-float(depth)] + [0.0] * zcells + [float(depth)]
    table = [[[[[side_x[ex], side_x[ey], side_z[ez]][comp] for ez in range(zcells + 2)] for ey in range(4)] for ex in range(4)] for comp in range(3)]
    return jnp.asarray(table, jnp.float32)

def block_step(table_feat, table_places, rbf_weight, radial_weight, mix_expanded, out_expanded, energy_weight, norm_expanded, reach_max, grad_table, block):
    own_feat, own_places, neigh_rows, live_counts = block
    atom_rows, slot_count = neigh_rows.shape
    channels = energy_weight.shape[0]
    coefficients = own_feat.shape[1] // channels
    degrees = radial_weight.shape[1] // channels
    edge_rows = atom_rows * slot_count
    flat_rows = neigh_rows.reshape(edge_rows)
    near_feat = jnp.take(table_feat, flat_rows, axis=0).reshape(edge_rows, coefficients, channels)
    near_places = jnp.take(table_places, flat_rows, axis=1)
    relative = near_places - jnp.repeat(own_places, slot_count, axis=1)
    distance = jnp.sqrt(lax.optimization_barrier(jnp.sum(relative * relative, axis=0)))
    nbasis = rbf_weight.shape[0]
    spacing = reach_max / (nbasis - 1)
    centred = (distance[:, None] - spacing * jnp.arange(nbasis, dtype=jnp.float32)[None, :]) / spacing
    basis_vals = jnp.exp(-0.5 * centred * centred)
    preact = product('eb,bh->eh', basis_vals.astype(jnp.bfloat16), rbf_weight)
    hidden = jax.nn.silu(preact).astype(jnp.bfloat16)
    radial = product('eh,hf->ef', hidden, radial_weight).reshape(edge_rows, degrees, channels)
    table_deg = degree_of(coefficients)
    scaled = (near_feat * radial[:, table_deg, :]).astype(jnp.bfloat16)
    mixed = product('ekc,kcd->ekd', scaled, mix_expanded)
    gating = jax.nn.sigmoid(mixed[:, :1, :])
    message = mixed * gating
    live_mask = (jnp.arange(slot_count, dtype=jnp.int32)[None, :] < live_counts[:, None]).astype(jnp.float32)
    norm_scale = 1.0 / math.sqrt(slot_count)
    summed = lax.optimization_barrier(jnp.sum(message.reshape(atom_rows, slot_count, coefficients, channels) * live_mask[:, :, None, None], axis=1)) * norm_scale
    updated = own_feat.reshape(atom_rows, coefficients, channels).astype(jnp.float32) + product('akc,kcd->akd', summed.astype(jnp.bfloat16), out_expanded)
    scalar_part = updated[:, 0, :]
    energy = lax.optimization_barrier(jnp.sum(energy_weight[None, :] * jax.nn.silu(scalar_part), axis=1)) + lax.optimization_barrier(jnp.sum(norm_expanded[None] * updated * updated, axis=(1, 2)))
    logistic = jax.nn.sigmoid(scalar_part)
    grad_updated = jnp.concatenate([(energy_weight[None, :] * logistic * (1.0 + scalar_part * (1.0 - logistic)))[:, None, :], 2.0 * norm_expanded[None, 1:, :] * updated[:, 1:, :]], axis=1)
    grad_summed = product('akd,kcd->akc', grad_updated.astype(jnp.bfloat16), out_expanded) * norm_scale
    grad_message = (grad_summed[:, None, :, :] * live_mask[:, :, None, None]).reshape(edge_rows, coefficients, channels)
    grad_first = grad_message[:, :1, :] * gating * (1.0 + mixed[:, :1, :] * (1.0 - gating)) + lax.optimization_barrier(jnp.sum(grad_message[:, 1:, :] * mixed[:, 1:, :], axis=1, keepdims=True)) * gating * (1.0 - gating)
    grad_mixed = jnp.concatenate([grad_first, grad_message[:, 1:, :] * gating], axis=1).astype(jnp.bfloat16)
    grad_scaled = product('ekd,kcd->ekc', grad_mixed, mix_expanded)
    weighted = grad_scaled * near_feat
    grad_radial = jnp.stack([lax.optimization_barrier(jnp.sum(weighted[:, degree * degree:(degree + 1) * (degree + 1), :], axis=1)) for degree in range(degrees)], axis=1)
    grad_hidden = product('ef,hf->eh', grad_radial.reshape(edge_rows, degrees * channels).astype(jnp.bfloat16), radial_weight)
    logistic_pre = jax.nn.sigmoid(preact)
    grad_preact = grad_hidden * logistic_pre * (1.0 + preact * (1.0 - logistic_pre))
    grad_basis = product('eh,bh->eb', grad_preact.astype(jnp.bfloat16), rbf_weight)
    grad_dist = lax.optimization_barrier(jnp.sum(grad_basis * basis_vals * centred, axis=1)) * (-1.0 / spacing)
    pull_vec = relative * (grad_dist / distance)[None, :]
    grad_own = -lax.optimization_barrier(jnp.sum(pull_vec.reshape(3, atom_rows, slot_count), axis=2))
    grad_table = grad_table.at[:, flat_rows].add(pull_vec)
    return (grad_table, (updated.reshape(atom_rows, coefficients * channels).astype(jnp.bfloat16), energy, grad_own))

def domain_layer(own_feat, own_places, ghost_feat, ghost_places, neigh_rows, live_counts, rbf_weight, radial_weight, mix_weight, out_weight, energy_weight, norm_weight):
    atom_rows = own_feat.shape[0]
    channels = energy_weight.shape[0]
    coefficients = own_feat.shape[1] // channels
    table_deg = degree_of(coefficients)
    mix_expanded = mix_weight[table_deg]
    out_expanded = out_weight[table_deg]
    upper_deg = table_deg[1:]
    divisor = jnp.asarray(2 * upper_deg + 1, jnp.float32)
    norm_expanded = jnp.concatenate([jnp.zeros((1, channels), jnp.float32), norm_weight[upper_deg - 1] / divisor[:, None]], axis=0)
    table_feat = jnp.concatenate([own_feat, ghost_feat], axis=0)
    table_places = jnp.concatenate([own_places, ghost_places], axis=1)
    blocks = atom_rows // 8
    layer_depth = atom_rows // 16
    reach_max = 2.0 * math.sqrt(32.0 + layer_depth * layer_depth)
    scanned = (own_feat.reshape(blocks, 8, -1), jnp.transpose(own_places.reshape(3, blocks, 8), (1, 0, 2)), neigh_rows.reshape(blocks, 8, -1), live_counts.reshape(blocks, 8))
    advance = partial(block_step, table_feat, table_places, rbf_weight, radial_weight, mix_expanded, out_expanded, energy_weight, norm_expanded, reach_max)
    grad_table, (updated, energy, grad_own) = lax.scan(advance, jnp.zeros(table_places.shape, jnp.float32), scanned)
    grad_own = jnp.transpose(grad_own, (1, 0, 2)).reshape(3, atom_rows) + grad_table[:, :atom_rows]
    return (updated.reshape(atom_rows, -1), energy.reshape(atom_rows), grad_own, grad_table[:, atom_rows:])

def fold_domains(stacked, dom_axis, ext_axis, count):
    slots = [None] * count
    for ext in range(count + 2):
        place = ext - 1
        offset = place // count
        slot = place % count
        piece = jnp.roll(lax.index_in_dim(stacked, ext, axis=ext_axis, keepdims=False), offset, axis=dom_axis)
        slots[slot] = piece if slots[slot] is None else slots[slot] + piece
    return jnp.stack(slots, axis=ext_axis)

def reference(features, positions, neighbours, counts, cell_atoms, rbf_weight, radial_weight, mix_weight, out_weight, energy_weight, norm_weight):
    span_x, span_y, span_z, atom_rows, feat = features.shape
    zcells = atom_rows // 32
    cell_feat = jnp.take_along_axis(features, cell_atoms[..., None], axis=3).reshape(span_x, span_y, span_z, 2, 2, zcells, 8, feat)
    cell_feat = jnp.transpose(cell_feat, (0, 3, 1, 4, 2, 5, 6, 7)).reshape(span_x * 2, span_y * 2, span_z * zcells, 8, feat)
    feat_pad = jnp.pad(cell_feat, ((1, 1), (1, 1), (1, 1), (0, 0), (0, 0)), mode='wrap')
    cell_places = jnp.take_along_axis(positions, cell_atoms[:, :, :, None, :], axis=4).reshape(span_x, span_y, span_z, 3, 2, 2, zcells, 8)
    cell_places = jnp.transpose(cell_places, (3, 0, 4, 1, 5, 2, 6, 7)).reshape(3, span_x * 2, span_y * 2, span_z * zcells, 8)
    places_pad = jnp.pad(cell_places, ((0, 0), (1, 1), (1, 1), (1, 1), (0, 0)), mode='wrap')
    shifts = image_shifts(zcells)
    zero = jnp.zeros((), jnp.int32)

    def per_domain(domain):
        index_x = (domain // (span_y * span_z)).astype(jnp.int32)
        index_y = (domain // span_z % span_y).astype(jnp.int32)
        index_z = (domain % span_z).astype(jnp.int32)
        ghost_feat = lax.dynamic_slice(feat_pad, (index_x * 2, index_y * 2, index_z * zcells, zero, zero), (4, 4, zcells + 2, 8, feat)).reshape(-1, feat)
        ghost_places = (lax.dynamic_slice(places_pad, (zero, index_x * 2, index_y * 2, index_z * zcells, zero), (3, 4, 4, zcells + 2, 8)) + shifts[..., None]).reshape(3, -1)
        return domain_layer(features[index_x, index_y, index_z], positions[index_x, index_y, index_z], ghost_feat, ghost_places, neighbours[index_x, index_y, index_z], counts[index_x, index_y, index_z], rbf_weight, radial_weight, mix_weight, out_weight, energy_weight, norm_weight)
    updated, energy, grad_own, grad_ghost = lax.map(per_domain, jnp.arange(span_x * span_y * span_z, dtype=jnp.int32))
    grad_ghost = grad_ghost.reshape(span_x, span_y, span_z, 3, 4, 4, zcells + 2, 8)
    folded = fold_domains(grad_ghost, 0, 4, 2)
    folded = fold_domains(folded, 1, 5, 2)
    folded = fold_domains(folded, 2, 6, zcells)
    cell_grad = folded.reshape(span_x, span_y, span_z, 3, atom_rows)
    onehot = (cell_atoms[..., :, None] == jnp.arange(atom_rows, dtype=jnp.int32)).astype(jnp.float32)
    back_own = lax.optimization_barrier(jnp.sum(cell_grad[..., :, :, None] * onehot[..., None, :, :], axis=4))
    forces = -(grad_own.reshape(span_x, span_y, span_z, 3, atom_rows) + back_own)
    return (updated.reshape(features.shape), energy.reshape(span_x, span_y, span_z, atom_rows), forces)
```

```python
import math

import jax
import jax.numpy as jnp
from jax import lax
from jax.experimental import pallas as pl
from jax.experimental.pallas import tpu as pltpu
from jax.sharding import PartitionSpec as P

F32 = jnp.float32
BF16 = jnp.bfloat16
CH = 128
PAIRS = 12
OWN_ROWS = 256
GH_ROWS = 128
VMEM = 56 * 1024 * 1024


def mm(a, b):
    return jnp.dot(a, b, preferred_element_type=F32)


def mm_nt(a, b):
    return lax.dot_general(a, b, (((1,), (1,)), ((), ())), preferred_element_type=F32)


def iota(shape, dim):
    return lax.broadcasted_iota(jnp.int32, shape, dim)


def flip(w):
    return w.astype(F32).T.astype(BF16)


def cells_kernel(feat_ref, pos_ref, meta_ref, cells_ref, own_pos_ref, rows_ref):
    atoms, feat = feat_ref.shape
    rows_ref[...] = jnp.zeros_like(rows_ref)
    places = pos_ref[...]
    first = places.astype(BF16).astype(F32)
    second = (places - first).astype(BF16).astype(F32)
    third = places - first - second
    rows_ref[0:3, :] = first
    rows_ref[4:7, :] = second
    rows_ref[8:11, :] = third
    pieces = rows_ref[...].astype(BF16)
    lane = iota((atoms, atoms), 1)
    pick = (meta_ref[:, 33:34] == lane).astype(BF16)
    same = (iota((atoms, atoms), 0) == lane).astype(BF16)
    own_pos_ref[...] = mm_nt(same, pieces).astype(BF16)
    cells_ref[:, feat:] = mm_nt(pick, pieces).astype(BF16)
    for at in range(0, feat, 640):
        cells_ref[:, at : at + 640] = mm(pick, feat_ref[:, at : at + 640]).astype(BF16)


def make_cells(feats, places, meta):
    atoms, feat = feats.shape
    return pl.pallas_call(
        cells_kernel,
        out_shape=(
            jax.ShapeDtypeStruct((atoms, feat + CH), BF16),
            jax.ShapeDtypeStruct((atoms, CH), BF16),
        ),
        scratch_shapes=[pltpu.VMEM((CH, atoms), F32)],
        name="cells",
    )(feats, places, meta)


def degrees_of(pair):
    low = 1 + (pair >= 2) + (pair >= 4) + (pair >= 8)
    high = 1 + (pair >= 1) + (pair >= 4) + (pair >= 7)
    kind = (pair >= 1) + (pair >= 2) + (pair >= 4) + (pair >= 7) + (pair >= 8)
    return low, high, kind


KINDS = ((1, 1), (1, 2), (2, 2), (3, 3), (3, 4), (4, 4))


def degrees_dyn(pair):
    def over(at):
        return (pair >= at).astype(jnp.int32)

    low = 1 + over(2) + over(4) + over(8)
    high = 1 + over(1) + over(4) + over(7)
    kind = over(1) + over(2) + over(4) + over(7) + over(8)
    return low, high, kind


def layer_kernel(
    own_ref,
    own_pos_ref,
    gh_ref,
    meta_ref,
    rbf_ref,
    rad_ref,
    mix_ref,
    out_ref,
    ew_ref,
    nw_ref,
    new_ref,
    en_ref,
    fown_ref,
    fgh_ref,
    oh_own,
    oh_gh,
    d_gh,
    dt_gh,
    unit_s,
    bc_s,
    pre_s,
    radial_s,
    nf0_s,
    m0_s,
    gate_s,
    dot_s,
    gr_s,
    nf_s,
    mx_s,
    wm,
    wmt,
    wo,
    wot,
    radt,
    rbft,
    nw2,
    ghpos,
    acc_s,
    gs_s,
    gs0_s,
    en_s,
    src_s,
    fo_s,
):
    atoms = own_ref.shape[0]
    feat = own_ref.shape[1]
    slots = 32
    half = slots // 2
    own_edges = atoms * half
    ghosts = gh_ref.shape[0]
    nbasis = rbf_ref.shape[0]
    depth = atoms // 16
    spacing = 2.0 * math.sqrt(32.0 + depth * depth) / (nbasis - 1)
    norm = 1.0 / math.sqrt(slots)
    per_step = OWN_ROWS // atoms
    own_steps = own_edges // OWN_ROWS

    wm[...] = jnp.zeros_like(wm)
    wmt[...] = jnp.zeros_like(wmt)
    wo[...] = jnp.zeros_like(wo)
    wot[...] = jnp.zeros_like(wot)
    for degree in range(5):
        mix = mix_ref[degree]
        out = out_ref[degree]
        mix_t = flip(mix)
        out_t = flip(out)
        if degree == 0:
            wm[6, 0:CH, 0:CH] = mix
            wmt[6, 0:CH, 0:CH] = mix_t
            wo[6, 0:CH, 0:CH] = out
            wot[6, 0:CH, 0:CH] = out_t
        for kind, both in enumerate(KINDS):
            for side in range(2):
                if both[side] == degree:
                    part = slice(side * CH, side * CH + CH)
                    wm[kind, part, part] = mix
                    wmt[kind, part, part] = mix_t
                    wo[kind, part, part] = out
                    wot[kind, part, part] = out_t
    for degree in range(5):
        radt[degree * CH : (degree + 1) * CH, :] = flip(
            rad_ref[:, degree * CH : (degree + 1) * CH]
        )
    for part in range(nbasis // CH):
        rbft[:, part * CH : (part + 1) * CH] = flip(rbf_ref[part * CH : (part + 1) * CH, :])
    for kind, both in enumerate(KINDS):
        for side in range(2):
            degree = both[side]
            nw2[kind, :, side * CH : (side + 1) * CH] = nw_ref[degree - 1 : degree, :] * (
                1.0 / (2 * degree + 1)
            )

    counts = meta_ref[:, 32:33]
    lane_atom = iota((atoms, atoms), 1)
    for slot in range(half):
        hit = jnp.logical_and(meta_ref[:, slot : slot + 1] == lane_atom, counts > slot)
        oh_own[slot * atoms : (slot + 1) * atoms, :] = hit.astype(F32).astype(BF16)

    live = jnp.maximum(counts - half, 0).astype(F32)
    sub_atom = iota((atoms, atoms), 0)
    live_b = jnp.broadcast_to(live, (atoms, atoms))
    end_row = jnp.sum(jnp.where(sub_atom <= lane_atom, live_b, 0.0), axis=0, keepdims=True)
    live_row = jnp.sum(jnp.where(sub_atom == lane_atom, live_b, 0.0), axis=0, keepdims=True)
    start_row = end_row - live_row
    end_col = jnp.sum(
        jnp.where(lane_atom <= sub_atom, jnp.broadcast_to(live_row, (atoms, atoms)), 0.0),
        axis=1,
        keepdims=True,
    )
    start_col = end_col - live
    total = jnp.sum(live)
    gh_steps = (total.astype(jnp.int32) + (GH_ROWS - 1)) // GH_ROWS
    ghost_row = meta_ref[:, half:slots] - atoms
    row_high = (ghost_row // 16).astype(F32).astype(BF16)
    row_low = (ghost_row % 16).astype(F32).astype(BF16)

    row = iota((ghosts, CH), 0)
    lane = iota((ghosts, CH), 1)
    zcells = atoms // 32
    per_y = (zcells + 2) * 8
    ext_x = row // (4 * per_y)
    ext_y = row // per_y % 4
    ext_z = row // 8 % (zcells + 2)

    def side_of(ext, last, size):
        return jnp.where(ext == 0, -size, jnp.where(ext == last, size, 0.0))

    shift = jnp.where(lane == 12, side_of(ext_x, 3, 4.0), 0.0)
    shift = jnp.where(lane == 13, side_of(ext_y, 3, 4.0), shift)
    shift = jnp.where(lane == 14, side_of(ext_z, zcells + 1, 2.0 * zcells), shift)
    ghpos[...] = (gh_ref[:, feat:].astype(F32) + shift).astype(BF16)

    def geometry(rows, near, here):
        diff = near - here
        rel = (diff + pltpu.roll(diff, CH - 4, 1)) + (
            pltpu.roll(diff, CH - 8, 1) + pltpu.roll(diff, CH - 12, 1)
        )
        rel = jnp.where(iota(rel.shape, 1) < 3, rel, 0.0)
        square = jnp.sum(rel * rel, axis=1, keepdims=True)
        inverse = lax.rsqrt(jnp.where(square > 0.0, square, 1.0))
        unit_s[rows, :] = rel * inverse
        dist = square * inverse
        centred = dist * (1.0 / spacing) - iota((rel.shape[0], nbasis), 1).astype(F32)
        basis = jnp.exp(-0.5 * centred * centred)
        bc_s[rows, :] = basis * centred
        pre = mm(basis.astype(BF16), rbf_ref[...])
        pre_s[rows, :] = pre
        hidden = (pre * jax.nn.sigmoid(pre)).astype(BF16)
        radial = mm(hidden, rad_ref[...])
        for degree in range(5):
            radial_s[degree, rows, :] = radial[:, degree * CH : (degree + 1) * CH]

    def forward0(rows, onehot, table):
        near = mm(onehot, table)
        scaled = (near * radial_s[0, rows, :]).astype(BF16)
        mixed = mm(scaled, wm[6, 0:CH, 0:CH])
        gate = jax.nn.sigmoid(mixed)
        nf0_s[rows, :] = near
        m0_s[rows, :] = mixed
        gate_s[rows, :] = gate
        dot_s[rows, :] = jnp.zeros_like(gate)
        for degree in range(1, 5):
            gr_s[degree, rows, :] = jnp.zeros_like(gate)
        return mixed * gate

    def over_slots(values):
        return jnp.sum(values.reshape(per_step, atoms, values.shape[1]), axis=0)

    def tiled(values):
        return jnp.concatenate([values] * per_step, axis=0)

    own_pos = own_pos_ref[...].astype(F32)
    own0 = own_ref[:, 0:CH]
    total0 = jnp.zeros((atoms, CH), F32)
    for step in range(own_steps):
        rows = pl.ds(step * OWN_ROWS, OWN_ROWS)
        onehot = oh_own[rows, :]
        geometry(rows, mm(onehot, own_pos_ref[...]), tiled(own_pos))
        total0 += over_slots(forward0(rows, onehot, own0))
    acc_s[:, 0:CH] = total0

    def ghost_start(step, carry):
        base = pl.multiple_of(step * GH_ROWS, GH_ROWS)
        here = pl.ds(base, GH_ROWS)
        rows = pl.ds(pl.multiple_of(own_edges + base, GH_ROWS), GH_ROWS)
        edge = (iota((GH_ROWS, atoms), 0) + base).astype(F32)
        mine = jnp.logical_and(edge >= start_row, edge < end_row).astype(F32)
        source = mine.astype(BF16)
        d_gh[here, :] = source
        edge_t = (iota((atoms, GH_ROWS), 1) + base).astype(F32)
        mine_t = jnp.logical_and(edge_t >= start_col, edge_t < end_col)
        dt_gh[step, :, :] = mine_t.astype(F32).astype(BF16)
        edge_col = edge[:, 0:1]
        slot = edge_col - jnp.sum(mine * start_row, axis=1, keepdims=True)
        listed = mm(source, row_high) * 16.0 + mm(source, row_low)
        at_slot = iota((GH_ROWS, half), 1).astype(F32) == slot
        which = jnp.sum(jnp.where(at_slot, listed, 0.0), axis=1, keepdims=True)
        which = jnp.where(edge_col < total, which, -1.0)
        onehot = (iota((GH_ROWS, ghosts), 1).astype(F32) == which).astype(F32).astype(BF16)
        oh_gh[here, :] = onehot
        geometry(rows, mm(onehot, ghpos[...]), mm(source, own_pos_ref[...]))
        message = forward0(rows, onehot, gh_ref[:, 0:CH])
        acc_s[:, 0:CH] += mm(dt_gh[step], message.astype(BF16))
        return carry

    lax.fori_loop(0, gh_steps, ghost_start, 0)

    low0 = (acc_s[:, 0:CH] * norm).astype(BF16)
    updated0 = own0.astype(F32) + mm(low0, wo[6, 0:CH, 0:CH])
    new_ref[:, 0:CH] = updated0.astype(BF16)
    logistic = jax.nn.sigmoid(updated0)
    weight0 = ew_ref[...]
    en_s[...] = weight0 * updated0 * logistic
    grad0 = (weight0 * logistic * (1.0 + updated0 * (1.0 - logistic))).astype(BF16)
    gs0_s[...] = mm(grad0, wot[6, 0:CH, 0:CH]) * norm

    def forward(rows, onehot, table, low, high, weight):
        near = mm(onehot, table)
        nf_s[rows, :] = near.astype(BF16)
        left = near[:, 0:CH] * radial_s[low, rows, :]
        right = near[:, CH:] * radial_s[high, rows, :]
        scaled = jnp.concatenate([left, right], axis=1).astype(BF16)
        mixed = mm(scaled, weight)
        mx_s[rows, :] = mixed.astype(BF16)
        gate = gate_s[rows, :]
        return mixed * jnp.concatenate([gate, gate], axis=1)

    def backward(rows, grad, low, high, weight_t):
        gate = gate_s[rows, :]
        product = grad * mx_s[rows, :].astype(F32)
        dot_s[rows, :] += product[:, 0:CH] + product[:, CH:]
        grad_mixed = (grad * jnp.concatenate([gate, gate], axis=1)).astype(BF16)
        weighted = mm(grad_mixed, weight_t) * nf_s[rows, :].astype(F32)
        gr_s[low, rows, :] += weighted[:, 0:CH]
        gr_s[high, rows, :] += weighted[:, CH:]

    def pair_step(pair, carry):
        low, high, kind = degrees_dyn(pair)
        cols = pl.ds(pl.multiple_of(CH + pair * 2 * CH, CH), 2 * CH)
        own = own_ref[:, cols]
        weight = wm[kind]
        summed = jnp.zeros((atoms, 2 * CH), F32)
        for step in range(own_steps):
            rows = pl.ds(step * OWN_ROWS, OWN_ROWS)
            summed += over_slots(forward(rows, oh_own[rows, :], own, low, high, weight))
        acc_s[...] = summed

        def ghost_forward(step, inner):
            base = pl.multiple_of(step * GH_ROWS, GH_ROWS)
            rows = pl.ds(pl.multiple_of(own_edges + base, GH_ROWS), GH_ROWS)
            message = forward(
                rows, oh_gh[pl.ds(base, GH_ROWS), :], gh_ref[:, cols], low, high, wm[kind]
            )
            acc_s[...] += mm(dt_gh[step], message.astype(BF16))
            return inner

        lax.fori_loop(0, gh_steps, ghost_forward, 0)

        summed_low = (acc_s[...] * norm).astype(BF16)
        updated = own.astype(F32) + mm(summed_low, wo[kind])
        new_ref[:, cols] = updated.astype(BF16)
        scale = nw2[kind] * updated
        energy = scale * updated
        en_s[...] += energy[:, 0:CH] + energy[:, CH:]
        grad_summed = mm((2.0 * scale).astype(BF16), wot[kind]) * norm
        gs_s[...] = grad_summed.astype(BF16)
        weight_t = wmt[kind]
        grad_tiled = tiled(grad_summed)
        for step in range(own_steps):
            rows = pl.ds(step * OWN_ROWS, OWN_ROWS)
            backward(rows, grad_tiled, low, high, weight_t)

        def ghost_backward(step, inner):
            base = pl.multiple_of(step * GH_ROWS, GH_ROWS)
            rows = pl.ds(pl.multiple_of(own_edges + base, GH_ROWS), GH_ROWS)
            grad = mm(d_gh[pl.ds(base, GH_ROWS), :], gs_s[...])
            backward(rows, grad, low, high, wmt[kind])
            return inner

        lax.fori_loop(0, gh_steps, ghost_backward, 0)
        return carry

    lax.fori_loop(0, PAIRS, pair_step, 0)

    def finish(rows, grad):
        gate = gate_s[rows, :]
        first = grad * gate * (1.0 + m0_s[rows, :] * (1.0 - gate)) + dot_s[rows, :] * gate * (
            1.0 - gate
        )
        weighted = mm(first.astype(BF16), wmt[6, 0:CH, 0:CH]) * nf0_s[rows, :]
        radial_grad = jnp.concatenate(
            [weighted] + [gr_s[degree, rows, :] for degree in range(1, 5)], axis=1
        ).astype(BF16)
        hidden_grad = mm(radial_grad, radt[...])
        pre = pre_s[rows, :]
        logistic_pre = jax.nn.sigmoid(pre)
        pre_grad = (hidden_grad * logistic_pre * (1.0 + pre * (1.0 - logistic_pre))).astype(BF16)
        basis_grad = mm(pre_grad, rbft[...])
        dist_grad = jnp.sum(basis_grad * bc_s[rows, :], axis=1, keepdims=True) * (-1.0 / spacing)
        pull = unit_s[rows, :] * dist_grad
        across = pull.T[0:8, :]
        top = across.astype(BF16)
        rest = (across - top.astype(F32)).astype(BF16)
        return pull, top, rest

    grad0_tiled = tiled(gs0_s[...])
    src = jnp.zeros((atoms, CH), F32)
    onto = jnp.zeros((8, atoms), F32)
    for step in range(own_steps):
        rows = pl.ds(step * OWN_ROWS, OWN_ROWS)
        pull, top, rest = finish(rows, grad0_tiled)
        src += over_slots(pull)
        onehot = oh_own[rows, :]
        onto += mm(top, onehot) + mm(rest, onehot)
    src_s[...] = src
    fgh_ref[...] = jnp.zeros_like(fgh_ref)
    gs_s[:, 0:CH] = gs0_s[...].astype(BF16)

    def ghost_finish(step, carry):
        base = pl.multiple_of(step * GH_ROWS, GH_ROWS)
        here = pl.ds(base, GH_ROWS)
        rows = pl.ds(pl.multiple_of(own_edges + base, GH_ROWS), GH_ROWS)
        grad = mm(d_gh[here, :], gs_s[:, 0:CH])
        pull, top, rest = finish(rows, grad)
        pull_top = pull.astype(BF16)
        pull_rest = (pull - pull_top.astype(F32)).astype(BF16)
        spread = dt_gh[step]
        src_s[...] += mm(spread, pull_top) + mm(spread, pull_rest)
        onehot = oh_gh[here, :]
        fgh_ref[...] += mm(top, onehot) + mm(rest, onehot)
        return carry

    lax.fori_loop(0, gh_steps, ghost_finish, 0)
    fown_ref[...] = onto - src_s[...].T[0:8, :]
    en_ref[...] = jnp.sum(en_s[...].T, axis=0, keepdims=True)


def layer(feats, own_pos, ghost, meta, rbf, rad, mix, out, ew, nw):
    atoms, feat = feats.shape
    ghosts = ghost.shape[0]
    edges = atoms * 32
    half = edges // 2
    nbasis = rbf.shape[0]
    scratch = [
        pltpu.VMEM((half, atoms), BF16),
        pltpu.VMEM((half, ghosts), BF16),
        pltpu.VMEM((half, atoms), BF16),
        pltpu.VMEM((half // GH_ROWS, atoms, GH_ROWS), BF16),
        pltpu.VMEM((edges, CH), F32),
        pltpu.VMEM((edges, nbasis), F32),
        pltpu.VMEM((edges, CH), F32),
        pltpu.VMEM((5, edges, CH), F32),
        pltpu.VMEM((edges, CH), F32),
        pltpu.VMEM((edges, CH), F32),
        pltpu.VMEM((edges, CH), F32),
        pltpu.VMEM((edges, CH), F32),
        pltpu.VMEM((5, edges, CH), F32),
        pltpu.VMEM((edges, 2 * CH), BF16),
        pltpu.VMEM((edges, 2 * CH), BF16),
        pltpu.VMEM((7, 2 * CH, 2 * CH), BF16),
        pltpu.VMEM((7, 2 * CH, 2 * CH), BF16),
        pltpu.VMEM((7, 2 * CH, 2 * CH), BF16),
        pltpu.VMEM((7, 2 * CH, 2 * CH), BF16),
        pltpu.VMEM((5 * CH, CH), BF16),
        pltpu.VMEM((CH, nbasis), BF16),
        pltpu.VMEM((6, 1, 2 * CH), F32),
        pltpu.VMEM((ghosts, CH), BF16),
        pltpu.VMEM((atoms, 2 * CH), F32),
        pltpu.VMEM((atoms, 2 * CH), BF16),
        pltpu.VMEM((atoms, CH), F32),
        pltpu.VMEM((atoms, CH), F32),
        pltpu.VMEM((atoms, CH), F32),
        pltpu.VMEM((8, atoms), F32),
    ]
    return pl.pallas_call(
        layer_kernel,
        out_shape=(
            jax.ShapeDtypeStruct((atoms, feat), BF16),
            jax.ShapeDtypeStruct((1, atoms), F32),
            jax.ShapeDtypeStruct((8, atoms), F32),
            jax.ShapeDtypeStruct((8, ghosts), F32),
        ),
        scratch_shapes=scratch,
        compiler_params=pltpu.CompilerParams(vmem_limit_bytes=VMEM),
        name="layer",
    )(feats, own_pos, ghost, meta, rbf, rad, mix, out, ew, nw)


def halo(block, axis, dim):
    peers, length = lax.axis_size(axis), block.shape[dim]
    up = [(i, (i + 1) % peers) for i in range(peers)]
    down = [(j, i) for i, j in up]
    last = lax.slice_in_dim(block, length - 1, length, axis=dim)
    first = lax.slice_in_dim(block, 0, 1, axis=dim)
    if peers == 2 and length == 2:
        other = lax.ppermute(block, axis, up)
        before = lax.slice_in_dim(other, length - 1, length, axis=dim)
        after = lax.slice_in_dim(other, 0, 1, axis=dim)
    else:
        before = lax.ppermute(last, axis, up)
        after = lax.ppermute(first, axis, down)
    return jnp.concatenate([before, block, after], axis=dim)


def fold(block, axis, dim):
    peers, length = lax.axis_size(axis), block.shape[dim]
    up = [(i, (i + 1) % peers) for i in range(peers)]
    down = [(j, i) for i, j in up]
    to_upper = lax.slice_in_dim(block, length - 1, length, axis=dim)
    to_lower = lax.slice_in_dim(block, 0, 1, axis=dim)
    from_lower = lax.ppermute(to_upper, axis, up)
    from_upper = lax.ppermute(to_lower, axis, down)
    first = lax.slice_in_dim(block, 1, 2, axis=dim) + from_lower
    last = lax.slice_in_dim(block, length - 2, length - 1, axis=dim) + from_upper
    inner = lax.slice_in_dim(block, 2, length - 2, axis=dim)
    return jnp.concatenate([first, inner, last], axis=dim)


def local(
    features,
    positions,
    neighbours,
    counts,
    cell_atoms,
    rbf_weight,
    radial_weight,
    mix_weight,
    out_weight,
    energy_weight,
    norm_weight,
):
    atoms = features.shape[3]
    zcells = atoms // 32
    feats = features[0, 0, 0]
    places = positions[0, 0, 0]
    order = cell_atoms[0, 0, 0]
    meta = jnp.concatenate(
        [neighbours[0, 0, 0], counts[0, 0, 0][:, None], order[:, None]], axis=1
    )
    cells, own_pos = make_cells(feats, places, meta)
    ghost = cells.reshape(2, 2, zcells, 8, -1)
    ghost = halo(ghost, "gz", 2)
    ghost = halo(ghost, "gy", 1)
    ghost = halo(ghost, "gx", 0)
    new, energy, grad_own, grad_ghost = layer(
        feats,
        own_pos,
        ghost.reshape(-1, ghost.shape[-1]),
        meta,
        rbf_weight,
        radial_weight,
        mix_weight,
        out_weight,
        energy_weight[None],
        norm_weight,
    )
    grads = grad_ghost[0:3].reshape(3, 4, 4, zcells + 2, 8)
    grads = fold(grads, "gx", 1)
    grads = fold(grads, "gy", 2)
    grads = fold(grads, "gz", 3)
    onehot = (order[:, None] == jnp.arange(atoms, dtype=jnp.int32)[None, :]).astype(F32)
    back = jnp.sum(grads.reshape(3, atoms)[:, :, None] * onehot[None], axis=1)
    forces = -(grad_own[0:3] + back)
    return (new[None, None, None], energy[None, None], forces[None, None, None])


def solution(mesh):
    split = P("gx", "gy", "gz", None, None)
    flat = P("gx", "gy", "gz", None)
    return jax.shard_map(
        local,
        mesh=mesh,
        in_specs=(split, split, split, flat, flat, P(), P(), P(), P(), P(), P()),
        out_specs=(split, flat, split),
        check_vma=False,
    )
```

```python
import functools
import math

import jax
import jax.numpy as jnp
from jax import lax
from jax.experimental import pallas as pl
from jax.experimental.pallas import tpu as pltpu
from jax.sharding import PartitionSpec as P

F32 = jnp.float32
BF16 = jnp.bfloat16
CH = 128
SLOTS = 32
HALF = 16
STEP = 256
OWN_STEPS = 4
GH_STEPS = 2
VMEM = 56 * 1024 * 1024
SPACE = pltpu.VMEM
PAIR_DEGREES = (
    (1, 1), (1, 2), (2, 2), (2, 2),
    (3, 3), (3, 3), (3, 3), (3, 4),
    (4, 4), (4, 4), (4, 4), (4, 4),
)
GROUPS = ((0, 4), (4, 8), (8, 12))


def mm(a, b):
    return jnp.dot(a, b, preferred_element_type=F32)


def mm_nt(a, b):
    return lax.dot_general(a, b, (((1,), (1,)), ((), ())), preferred_element_type=F32)


def iota(shape, dim):
    return lax.broadcasted_iota(jnp.int32, shape, dim)


def flip(w):
    return w.astype(F32).T.astype(BF16)


def pair_cols(pair):
    return slice(CH + pair * 2 * CH, CH + (pair + 1) * 2 * CH)


def struct(*shape, dtype=F32):
    return jax.ShapeDtypeStruct(shape, dtype)


def call(kernel, name, out_shape, scratch, flops, args, specs=None):
    size = sum(a.size * a.dtype.itemsize for a in list(args) + list(out_shape))
    return pl.pallas_call(
        kernel,
        out_shape=out_shape,
        in_specs=specs or [pl.BlockSpec(memory_space=SPACE)] * len(args),
        out_specs=tuple(pl.BlockSpec(memory_space=SPACE) for _ in out_shape),
        scratch_shapes=scratch,
        compiler_params=pltpu.CompilerParams(vmem_limit_bytes=VMEM),
        cost_estimate=pl.CostEstimate(flops=flops, bytes_accessed=size, transcendentals=0),
        name=name,
    )(*args)


def cells_kernel(feat_ref, pos_ref, near_ref, counts_ref, order_ref, *refs):
    out_refs, (own_pos_ref, meta_ref, rows_ref, pos_rows) = refs[:3], refs[3:]
    atoms = feat_ref.shape[0]
    rows_ref[...] = jnp.zeros_like(rows_ref)
    rows_ref[0:SLOTS, :] = near_ref[...].astype(F32)
    rows_ref[SLOTS : SLOTS + 1, :] = counts_ref[...].astype(F32)
    rows_ref[SLOTS + 1 : SLOTS + 2, :] = order_ref[...].astype(F32)
    meta = rows_ref[...].T
    meta_ref[...] = meta
    pos_rows[...] = jnp.zeros_like(pos_rows)
    for comp in range(3):
        places = pos_ref[comp]
        first = places.astype(BF16).astype(F32)
        second = (places - first).astype(BF16).astype(F32)
        pos_rows[comp : comp + 1, :] = first
        pos_rows[4 + comp : 5 + comp, :] = second
        pos_rows[8 + comp : 9 + comp, :] = places - first - second
    pieces = pos_rows[...].astype(BF16)
    lane = iota((atoms, atoms), 1).astype(F32)
    pick = (meta[:, SLOTS + 1 : SLOTS + 2] == lane).astype(F32).astype(BF16)
    same = (iota((atoms, atoms), 0) == iota((atoms, atoms), 1)).astype(F32).astype(BF16)
    own_pos_ref[...] = mm_nt(same, pieces).astype(BF16)
    for group, (begin, end) in enumerate(GROUPS):
        at = 0 if group == 0 else pair_cols(begin).start
        till = pair_cols(end - 1).stop
        out_refs[group][:, 0 : till - at] = mm(pick, feat_ref[:, at:till]).astype(BF16)
        if group == 0:
            out_refs[group][:, till:] = mm_nt(pick, pieces).astype(BF16)


def make_cells(feats, places, near, counts, order):
    atoms = feats.shape[0]
    widths = [CH * 2 * (end - begin) for begin, end in GROUPS]
    widths[0] += 2 * CH
    out_shape = tuple(struct(atoms, width, dtype=BF16) for width in widths) + (
        struct(atoms, CH, dtype=BF16),
        struct(atoms, CH),
    )
    scratch = [pltpu.VMEM((CH, atoms), F32), pltpu.VMEM((CH, atoms), F32)]
    args = (feats, places, near, counts, order)
    return call(cells_kernel, "cells", out_shape, scratch, 1 << 26, args)


def spacing_of(atoms, nbasis):
    depth = atoms // 16
    return 2.0 * math.sqrt(32.0 + depth * depth) / (nbasis - 1)


def own_onehots(meta_ref, oh_own):
    atoms = meta_ref.shape[0]
    counts = meta_ref[:, SLOTS : SLOTS + 1]
    lane_atom = iota((atoms, atoms), 1).astype(F32)
    for slot in range(HALF):
        hit = jnp.logical_and(meta_ref[:, slot : slot + 1] == lane_atom, counts > slot)
        oh_own[slot * atoms : (slot + 1) * atoms, :] = hit.astype(F32).astype(BF16)


def geometry(near, here):
    diff = near - here
    rel = (diff + pltpu.roll(diff, CH - 4, 1)) + (
        pltpu.roll(diff, CH - 8, 1) + pltpu.roll(diff, CH - 12, 1)
    )
    lane = iota(rel.shape, 1)
    rel = jnp.where(lane < 3, rel, 0.0)
    square = jnp.sum(rel * rel, axis=1, keepdims=True)
    inverse = lax.rsqrt(jnp.where(square > 0.0, square, 1.0))
    dist = square * inverse
    return jnp.where(lane == 3, dist, rel * inverse), dist


def centred_of(dist, spacing, nbasis):
    return dist * (1.0 / spacing) - iota((dist.shape[0], nbasis), 1).astype(F32)


def radial_net(dist, spacing, rbf_ref, rad_ref):
    centred = centred_of(dist, spacing, rbf_ref.shape[0])
    basis = jnp.exp(-0.5 * centred * centred)
    pre = mm(basis.astype(BF16), rbf_ref[...])
    hidden = (pre * jax.nn.sigmoid(pre)).astype(BF16)
    return pre, mm(hidden, rad_ref[...]).astype(BF16)


def own_spread(atoms):
    shape = (atoms, STEP)
    return (iota(shape, 1) % atoms == iota(shape, 0)).astype(F32).astype(BF16)


def tiled(values):
    return jnp.concatenate([values] * (STEP // values.shape[0]), axis=0)


def live_ghosts(meta_ref):
    return jnp.maximum(meta_ref[:, SLOTS : SLOTS + 1] - HALF, 0.0)


def step_count(meta_ref):
    total = jnp.sum(live_ghosts(meta_ref)).astype(jnp.int32)
    return jnp.maximum((total + (STEP - 1)) // STEP, GH_STEPS)


def own_rows(step):
    return pl.ds(step * STEP, STEP)


def ghost_rows(step):
    if isinstance(step, int):
        return pl.ds(step * STEP, STEP), pl.ds((OWN_STEPS + step) * STEP, STEP)
    base = pl.multiple_of(step * STEP, STEP)
    later = pl.multiple_of(OWN_STEPS * STEP + step * STEP, STEP)
    return pl.ds(base, STEP), pl.ds(later, STEP)


def over_ghost_steps(steps, body):
    for step in range(GH_STEPS):
        body(step)

    def again(step, carry):
        body(step)
        return carry

    lax.fori_loop(GH_STEPS, steps, again, 0)


def block_diagonal(kinds, mix_ref, out_ref, wm, wmt, wo, wot):
    zero = jnp.zeros((CH, CH), BF16)
    for kind, both in enumerate(kinds):
        for ref in (wm, wmt, wo, wot):
            ref[kind, 0:CH, CH:] = zero
            ref[kind, CH:, 0:CH] = zero
    for degree in sorted({d for both in kinds for d in both}):
        mix, out = mix_ref[degree], out_ref[degree]
        mix_t, out_t = flip(mix), flip(out)
        for kind, both in enumerate(kinds):
            for side in range(2):
                if both[side] == degree:
                    part = slice(side * CH, side * CH + CH)
                    wm[kind, part, part] = mix
                    wmt[kind, part, part] = mix_t
                    wo[kind, part, part] = out
                    wot[kind, part, part] = out_t


def fetch(pieces, table, sems):
    copies = []
    at = 0
    for index, piece in enumerate(pieces):
        rows = piece.shape[0]
        copies.append(
            pltpu.make_async_copy(piece, table.at[pl.ds(at, rows), :], sems.at[index])
        )
        at += rows
    for copy in copies:
        copy.start()
    return copies


def run_pairs(
    pairs, kinds, first_col, own_ref, table, new_ref, new_base, oh_own, oh_gh, d_gh, dt_gh,
    gate_ref, radial_of, nw_ref, steps, wm, wmt, wo, wot, nf_s, mx_s, acc_s, gs_s, dot_ref,
    grad_refs, en_ref,
):
    atoms = own_ref.shape[0]
    norm = 1.0 / math.sqrt(SLOTS)
    spread_own = own_spread(atoms)
    seen = set()

    def gate_of(rows):
        gate = gate_ref[rows, :]
        return jnp.concatenate([gate, gate], axis=1)

    for quad in range(0, len(pairs), 2):
        both = pairs[quad : quad + 2]
        infos = []
        for index, pair in enumerate(both):
            degrees = PAIR_DEGREES[pair]
            cols = pair_cols(pair)
            local = slice(cols.start - first_col, cols.stop - first_col)
            infos.append((index, degrees, kinds.index(degrees), cols, local))

        def forward(index, degrees, kind, rows, onehot, feats):
            near = mm(onehot, feats).astype(BF16)
            nf_s[index, rows, :] = near
            radial = jnp.concatenate([radial_of(d, rows) for d in degrees], axis=1)
            mixed = mm(near * radial, wm[kind]).astype(BF16)
            mx_s[index, rows, :] = mixed
            return mixed * gate_of(rows)

        def backward(rows, grads):
            parts = {}
            dots = None
            gate = gate_of(rows)
            for (index, degrees, kind, cols, local), grad in zip(infos, grads):
                product = grad * mx_s[index, rows, :]
                dot = (product[:, 0:CH] + product[:, CH:]).astype(F32)
                dots = dot if dots is None else dots + dot
                weighted = mm(grad * gate, wmt[kind]) * nf_s[index, rows, :].astype(F32)
                for side in range(2):
                    part = weighted[:, side * CH : (side + 1) * CH]
                    degree = degrees[side]
                    parts[degree] = parts[degree] + part if degree in parts else part
            dot_ref[rows, :] = dots if quad == 0 else dot_ref[rows, :] + dots
            for degree, part in parts.items():
                ref = grad_refs[degree]
                ref[rows, :] = ref[rows, :] + part if degree in seen else part

        for index, degrees, kind, cols, local in infos:
            own = own_ref[:, cols]
            summed = None
            for step in range(OWN_STEPS):
                rows = own_rows(step)
                message = forward(index, degrees, kind, rows, oh_own[rows, :], own)
                part = mm(spread_own, message)
                summed = part if summed is None else summed + part
            acc_s[index] = summed

        def ghost_forward(step):
            here, rows = ghost_rows(step)
            for index, degrees, kind, cols, local in infos:
                message = forward(index, degrees, kind, rows, oh_gh[here, :], table[:, local])
                acc_s[index] += mm(dt_gh[step], message)

        over_ghost_steps(steps, ghost_forward)

        for index, degrees, kind, cols, local in infos:
            summed_low = (acc_s[index] * norm).astype(BF16)
            updated = own_ref[:, cols].astype(F32) + mm(summed_low, wo[kind])
            at = cols.start - new_base
            new_ref[:, at : at + 2 * CH] = updated.astype(BF16)
            weight = jnp.concatenate(
                [nw_ref[d - 1 : d, :] * (1.0 / (2 * d + 1)) for d in degrees], axis=1
            )
            scale = weight * updated
            energy = scale * updated
            en_ref[...] += energy[:, 0:CH] + energy[:, CH:]
            gs_s[index] = (mm((2.0 * scale).astype(BF16), wot[kind]) * norm).astype(BF16)

        grads_own = [tiled(gs_s[index]) for index in range(len(both))]
        for step in range(OWN_STEPS):
            backward(own_rows(step), grads_own)

        def ghost_backward(step):
            here, rows = ghost_rows(step)
            source = d_gh[here, :]
            backward(rows, [mm(source, gs_s[i]).astype(BF16) for i in range(len(both))])

        over_ghost_steps(steps, ghost_backward)
        for pair in both:
            seen.update(PAIR_DEGREES[pair])


def pair_scratch(atoms, edges, kinds):
    count = len(kinds)
    return [pltpu.VMEM((count, 2 * CH, 2 * CH), BF16) for _ in range(4)] + [
        pltpu.VMEM((2, edges, 2 * CH), BF16),
        pltpu.VMEM((2, edges, 2 * CH), BF16),
        pltpu.VMEM((2, atoms, 2 * CH), F32),
        pltpu.VMEM((2, atoms, 2 * CH), BF16),
    ]


def own_kernel(meta_ref, own_pos_ref, rbf_ref, rad_ref, oh_own, radial_ref, pre_ref, unit_ref):
    atoms = meta_ref.shape[0]
    spacing = spacing_of(atoms, rbf_ref.shape[0])
    own_onehots(meta_ref, oh_own)
    here = tiled(own_pos_ref[...].astype(F32))
    for step in range(OWN_STEPS):
        rows = own_rows(step)
        unit, dist = geometry(mm(oh_own[rows, :], own_pos_ref[...]), here)
        unit_ref[rows, :] = unit
        pre, radial = radial_net(dist, spacing, rbf_ref, rad_ref)
        pre_ref[rows, :] = pre
        for degree in range(5):
            radial_ref[degree, rows, :] = radial[:, degree * CH : (degree + 1) * CH]


def own_stage(meta, own_pos, rbf, rad):
    atoms = meta.shape[0]
    edges = atoms * HALF
    out_shape = (
        struct(edges, atoms, dtype=BF16),
        struct(5, edges, CH, dtype=BF16),
        struct(edges, CH),
        struct(edges, CH),
    )
    return call(own_kernel, "own_edges", out_shape, [], 1 << 31, (meta, own_pos, rbf, rad))


def first_kernel(
    low_ref, mid_ref, high_ref, own_ref, own_pos_ref, meta_ref, rbf_ref, rad_ref, mix_ref,
    out_ref, ew_ref, nw_ref, oh_own, radial_own,
    new_ref, oh_gh, d_gh, dt_gh, radial_gh, pre_ref, unit_ref, m0_ref, gate_ref, nf0_ref,
    gs0_ref, dot_ref, gr1_ref, gr2_ref, en_ref,
    table, sems, ghpos, wm, wmt, wo, wot, nf_s, mx_s, acc_s, gs_s,
):
    pairs = tuple(range(*GROUPS[0]))
    kinds = sorted({PAIR_DEGREES[pair] for pair in pairs})
    copies = fetch((low_ref, mid_ref, high_ref), table, sems)
    atoms = own_ref.shape[0]
    ghosts = table.shape[0]
    spacing = spacing_of(atoms, rbf_ref.shape[0])
    norm = 1.0 / math.sqrt(SLOTS)
    block_diagonal(kinds, mix_ref, out_ref, wm, wmt, wo, wot)

    live = live_ghosts(meta_ref)
    sub_atom = iota((atoms, atoms), 0)
    lane_atom = iota((atoms, atoms), 1)
    live_b = jnp.broadcast_to(live, (atoms, atoms))
    end_row = jnp.sum(jnp.where(sub_atom <= lane_atom, live_b, 0.0), axis=0, keepdims=True)
    live_row = jnp.sum(jnp.where(sub_atom == lane_atom, live_b, 0.0), axis=0, keepdims=True)
    start_row = end_row - live_row
    row_b = jnp.broadcast_to(live_row, (atoms, atoms))
    end_col = jnp.sum(jnp.where(lane_atom <= sub_atom, row_b, 0.0), axis=1, keepdims=True)
    start_col = end_col - live
    total = jnp.sum(live)
    steps = step_count(meta_ref)
    ghost_row = meta_ref[:, HALF:SLOTS] - atoms
    high_part = jnp.floor(ghost_row * (1.0 / 16.0))
    row_high = high_part.astype(BF16)
    row_low = (ghost_row - 16.0 * high_part).astype(BF16)

    row = iota((ghosts, CH), 0)
    lane = iota((ghosts, CH), 1)
    zcells = atoms // 32
    per_y = (zcells + 2) * 8
    ext_x = row // (4 * per_y)
    ext_y = row // per_y % 4
    ext_z = row // 8 % (zcells + 2)

    def side_of(ext, last, size):
        return jnp.where(ext == 0, -size, jnp.where(ext == last, size, 0.0))

    shift = jnp.where(lane == 12, side_of(ext_x, 3, 4.0), 0.0)
    shift = jnp.where(lane == 13, side_of(ext_y, 3, 4.0), shift)
    shift = jnp.where(lane == 14, side_of(ext_z, zcells + 1, 2.0 * zcells), shift)
    for copy in copies:
        copy.wait()
    ghpos[...] = (table[:, table.shape[1] - CH :].astype(F32) + shift).astype(BF16)

    def radial_of(degree, rows):
        return radial_gh[degree, pl.ds(rows.start - OWN_STEPS * STEP, STEP), :]

    def forward0(rows, onehot, feats, radial):
        near = mm(onehot, feats).astype(BF16)
        nf0_ref[rows, :] = near
        mixed = mm(near * radial, mix_ref[0])
        m0_ref[rows, :] = mixed
        gate = jax.nn.sigmoid(mixed)
        gate_ref[rows, :] = gate.astype(BF16)
        return (mixed * gate).astype(BF16)

    own0 = own_ref[:, 0:CH]
    spread_own = own_spread(atoms)
    summed = None
    for step in range(OWN_STEPS):
        rows = own_rows(step)
        message = forward0(rows, oh_own[rows, :], own0, radial_own[0, rows, :])
        part = mm(spread_own, message)
        summed = part if summed is None else summed + part
    acc_s[0, :, 0:CH] = summed

    def ghost_start(step):
        here, rows = ghost_rows(step)
        base = step * STEP
        edge = (iota((STEP, atoms), 0) + base).astype(F32)
        mine = jnp.logical_and(edge >= start_row, edge < end_row).astype(F32)
        source = mine.astype(BF16)
        d_gh[here, :] = source
        edge_t = (iota((atoms, STEP), 1) + base).astype(F32)
        mine_t = jnp.logical_and(edge_t >= start_col, edge_t < end_col)
        spread = mine_t.astype(F32).astype(BF16)
        dt_gh[step, :, :] = spread
        edge_col = edge[:, 0:1]
        slot = edge_col - jnp.sum(mine * start_row, axis=1, keepdims=True)
        listed = mm(source, row_high) * 16.0 + mm(source, row_low)
        at_slot = iota((STEP, HALF), 1).astype(F32) == slot
        which = jnp.sum(jnp.where(at_slot, listed, 0.0), axis=1, keepdims=True)
        which = jnp.where(edge_col < total, which, -1.0)
        onehot = (iota((STEP, ghosts), 1).astype(F32) == which).astype(F32).astype(BF16)
        oh_gh[here, :] = onehot
        unit, dist = geometry(mm(onehot, ghpos[...]), mm(source, own_pos_ref[...]))
        unit_ref[here, :] = unit
        pre, radial = radial_net(dist, spacing, rbf_ref, rad_ref)
        pre_ref[here, :] = pre
        for degree in range(5):
            radial_gh[degree, here, :] = radial[:, degree * CH : (degree + 1) * CH]
        message = forward0(rows, onehot, table[:, 0:CH], radial[:, 0:CH])
        acc_s[0, :, 0:CH] += mm(spread, message)

    over_ghost_steps(steps, ghost_start)

    low0 = (acc_s[0, :, 0:CH] * norm).astype(BF16)
    updated0 = own0.astype(F32) + mm(low0, out_ref[0])
    new_ref[:, 0:CH] = updated0.astype(BF16)
    logistic = jax.nn.sigmoid(updated0)
    weight0 = ew_ref[...]
    en_ref[...] = weight0 * updated0 * logistic
    grad0 = (weight0 * logistic * (1.0 + updated0 * (1.0 - logistic))).astype(BF16)
    gs0_ref[...] = mm_nt(grad0, out_ref[0]) * norm

    def radial_any(degree, rows):
        if isinstance(rows.start, int) and rows.start < OWN_STEPS * STEP:
            return radial_own[degree, rows, :]
        return radial_of(degree, rows)

    run_pairs(
        pairs, kinds, 0, own_ref, table, new_ref, 0, oh_own, oh_gh, d_gh, dt_gh, gate_ref,
        radial_any, nw_ref, steps, wm, wmt, wo, wot, nf_s, mx_s, acc_s, gs_s, dot_ref,
        {1: gr1_ref, 2: gr2_ref}, en_ref,
    )


def any_specs(count, total):
    return [pl.BlockSpec(memory_space=pl.ANY)] * count + [
        pl.BlockSpec(memory_space=SPACE)
    ] * (total - count)


def first_stage(pieces, feats, own_pos, meta, rbf, rad, mix, out, ew, nw, oh_own, radial_own):
    atoms = feats.shape[0]
    half = atoms * HALF
    edges = 2 * half
    width = pieces[0].shape[1]
    ghosts = sum(piece.shape[0] for piece in pieces)
    kinds = sorted({PAIR_DEGREES[pair] for pair in range(*GROUPS[0])})
    out_shape = (
        struct(atoms, width - CH, dtype=BF16),
        struct(half, ghosts, dtype=BF16),
        struct(half, atoms, dtype=BF16),
        struct(half // STEP, atoms, STEP, dtype=BF16),
        struct(5, half, CH, dtype=BF16),
        struct(half, CH),
        struct(half, CH),
        struct(edges, CH),
        struct(edges, CH, dtype=BF16),
        struct(edges, CH, dtype=BF16),
        struct(atoms, CH),
        struct(edges, CH),
        struct(edges, CH),
        struct(edges, CH),
        struct(atoms, CH),
    )
    scratch = [
        pltpu.VMEM((ghosts, width), BF16),
        pltpu.SemaphoreType.DMA((3,)),
        pltpu.VMEM((ghosts, CH), BF16),
    ] + pair_scratch(atoms, edges, kinds)
    args = tuple(pieces) + (
        feats, own_pos, meta, rbf, rad, mix, out, ew, nw, oh_own, radial_own
    )
    return call(
        first_kernel, "first_group", out_shape, scratch, 1 << 33, args, any_specs(3, len(args))
    )


def second_kernel(
    low_ref, mid_ref, high_ref, own_ref, meta_ref, mix_ref, out_ref, nw_ref, oh_own, radial_own,
    oh_gh, d_gh, dt_gh, radial_gh, gate_ref,
    new_ref, dot_ref, gr3_ref, gr4_ref, en_ref,
    table, sems, wm, wmt, wo, wot, nf_s, mx_s, acc_s, gs_s,
):
    pairs = tuple(range(*GROUPS[1]))
    kinds = sorted({PAIR_DEGREES[pair] for pair in pairs})
    copies = fetch((low_ref, mid_ref, high_ref), table, sems)
    block_diagonal(kinds, mix_ref, out_ref, wm, wmt, wo, wot)
    en_ref[...] = jnp.zeros_like(en_ref)
    base = pair_cols(pairs[0]).start

    def radial_any(degree, rows):
        if isinstance(rows.start, int) and rows.start < OWN_STEPS * STEP:
            return radial_own[degree, rows, :]
        return radial_gh[degree, pl.ds(rows.start - OWN_STEPS * STEP, STEP), :]

    for copy in copies:
        copy.wait()
    run_pairs(
        pairs, kinds, base, own_ref, table, new_ref, base, oh_own, oh_gh, d_gh, dt_gh, gate_ref,
        radial_any, nw_ref, step_count(meta_ref), wm, wmt, wo, wot, nf_s, mx_s, acc_s, gs_s,
        dot_ref, {3: gr3_ref, 4: gr4_ref}, en_ref,
    )


def second_stage(pieces, feats, meta, mix, out, nw, oh_own, radial_own, oh_gh, d_gh, dt_gh,
                 radial_gh, gate):
    atoms = feats.shape[0]
    edges = atoms * SLOTS
    width = pieces[0].shape[1]
    ghosts = sum(piece.shape[0] for piece in pieces)
    kinds = sorted({PAIR_DEGREES[pair] for pair in range(*GROUPS[1])})
    out_shape = (
        struct(atoms, width, dtype=BF16),
        struct(edges, CH),
        struct(edges, CH),
        struct(edges, CH),
        struct(atoms, CH),
    )
    scratch = [
        pltpu.VMEM((ghosts, width), BF16),
        pltpu.SemaphoreType.DMA((3,)),
    ] + pair_scratch(atoms, edges, kinds)
    args = tuple(pieces) + (
        feats, meta, mix, out, nw, oh_own, radial_own, oh_gh, d_gh, dt_gh, radial_gh, gate
    )
    return call(
        second_kernel, "second_group", out_shape, scratch, 1 << 33, args,
        any_specs(3, len(args)),
    )


def third_kernel(
    low_ref, mid_ref, high_ref, own_ref, meta_ref, mix_ref, out_ref, nw_ref, oh_own, radial_own,
    oh_gh, d_gh, dt_gh, radial_gh, gate_ref,
    rbf_ref, rad_ref, pre_own, pre_gh, unit_own, unit_gh, m0_ref, nf0_ref, gs0_ref,
    dot_a, dot_b, gr1_ref, gr2_ref, gr3_ref, gr4_a, en_a, en_b, new_a, new_b,
    new_ref, energy_ref, fown_ref, flow_ref, fmid_ref, fhigh_ref,
    table, sems, wm, wmt, wo, wot, nf_s, mx_s, acc_s, gs_s,
    dot_c, gr4_b, en_s, radt, rbft, src_s, fgh_s,
):
    pairs = tuple(range(*GROUPS[2]))
    kinds = sorted({PAIR_DEGREES[pair] for pair in pairs})
    copies = fetch((low_ref, mid_ref, high_ref), table, sems)
    atoms = own_ref.shape[0]
    nbasis = rbf_ref.shape[0]
    spacing = spacing_of(atoms, nbasis)
    block_diagonal(kinds, mix_ref, out_ref, wm, wmt, wo, wot)
    for degree in range(5):
        part = slice(degree * CH, (degree + 1) * CH)
        radt[part, :] = flip(rad_ref[:, part])
    for index in range(nbasis // CH):
        part = slice(index * CH, (index + 1) * CH)
        rbft[:, part] = flip(rbf_ref[part, :])
    mix0_t = flip(mix_ref[0])
    en_s[...] = en_a[...] + en_b[...]
    new_ref[:, 0 : new_a.shape[1]] = new_a[...]
    new_ref[:, new_a.shape[1] : new_a.shape[1] + new_b.shape[1]] = new_b[...]
    base = pair_cols(pairs[0]).start
    steps = step_count(meta_ref)

    def radial_any(degree, rows):
        if isinstance(rows.start, int) and rows.start < OWN_STEPS * STEP:
            return radial_own[degree, rows, :]
        return radial_gh[degree, pl.ds(rows.start - OWN_STEPS * STEP, STEP), :]

    for copy in copies:
        copy.wait()
    run_pairs(
        pairs, kinds, base, own_ref, table, new_ref, 0, oh_own, oh_gh, d_gh, dt_gh, gate_ref,
        radial_any, nw_ref, steps, wm, wmt, wo, wot, nf_s, mx_s, acc_s, gs_s, dot_c,
        {4: gr4_b}, en_s,
    )

    def finish(rows, grad, pre, unit):
        mixed = m0_ref[rows, :]
        gate = jax.nn.sigmoid(mixed)
        dot = dot_a[rows, :] + dot_b[rows, :] + dot_c[rows, :]
        first = grad * gate * (1.0 + mixed * (1.0 - gate)) + dot * gate * (1.0 - gate)
        weighted = mm(first.astype(BF16), mix0_t) * nf0_ref[rows, :].astype(F32)
        parts = [weighted, gr1_ref[rows, :], gr2_ref[rows, :], gr3_ref[rows, :]]
        parts.append(gr4_a[rows, :] + gr4_b[rows, :])
        radial_grad = jnp.concatenate([part.astype(BF16) for part in parts], axis=1)
        hidden_grad = mm(radial_grad, radt[...])
        logistic = jax.nn.sigmoid(pre)
        pre_grad = (hidden_grad * logistic * (1.0 + pre * (1.0 - logistic))).astype(BF16)
        centred = centred_of(unit[:, 3:4], spacing, nbasis)
        slope = jnp.exp(-0.5 * centred * centred) * centred
        basis_grad = mm(pre_grad, rbft[...])
        dist_grad = jnp.sum(basis_grad * slope, axis=1, keepdims=True) * (-1.0 / spacing)
        pull = unit * dist_grad
        across = pull.T[0:8, :]
        top = across.astype(BF16)
        rest = (across - top.astype(F32)).astype(BF16)
        return pull, top, rest

    fgh_s[...] = jnp.zeros_like(fgh_s)
    src_s[...] = jnp.zeros_like(src_s)
    gs0 = gs0_ref[...]
    gs0_low = gs0.astype(BF16)

    def ghost_finish(step):
        here, rows = ghost_rows(step)
        grad = mm(d_gh[here, :], gs0_low)
        pull, top, rest = finish(rows, grad, pre_gh[here, :], unit_gh[here, :])
        pull_top = pull.astype(BF16)
        pull_rest = (pull - pull_top.astype(F32)).astype(BF16)
        spread = dt_gh[step]
        src_s[...] += mm(spread, pull_top) + mm(spread, pull_rest)
        onehot = oh_gh[here, :]
        fgh_s[...] += mm(top, onehot) + mm(rest, onehot)

    over_ghost_steps(steps, ghost_finish)
    low, mid = flow_ref.shape[1], fmid_ref.shape[1]
    flow_ref[...] = fgh_s[:, 0:low]
    fmid_ref[...] = fgh_s[:, low : low + mid]
    fhigh_ref[...] = fgh_s[:, low + mid :]

    grad_own = tiled(gs0)
    src = src_s[...]
    onto = jnp.zeros((8, atoms), F32)
    for step in range(OWN_STEPS):
        rows = own_rows(step)
        pull, top, rest = finish(rows, grad_own, pre_own[rows, :], unit_own[rows, :])
        src += jnp.sum(pull.reshape(STEP // atoms, atoms, CH), axis=0)
        onehot = oh_own[rows, :]
        onto += mm(top, onehot) + mm(rest, onehot)
    fown_ref[...] = onto - src.T[0:8, :]
    energy_ref[...] = jnp.sum(en_s[...].T, axis=0, keepdims=True)


def third_stage(pieces, feats, *rest):
    atoms, feat = feats.shape
    edges = atoms * SLOTS
    width = pieces[0].shape[1]
    sizes = [piece.shape[0] for piece in pieces]
    ghosts = sum(sizes)
    nbasis = rest[11].shape[0]
    kinds = sorted({PAIR_DEGREES[pair] for pair in range(*GROUPS[2])})
    out_shape = (
        struct(atoms, feat, dtype=BF16),
        struct(1, atoms),
        struct(8, atoms),
    ) + tuple(struct(8, size) for size in sizes)
    scratch = [
        pltpu.VMEM((ghosts, width), BF16),
        pltpu.SemaphoreType.DMA((3,)),
    ] + pair_scratch(atoms, edges, kinds) + [
        pltpu.VMEM((edges, CH), F32),
        pltpu.VMEM((edges, CH), F32),
        pltpu.VMEM((atoms, CH), F32),
        pltpu.VMEM((5 * CH, CH), BF16),
        pltpu.VMEM((CH, nbasis), BF16),
        pltpu.VMEM((atoms, CH), F32),
        pltpu.VMEM((8, ghosts), F32),
    ]
    args = tuple(pieces) + (feats,) + rest
    return call(
        third_kernel, "third_group", out_shape, scratch, 1 << 33, args, any_specs(3, len(args))
    )


def layer(pieces, feats, own_pos, meta, rbf, rad, mix, out, ew, nw):
    oh_own, radial_own, pre_own, unit_own = own_stage(meta, own_pos, rbf, rad)
    (
        new_a, oh_gh, d_gh, dt_gh, radial_gh, pre_gh, unit_gh, m0, gate, nf0, gs0, dot_a, gr1,
        gr2, en_a,
    ) = first_stage(
        pieces[0], feats, own_pos, meta, rbf, rad, mix, out, ew, nw, oh_own, radial_own
    )
    new_b, dot_b, gr3, gr4, en_b = second_stage(
        pieces[1], feats, meta, mix, out, nw, oh_own, radial_own, oh_gh, d_gh, dt_gh, radial_gh,
        gate,
    )
    return third_stage(
        pieces[2], feats, meta, mix, out, nw, oh_own, radial_own, oh_gh, d_gh, dt_gh, radial_gh,
        gate, rbf, rad, pre_own, pre_gh, unit_own, unit_gh, m0, nf0, gs0, dot_a, dot_b, gr1, gr2,
        gr3, gr4, en_a, en_b, new_a, new_b,
    )


def ring(axis):
    peers = lax.axis_size(axis)
    up = [(i, (i + 1) % peers) for i in range(peers)]
    return up, [(j, i) for i, j in up]


def neighbours_of(block, axis, dim):
    up, down = ring(axis)
    length = block.shape[dim]
    if len(up) == 2 and length == 2:
        other = lax.ppermute(block, axis, up)
        return (
            lax.slice_in_dim(other, length - 1, length, axis=dim),
            lax.slice_in_dim(other, 0, 1, axis=dim),
        )
    before = lax.ppermute(lax.slice_in_dim(block, length - 1, length, axis=dim), axis, up)
    after = lax.ppermute(lax.slice_in_dim(block, 0, 1, axis=dim), axis, down)
    return before, after


def exchange(cells):
    block = cells.reshape(2, 2, 2, 8, cells.shape[1])
    for axis, dim in (("gz", 2), ("gy", 1)):
        before, after = neighbours_of(block, axis, dim)
        block = jnp.concatenate([before, block, after], axis=dim)
    before, after = neighbours_of(block, "gx", 0)
    return tuple(piece.reshape(-1, cells.shape[1]) for piece in (before, block, after))


def forces_kernel(mid_ref, low_ref, high_ref, own_ref, meta_ref, out_ref):
    atoms = own_ref.shape[1]
    values = mid_ref[...]
    lanes = values.shape[1]
    lane = iota(values.shape, 1)
    ext_z = lane // 8 % 4
    values += jnp.where(ext_z == 1, pltpu.roll(low_ref[...], lanes - 16, 1), 0.0)
    values += jnp.where(ext_z == 2, pltpu.roll(high_ref[...], 16, 1), 0.0)
    lane = iota((atoms, lanes), 1)
    ext_x, ext_y, ext_z = lane // 128, lane // 32 % 4, lane // 8 % 4
    slot = ((2 * ext_x + ext_y - 1) * 2 + ext_z - 1) * 8 + lane % 8
    inside = jnp.logical_and(
        jnp.logical_or(ext_y == 1, ext_y == 2), jnp.logical_or(ext_z == 1, ext_z == 2)
    )
    to_slot = jnp.logical_and(iota((atoms, lanes), 0) == slot, inside)
    to_slot = to_slot.astype(F32).astype(BF16)
    order = meta_ref[:, SLOTS + 1 : SLOTS + 2]
    to_atom = (order == iota((atoms, atoms), 1).astype(F32)).astype(F32).astype(BF16)
    total = own_ref[...]
    for _ in range(3):
        top = values.astype(BF16)
        values = values - top.astype(F32)
        total += mm(mm_nt(top, to_slot).astype(BF16), to_atom)
    for comp in range(3):
        out_ref[comp] = -total[comp : comp + 1, :]


def give_back(low, mid, high, own, meta):
    up, down = ring("gx")
    from_low = lax.ppermute(high, "gx", up)
    from_high = lax.ppermute(low, "gx", down)
    mid = mid + jnp.concatenate([from_low, from_high], axis=1)
    up, down = ring("gy")
    from_low = lax.ppermute(mid, "gy", up)
    from_high = lax.ppermute(mid, "gy", down)
    ext_y = jnp.arange(mid.shape[1], dtype=jnp.int32)[None] // 32 % 4
    mid = (
        mid
        + jnp.where(ext_y == 1, jnp.roll(from_low, -64, axis=1), 0.0)
        + jnp.where(ext_y == 2, jnp.roll(from_high, 64, axis=1), 0.0)
    )
    up, down = ring("gz")
    from_low = lax.ppermute(mid, "gz", up)
    from_high = from_low if len(up) == 2 else lax.ppermute(mid, "gz", down)
    args = (mid, from_low, from_high, own, meta)
    out_shape = (struct(3, 1, own.shape[1]),)
    return call(forces_kernel, "forces", out_shape, [], 1 << 20, args)[0]


def local(
    features,
    positions,
    neighbours,
    counts,
    cell_atoms,
    rbf_weight,
    radial_weight,
    mix_weight,
    out_weight,
    energy_weight,
    norm_weight,
):
    feats = features[0, 0, 0]
    places = jnp.swapaxes(positions[0, 0], 0, 1)
    *cells, own_pos, meta = make_cells(
        feats, places, neighbours[0, 0, 0].T, counts[0, 0], cell_atoms[0, 0]
    )
    pieces = [exchange(part) for part in cells]
    new, energy, own, low, mid, high = layer(
        pieces, feats, own_pos, meta, rbf_weight, radial_weight, mix_weight, out_weight,
        energy_weight[None], norm_weight,
    )
    forces = give_back(low, mid, high, own, meta)
    return (
        new[None, None, None],
        energy[None, None],
        jnp.swapaxes(forces, 0, 1)[None, None],
    )


def solution(mesh):
    split = P("gx", "gy", "gz", None, None)
    flat = P("gx", "gy", "gz", None)
    return jax.shard_map(
        local,
        mesh=mesh,
        in_specs=(split, split, split, flat, flat, P(), P(), P(), P(), P(), P()),
        out_specs=(split, flat, split),
        check_vma=False,
    )
```

```python
import functools
import math

import jax
import jax.numpy as jnp
from jax import lax
from jax.experimental import pallas as pl
from jax.experimental.pallas import tpu as pltpu
from jax.sharding import PartitionSpec as P

F32 = jnp.float32
BF16 = jnp.bfloat16
CH = 128
SLOTS = 32
HALF = 16
STEP = 256
OWN_STEPS = 4
GH_STEPS = 2
VMEM = 56 * 1024 * 1024
SPACE = pltpu.VMEM
PAIR_DEGREES = (
    (1, 1), (1, 2), (2, 2), (2, 2),
    (3, 3), (3, 3), (3, 3), (3, 4),
    (4, 4), (4, 4), (4, 4), (4, 4),
)
GROUPS = ((0, 4), (4, 8), (8, 12))


def mm(a, b):
    return jnp.dot(a, b, preferred_element_type=F32)


def mm_nt(a, b):
    return lax.dot_general(a, b, (((1,), (1,)), ((), ())), preferred_element_type=F32)


def iota(shape, dim):
    return lax.broadcasted_iota(jnp.int32, shape, dim)


def flip(w):
    return w.astype(F32).T.astype(BF16)


def pair_cols(pair):
    return slice(CH + pair * 2 * CH, CH + (pair + 1) * 2 * CH)


def struct(*shape, dtype=F32):
    return jax.ShapeDtypeStruct(shape, dtype)


def call(kernel, name, out_shape, scratch, flops, args, specs=None):
    size = sum(a.size * a.dtype.itemsize for a in list(args) + list(out_shape))
    return pl.pallas_call(
        kernel,
        out_shape=out_shape,
        in_specs=specs or [pl.BlockSpec(memory_space=SPACE)] * len(args),
        out_specs=tuple(pl.BlockSpec(memory_space=SPACE) for _ in out_shape),
        scratch_shapes=scratch,
        compiler_params=pltpu.CompilerParams(vmem_limit_bytes=VMEM),
        cost_estimate=pl.CostEstimate(flops=flops, bytes_accessed=size, transcendentals=0),
        name=name,
    )(*args)


def cells_kernel(feat_ref, pos_ref, near_ref, counts_ref, order_ref, *refs):
    out_refs, (own_pos_ref, meta_ref, rows_ref, pos_rows) = refs[:3], refs[3:]
    atoms = feat_ref.shape[0]
    rows_ref[...] = jnp.zeros_like(rows_ref)
    rows_ref[0:SLOTS, :] = near_ref[...].astype(F32)
    rows_ref[SLOTS : SLOTS + 1, :] = counts_ref[...].astype(F32)
    rows_ref[SLOTS + 1 : SLOTS + 2, :] = order_ref[...].astype(F32)
    meta = rows_ref[...].T
    meta_ref[...] = meta
    pos_rows[...] = jnp.zeros_like(pos_rows)
    for comp in range(3):
        places = pos_ref[comp]
        first = places.astype(BF16).astype(F32)
        second = (places - first).astype(BF16).astype(F32)
        pos_rows[comp : comp + 1, :] = first
        pos_rows[4 + comp : 5 + comp, :] = second
        pos_rows[8 + comp : 9 + comp, :] = places - first - second
    pieces = pos_rows[...].astype(BF16)
    lane = iota((atoms, atoms), 1).astype(F32)
    pick = (meta[:, SLOTS + 1 : SLOTS + 2] == lane).astype(F32).astype(BF16)
    same = (iota((atoms, atoms), 0) == iota((atoms, atoms), 1)).astype(F32).astype(BF16)
    own_pos_ref[...] = mm_nt(same, pieces).astype(BF16)
    for group, (begin, end) in enumerate(GROUPS):
        at = 0 if group == 0 else pair_cols(begin).start
        till = pair_cols(end - 1).stop
        out_refs[group][:, 0 : till - at] = mm(pick, feat_ref[:, at:till]).astype(BF16)
        if group == 0:
            out_refs[group][:, till:] = mm_nt(pick, pieces).astype(BF16)


def make_cells(feats, places, near, counts, order):
    atoms = feats.shape[0]
    widths = [CH * 2 * (end - begin) for begin, end in GROUPS]
    widths[0] += 2 * CH
    out_shape = tuple(struct(atoms, width, dtype=BF16) for width in widths) + (
        struct(atoms, CH, dtype=BF16),
        struct(atoms, CH),
    )
    scratch = [pltpu.VMEM((CH, atoms), F32), pltpu.VMEM((CH, atoms), F32)]
    args = (feats, places, near, counts, order)
    return call(cells_kernel, "cells", out_shape, scratch, 1 << 26, args)


def spacing_of(atoms, nbasis):
    depth = atoms // 16
    return 2.0 * math.sqrt(32.0 + depth * depth) / (nbasis - 1)


def own_onehots(meta_ref, oh_own):
    atoms = meta_ref.shape[0]
    counts = meta_ref[:, SLOTS : SLOTS + 1]
    lane_atom = iota((atoms, atoms), 1).astype(F32)
    for slot in range(HALF):
        hit = jnp.logical_and(meta_ref[:, slot : slot + 1] == lane_atom, counts > slot)
        oh_own[slot * atoms : (slot + 1) * atoms, :] = hit.astype(F32).astype(BF16)


def geometry(near, here):
    diff = near - here
    rel = (diff + pltpu.roll(diff, CH - 4, 1)) + (
        pltpu.roll(diff, CH - 8, 1) + pltpu.roll(diff, CH - 12, 1)
    )
    lane = iota(rel.shape, 1)
    rel = jnp.where(lane < 3, rel, 0.0)
    square = jnp.sum(rel * rel, axis=1, keepdims=True)
    inverse = lax.rsqrt(jnp.where(square > 0.0, square, 1.0))
    dist = square * inverse
    return jnp.where(lane == 3, dist, rel * inverse), dist


def centred_of(dist, spacing, nbasis):
    return dist * (1.0 / spacing) - iota((dist.shape[0], nbasis), 1).astype(F32)


def radial_net(dist, spacing, rbf_ref, rad_ref):
    centred = centred_of(dist, spacing, rbf_ref.shape[0])
    basis = jnp.exp(-0.5 * centred * centred)
    pre = mm(basis.astype(BF16), rbf_ref[...])
    hidden = (pre * jax.nn.sigmoid(pre)).astype(BF16)
    return pre, mm(hidden, rad_ref[...]).astype(BF16)


def own_spread(atoms, size=STEP):
    shape = (atoms, size)
    return (iota(shape, 1) % atoms == iota(shape, 0)).astype(F32).astype(BF16)


def tiled(values, size=STEP):
    return jnp.concatenate([values] * (size // values.shape[0]), axis=0)


def live_ghosts(meta_ref):
    return jnp.maximum(meta_ref[:, SLOTS : SLOTS + 1] - HALF, 0.0)


def step_count(meta_ref):
    total = jnp.sum(live_ghosts(meta_ref)).astype(jnp.int32)
    rows = GH_STEPS * STEP
    return jnp.maximum((total + (rows - 1)) // rows, 1) * GH_STEPS


def own_rows(step, size=STEP):
    return pl.ds(step * size, size)


def ghost_rows(step, size=STEP):
    first = OWN_STEPS * STEP
    if isinstance(step, int):
        return pl.ds(step * size, size), pl.ds(first + step * size, size)
    base = pl.multiple_of(step * size, size)
    return pl.ds(base, size), pl.ds(pl.multiple_of(first + base, size), size)


def over_ghost_steps(steps, body, size=STEP):
    static = GH_STEPS * STEP // size
    for step in range(static):
        body(step)

    def again(step, carry):
        body(step)
        return carry

    lax.fori_loop(static, (steps * STEP + (size - 1)) // size, again, 0)


def block_diagonal(kinds, mix_ref, out_ref, wm, wmt, wo, wot):
    zero = jnp.zeros((CH, CH), BF16)
    for kind, both in enumerate(kinds):
        for ref in (wm, wmt, wo, wot):
            ref[kind, 0:CH, CH:] = zero
            ref[kind, CH:, 0:CH] = zero
    for degree in sorted({d for both in kinds for d in both}):
        mix, out = mix_ref[degree], out_ref[degree]
        mix_t, out_t = flip(mix), flip(out)
        for kind, both in enumerate(kinds):
            for side in range(2):
                if both[side] == degree:
                    part = slice(side * CH, side * CH + CH)
                    wm[kind, part, part] = mix
                    wmt[kind, part, part] = mix_t
                    wo[kind, part, part] = out
                    wot[kind, part, part] = out_t


def fetch(pieces, table, sems):
    copies = []
    at = 0
    for index, piece in enumerate(pieces):
        rows = piece.shape[0]
        copies.append(
            pltpu.make_async_copy(piece, table.at[pl.ds(at, rows), :], sems.at[index])
        )
        at += rows
    for copy in copies:
        copy.start()
    return copies


def run_pairs(
    pairs, kinds, first_col, own_ref, table, new_ref, new_base, oh_own, oh_gh, d_gh, dt_gh,
    gate_ref, radial_of, nw_ref, steps, wm, wmt, wo, wot, nf_s, mx_s, acc_s, gs_s, dot_ref,
    grad_refs, en_ref, size=STEP,
):
    atoms = own_ref.shape[0]
    norm = 1.0 / math.sqrt(SLOTS)
    spread_own = own_spread(atoms, size)
    own_steps = OWN_STEPS * STEP // size
    begin, end = pair_cols(pairs[0]).start, pair_cols(pairs[-1]).stop
    own_cols = slice(begin, end)
    table_cols = slice(begin - first_col, end - first_col)
    infos = []
    for index, pair in enumerate(pairs):
        degrees = PAIR_DEGREES[pair]
        infos.append((slice(index * 2 * CH, (index + 1) * 2 * CH), degrees, kinds.index(degrees)))

    def gate_of(rows):
        gate = gate_ref[rows, :]
        return jnp.concatenate([gate, gate], axis=1)

    def forward(rows, onehot, feats):
        near = mm(onehot, feats).astype(BF16)
        nf_s[rows, :] = near
        gate = gate_of(rows)
        messages = []
        for cols, degrees, kind in infos:
            radial = jnp.concatenate([radial_of(d, rows) for d in degrees], axis=1)
            mixed = mm(near[:, cols] * radial, wm[kind]).astype(BF16)
            mx_s[rows, cols] = mixed
            messages.append(mixed * gate)
        return jnp.concatenate(messages, axis=1)

    def backward(rows, grad):
        parts = {}
        dots = None
        gate = gate_of(rows)
        for cols, degrees, kind in infos:
            product = grad[:, cols] * mx_s[rows, cols]
            dot = (product[:, 0:CH] + product[:, CH:]).astype(F32)
            dots = dot if dots is None else dots + dot
            weighted = mm(grad[:, cols] * gate, wmt[kind]) * nf_s[rows, cols].astype(F32)
            for side in range(2):
                part = weighted[:, side * CH : (side + 1) * CH]
                degree = degrees[side]
                parts[degree] = parts[degree] + part if degree in parts else part
        dot_ref[rows, :] = dots
        for degree, part in parts.items():
            grad_refs[degree][rows, :] = part

    own = own_ref[:, own_cols]
    summed = None
    for step in range(own_steps):
        rows = own_rows(step, size)
        part = mm(spread_own, forward(rows, oh_own[rows, :], own))
        summed = part if summed is None else summed + part
    acc_s[...] = summed

    def ghost_forward(step):
        here, rows = ghost_rows(step, size)
        message = forward(rows, oh_gh[here, :], table[:, table_cols])
        acc_s[...] += mm(dt_gh[:, here], message)

    over_ghost_steps(steps, ghost_forward, size)

    for cols, degrees, kind in infos:
        summed_low = (acc_s[:, cols] * norm).astype(BF16)
        updated = own[:, cols].astype(F32) + mm(summed_low, wo[kind])
        at = begin - new_base + cols.start
        new_ref[:, at : at + 2 * CH] = updated.astype(BF16)
        weight = jnp.concatenate(
            [nw_ref[d - 1 : d, :] * (1.0 / (2 * d + 1)) for d in degrees], axis=1
        )
        scale = weight * updated
        energy = scale * updated
        en_ref[...] += energy[:, 0:CH] + energy[:, CH:]
        gs_s[:, cols] = (mm((2.0 * scale).astype(BF16), wot[kind]) * norm).astype(BF16)

    grad_own = tiled(gs_s[...], size)
    for step in range(own_steps):
        backward(own_rows(step, size), grad_own)

    def ghost_backward(step):
        here, rows = ghost_rows(step, size)
        backward(rows, mm(d_gh[here, :], gs_s[...]).astype(BF16))

    over_ghost_steps(steps, ghost_backward, size)


def pair_scratch(atoms, edges, kinds):
    count = len(kinds)
    return [pltpu.VMEM((count, 2 * CH, 2 * CH), BF16) for _ in range(4)] + [
        pltpu.VMEM((edges, 8 * CH), BF16),
        pltpu.VMEM((edges, 8 * CH), BF16),
        pltpu.VMEM((atoms, 8 * CH), F32),
        pltpu.VMEM((atoms, 8 * CH), BF16),
    ]


def own_kernel(meta_ref, own_pos_ref, rbf_ref, rad_ref, oh_own, radial_ref, pre_ref, unit_ref):
    atoms = meta_ref.shape[0]
    spacing = spacing_of(atoms, rbf_ref.shape[0])
    own_onehots(meta_ref, oh_own)
    here = tiled(own_pos_ref[...].astype(F32))
    for step in range(OWN_STEPS):
        rows = own_rows(step)
        unit, dist = geometry(mm(oh_own[rows, :], own_pos_ref[...]), here)
        unit_ref[rows, :] = unit
        pre, radial = radial_net(dist, spacing, rbf_ref, rad_ref)
        pre_ref[rows, :] = pre
        for degree in range(5):
            radial_ref[degree, rows, :] = radial[:, degree * CH : (degree + 1) * CH]


def own_stage(meta, own_pos, rbf, rad):
    atoms = meta.shape[0]
    edges = atoms * HALF
    out_shape = (
        struct(edges, atoms, dtype=BF16),
        struct(5, edges, CH, dtype=BF16),
        struct(edges, CH),
        struct(edges, CH),
    )
    return call(own_kernel, "own_edges", out_shape, [], 1 << 31, (meta, own_pos, rbf, rad))


def first_kernel(
    low_ref, mid_ref, high_ref, own_ref, own_pos_ref, meta_ref, rbf_ref, rad_ref, mix_ref,
    out_ref, ew_ref, nw_ref, oh_own, radial_own,
    new_ref, oh_gh, d_gh, dt_gh, radial_gh, pre_ref, unit_ref, m0_ref, gate_ref, nf0_ref,
    gs0_ref, dot_ref, gr1_ref, gr2_ref, en_ref,
    table, sems, ghpos, wm, wmt, wo, wot, nf_s, mx_s, acc_s, gs_s,
):
    pairs = tuple(range(*GROUPS[0]))
    kinds = sorted({PAIR_DEGREES[pair] for pair in pairs})
    copies = fetch((low_ref, mid_ref, high_ref), table, sems)
    atoms = own_ref.shape[0]
    ghosts = table.shape[0]
    spacing = spacing_of(atoms, rbf_ref.shape[0])
    norm = 1.0 / math.sqrt(SLOTS)
    block_diagonal(kinds, mix_ref, out_ref, wm, wmt, wo, wot)

    live = live_ghosts(meta_ref)
    sub_atom = iota((atoms, atoms), 0)
    lane_atom = iota((atoms, atoms), 1)
    live_b = jnp.broadcast_to(live, (atoms, atoms))
    end_row = jnp.sum(jnp.where(sub_atom <= lane_atom, live_b, 0.0), axis=0, keepdims=True)
    live_row = jnp.sum(jnp.where(sub_atom == lane_atom, live_b, 0.0), axis=0, keepdims=True)
    start_row = end_row - live_row
    row_b = jnp.broadcast_to(live_row, (atoms, atoms))
    end_col = jnp.sum(jnp.where(lane_atom <= sub_atom, row_b, 0.0), axis=1, keepdims=True)
    start_col = end_col - live
    total = jnp.sum(live)
    steps = step_count(meta_ref)
    ghost_row = meta_ref[:, HALF:SLOTS] - atoms
    high_part = jnp.floor(ghost_row * (1.0 / 16.0))
    row_high = high_part.astype(BF16)
    row_low = (ghost_row - 16.0 * high_part).astype(BF16)

    row = iota((ghosts, CH), 0)
    lane = iota((ghosts, CH), 1)
    zcells = atoms // 32
    per_y = (zcells + 2) * 8
    ext_x = row // (4 * per_y)
    ext_y = row // per_y % 4
    ext_z = row // 8 % (zcells + 2)

    def side_of(ext, last, size):
        return jnp.where(ext == 0, -size, jnp.where(ext == last, size, 0.0))

    shift = jnp.where(lane == 12, side_of(ext_x, 3, 4.0), 0.0)
    shift = jnp.where(lane == 13, side_of(ext_y, 3, 4.0), shift)
    shift = jnp.where(lane == 14, side_of(ext_z, zcells + 1, 2.0 * zcells), shift)
    for copy in copies:
        copy.wait()
    ghpos[...] = (table[:, table.shape[1] - CH :].astype(F32) + shift).astype(BF16)

    def forward0(rows, onehot, feats, radial):
        near = mm(onehot, feats).astype(BF16)
        nf0_ref[rows, :] = near
        mixed = mm(near * radial, mix_ref[0])
        m0_ref[rows, :] = mixed
        gate = jax.nn.sigmoid(mixed)
        gate_ref[rows, :] = gate.astype(BF16)
        return (mixed * gate).astype(BF16)

    own0 = own_ref[:, 0:CH]
    spread_own = own_spread(atoms)
    summed = None
    for step in range(OWN_STEPS):
        rows = own_rows(step)
        message = forward0(rows, oh_own[rows, :], own0, radial_own[0, rows, :])
        part = mm(spread_own, message)
        summed = part if summed is None else summed + part
    acc_s[:, 0:CH] = summed

    def ghost_start(step):
        here, rows = ghost_rows(step)
        base = step * STEP
        edge = (iota((STEP, atoms), 0) + base).astype(F32)
        mine = jnp.logical_and(edge >= start_row, edge < end_row).astype(F32)
        source = mine.astype(BF16)
        d_gh[here, :] = source
        edge_t = (iota((atoms, STEP), 1) + base).astype(F32)
        mine_t = jnp.logical_and(edge_t >= start_col, edge_t < end_col)
        spread = mine_t.astype(F32).astype(BF16)
        dt_gh[:, here] = spread
        edge_col = edge[:, 0:1]
        slot = edge_col - jnp.sum(mine * start_row, axis=1, keepdims=True)
        listed = mm(source, row_high) * 16.0 + mm(source, row_low)
        at_slot = iota((STEP, HALF), 1).astype(F32) == slot
        which = jnp.sum(jnp.where(at_slot, listed, 0.0), axis=1, keepdims=True)
        which = jnp.where(edge_col < total, which, -1.0)
        onehot = (iota((STEP, ghosts), 1).astype(F32) == which).astype(F32).astype(BF16)
        oh_gh[here, :] = onehot
        unit, dist = geometry(mm(onehot, ghpos[...]), mm(source, own_pos_ref[...]))
        unit_ref[here, :] = unit
        pre, radial = radial_net(dist, spacing, rbf_ref, rad_ref)
        pre_ref[here, :] = pre
        for degree in range(5):
            radial_gh[degree, here, :] = radial[:, degree * CH : (degree + 1) * CH]
        message = forward0(rows, onehot, table[:, 0:CH], radial[:, 0:CH])
        acc_s[:, 0:CH] += mm(spread, message)

    over_ghost_steps(steps, ghost_start)

    low0 = (acc_s[:, 0:CH] * norm).astype(BF16)
    updated0 = own0.astype(F32) + mm(low0, out_ref[0])
    new_ref[:, 0:CH] = updated0.astype(BF16)
    logistic = jax.nn.sigmoid(updated0)
    weight0 = ew_ref[...]
    en_ref[...] = weight0 * updated0 * logistic
    grad0 = (weight0 * logistic * (1.0 + updated0 * (1.0 - logistic))).astype(BF16)
    gs0_ref[...] = mm_nt(grad0, out_ref[0]) * norm

    def radial_any(degree, rows):
        if isinstance(rows.start, int) and rows.start < OWN_STEPS * STEP:
            return radial_own[degree, rows, :]
        return radial_gh[degree, pl.ds(rows.start - OWN_STEPS * STEP, rows.size), :]

    run_pairs(
        pairs, kinds, 0, own_ref, table, new_ref, 0, oh_own, oh_gh, d_gh, dt_gh, gate_ref,
        radial_any, nw_ref, steps, wm, wmt, wo, wot, nf_s, mx_s, acc_s, gs_s, dot_ref,
        {1: gr1_ref, 2: gr2_ref}, en_ref,
    )


def any_specs(count, total):
    return [pl.BlockSpec(memory_space=pl.ANY)] * count + [
        pl.BlockSpec(memory_space=SPACE)
    ] * (total - count)


def first_stage(pieces, feats, own_pos, meta, rbf, rad, mix, out, ew, nw, oh_own, radial_own):
    atoms = feats.shape[0]
    half = atoms * HALF
    edges = 2 * half
    width = pieces[0].shape[1]
    ghosts = sum(piece.shape[0] for piece in pieces)
    kinds = sorted({PAIR_DEGREES[pair] for pair in range(*GROUPS[0])})
    out_shape = (
        struct(atoms, width - CH, dtype=BF16),
        struct(half, ghosts, dtype=BF16),
        struct(half, atoms, dtype=BF16),
        struct(atoms, half, dtype=BF16),
        struct(5, half, CH, dtype=BF16),
        struct(half, CH),
        struct(half, CH),
        struct(edges, CH),
        struct(edges, CH, dtype=BF16),
        struct(edges, CH, dtype=BF16),
        struct(atoms, CH),
        struct(edges, CH),
        struct(edges, CH),
        struct(edges, CH),
        struct(atoms, CH),
    )
    scratch = [
        pltpu.VMEM((ghosts, width), BF16),
        pltpu.SemaphoreType.DMA((3,)),
        pltpu.VMEM((ghosts, CH), BF16),
    ] + pair_scratch(atoms, edges, kinds)
    args = tuple(pieces) + (
        feats, own_pos, meta, rbf, rad, mix, out, ew, nw, oh_own, radial_own
    )
    return call(
        first_kernel, "first_group", out_shape, scratch, 1 << 33, args, any_specs(3, len(args))
    )


def second_kernel(
    low_ref, mid_ref, high_ref, own_ref, meta_ref, mix_ref, out_ref, nw_ref, oh_own, radial_own,
    oh_gh, d_gh, dt_gh, radial_gh, gate_ref,
    new_ref, dot_ref, gr3_ref, gr4_ref, en_ref,
    table, sems, wm, wmt, wo, wot, nf_s, mx_s, acc_s, gs_s,
):
    pairs = tuple(range(*GROUPS[1]))
    kinds = sorted({PAIR_DEGREES[pair] for pair in pairs})
    copies = fetch((low_ref, mid_ref, high_ref), table, sems)
    block_diagonal(kinds, mix_ref, out_ref, wm, wmt, wo, wot)
    en_ref[...] = jnp.zeros_like(en_ref)
    base = pair_cols(pairs[0]).start

    def radial_any(degree, rows):
        if isinstance(rows.start, int) and rows.start < OWN_STEPS * STEP:
            return radial_own[degree, rows, :]
        return radial_gh[degree, pl.ds(rows.start - OWN_STEPS * STEP, rows.size), :]

    for copy in copies:
        copy.wait()
    run_pairs(
        pairs, kinds, base, own_ref, table, new_ref, base, oh_own, oh_gh, d_gh, dt_gh, gate_ref,
        radial_any, nw_ref, step_count(meta_ref), wm, wmt, wo, wot, nf_s, mx_s, acc_s, gs_s,
        dot_ref, {3: gr3_ref, 4: gr4_ref}, en_ref,
    )


def second_stage(pieces, feats, meta, mix, out, nw, oh_own, radial_own, oh_gh, d_gh, dt_gh,
                 radial_gh, gate):
    atoms = feats.shape[0]
    edges = atoms * SLOTS
    width = pieces[0].shape[1]
    ghosts = sum(piece.shape[0] for piece in pieces)
    kinds = sorted({PAIR_DEGREES[pair] for pair in range(*GROUPS[1])})
    out_shape = (
        struct(atoms, width, dtype=BF16),
        struct(edges, CH),
        struct(edges, CH),
        struct(edges, CH),
        struct(atoms, CH),
    )
    scratch = [
        pltpu.VMEM((ghosts, width), BF16),
        pltpu.SemaphoreType.DMA((3,)),
    ] + pair_scratch(atoms, edges, kinds)
    args = tuple(pieces) + (
        feats, meta, mix, out, nw, oh_own, radial_own, oh_gh, d_gh, dt_gh, radial_gh, gate
    )
    return call(
        second_kernel, "second_group", out_shape, scratch, 1 << 33, args,
        any_specs(3, len(args)),
    )


def third_kernel(
    low_ref, mid_ref, high_ref, own_ref, meta_ref, mix_ref, out_ref, nw_ref, oh_own, radial_own,
    oh_gh, d_gh, dt_gh, radial_gh, gate_ref,
    rbf_ref, rad_ref, pre_own, pre_gh, unit_own, unit_gh, m0_ref, nf0_ref, gs0_ref,
    dot_a, dot_b, gr1_ref, gr2_ref, gr3_ref, gr4_a, en_a, en_b, new_a, new_b,
    new_ref, energy_ref, fown_ref, flow_ref, fmid_ref, fhigh_ref,
    table, sems, wm, wmt, wo, wot, nf_s, mx_s, acc_s, gs_s,
    dot_c, gr4_b, en_s, radt, rbft, src_s, fgh_s,
):
    pairs = tuple(range(*GROUPS[2]))
    kinds = sorted({PAIR_DEGREES[pair] for pair in pairs})
    copies = fetch((low_ref, mid_ref, high_ref), table, sems)
    atoms = own_ref.shape[0]
    nbasis = rbf_ref.shape[0]
    spacing = spacing_of(atoms, nbasis)
    block_diagonal(kinds, mix_ref, out_ref, wm, wmt, wo, wot)
    for degree in range(5):
        part = slice(degree * CH, (degree + 1) * CH)
        radt[part, :] = flip(rad_ref[:, part])
    for index in range(nbasis // CH):
        part = slice(index * CH, (index + 1) * CH)
        rbft[:, part] = flip(rbf_ref[part, :])
    mix0_t = flip(mix_ref[0])
    en_s[...] = en_a[...] + en_b[...]
    new_ref[:, 0 : new_a.shape[1]] = new_a[...]
    new_ref[:, new_a.shape[1] : new_a.shape[1] + new_b.shape[1]] = new_b[...]
    base = pair_cols(pairs[0]).start
    steps = step_count(meta_ref)

    def radial_any(degree, rows):
        if isinstance(rows.start, int) and rows.start < OWN_STEPS * STEP:
            return radial_own[degree, rows, :]
        return radial_gh[degree, pl.ds(rows.start - OWN_STEPS * STEP, rows.size), :]

    for copy in copies:
        copy.wait()
    run_pairs(
        pairs, kinds, base, own_ref, table, new_ref, 0, oh_own, oh_gh, d_gh, dt_gh, gate_ref,
        radial_any, nw_ref, steps, wm, wmt, wo, wot, nf_s, mx_s, acc_s, gs_s, dot_c,
        {4: gr4_b}, en_s, 2 * STEP,
    )

    def finish(rows, grad, pre, unit):
        mixed = m0_ref[rows, :]
        gate = jax.nn.sigmoid(mixed)
        dot = dot_a[rows, :] + dot_b[rows, :] + dot_c[rows, :]
        first = grad * gate * (1.0 + mixed * (1.0 - gate)) + dot * gate * (1.0 - gate)
        weighted = mm(first.astype(BF16), mix0_t) * nf0_ref[rows, :].astype(F32)
        parts = [weighted, gr1_ref[rows, :], gr2_ref[rows, :], gr3_ref[rows, :]]
        parts.append(gr4_a[rows, :] + gr4_b[rows, :])
        radial_grad = jnp.concatenate([part.astype(BF16) for part in parts], axis=1)
        hidden_grad = mm(radial_grad, radt[...])
        logistic = jax.nn.sigmoid(pre)
        pre_grad = (hidden_grad * logistic * (1.0 + pre * (1.0 - logistic))).astype(BF16)
        centred = centred_of(unit[:, 3:4], spacing, nbasis)
        slope = jnp.exp(-0.5 * centred * centred) * centred
        basis_grad = mm(pre_grad, rbft[...])
        dist_grad = jnp.sum(basis_grad * slope, axis=1, keepdims=True) * (-1.0 / spacing)
        pull = unit * dist_grad
        across = pull.T[0:8, :]
        top = across.astype(BF16)
        rest = (across - top.astype(F32)).astype(BF16)
        return pull, top, rest

    fgh_s[...] = jnp.zeros_like(fgh_s)
    src_s[...] = jnp.zeros_like(src_s)
    gs0 = gs0_ref[...]
    gs0_low = gs0.astype(BF16)

    def ghost_finish(step):
        here, rows = ghost_rows(step)
        grad = mm(d_gh[here, :], gs0_low)
        pull, top, rest = finish(rows, grad, pre_gh[here, :], unit_gh[here, :])
        pull_top = pull.astype(BF16)
        pull_rest = (pull - pull_top.astype(F32)).astype(BF16)
        spread = dt_gh[:, here]
        src_s[...] += mm(spread, pull_top) + mm(spread, pull_rest)
        onehot = oh_gh[here, :]
        fgh_s[...] += mm(top, onehot) + mm(rest, onehot)

    over_ghost_steps(steps, ghost_finish)
    low, mid = flow_ref.shape[1], fmid_ref.shape[1]
    flow_ref[...] = fgh_s[:, 0:low]
    fmid_ref[...] = fgh_s[:, low : low + mid]
    fhigh_ref[...] = fgh_s[:, low + mid :]

    grad_own = tiled(gs0)
    src = src_s[...]
    onto = jnp.zeros((8, atoms), F32)
    for step in range(OWN_STEPS):
        rows = own_rows(step)
        pull, top, rest = finish(rows, grad_own, pre_own[rows, :], unit_own[rows, :])
        src += jnp.sum(pull.reshape(STEP // atoms, atoms, CH), axis=0)
        onehot = oh_own[rows, :]
        onto += mm(top, onehot) + mm(rest, onehot)
    fown_ref[...] = onto - src.T[0:8, :]
    energy_ref[...] = jnp.sum(en_s[...].T, axis=0, keepdims=True)


def third_stage(pieces, feats, *rest):
    atoms, feat = feats.shape
    edges = atoms * SLOTS
    width = pieces[0].shape[1]
    sizes = [piece.shape[0] for piece in pieces]
    ghosts = sum(sizes)
    nbasis = rest[11].shape[0]
    kinds = sorted({PAIR_DEGREES[pair] for pair in range(*GROUPS[2])})
    out_shape = (
        struct(atoms, feat, dtype=BF16),
        struct(1, atoms),
        struct(8, atoms),
    ) + tuple(struct(8, size) for size in sizes)
    scratch = [
        pltpu.VMEM((ghosts, width), BF16),
        pltpu.SemaphoreType.DMA((3,)),
    ] + pair_scratch(atoms, edges, kinds) + [
        pltpu.VMEM((edges, CH), F32),
        pltpu.VMEM((edges, CH), F32),
        pltpu.VMEM((atoms, CH), F32),
        pltpu.VMEM((5 * CH, CH), BF16),
        pltpu.VMEM((CH, nbasis), BF16),
        pltpu.VMEM((atoms, CH), F32),
        pltpu.VMEM((8, ghosts), F32),
    ]
    args = tuple(pieces) + (feats,) + rest
    return call(
        third_kernel, "third_group", out_shape, scratch, 1 << 33, args, any_specs(3, len(args))
    )


def ring(axis):
    peers = lax.axis_size(axis)
    up = [(i, (i + 1) % peers) for i in range(peers)]
    return up, [(j, i) for i, j in up]


def neighbours_of(block, axis, dim):
    up, down = ring(axis)
    length = block.shape[dim]
    if len(up) == 2 and length == 2:
        other = lax.ppermute(block, axis, up)
        return (
            lax.slice_in_dim(other, length - 1, length, axis=dim),
            lax.slice_in_dim(other, 0, 1, axis=dim),
        )
    before = lax.ppermute(lax.slice_in_dim(block, length - 1, length, axis=dim), axis, up)
    after = lax.ppermute(lax.slice_in_dim(block, 0, 1, axis=dim), axis, down)
    return before, after


def grown(block, axis, dim):
    before, after = neighbours_of(block, axis, dim)
    return jnp.concatenate([before, block, after], axis=dim)


def ghost_pieces(block):
    before, after = neighbours_of(block, "gx", 0)
    return tuple(piece.reshape(-1, block.shape[-1]) for piece in (before, block, after))


def forces_kernel(mid_ref, low_ref, high_ref, own_ref, meta_ref, out_ref):
    atoms = own_ref.shape[1]
    values = mid_ref[...]
    lanes = values.shape[1]
    lane = iota(values.shape, 1)
    ext_z = lane // 8 % 4
    values += jnp.where(ext_z == 1, pltpu.roll(low_ref[...], lanes - 16, 1), 0.0)
    values += jnp.where(ext_z == 2, pltpu.roll(high_ref[...], 16, 1), 0.0)
    lane = iota((atoms, lanes), 1)
    ext_x, ext_y, ext_z = lane // 128, lane // 32 % 4, lane // 8 % 4
    slot = ((2 * ext_x + ext_y - 1) * 2 + ext_z - 1) * 8 + lane % 8
    inside = jnp.logical_and(
        jnp.logical_or(ext_y == 1, ext_y == 2), jnp.logical_or(ext_z == 1, ext_z == 2)
    )
    to_slot = jnp.logical_and(iota((atoms, lanes), 0) == slot, inside)
    to_slot = to_slot.astype(F32).astype(BF16)
    order = meta_ref[:, SLOTS + 1 : SLOTS + 2]
    to_atom = (order == iota((atoms, atoms), 1).astype(F32)).astype(F32).astype(BF16)
    total = own_ref[...]
    for _ in range(3):
        top = values.astype(BF16)
        values = values - top.astype(F32)
        total += mm(mm_nt(top, to_slot).astype(BF16), to_atom)
    for comp in range(3):
        out_ref[comp] = -total[comp : comp + 1, :]


def give_back(low, mid, high, own, meta):
    up, down = ring("gx")
    from_low = lax.ppermute(high, "gx", up)
    from_high = lax.ppermute(low, "gx", down)
    mid = mid + jnp.concatenate([from_low, from_high], axis=1)
    up, down = ring("gy")
    from_low = lax.ppermute(mid, "gy", up)
    from_high = lax.ppermute(mid, "gy", down)
    ext_y = jnp.arange(mid.shape[1], dtype=jnp.int32)[None] // 32 % 4
    mid = (
        mid
        + jnp.where(ext_y == 1, jnp.roll(from_low, -64, axis=1), 0.0)
        + jnp.where(ext_y == 2, jnp.roll(from_high, 64, axis=1), 0.0)
    )
    up, down = ring("gz")
    from_low = lax.ppermute(mid, "gz", up)
    from_high = from_low if len(up) == 2 else lax.ppermute(mid, "gz", down)
    args = (mid, from_low, from_high, own, meta)
    out_shape = (struct(3, 1, own.shape[1]),)
    return call(forces_kernel, "forces", out_shape, [], 1 << 20, args)[0]


def local(
    features,
    positions,
    neighbours,
    counts,
    cell_atoms,
    rbf_weight,
    radial_weight,
    mix_weight,
    out_weight,
    energy_weight,
    norm_weight,
):
    feats = features[0, 0, 0]
    places = jnp.swapaxes(positions[0, 0], 0, 1)
    *cells, own_pos, meta = make_cells(
        feats, places, neighbours[0, 0, 0].T, counts[0, 0], cell_atoms[0, 0]
    )
    hold = lax.optimization_barrier
    blocks = [part.reshape(2, 2, 2, 8, part.shape[1]) for part in cells]
    block0, block1, block2 = (grown(block, "gz", 2) for block in blocks)
    block0, own_pos, meta = hold((block0, own_pos, meta))
    block0 = grown(block0, "gy", 1)
    oh_own, radial_own, pre_own, unit_own = own_stage(meta, own_pos, rbf_weight, radial_weight)
    block0, block1 = hold((block0, block1))
    pieces0 = ghost_pieces(block0)
    block1 = grown(block1, "gy", 1)
    pieces0, block1, block2 = hold((pieces0, block1, block2))
    pieces1 = ghost_pieces(block1)
    block2 = grown(block2, "gy", 1)
    (
        new_a, oh_gh, d_gh, dt_gh, radial_gh, pre_gh, unit_gh, m0, gate, nf0, gs0, dot_a, gr1,
        gr2, en_a,
    ) = first_stage(
        pieces0, feats, own_pos, meta, rbf_weight, radial_weight, mix_weight, out_weight,
        energy_weight[None], norm_weight, oh_own, radial_own,
    )
    gate, block2 = hold((gate, block2))
    pieces2 = ghost_pieces(block2)
    shared = (
        feats, meta, mix_weight, out_weight, norm_weight, oh_own, radial_own, oh_gh, d_gh, dt_gh,
        radial_gh, gate,
    )
    new_b, dot_b, gr3, gr4, en_b = second_stage(pieces1, *shared)
    new, energy, own, low, mid, high = third_stage(
        pieces2, *shared, rbf_weight, radial_weight, pre_own, pre_gh, unit_own, unit_gh, m0, nf0,
        gs0, dot_a, dot_b, gr1, gr2, gr3, gr4, en_a, en_b, new_a, new_b,
    )
    forces = give_back(low, mid, high, own, meta)
    return (
        new[None, None, None],
        energy[None, None],
        jnp.swapaxes(forces, 0, 1)[None, None],
    )


def solution(mesh):
    split = P("gx", "gy", "gz", None, None)
    flat = P("gx", "gy", "gz", None)
    return jax.shard_map(
        local,
        mesh=mesh,
        in_specs=(split, split, split, flat, flat, P(), P(), P(), P(), P(), P()),
        out_specs=(split, flat, split),
        check_vma=False,
    )
```

```python
import math

import jax
import jax.numpy as jnp
from jax import lax
from jax.experimental import pallas as pl
from jax.experimental.pallas import tpu as pltpu
from jax.sharding import PartitionSpec as P

F32 = jnp.float32
BF16 = jnp.bfloat16
CH = 128
SLOTS = 32
HALF = 16
STEP = 256
OWN_STEPS = 4
GH_STEPS = 2
MIB = 1024 * 1024
SPACE = pltpu.VMEM
PAIR_DEGREES = (
    (1, 1), (1, 2), (2, 2), (2, 2),
    (3, 3), (3, 3), (3, 3), (3, 4),
    (4, 4), (4, 4), (4, 4), (4, 4),
)
GROUPS = ((0, 4), (4, 8), (8, 12))


def mm(a, b):
    return jnp.dot(a, b, preferred_element_type=F32)


def mm_nt(a, b):
    return lax.dot_general(a, b, (((1,), (1,)), ((), ())), preferred_element_type=F32)


def iota(shape, dim):
    return lax.broadcasted_iota(jnp.int32, shape, dim)


def flip(w):
    return w.astype(F32).T.astype(BF16)


def pair_cols(pair):
    return slice(CH + pair * 2 * CH, CH + (pair + 1) * 2 * CH)


def struct(*shape, dtype=F32):
    return jax.ShapeDtypeStruct(shape, dtype)


def call(kernel, name, out_shape, scratch, flops, args, specs=None, limit=16):
    size = sum(a.size * a.dtype.itemsize for a in list(args) + list(out_shape))
    return pl.pallas_call(
        kernel,
        out_shape=out_shape,
        in_specs=specs or [pl.BlockSpec(memory_space=SPACE)] * len(args),
        out_specs=tuple(pl.BlockSpec(memory_space=SPACE) for _ in out_shape),
        scratch_shapes=scratch,
        compiler_params=pltpu.CompilerParams(vmem_limit_bytes=limit * MIB),
        cost_estimate=pl.CostEstimate(flops=flops, bytes_accessed=size, transcendentals=0),
        name=name,
    )(*args)


def cells_kernel(feat_ref, pos_ref, near_ref, counts_ref, order_ref, *refs):
    out_refs, (own_pos_ref, meta_ref, rows_ref, pos_rows) = refs[:3], refs[3:]
    atoms = feat_ref.shape[0]
    rows_ref[...] = jnp.zeros_like(rows_ref)
    rows_ref[0:SLOTS, :] = near_ref[...].astype(F32)
    rows_ref[SLOTS : SLOTS + 1, :] = counts_ref[...].astype(F32)
    rows_ref[SLOTS + 1 : SLOTS + 2, :] = order_ref[...].astype(F32)
    meta = rows_ref[...].T
    meta_ref[...] = meta
    pos_rows[...] = jnp.zeros_like(pos_rows)
    for comp in range(3):
        places = pos_ref[comp]
        first = places.astype(BF16).astype(F32)
        second = (places - first).astype(BF16).astype(F32)
        pos_rows[comp : comp + 1, :] = first
        pos_rows[4 + comp : 5 + comp, :] = second
        pos_rows[8 + comp : 9 + comp, :] = places - first - second
    pieces = pos_rows[...].astype(BF16)
    lane = iota((atoms, atoms), 1).astype(F32)
    pick = (meta[:, SLOTS + 1 : SLOTS + 2] == lane).astype(F32).astype(BF16)
    same = (iota((atoms, atoms), 0) == iota((atoms, atoms), 1)).astype(F32).astype(BF16)
    own_pos_ref[...] = mm_nt(same, pieces).astype(BF16)
    for group, (begin, end) in enumerate(GROUPS):
        at = 0 if group == 0 else pair_cols(begin).start
        till = pair_cols(end - 1).stop
        out_refs[group][:, 0 : till - at] = mm(pick, feat_ref[:, at:till]).astype(BF16)
        if group == 0:
            out_refs[group][:, till:] = mm_nt(pick, pieces).astype(BF16)


def make_cells(feats, places, near, counts, order):
    atoms = feats.shape[0]
    widths = [CH * 2 * (end - begin) for begin, end in GROUPS]
    widths[0] += 2 * CH
    out_shape = tuple(struct(atoms, width, dtype=BF16) for width in widths) + (
        struct(atoms, CH, dtype=BF16),
        struct(atoms, CH),
    )
    scratch = [pltpu.VMEM((CH, atoms), F32), pltpu.VMEM((CH, atoms), F32)]
    args = (feats, places, near, counts, order)
    return call(cells_kernel, "cells", out_shape, scratch, 1 << 26, args)


def spacing_of(atoms, nbasis):
    depth = atoms // 16
    return 2.0 * math.sqrt(32.0 + depth * depth) / (nbasis - 1)


def own_onehots(meta_ref, oh_own):
    atoms = meta_ref.shape[0]
    counts = meta_ref[:, SLOTS : SLOTS + 1]
    lane_atom = iota((atoms, atoms), 1).astype(F32)
    for slot in range(HALF):
        hit = jnp.logical_and(meta_ref[:, slot : slot + 1] == lane_atom, counts > slot)
        oh_own[slot * atoms : (slot + 1) * atoms, :] = hit.astype(F32).astype(BF16)


def geometry(near, here):
    diff = near - here
    rel = (diff + pltpu.roll(diff, CH - 4, 1)) + (
        pltpu.roll(diff, CH - 8, 1) + pltpu.roll(diff, CH - 12, 1)
    )
    lane = iota(rel.shape, 1)
    rel = jnp.where(lane < 3, rel, 0.0)
    square = jnp.sum(rel * rel, axis=1, keepdims=True)
    inverse = lax.rsqrt(jnp.where(square > 0.0, square, 1.0))
    dist = square * inverse
    return jnp.where(lane == 3, dist, rel * inverse), dist


def centred_of(dist, spacing, nbasis):
    return dist * (1.0 / spacing) - iota((dist.shape[0], nbasis), 1).astype(F32)


def radial_net(dist, spacing, rbf_ref, rad_ref):
    centred = centred_of(dist, spacing, rbf_ref.shape[0])
    basis = jnp.exp(-0.5 * centred * centred)
    pre = mm(basis.astype(BF16), rbf_ref[...])
    hidden = (pre * jax.nn.sigmoid(pre)).astype(BF16)
    return pre, mm(hidden, rad_ref[...]).astype(BF16)


def own_spread(atoms, size=STEP):
    shape = (atoms, size)
    return (iota(shape, 1) % atoms == iota(shape, 0)).astype(F32).astype(BF16)


def tiled(values, size=STEP):
    return jnp.concatenate([values] * (size // values.shape[0]), axis=0)


def live_ghosts(meta_ref):
    return jnp.maximum(meta_ref[:, SLOTS : SLOTS + 1] - HALF, 0.0)


def step_count(meta_ref):
    total = jnp.sum(live_ghosts(meta_ref)).astype(jnp.int32)
    rows = GH_STEPS * STEP
    return jnp.maximum((total + (rows - 1)) // rows, 1) * GH_STEPS


def own_rows(step, size=STEP):
    return pl.ds(step * size, size)


def ghost_rows(step, size=STEP):
    first = OWN_STEPS * STEP
    if isinstance(step, int):
        return pl.ds(step * size, size), pl.ds(first + step * size, size)
    base = pl.multiple_of(step * size, size)
    return pl.ds(base, size), pl.ds(pl.multiple_of(first + base, size), size)


class Halves:
    def __init__(self, own, ghost):
        self.own, self.ghost = own, ghost
        self.dtype = own.dtype

    def place(self, rows):
        first = OWN_STEPS * STEP
        if not isinstance(rows.start, int):
            return self.ghost, pl.ds(pl.multiple_of(rows.start - first, rows.size), rows.size)
        if rows.start < first:
            return self.own, rows
        return self.ghost, pl.ds(rows.start - first, rows.size)

    def __getitem__(self, at):
        ref, rows = self.place(at[0])
        return ref[rows, at[1]]

    def __setitem__(self, at, value):
        ref, rows = self.place(at[0])
        ref[rows, at[1]] = value


def over_ghost_steps(steps, body, size=STEP):
    static = GH_STEPS * STEP // size
    for step in range(static):
        body(step)

    def again(step, carry):
        body(step)
        return carry

    lax.fori_loop(static, (steps * STEP + (size - 1)) // size, again, 0)


def block_diagonal(kinds, mix_ref, out_ref, wm, wmt, wo, wot):
    zero = jnp.zeros((CH, CH), BF16)
    for kind, both in enumerate(kinds):
        for ref in (wm, wmt, wo, wot):
            ref[kind, 0:CH, CH:] = zero
            ref[kind, CH:, 0:CH] = zero
    for degree in sorted({d for both in kinds for d in both}):
        mix, out = mix_ref[degree], out_ref[degree]
        mix_t, out_t = flip(mix), flip(out)
        for kind, both in enumerate(kinds):
            for side in range(2):
                if both[side] == degree:
                    part = slice(side * CH, side * CH + CH)
                    wm[kind, part, part] = mix
                    wmt[kind, part, part] = mix_t
                    wo[kind, part, part] = out
                    wot[kind, part, part] = out_t


def fetch(pieces, table, sems):
    copies = []
    at = 0
    for index, piece in enumerate(pieces):
        rows = piece.shape[0]
        copies.append(
            pltpu.make_async_copy(piece, table.at[pl.ds(at, rows), :], sems.at[index])
        )
        at += rows
    for copy in copies:
        copy.start()
    return copies


def run_pairs(
    pairs, kinds, first_col, own_ref, table, new_ref, new_base, oh_own, oh_gh, d_gh, dt_gh,
    gate_ref, radial_of, nw_ref, steps, wm, wmt, wo, wot, nf_s, mx_s, acc_s, gs_s, dot_ref,
    grad_refs, en_ref, size=STEP,
):
    atoms = own_ref.shape[0]
    norm = 1.0 / math.sqrt(SLOTS)
    spread_own = own_spread(atoms, size)
    own_steps = OWN_STEPS * STEP // size
    begin, end = pair_cols(pairs[0]).start, pair_cols(pairs[-1]).stop
    own_cols = slice(begin, end)
    table_cols = slice(begin - first_col, end - first_col)
    infos = []
    for index, pair in enumerate(pairs):
        degrees = PAIR_DEGREES[pair]
        infos.append((slice(index * 2 * CH, (index + 1) * 2 * CH), degrees, kinds.index(degrees)))

    def gate_of(rows):
        gate = gate_ref[rows, :]
        return jnp.concatenate([gate, gate], axis=1)

    def forward(rows, onehot, feats):
        near = mm(onehot, feats).astype(BF16)
        nf_s[rows, :] = near
        gate = gate_of(rows)
        messages = []
        for cols, degrees, kind in infos:
            radial = jnp.concatenate([radial_of(d, rows) for d in degrees], axis=1)
            mixed = mm(near[:, cols] * radial, wm[kind]).astype(BF16)
            mx_s[rows, cols] = mixed
            messages.append(mixed * gate)
        return jnp.concatenate(messages, axis=1)

    def backward(rows, grad):
        parts = {}
        dots = None
        gate = gate_of(rows)
        for cols, degrees, kind in infos:
            product = grad[:, cols] * mx_s[rows, cols]
            dot = (product[:, 0:CH] + product[:, CH:]).astype(F32)
            dots = dot if dots is None else dots + dot
            weighted = mm(grad[:, cols] * gate, wmt[kind]) * nf_s[rows, cols].astype(F32)
            for side in range(2):
                part = weighted[:, side * CH : (side + 1) * CH]
                degree = degrees[side]
                parts[degree] = parts[degree] + part if degree in parts else part
        dot_ref[rows, :] = dots.astype(dot_ref.dtype)
        for degree, part in parts.items():
            grad_refs[degree][rows, :] = part.astype(grad_refs[degree].dtype)

    own = own_ref[:, own_cols]
    summed = None
    for step in range(own_steps):
        rows = own_rows(step, size)
        part = mm(spread_own, forward(rows, oh_own[rows, :], own))
        summed = part if summed is None else summed + part
    acc_s[...] = summed

    def ghost_forward(step):
        here, rows = ghost_rows(step, size)
        message = forward(rows, oh_gh[here, :], table[:, table_cols])
        acc_s[...] += mm(dt_gh[:, here], message)

    over_ghost_steps(steps, ghost_forward, size)

    for cols, degrees, kind in infos:
        summed_low = (acc_s[:, cols] * norm).astype(BF16)
        updated = own[:, cols].astype(F32) + mm(summed_low, wo[kind])
        at = begin - new_base + cols.start
        new_ref[:, at : at + 2 * CH] = updated.astype(BF16)
        weight = jnp.concatenate(
            [nw_ref[d - 1 : d, :] * (1.0 / (2 * d + 1)) for d in degrees], axis=1
        )
        scale = weight * updated
        energy = scale * updated
        en_ref[...] += energy[:, 0:CH] + energy[:, CH:]
        gs_s[:, cols] = (mm((2.0 * scale).astype(BF16), wot[kind]) * norm).astype(BF16)

    grad_own = tiled(gs_s[...], size)
    for step in range(own_steps):
        backward(own_rows(step, size), grad_own)

    def ghost_backward(step):
        here, rows = ghost_rows(step, size)
        backward(rows, mm(d_gh[here, :], gs_s[...]).astype(BF16))

    over_ghost_steps(steps, ghost_backward, size)


def pair_scratch(atoms, edges, kinds):
    count = len(kinds)
    return [pltpu.VMEM((count, 2 * CH, 2 * CH), BF16) for _ in range(4)] + [
        pltpu.VMEM((edges, 8 * CH), BF16),
        pltpu.VMEM((edges, 8 * CH), BF16),
        pltpu.VMEM((atoms, 8 * CH), F32),
        pltpu.VMEM((atoms, 8 * CH), BF16),
    ]


def own_kernel(
    meta_ref, own_pos_ref, rbf_ref, rad_ref, mix_ref,
    oh_own, pre_ref, unit_ref, radt_ref, rbft_ref, mixt_ref, home_ref, *radial_refs
):
    atoms = meta_ref.shape[0]
    nbasis = rbf_ref.shape[0]
    spacing = spacing_of(atoms, nbasis)
    own_onehots(meta_ref, oh_own)
    here = tiled(own_pos_ref[...].astype(F32))
    for step in range(OWN_STEPS):
        rows = own_rows(step)
        unit, dist = geometry(mm(oh_own[rows, :], own_pos_ref[...]), here)
        unit_ref[rows, :] = unit
        pre, radial = radial_net(dist, spacing, rbf_ref, rad_ref)
        pre_ref[rows, :] = pre.astype(BF16)
        for degree, ref in enumerate(radial_refs):
            ref[rows, :] = radial[:, degree * CH : (degree + 1) * CH]
    for degree in range(5):
        part = slice(degree * CH, (degree + 1) * CH)
        radt_ref[part, :] = flip(rad_ref[:, part])
    for index in range(nbasis // CH):
        part = slice(index * CH, (index + 1) * CH)
        rbft_ref[:, part] = flip(rbf_ref[part, :])
    mixt_ref[...] = flip(mix_ref[0])
    lanes = home_ref.shape[1]
    lane = iota((atoms, lanes), 1)
    ext_x, ext_y, ext_z = lane // 128, lane // 32 % 4, lane // 8 % 4
    slot = ((2 * ext_x + ext_y - 1) * 2 + ext_z - 1) * 8 + lane % 8
    inside = jnp.logical_and(
        jnp.logical_or(ext_y == 1, ext_y == 2), jnp.logical_or(ext_z == 1, ext_z == 2)
    )
    to_slot = jnp.logical_and(iota((atoms, lanes), 0) == slot, inside)
    to_slot = to_slot.astype(F32).astype(BF16)
    order = meta_ref[:, SLOTS + 1 : SLOTS + 2]
    to_atom = (order == iota((atoms, atoms), 1).astype(F32)).astype(F32)
    home_ref[...] = mm(to_atom.T.astype(BF16), to_slot).astype(BF16)


def own_stage(meta, own_pos, rbf, rad, mix):
    atoms = meta.shape[0]
    edges = atoms * HALF
    out_shape = (
        struct(edges, atoms, dtype=BF16),
        struct(edges, CH, dtype=BF16),
        struct(edges, CH),
        struct(*rad.shape[::-1], dtype=BF16),
        struct(*rbf.shape[::-1], dtype=BF16),
        struct(CH, CH, dtype=BF16),
        struct(atoms, 256, dtype=BF16),
    ) + (struct(edges, CH, dtype=BF16),) * 5
    args = (meta, own_pos, rbf, rad, mix)
    return call(own_kernel, "own_edges", out_shape, [], 1 << 31, args)


def first_kernel(
    low_ref, mid_ref, high_ref, own_ref, own_pos_ref, meta_ref, rbf_ref, rad_ref, mix_ref,
    out_ref, ew_ref, nw_ref, oh_own, radial_own0, radial_own1, radial_own2,
    new_ref, oh_gh, d_gh, dt_gh, radial_gh3, radial_gh4, pre_ref, unit_ref, gs0_ref, en_ref,
    m0_own, m0_gh, gate_own, gate_gh, nf0_own, nf0_gh, dot_own, dot_gh, gr1_own, gr1_gh, gr2_own,
    gr2_gh,
    table, sems, ghpos, radial_gh0, radial_gh1, radial_gh2, wm, wmt, wo, wot, nf_s, mx_s, acc_s,
    gs_s,
):
    m0_ref, gate_ref, nf0_ref = Halves(m0_own, m0_gh), Halves(gate_own, gate_gh), Halves(nf0_own, nf0_gh)
    dot_ref, gr1_ref, gr2_ref = Halves(dot_own, dot_gh), Halves(gr1_own, gr1_gh), Halves(gr2_own, gr2_gh)
    radial_gh = (radial_gh0, radial_gh1, radial_gh2, radial_gh3, radial_gh4)
    radials = [Halves(radial_own0, radial_gh0), Halves(radial_own1, radial_gh1)]
    radials.append(Halves(radial_own2, radial_gh2))
    pairs = tuple(range(*GROUPS[0]))
    kinds = sorted({PAIR_DEGREES[pair] for pair in pairs})
    copies = fetch((low_ref, mid_ref, high_ref), table, sems)
    atoms = own_ref.shape[0]
    ghosts = table.shape[0]
    spacing = spacing_of(atoms, rbf_ref.shape[0])
    norm = 1.0 / math.sqrt(SLOTS)
    block_diagonal(kinds, mix_ref, out_ref, wm, wmt, wo, wot)

    live = live_ghosts(meta_ref)
    sub_atom = iota((atoms, atoms), 0)
    lane_atom = iota((atoms, atoms), 1)
    live_b = jnp.broadcast_to(live, (atoms, atoms))
    end_row = jnp.sum(jnp.where(sub_atom <= lane_atom, live_b, 0.0), axis=0, keepdims=True)
    live_row = jnp.sum(jnp.where(sub_atom == lane_atom, live_b, 0.0), axis=0, keepdims=True)
    start_row = end_row - live_row
    row_b = jnp.broadcast_to(live_row, (atoms, atoms))
    end_col = jnp.sum(jnp.where(lane_atom <= sub_atom, row_b, 0.0), axis=1, keepdims=True)
    start_col = end_col - live
    total = jnp.sum(live)
    steps = step_count(meta_ref)
    ghost_row = meta_ref[:, HALF:SLOTS] - atoms
    high_part = jnp.floor(ghost_row * (1.0 / 16.0))
    row_high = high_part.astype(BF16)
    row_low = (ghost_row - 16.0 * high_part).astype(BF16)

    row = iota((ghosts, CH), 0)
    lane = iota((ghosts, CH), 1)
    zcells = atoms // 32
    per_y = (zcells + 2) * 8
    ext_x = row // (4 * per_y)
    ext_y = row // per_y % 4
    ext_z = row // 8 % (zcells + 2)

    def side_of(ext, last, size):
        return jnp.where(ext == 0, -size, jnp.where(ext == last, size, 0.0))

    shift = jnp.where(lane == 12, side_of(ext_x, 3, 4.0), 0.0)
    shift = jnp.where(lane == 13, side_of(ext_y, 3, 4.0), shift)
    shift = jnp.where(lane == 14, side_of(ext_z, zcells + 1, 2.0 * zcells), shift)
    for copy in copies:
        copy.wait()
    ghpos[...] = (table[:, table.shape[1] - CH :].astype(F32) + shift).astype(BF16)

    def forward0(rows, onehot, feats, radial):
        near = mm(onehot, feats).astype(BF16)
        nf0_ref[rows, :] = near
        mixed = mm(near * radial, mix_ref[0])
        m0_ref[rows, :] = mixed.astype(BF16)
        gate = jax.nn.sigmoid(mixed)
        gate_ref[rows, :] = gate.astype(BF16)
        return (mixed * gate).astype(BF16)

    own0 = own_ref[:, 0:CH]
    spread_own = own_spread(atoms)
    summed = None
    for step in range(OWN_STEPS):
        rows = own_rows(step)
        message = forward0(rows, oh_own[rows, :], own0, radial_own0[rows, :])
        part = mm(spread_own, message)
        summed = part if summed is None else summed + part
    acc_s[:, 0:CH] = summed

    def ghost_start(step):
        here, rows = ghost_rows(step)
        base = step * STEP
        edge = (iota((STEP, atoms), 0) + base).astype(F32)
        mine = jnp.logical_and(edge >= start_row, edge < end_row).astype(F32)
        source = mine.astype(BF16)
        d_gh[here, :] = source
        edge_t = (iota((atoms, STEP), 1) + base).astype(F32)
        mine_t = jnp.logical_and(edge_t >= start_col, edge_t < end_col)
        spread = mine_t.astype(F32).astype(BF16)
        dt_gh[:, here] = spread
        edge_col = edge[:, 0:1]
        slot = edge_col - jnp.sum(mine * start_row, axis=1, keepdims=True)
        listed = mm(source, row_high) * 16.0 + mm(source, row_low)
        at_slot = iota((STEP, HALF), 1).astype(F32) == slot
        which = jnp.sum(jnp.where(at_slot, listed, 0.0), axis=1, keepdims=True)
        which = jnp.where(edge_col < total, which, -1.0)
        onehot = (iota((STEP, ghosts), 1).astype(F32) == which).astype(F32).astype(BF16)
        oh_gh[here, :] = onehot
        unit, dist = geometry(mm(onehot, ghpos[...]), mm(source, own_pos_ref[...]))
        unit_ref[here, :] = unit
        pre, radial = radial_net(dist, spacing, rbf_ref, rad_ref)
        pre_ref[here, :] = pre.astype(BF16)
        for degree in range(5):
            radial_gh[degree][here, :] = radial[:, degree * CH : (degree + 1) * CH]
        message = forward0(rows, onehot, table[:, 0:CH], radial[:, 0:CH])
        acc_s[:, 0:CH] += mm(spread, message)

    over_ghost_steps(steps, ghost_start)

    low0 = (acc_s[:, 0:CH] * norm).astype(BF16)
    updated0 = own0.astype(F32) + mm(low0, out_ref[0])
    new_ref[:, 0:CH] = updated0.astype(BF16)
    logistic = jax.nn.sigmoid(updated0)
    weight0 = ew_ref[...]
    en_ref[...] = weight0 * updated0 * logistic
    grad0 = (weight0 * logistic * (1.0 + updated0 * (1.0 - logistic))).astype(BF16)
    gs0_ref[...] = mm_nt(grad0, out_ref[0]) * norm

    def radial_any(degree, rows):
        return radials[degree][rows, :]

    run_pairs(
        pairs, kinds, 0, own_ref, table, new_ref, 0, oh_own, oh_gh, d_gh, dt_gh, gate_ref,
        radial_any, nw_ref, steps, wm, wmt, wo, wot, nf_s, mx_s, acc_s, gs_s, dot_ref,
        {1: gr1_ref, 2: gr2_ref}, en_ref,
    )


def any_specs(count, total):
    return [pl.BlockSpec(memory_space=pl.ANY)] * count + [
        pl.BlockSpec(memory_space=SPACE)
    ] * (total - count)


def first_stage(pieces, feats, own_pos, meta, rbf, rad, mix, out, ew, nw, oh_own, *radial_own):
    atoms = feats.shape[0]
    half = atoms * HALF
    edges = 2 * half
    width = pieces[0].shape[1]
    ghosts = sum(piece.shape[0] for piece in pieces)
    kinds = sorted({PAIR_DEGREES[pair] for pair in range(*GROUPS[0])})
    out_shape = (
        struct(atoms, width - CH, dtype=BF16),
        struct(half, ghosts, dtype=BF16),
        struct(half, atoms, dtype=BF16),
        struct(atoms, half, dtype=BF16),
        struct(half, CH, dtype=BF16),
        struct(half, CH, dtype=BF16),
        struct(half, CH, dtype=BF16),
        struct(half, CH),
        struct(atoms, CH),
        struct(atoms, CH),
    ) + (struct(half, CH, dtype=BF16),) * 12
    scratch = [
        pltpu.VMEM((ghosts, width), BF16),
        pltpu.SemaphoreType.DMA((3,)),
        pltpu.VMEM((ghosts, CH), BF16),
    ] + [pltpu.VMEM((half, CH), BF16)] * 3 + pair_scratch(atoms, edges, kinds)
    args = tuple(pieces) + (
        feats, own_pos, meta, rbf, rad, mix, out, ew, nw, oh_own
    ) + radial_own
    return call(
        first_kernel, "first_group", out_shape, scratch, 1 << 33, args, any_specs(3, len(args)),
        32,
    )


def second_kernel(
    low_ref, mid_ref, high_ref, own_ref, meta_ref, mix_ref, out_ref, nw_ref, oh_own, oh_gh, d_gh,
    dt_gh, gate_own, gate_gh, radial_own4, radial_gh4, radial_own3, radial_gh3,
    new_ref, en_ref, dot_own, dot_gh, gr3_own, gr3_gh, gr4_own, gr4_gh,
    table, sems, wm, wmt, wo, wot, nf_s, mx_s, acc_s, gs_s,
):
    radials = {3: Halves(radial_own3, radial_gh3), 4: Halves(radial_own4, radial_gh4)}
    gate_ref = Halves(gate_own, gate_gh)
    dot_ref, gr3_ref, gr4_ref = Halves(dot_own, dot_gh), Halves(gr3_own, gr3_gh), Halves(gr4_own, gr4_gh)
    pairs = tuple(range(*GROUPS[1]))
    kinds = sorted({PAIR_DEGREES[pair] for pair in pairs})
    copies = fetch((low_ref, mid_ref, high_ref), table, sems)
    block_diagonal(kinds, mix_ref, out_ref, wm, wmt, wo, wot)
    en_ref[...] = jnp.zeros_like(en_ref)
    base = pair_cols(pairs[0]).start

    def radial_any(degree, rows):
        return radials[degree][rows, :]

    for copy in copies:
        copy.wait()
    run_pairs(
        pairs, kinds, base, own_ref, table, new_ref, base, oh_own, oh_gh, d_gh, dt_gh, gate_ref,
        radial_any, nw_ref, step_count(meta_ref), wm, wmt, wo, wot, nf_s, mx_s, acc_s, gs_s,
        dot_ref, {3: gr3_ref, 4: gr4_ref}, en_ref,
    )


def second_stage(pieces, feats, *rest):
    atoms = feats.shape[0]
    edges = atoms * SLOTS
    width = pieces[0].shape[1]
    ghosts = sum(piece.shape[0] for piece in pieces)
    kinds = sorted({PAIR_DEGREES[pair] for pair in range(*GROUPS[1])})
    out_shape = (
        struct(atoms, width, dtype=BF16),
        struct(atoms, CH),
    ) + (struct(atoms * HALF, CH, dtype=BF16),) * 6
    scratch = [
        pltpu.VMEM((ghosts, width), BF16),
        pltpu.SemaphoreType.DMA((3,)),
    ] + pair_scratch(atoms, edges, kinds)
    args = tuple(pieces) + (feats,) + rest
    return call(
        second_kernel, "second_group", out_shape, scratch, 1 << 33, args,
        any_specs(3, len(args)), 28,
    )


def finish(
    grad, mixed, near, dots, parts, pre, unit, spacing, radt_ref, rbft_ref, mixt_ref
):
    mixed = mixed.astype(F32)
    gate = jax.nn.sigmoid(mixed)
    first = grad * gate * (1.0 + mixed * (1.0 - gate)) + dots * gate * (1.0 - gate)
    weighted = mm(first.astype(BF16), mixt_ref[...]) * near.astype(F32)
    radial_grad = jnp.concatenate([weighted.astype(BF16)] + parts, axis=1)
    hidden_grad = mm(radial_grad, radt_ref[...])
    pre = pre.astype(F32)
    logistic = jax.nn.sigmoid(pre)
    pre_grad = (hidden_grad * logistic * (1.0 + pre * (1.0 - logistic))).astype(BF16)
    centred = centred_of(unit[:, 3:4], spacing, rbft_ref.shape[1])
    slope = jnp.exp(-0.5 * centred * centred) * centred
    basis_grad = mm(pre_grad, rbft_ref[...])
    dist_grad = jnp.sum(basis_grad * slope, axis=1, keepdims=True) * (-1.0 / spacing)
    pull = unit * dist_grad
    across = pull.T[0:8, :]
    top = across.astype(BF16)
    rest = (across - top.astype(F32)).astype(BF16)
    return pull, top, rest


def sum_of(refs, rows):
    total = refs[0][rows, :].astype(F32)
    for ref in refs[1:]:
        total += ref[rows, :].astype(F32)
    return total


def third_kernel(
    low_ref, mid_ref, high_ref, own_ref, meta_ref, mix_ref, out_ref, nw_ref, oh_own, oh_gh, d_gh,
    dt_gh, gate_own, gate_gh, radial_own4, radial_gh4,
    radt_ref, rbft_ref, mixt_ref, gs0_ref, en_a, en_b, new_a, new_b, pre_gh, unit_gh,
    m0_ref, nf0_ref, dot_a, dot_b, gr1_ref, gr2_ref, gr3_ref, gr4_a,
    new_ref, energy_ref, src_ref, flow_ref, fmid_ref, fhigh_ref, dot_own, gr4_own,
    table, sems, wm, wmt, wo, wot, nf_s, mx_s, acc_s, gs_s, dot_c, gr4_b, en_s, fgh_s,
):
    gate_ref = Halves(gate_own, gate_gh)
    radials = {4: Halves(radial_own4, radial_gh4)}
    pairs = tuple(range(*GROUPS[2]))
    kinds = sorted({PAIR_DEGREES[pair] for pair in pairs})
    copies = fetch((low_ref, mid_ref, high_ref), table, sems)
    atoms = own_ref.shape[0]
    spacing = spacing_of(atoms, rbft_ref.shape[1])
    block_diagonal(kinds, mix_ref, out_ref, wm, wmt, wo, wot)
    en_s[...] = en_a[...] + en_b[...]
    new_ref[:, 0 : new_a.shape[1]] = new_a[...]
    new_ref[:, new_a.shape[1] : new_a.shape[1] + new_b.shape[1]] = new_b[...]
    base = pair_cols(pairs[0]).start
    steps = step_count(meta_ref)

    def radial_any(degree, rows):
        return radials[degree][rows, :]

    for copy in copies:
        copy.wait()
    run_pairs(
        pairs, kinds, base, own_ref, table, new_ref, 0, oh_own, oh_gh, d_gh, dt_gh, gate_ref,
        radial_any, nw_ref, steps, wm, wmt, wo, wot, nf_s, mx_s, acc_s, gs_s,
        Halves(dot_own, dot_c), {4: Halves(gr4_own, gr4_b)}, en_s,
    )
    energy_ref[...] = jnp.sum(en_s[...].T, axis=0, keepdims=True)

    fgh_s[...] = jnp.zeros_like(fgh_s)
    src_ref[...] = jnp.zeros_like(src_ref)
    gs0_low = gs0_ref[...].astype(BF16)

    def ghost_finish(step):
        here, rows = ghost_rows(step)
        grad = mm(d_gh[here, :], gs0_low)
        dots = sum_of((dot_a, dot_b, dot_c), here)
        parts = [gr1_ref[here, :], gr2_ref[here, :], gr3_ref[here, :]]
        parts.append(sum_of((gr4_a, gr4_b), here).astype(BF16))
        pull, top, rest = finish(
            grad, m0_ref[here, :], nf0_ref[here, :], dots, parts, pre_gh[here, :],
            unit_gh[here, :], spacing, radt_ref, rbft_ref, mixt_ref,
        )
        pull_top = pull.astype(BF16)
        pull_rest = (pull - pull_top.astype(F32)).astype(BF16)
        spread = dt_gh[:, here]
        src_ref[...] += mm(spread, pull_top) + mm(spread, pull_rest)
        onehot = oh_gh[here, :]
        fgh_s[...] += mm(top, onehot) + mm(rest, onehot)

    over_ghost_steps(steps, ghost_finish)
    low, mid = flow_ref.shape[1], fmid_ref.shape[1]
    flow_ref[...] = fgh_s[:, 0:low]
    fmid_ref[...] = fgh_s[:, low : low + mid]
    fhigh_ref[...] = fgh_s[:, low + mid :]


def third_stage(pieces, feats, *rest):
    atoms, feat = feats.shape
    half = atoms * HALF
    edges = 2 * half
    width = pieces[0].shape[1]
    sizes = [piece.shape[0] for piece in pieces]
    ghosts = sum(sizes)
    kinds = sorted({PAIR_DEGREES[pair] for pair in range(*GROUPS[2])})
    out_shape = (
        struct(atoms, feat, dtype=BF16),
        struct(1, atoms),
        struct(atoms, CH),
    ) + tuple(struct(8, size) for size in sizes) + (struct(half, CH, dtype=BF16),) * 2
    scratch = [
        pltpu.VMEM((ghosts, width), BF16),
        pltpu.SemaphoreType.DMA((3,)),
    ] + pair_scratch(atoms, edges, kinds) + [
        pltpu.VMEM((half, CH), BF16),
        pltpu.VMEM((half, CH), BF16),
        pltpu.VMEM((atoms, CH), F32),
        pltpu.VMEM((8, ghosts), F32),
    ]
    args = tuple(pieces) + (feats,) + rest
    return call(
        third_kernel, "third_group", out_shape, scratch, 1 << 33, args, any_specs(3, len(args)),
        30,
    )


def own_back_kernel(
    oh_own, pre_own, unit_own, radt_ref, rbft_ref, mixt_ref, gs0_ref, src_ref,
    m0_ref, nf0_ref, dot_a, dot_b, dot_c, gr1_ref, gr2_ref, gr3_ref, gr4_a, gr4_b,
    force_ref,
):
    atoms = oh_own.shape[1]
    spacing = spacing_of(atoms, rbft_ref.shape[1])
    grad = tiled(gs0_ref[...])
    src = src_ref[...]
    onto = jnp.zeros((8, atoms), F32)
    for step in range(OWN_STEPS):
        rows = own_rows(step)
        parts = [gr1_ref[rows, :], gr2_ref[rows, :], gr3_ref[rows, :]]
        parts.append(sum_of((gr4_a, gr4_b), rows).astype(BF16))
        pull, top, rest = finish(
            grad, m0_ref[rows, :], nf0_ref[rows, :], sum_of((dot_a, dot_b, dot_c), rows), parts,
            pre_own[rows, :], unit_own[rows, :], spacing, radt_ref, rbft_ref, mixt_ref,
        )
        src += jnp.sum(pull.reshape(STEP // atoms, atoms, CH), axis=0)
        onehot = oh_own[rows, :]
        onto += mm(top, onehot) + mm(rest, onehot)
    force_ref[...] = onto - src.T[0:8, :]


def own_back_stage(*args):
    oh_own = args[0]
    out_shape = (struct(8, oh_own.shape[1]),)
    return call(own_back_kernel, "own_back", out_shape, [], 1 << 31, args)[0]


def ring(axis):
    peers = lax.axis_size(axis)
    up = [(i, (i + 1) % peers) for i in range(peers)]
    return up, [(j, i) for i, j in up]


def neighbours_of(block, axis, dim):
    up, down = ring(axis)
    length = block.shape[dim]
    if len(up) == 2 and length == 2:
        other = lax.ppermute(block, axis, up)
        return (
            lax.slice_in_dim(other, length - 1, length, axis=dim),
            lax.slice_in_dim(other, 0, 1, axis=dim),
        )
    before = lax.ppermute(lax.slice_in_dim(block, length - 1, length, axis=dim), axis, up)
    after = lax.ppermute(lax.slice_in_dim(block, 0, 1, axis=dim), axis, down)
    return before, after


def grown(block, axis, dim):
    before, after = neighbours_of(block, axis, dim)
    return jnp.concatenate([before, block, after], axis=dim)


def ghost_pieces(block):
    before, after = neighbours_of(block, "gx", 0)
    return tuple(piece.reshape(-1, block.shape[-1]) for piece in (before, block, after))


def forces_kernel(mid_ref, low_ref, high_ref, own_ref, home_ref, out_ref):
    values = mid_ref[...]
    lanes = values.shape[1]
    ext_z = iota(values.shape, 1) // 8 % 4
    values += jnp.where(ext_z == 1, pltpu.roll(low_ref[...], lanes - 16, 1), 0.0)
    values += jnp.where(ext_z == 2, pltpu.roll(high_ref[...], 16, 1), 0.0)
    first = values.astype(BF16)
    values -= first.astype(F32)
    second = values.astype(BF16)
    third = (values - second.astype(F32)).astype(BF16)
    home = home_ref[...]
    total = own_ref[...] + (mm_nt(first, home) + (mm_nt(second, home) + mm_nt(third, home)))
    for comp in range(3):
        out_ref[comp] = -total[comp : comp + 1, :]


def give_back(low, mid, high, own, home):
    up, down = ring("gx")
    from_low = lax.ppermute(high, "gx", up)
    from_high = lax.ppermute(low, "gx", down)
    from_low, from_high, own = lax.optimization_barrier((from_low, from_high, own))
    mid = mid + jnp.concatenate([from_low, from_high], axis=1)
    up, down = ring("gy")
    from_low = lax.ppermute(mid, "gy", up)
    from_high = lax.ppermute(mid, "gy", down)
    ext_y = jnp.arange(mid.shape[1], dtype=jnp.int32)[None] // 32 % 4
    mid = (
        mid
        + jnp.where(ext_y == 1, jnp.roll(from_low, -64, axis=1), 0.0)
        + jnp.where(ext_y == 2, jnp.roll(from_high, 64, axis=1), 0.0)
    )
    up, down = ring("gz")
    from_low = lax.ppermute(mid, "gz", up)
    from_high = from_low if len(up) == 2 else lax.ppermute(mid, "gz", down)
    args = (mid, from_low, from_high, own, home)
    out_shape = (struct(3, 1, own.shape[1]),)
    return call(forces_kernel, "forces", out_shape, [], 1 << 20, args)[0]


def local(
    features,
    positions,
    neighbours,
    counts,
    cell_atoms,
    rbf_weight,
    radial_weight,
    mix_weight,
    out_weight,
    energy_weight,
    norm_weight,
):
    feats = features[0, 0, 0]
    places = jnp.swapaxes(positions[0, 0], 0, 1)
    *cells, own_pos, meta = make_cells(
        feats, places, neighbours[0, 0, 0].T, counts[0, 0], cell_atoms[0, 0]
    )
    hold = lax.optimization_barrier
    block0, block1, block2 = (part.reshape(2, 2, 2, 8, part.shape[1]) for part in cells)
    block0 = grown(block0, "gz", 2)
    block0, block1, block2, own_pos, meta = hold((block0, block1, block2, own_pos, meta))
    block1, block2 = (grown(block, "gz", 2) for block in (block1, block2))
    block0 = grown(block0, "gy", 1)
    oh_own, pre_own, unit_own, radt, rbft, mixt, home, *radial_own = own_stage(
        meta, own_pos, rbf_weight, radial_weight, mix_weight
    )
    block0, block1, oh_own = hold((block0, block1, oh_own))
    pieces0 = ghost_pieces(block0)
    block1 = grown(block1, "gy", 1)
    pieces0, block1, block2 = hold((pieces0, block1, block2))
    pieces1 = ghost_pieces(block1)
    block2 = grown(block2, "gy", 1)
    (
        new_a, oh_gh, d_gh, dt_gh, radial_gh3, radial_gh4, pre_gh, unit_gh, gs0, en_a, m0_own,
        m0_gh, gate_own, gate_gh, nf0_own, nf0_gh, dot_own_a, dot_gh_a, gr1_own, gr1_gh, gr2_own,
        gr2_gh,
    ) = first_stage(
        pieces0, feats, own_pos, meta, rbf_weight, radial_weight, mix_weight, out_weight,
        energy_weight[None], norm_weight, oh_own, *radial_own[:3],
    )
    gate_own, block2 = hold((gate_own, block2))
    pieces2 = ghost_pieces(block2)
    shared = (
        feats, meta, mix_weight, out_weight, norm_weight, oh_own, oh_gh, d_gh, dt_gh, gate_own,
        gate_gh, radial_own[4], radial_gh4,
    )
    new_b, en_b, dot_own_b, dot_gh_b, gr3_own, gr3_gh, gr4_own_a, gr4_gh_a = second_stage(
        pieces1, *shared, radial_own[3], radial_gh3
    )
    new, energy, src, low, mid, high, dot_own_c, gr4_own_b = third_stage(
        pieces2, *shared, radt, rbft, mixt, gs0, en_a, en_b, new_a, new_b, pre_gh, unit_gh, m0_gh,
        nf0_gh, dot_gh_a, dot_gh_b, gr1_gh, gr2_gh, gr3_gh, gr4_gh_a,
    )
    own = own_back_stage(
        oh_own, pre_own, unit_own, radt, rbft, mixt, gs0, src, m0_own, nf0_own, dot_own_a,
        dot_own_b, dot_own_c, gr1_own, gr2_own, gr3_own, gr4_own_a, gr4_own_b,
    )
    forces = give_back(low, mid, high, own, home)
    return (
        new[None, None, None],
        energy[None, None],
        jnp.swapaxes(forces, 0, 1)[None, None],
    )


def solution(mesh):
    split = P("gx", "gy", "gz", None, None)
    flat = P("gx", "gy", "gz", None)
    return jax.shard_map(
        local,
        mesh=mesh,
        in_specs=(split, split, split, flat, flat, P(), P(), P(), P(), P(), P()),
        out_specs=(split, flat, split),
        check_vma=False,
    )
```

```python
import functools
import math

import jax
import jax.numpy as jnp
from jax import lax
from jax.experimental import pallas as pl
from jax.experimental.pallas import tpu as pltpu
from jax.sharding import PartitionSpec as P

F32 = jnp.float32
BF16 = jnp.bfloat16
CH = 128
SLOTS = 32
HALF = 16
STEP = 256
OWN_STEPS = 4
GH_STEPS = 2
MIB = 1024 * 1024
SPACE = pltpu.VMEM
PAIR_DEGREES = (
    (1, 1), (1, 2), (2, 2), (2, 2),
    (3, 3), (3, 3), (3, 3), (3, 4),
    (4, 4), (4, 4), (4, 4), (4, 4),
)
GROUPS = ((0, 3), (3, 8), (8, 12))
KINDS = tuple(sorted({PAIR_DEGREES[pair] for pair in range(*group)}) for group in GROUPS)
DEGREES = tuple(sorted({d for both in kinds for d in both}) for kinds in KINDS)
GROUP_COLS = tuple(2 * CH * (end - begin) for begin, end in GROUPS)


def mm(a, b):
    return jnp.dot(a, b, preferred_element_type=F32)


def mm_nt(a, b):
    return lax.dot_general(a, b, (((1,), (1,)), ((), ())), preferred_element_type=F32)


def iota(shape, dim):
    return lax.broadcasted_iota(jnp.int32, shape, dim)


def flip(w):
    return w.astype(F32).T.astype(BF16)


def pair_cols(pair):
    return slice(CH + pair * 2 * CH, CH + (pair + 1) * 2 * CH)


def struct(*shape, dtype=F32):
    return jax.ShapeDtypeStruct(shape, dtype)


def call(kernel, name, out_shape, scratch, flops, args, specs=None, limit=16):
    size = sum(a.size * a.dtype.itemsize for a in list(args) + list(out_shape))
    return pl.pallas_call(
        kernel,
        out_shape=out_shape,
        in_specs=specs or [pl.BlockSpec(memory_space=SPACE)] * len(args),
        out_specs=tuple(pl.BlockSpec(memory_space=SPACE) for _ in out_shape),
        scratch_shapes=scratch,
        compiler_params=pltpu.CompilerParams(vmem_limit_bytes=limit * MIB),
        cost_estimate=pl.CostEstimate(flops=flops, bytes_accessed=size, transcendentals=0),
        name=name,
    )(*args)


def cells_kernel(
    feat_hbm, pos_hbm, near_hbm, counts_hbm, order_hbm,
    first_ref, rest_ref, own_pos_ref, meta_ref,
    feat_ref, pos_ref, near_ref, counts_ref, order_ref, rows_ref, pos_rows, sems,
):
    args = (pos_hbm, near_hbm, counts_hbm, order_hbm, feat_hbm)
    held = (pos_ref, near_ref, counts_ref, order_ref, feat_ref)
    copies = [
        pltpu.make_async_copy(arg, ref, sems.at[index])
        for index, (arg, ref) in enumerate(zip(args, held))
    ]
    for copy in copies:
        copy.start()
    rows_ref[...] = jnp.zeros_like(rows_ref)
    pos_rows[...] = jnp.zeros_like(pos_rows)
    for copy in copies[:4]:
        copy.wait()
    atoms = feat_ref.shape[0]
    rows_ref[0:SLOTS, :] = near_ref[...].astype(F32)
    rows_ref[SLOTS : SLOTS + 1, :] = counts_ref[...].astype(F32)
    rows_ref[SLOTS + 1 : SLOTS + 2, :] = order_ref[...].astype(F32)
    meta = rows_ref[...].T
    meta_ref[...] = meta
    for comp in range(3):
        places = pos_ref[comp]
        first = places.astype(BF16).astype(F32)
        second = (places - first).astype(BF16).astype(F32)
        pos_rows[comp : comp + 1, :] = first
        pos_rows[4 + comp : 5 + comp, :] = second
        pos_rows[8 + comp : 9 + comp, :] = places - first - second
    pieces = pos_rows[...].astype(BF16)
    lane = iota((atoms, atoms), 1).astype(F32)
    pick = (meta[:, SLOTS + 1 : SLOTS + 2] == lane).astype(F32).astype(BF16)
    same = (iota((atoms, atoms), 0) == iota((atoms, atoms), 1)).astype(F32).astype(BF16)
    own_pos_ref[...] = mm_nt(same, pieces).astype(BF16)
    first_ref[:, CH : 2 * CH] = mm_nt(pick, pieces).astype(BF16)
    copies[4].wait()
    first_ref[:, 0:CH] = mm(pick, feat_ref[:, 0:CH]).astype(BF16)
    cut = pair_cols(GROUPS[1][0]).start
    first_ref[:, 2 * CH :] = mm(pick, feat_ref[:, CH:cut]).astype(BF16)
    rest_ref[...] = mm(pick, feat_ref[:, cut:]).astype(BF16)


def make_cells(feats, places, near, counts, order):
    atoms = feats.shape[0]
    out_shape = (
        struct(atoms, 2 * CH + GROUP_COLS[0], dtype=BF16),
        struct(atoms, sum(GROUP_COLS[1:]), dtype=BF16),
        struct(atoms, CH, dtype=BF16),
        struct(atoms, CH),
    )
    args = (feats, places, near, counts, order)
    scratch = [pltpu.VMEM(arg.shape, arg.dtype) for arg in args]
    scratch += [pltpu.VMEM((CH, atoms), F32), pltpu.VMEM((CH, atoms), F32)]
    scratch += [pltpu.SemaphoreType.DMA((5,))]
    specs = [pl.BlockSpec(memory_space=pltpu.HBM)] * 5
    return call(cells_kernel, "cells", out_shape, scratch, 1 << 26, args, specs)


def spacing_of(atoms, nbasis):
    depth = atoms // 16
    return 2.0 * math.sqrt(32.0 + depth * depth) / (nbasis - 1)


def own_onehots(meta_ref, oh_own):
    atoms = meta_ref.shape[0]
    counts = meta_ref[:, SLOTS : SLOTS + 1]
    lane_atom = iota((atoms, atoms), 1).astype(F32)
    for slot in range(HALF):
        hit = jnp.logical_and(meta_ref[:, slot : slot + 1] == lane_atom, counts > slot)
        oh_own[slot * atoms : (slot + 1) * atoms, :] = hit.astype(F32).astype(BF16)


def geometry(near, here):
    diff = near - here
    rel = (diff + pltpu.roll(diff, CH - 4, 1)) + (
        pltpu.roll(diff, CH - 8, 1) + pltpu.roll(diff, CH - 12, 1)
    )
    lane = iota(rel.shape, 1)
    rel = jnp.where(lane < 3, rel, 0.0)
    square = jnp.sum(rel * rel, axis=1, keepdims=True)
    inverse = lax.rsqrt(jnp.where(square > 0.0, square, 1.0))
    dist = square * inverse
    return jnp.where(lane == 3, dist, rel * inverse), dist


def centred_of(dist, spacing, nbasis):
    return dist * (1.0 / spacing) - iota((dist.shape[0], nbasis), 1).astype(F32)


def radial_net(dist, spacing, rbf_ref, rad_ref):
    centred = centred_of(dist, spacing, rbf_ref.shape[0])
    basis = jnp.exp(-0.5 * centred * centred)
    pre = mm(basis.astype(BF16), rbf_ref[...])
    hidden = (pre * jax.nn.sigmoid(pre)).astype(BF16)
    return pre, mm(hidden, rad_ref[...]).astype(BF16)


def own_spread(atoms, size=STEP):
    shape = (atoms, size)
    return (iota(shape, 1) % atoms == iota(shape, 0)).astype(F32).astype(BF16)


def tiled(values, size=STEP):
    return jnp.concatenate([values] * (size // values.shape[0]), axis=0)


def live_ghosts(meta_ref):
    return jnp.maximum(meta_ref[:, SLOTS : SLOTS + 1] - HALF, 0.0)


def step_count(meta_ref):
    total = jnp.sum(live_ghosts(meta_ref)).astype(jnp.int32)
    rows = GH_STEPS * STEP
    return jnp.maximum((total + (rows - 1)) // rows, 1) * GH_STEPS


def own_rows(step, size=STEP):
    return pl.ds(step * size, size)


def ghost_rows(step, size=STEP):
    first = OWN_STEPS * STEP
    if isinstance(step, int):
        return pl.ds(step * size, size), pl.ds(first + step * size, size)
    base = pl.multiple_of(step * size, size)
    return pl.ds(base, size), pl.ds(pl.multiple_of(first + base, size), size)


class Halves:
    def __init__(self, own, ghost):
        self.own, self.ghost = own, ghost
        self.dtype = own.dtype

    def place(self, rows):
        first = OWN_STEPS * STEP
        if not isinstance(rows.start, int):
            return self.ghost, pl.ds(pl.multiple_of(rows.start - first, rows.size), rows.size)
        if rows.start < first:
            return self.own, rows
        return self.ghost, pl.ds(rows.start - first, rows.size)

    def __getitem__(self, at):
        ref, rows = self.place(at[0])
        return ref[rows, at[1]]

    def __setitem__(self, at, value):
        ref, rows = self.place(at[0])
        ref[rows, at[1]] = value


def over_ghost_steps(steps, body, size=STEP):
    static = GH_STEPS * STEP // size
    for step in range(static):
        body(step)

    def again(step, carry):
        body(step)
        return carry

    lax.fori_loop(static, (steps * STEP + (size - 1)) // size, again, 0)


def block_diagonal(kinds, mix_ref, out_ref, wm, wmt, wo, wot):
    zero = jnp.zeros((CH, CH), BF16)
    for kind, both in enumerate(kinds):
        for ref in (wm, wmt, wo, wot):
            ref[kind, 0:CH, CH:] = zero
            ref[kind, CH:, 0:CH] = zero
    for degree in sorted({d for both in kinds for d in both}):
        mix, out = mix_ref[degree], out_ref[degree]
        mix_t, out_t = flip(mix), flip(out)
        for kind, both in enumerate(kinds):
            for side in range(2):
                if both[side] == degree:
                    part = slice(side * CH, side * CH + CH)
                    wm[kind, part, part] = mix
                    wmt[kind, part, part] = mix_t
                    wo[kind, part, part] = out
                    wot[kind, part, part] = out_t


def fetch(pieces, cols, table, sems):
    low, high, ghosts = 0, 0, table.shape[0]
    if len(pieces) == 3:
        rows = [(piece, 0, piece.shape[0]) for piece in pieces]
    else:
        low_in, low_out, mid, high_in, high_out = pieces
        half = low_out.shape[0] // 2
        rows = [(low_out, 0, half), (low_in, 0, low_in.shape[0]), (low_out, half, half)]
        rows += [(mid, 0, mid.shape[0])]
        rows += [(high_out, 0, half), (high_in, 0, high_in.shape[0]), (high_out, half, half)]
    copies = []
    at = 0
    for index, (piece, start, count) in enumerate(rows):
        source = piece.at[pl.ds(start, count), cols]
        target = table.at[pl.ds(at, count), :]
        copies.append(pltpu.make_async_copy(source, target, sems.at[index]))
        at += count
    for copy in copies:
        copy.start()
    return copies


def run_pairs(
    pairs, kinds, own_ref, table, new_ref, new_base, oh_own, oh_gh, d_gh, dt_gh,
    gate_ref, radial_of, nw_ref, steps, wm, wmt, wo, wot, nf_s, mx_s, acc_s, gs_s, dot_ref,
    grad_refs, en_ref, size=STEP,
):
    atoms = own_ref.shape[0]
    norm = 1.0 / math.sqrt(SLOTS)
    spread_own = own_spread(atoms, size)
    own_steps = OWN_STEPS * STEP // size
    begin, end = pair_cols(pairs[0]).start, pair_cols(pairs[-1]).stop
    own_cols = slice(begin, end)
    infos = []
    for index, pair in enumerate(pairs):
        degrees = PAIR_DEGREES[pair]
        infos.append((slice(index * 2 * CH, (index + 1) * 2 * CH), degrees, kinds.index(degrees)))

    def gate_of(rows):
        gate = gate_ref[rows, :]
        return jnp.concatenate([gate, gate], axis=1)

    def forward(rows, onehot, feats):
        near = mm(onehot, feats).astype(BF16)
        nf_s[rows, :] = near
        gate = gate_of(rows)
        messages = []
        for cols, degrees, kind in infos:
            radial = jnp.concatenate([radial_of(d, rows) for d in degrees], axis=1)
            mixed = mm(near[:, cols] * radial, wm[kind]).astype(BF16)
            mx_s[rows, cols] = mixed
            messages.append(mixed * gate)
        return jnp.concatenate(messages, axis=1)

    def backward(rows, grad):
        parts = {}
        dots = None
        gate = gate_of(rows)
        for cols, degrees, kind in infos:
            product = grad[:, cols] * mx_s[rows, cols]
            dot = (product[:, 0:CH] + product[:, CH:]).astype(F32)
            dots = dot if dots is None else dots + dot
            weighted = mm(grad[:, cols] * gate, wmt[kind]) * nf_s[rows, cols].astype(F32)
            for side in range(2):
                part = weighted[:, side * CH : (side + 1) * CH]
                degree = degrees[side]
                parts[degree] = parts[degree] + part if degree in parts else part
        dot_ref[rows, :] = dots.astype(dot_ref.dtype)
        for degree, part in parts.items():
            grad_refs[degree][rows, :] = part.astype(grad_refs[degree].dtype)

    own = own_ref[:, own_cols]
    summed = None
    for step in range(own_steps):
        rows = own_rows(step, size)
        part = mm(spread_own, forward(rows, oh_own[rows, :], own))
        summed = part if summed is None else summed + part
    acc_s[...] = summed

    def ghost_forward(step):
        here, rows = ghost_rows(step, size)
        message = forward(rows, oh_gh[here, :], table[...])
        acc_s[...] += mm(dt_gh[:, here], message)

    over_ghost_steps(steps, ghost_forward, size)

    for cols, degrees, kind in infos:
        summed_low = (acc_s[:, cols] * norm).astype(BF16)
        updated = own[:, cols].astype(F32) + mm(summed_low, wo[kind])
        at = begin - new_base + cols.start
        new_ref[:, at : at + 2 * CH] = updated.astype(BF16)
        weight = jnp.concatenate(
            [nw_ref[d - 1 : d, :] * (1.0 / (2 * d + 1)) for d in degrees], axis=1
        )
        scale = weight * updated
        energy = scale * updated
        en_ref[...] += energy[:, 0:CH] + energy[:, CH:]
        gs_s[:, cols] = (mm((2.0 * scale).astype(BF16), wot[kind]) * norm).astype(BF16)

    grad_own = tiled(gs_s[...], size)
    for step in range(own_steps):
        backward(own_rows(step, size), grad_own)

    def ghost_backward(step):
        here, rows = ghost_rows(step, size)
        backward(rows, mm(d_gh[here, :], gs_s[...]).astype(BF16))

    over_ghost_steps(steps, ghost_backward, size)


def pair_scratch(atoms, edges, ghosts, group):
    count, width = len(KINDS[group]), GROUP_COLS[group]
    return (
        [pltpu.VMEM((ghosts, width), BF16), pltpu.SemaphoreType.DMA((7,))]
        + [pltpu.VMEM((count, 2 * CH, 2 * CH), BF16) for _ in range(4)]
        + [
            pltpu.VMEM((edges, width), BF16),
            pltpu.VMEM((edges, width), BF16),
            pltpu.VMEM((atoms, width), F32),
            pltpu.VMEM((atoms, width), BF16),
        ]
    )


def own_kernel(
    meta_ref, own_pos_ref, rbf_ref, rad_ref, mix_ref,
    oh_own, pre_ref, unit_ref, radt_ref, rbft_ref, mixt_ref, home_ref, *radial_refs
):
    atoms = meta_ref.shape[0]
    nbasis = rbf_ref.shape[0]
    spacing = spacing_of(atoms, nbasis)
    own_onehots(meta_ref, oh_own)
    here = tiled(own_pos_ref[...].astype(F32))
    for step in range(OWN_STEPS):
        rows = own_rows(step)
        unit, dist = geometry(mm(oh_own[rows, :], own_pos_ref[...]), here)
        unit_ref[rows, :] = unit
        pre, radial = radial_net(dist, spacing, rbf_ref, rad_ref)
        pre_ref[rows, :] = pre.astype(BF16)
        for degree, ref in enumerate(radial_refs):
            ref[rows, :] = radial[:, degree * CH : (degree + 1) * CH]
    for degree in range(5):
        part = slice(degree * CH, (degree + 1) * CH)
        radt_ref[part, :] = flip(rad_ref[:, part])
    for index in range(nbasis // CH):
        part = slice(index * CH, (index + 1) * CH)
        rbft_ref[:, part] = flip(rbf_ref[part, :])
    mixt_ref[...] = flip(mix_ref[0])
    lanes = home_ref.shape[1]
    lane = iota((atoms, lanes), 1)
    ext_x, ext_y, ext_z = lane // 128, lane // 32 % 4, lane // 8 % 4
    slot = ((2 * ext_x + ext_y - 1) * 2 + ext_z - 1) * 8 + lane % 8
    inside = jnp.logical_and(
        jnp.logical_or(ext_y == 1, ext_y == 2), jnp.logical_or(ext_z == 1, ext_z == 2)
    )
    to_slot = jnp.logical_and(iota((atoms, lanes), 0) == slot, inside)
    to_slot = to_slot.astype(F32).astype(BF16)
    order = meta_ref[:, SLOTS + 1 : SLOTS + 2]
    to_atom = (order == iota((atoms, atoms), 1).astype(F32)).astype(F32)
    home_ref[...] = mm(to_atom.T.astype(BF16), to_slot).astype(BF16)


def own_stage(meta, own_pos, rbf, rad, mix):
    atoms = meta.shape[0]
    edges = atoms * HALF
    out_shape = (
        struct(edges, atoms, dtype=BF16),
        struct(edges, CH, dtype=BF16),
        struct(edges, CH),
        struct(*rad.shape[::-1], dtype=BF16),
        struct(*rbf.shape[::-1], dtype=BF16),
        struct(CH, CH, dtype=BF16),
        struct(atoms, 256, dtype=BF16),
    ) + (struct(edges, CH, dtype=BF16),) * 5
    args = (meta, own_pos, rbf, rad, mix)
    return call(own_kernel, "own_edges", out_shape, [], 1 << 31, args)


def start_kernel(
    p0, p1, p2, p3, p4, own_ref, own_pos_ref, meta_ref, rbf_ref, rad_ref, mix_ref, out_ref,
    ew_ref, oh_own, radial_own0,
    new_ref, oh_gh, d_gh, dt_gh, pre_ref, unit_ref, gs0_ref, en_ref, m0_own, m0_gh, gate_own,
    gate_gh, nf0_own, nf0_gh, radial_gh1, radial_gh2, radial_gh3, radial_gh4,
    table, sems, ghpos, acc_s,
):
    m0_ref, gate_ref = Halves(m0_own, m0_gh), Halves(gate_own, gate_gh)
    nf0_ref = Halves(nf0_own, nf0_gh)
    radial_gh = (None, radial_gh1, radial_gh2, radial_gh3, radial_gh4)
    copies = fetch((p0, p1, p2, p3, p4), slice(0, 2 * CH), table, sems)
    atoms = own_ref.shape[0]
    ghosts = table.shape[0]
    spacing = spacing_of(atoms, rbf_ref.shape[0])
    norm = 1.0 / math.sqrt(SLOTS)

    live = live_ghosts(meta_ref)
    sub_atom = iota((atoms, atoms), 0)
    lane_atom = iota((atoms, atoms), 1)
    live_b = jnp.broadcast_to(live, (atoms, atoms))
    end_row = jnp.sum(jnp.where(sub_atom <= lane_atom, live_b, 0.0), axis=0, keepdims=True)
    live_row = jnp.sum(jnp.where(sub_atom == lane_atom, live_b, 0.0), axis=0, keepdims=True)
    start_row = end_row - live_row
    row_b = jnp.broadcast_to(live_row, (atoms, atoms))
    end_col = jnp.sum(jnp.where(lane_atom <= sub_atom, row_b, 0.0), axis=1, keepdims=True)
    start_col = end_col - live
    total = jnp.sum(live)
    steps = step_count(meta_ref)
    ghost_row = meta_ref[:, HALF:SLOTS] - atoms
    high_part = jnp.floor(ghost_row * (1.0 / 16.0))
    row_high = high_part.astype(BF16)
    row_low = (ghost_row - 16.0 * high_part).astype(BF16)

    row = iota((ghosts, CH), 0)
    lane = iota((ghosts, CH), 1)
    zcells = atoms // 32
    per_y = (zcells + 2) * 8
    ext_x = row // (4 * per_y)
    ext_y = row // per_y % 4
    ext_z = row // 8 % (zcells + 2)

    def side_of(ext, last, size):
        return jnp.where(ext == 0, -size, jnp.where(ext == last, size, 0.0))

    shift = jnp.where(lane == 12, side_of(ext_x, 3, 4.0), 0.0)
    shift = jnp.where(lane == 13, side_of(ext_y, 3, 4.0), shift)
    shift = jnp.where(lane == 14, side_of(ext_z, zcells + 1, 2.0 * zcells), shift)
    def forward0(rows, onehot, feats, radial):
        near = mm(onehot, feats).astype(BF16)
        nf0_ref[rows, :] = near
        mixed = mm(near * radial, mix_ref[0])
        m0_ref[rows, :] = mixed.astype(BF16)
        gate = jax.nn.sigmoid(mixed)
        gate_ref[rows, :] = gate.astype(BF16)
        return (mixed * gate).astype(BF16)

    own0 = own_ref[:, 0:CH]
    spread_own = own_spread(atoms)
    summed = None
    for step in range(OWN_STEPS):
        rows = own_rows(step)
        message = forward0(rows, oh_own[rows, :], own0, radial_own0[rows, :])
        part = mm(spread_own, message)
        summed = part if summed is None else summed + part
    acc_s[...] = summed
    for copy in copies:
        copy.wait()
    ghpos[...] = (table[:, CH:].astype(F32) + shift).astype(BF16)

    def ghost_start(step):
        here, rows = ghost_rows(step)
        base = step * STEP
        edge = (iota((STEP, atoms), 0) + base).astype(F32)
        mine = jnp.logical_and(edge >= start_row, edge < end_row).astype(F32)
        source = mine.astype(BF16)
        d_gh[here, :] = source
        edge_t = (iota((atoms, STEP), 1) + base).astype(F32)
        mine_t = jnp.logical_and(edge_t >= start_col, edge_t < end_col)
        spread = mine_t.astype(F32).astype(BF16)
        dt_gh[:, here] = spread
        edge_col = edge[:, 0:1]
        slot = edge_col - jnp.sum(mine * start_row, axis=1, keepdims=True)
        listed = mm(source, row_high) * 16.0 + mm(source, row_low)
        at_slot = iota((STEP, HALF), 1).astype(F32) == slot
        which = jnp.sum(jnp.where(at_slot, listed, 0.0), axis=1, keepdims=True)
        which = jnp.where(edge_col < total, which, -1.0)
        onehot = (iota((STEP, ghosts), 1).astype(F32) == which).astype(F32).astype(BF16)
        oh_gh[here, :] = onehot
        unit, dist = geometry(mm(onehot, ghpos[...]), mm(source, own_pos_ref[...]))
        unit_ref[here, :] = unit
        pre, radial = radial_net(dist, spacing, rbf_ref, rad_ref)
        pre_ref[here, :] = pre.astype(BF16)
        for degree in range(1, 5):
            radial_gh[degree][here, :] = radial[:, degree * CH : (degree + 1) * CH]
        message = forward0(rows, onehot, table[:, 0:CH], radial[:, 0:CH])
        acc_s[...] += mm(spread, message)

    over_ghost_steps(steps, ghost_start)

    low0 = (acc_s[...] * norm).astype(BF16)
    updated0 = own0.astype(F32) + mm(low0, out_ref[0])
    new_ref[:, 0:CH] = updated0.astype(BF16)
    logistic = jax.nn.sigmoid(updated0)
    weight0 = ew_ref[...]
    en_ref[...] = weight0 * updated0 * logistic
    grad0 = (weight0 * logistic * (1.0 + updated0 * (1.0 - logistic))).astype(BF16)
    gs0_ref[...] = mm_nt(grad0, out_ref[0]) * norm


def any_specs(count, total):
    return [pl.BlockSpec(memory_space=pl.ANY)] * count + [
        pl.BlockSpec(memory_space=SPACE)
    ] * (total - count)


def start_stage(pieces, feats, *rest):
    atoms = feats.shape[0]
    half = atoms * HALF
    ghosts = sum(piece.shape[0] for piece in pieces)
    out_shape = (
        struct(atoms, CH, dtype=BF16),
        struct(half, ghosts, dtype=BF16),
        struct(half, atoms, dtype=BF16),
        struct(atoms, half, dtype=BF16),
        struct(half, CH, dtype=BF16),
        struct(half, CH),
        struct(atoms, CH),
        struct(atoms, CH),
    ) + (struct(half, CH, dtype=BF16),) * 10
    scratch = [
        pltpu.VMEM((ghosts, 2 * CH), BF16),
        pltpu.SemaphoreType.DMA((7,)),
        pltpu.VMEM((ghosts, CH), BF16),
        pltpu.VMEM((atoms, CH), F32),
    ]
    args = tuple(pieces) + (feats,) + rest
    return call(
        start_kernel, "ghost_start", out_shape, scratch, 1 << 31, args,
        any_specs(len(pieces), len(args)), 24,
    )


def pairs_kernel(group, count, skip, *refs):
    pieces, refs = refs[:count], refs[count:]
    own_ref, meta_ref, mix_ref, out_ref, nw_ref, oh_own, oh_gh, d_gh, dt_gh = refs[:9]
    gate_ref = Halves(*refs[9:11])
    refs = refs[11:]
    degrees = DEGREES[group]
    radials = {}
    for degree in degrees:
        radials[degree], refs = Halves(*refs[:2]), refs[2:]
    new_ref, en_ref, dot_own, dot_gh = refs[:4]
    refs = refs[4:]
    grads = {}
    for degree in degrees:
        grads[degree], refs = Halves(*refs[:2]), refs[2:]
    table, sems, wm, wmt, wo, wot, nf_s, mx_s, acc_s, gs_s = refs
    copies = fetch(pieces, slice(skip, skip + GROUP_COLS[group]), table, sems)
    block_diagonal(KINDS[group], mix_ref, out_ref, wm, wmt, wo, wot)
    en_ref[...] = jnp.zeros_like(en_ref)
    pairs = tuple(range(*GROUPS[group]))

    def radial_any(degree, rows):
        return radials[degree][rows, :]

    for copy in copies:
        copy.wait()
    run_pairs(
        pairs, KINDS[group], own_ref, table, new_ref, pair_cols(pairs[0]).start, oh_own, oh_gh,
        d_gh, dt_gh, gate_ref, radial_any, nw_ref, step_count(meta_ref), wm, wmt, wo, wot, nf_s,
        mx_s, acc_s, gs_s, Halves(dot_own, dot_gh), grads, en_ref,
    )


def pairs_stage(group, skip, pieces, shared, radials):
    feats = shared[0]
    atoms = feats.shape[0]
    half = atoms * HALF
    ghosts = sum(piece.shape[0] for piece in pieces)
    degrees = DEGREES[group]
    out_shape = (
        struct(atoms, GROUP_COLS[group], dtype=BF16),
        struct(atoms, CH),
    ) + (struct(half, CH, dtype=BF16),) * (2 + 2 * len(degrees))
    args = tuple(pieces) + tuple(shared)
    for degree in degrees:
        args += radials[degree]
    new, energy, dot_own, dot_gh, *grads = call(
        functools.partial(pairs_kernel, group, len(pieces), skip), "pairs_" + "abc"[group],
        out_shape, pair_scratch(atoms, 2 * half, ghosts, group), 1 << 33, args,
        any_specs(len(pieces), len(args)), 32,
    )
    grads = {degree: tuple(grads[2 * i : 2 * i + 2]) for i, degree in enumerate(degrees)}
    return new, energy, dot_own, dot_gh, grads


def finish(
    grad, mixed, near, dots, parts, pre, unit, spacing, radt_ref, rbft_ref, mixt_ref
):
    mixed = mixed.astype(F32)
    gate = jax.nn.sigmoid(mixed)
    first = grad * gate * (1.0 + mixed * (1.0 - gate)) + dots * gate * (1.0 - gate)
    weighted = mm(first.astype(BF16), mixt_ref[...]) * near.astype(F32)
    radial_grad = jnp.concatenate([weighted.astype(BF16)] + parts, axis=1)
    hidden_grad = mm(radial_grad, radt_ref[...])
    pre = pre.astype(F32)
    logistic = jax.nn.sigmoid(pre)
    pre_grad = (hidden_grad * logistic * (1.0 + pre * (1.0 - logistic))).astype(BF16)
    centred = centred_of(unit[:, 3:4], spacing, rbft_ref.shape[1])
    slope = jnp.exp(-0.5 * centred * centred) * centred
    basis_grad = mm(pre_grad, rbft_ref[...])
    dist_grad = jnp.sum(basis_grad * slope, axis=1, keepdims=True) * (-1.0 / spacing)
    pull = unit * dist_grad
    across = pull.T[0:8, :]
    top = across.astype(BF16)
    rest = (across - top.astype(F32)).astype(BF16)
    return pull, top, rest


def sum_of(refs, rows):
    total = refs[0][rows, :].astype(F32)
    for ref in refs[1:]:
        total += ref[rows, :].astype(F32)
    return total


def degree_parts(refs, rows):
    by_degree = {}
    refs = list(refs)
    for degrees in DEGREES:
        for degree in degrees:
            by_degree.setdefault(degree, []).append(refs.pop(0))
    return [sum_of(by_degree[degree], rows).astype(BF16) for degree in range(1, 5)]


PARTIALS = sum(len(degrees) for degrees in DEGREES)


def third_kernel(
    low_ref, mid_ref, high_ref, own_ref, meta_ref, mix_ref, out_ref, nw_ref, oh_own, oh_gh, d_gh,
    dt_gh, gate_own, gate_gh, radial_own4, radial_gh4,
    radt_ref, rbft_ref, mixt_ref, gs0_ref, en_0, en_a, en_b, new_0, new_a, new_b, pre_gh, unit_gh,
    m0_ref, nf0_ref, dot_a, dot_b, *refs
):
    gr_gh, refs = refs[: PARTIALS - 1], refs[PARTIALS - 1 :]
    (
        new_ref, energy_ref, src_ref, flow_ref, fmid_ref, fhigh_ref, dot_own, gr_own,
        table, sems, wm, wmt, wo, wot, nf_s, mx_s, acc_s, gs_s, dot_c, gr_c, en_s, fgh_s,
    ) = refs
    group = 2
    gate_ref = Halves(gate_own, gate_gh)
    radial4 = Halves(radial_own4, radial_gh4)
    pairs = tuple(range(*GROUPS[group]))
    copies = fetch((low_ref, mid_ref, high_ref), slice(0, GROUP_COLS[group]), table, sems)
    atoms = own_ref.shape[0]
    spacing = spacing_of(atoms, rbft_ref.shape[1])
    block_diagonal(KINDS[group], mix_ref, out_ref, wm, wmt, wo, wot)
    en_s[...] = en_0[...] + en_a[...] + en_b[...]
    at = 0
    for part in (new_0, new_a, new_b):
        new_ref[:, at : at + part.shape[1]] = part[...]
        at += part.shape[1]
    steps = step_count(meta_ref)

    def radial_any(degree, rows):
        return radial4[rows, :]

    for copy in copies:
        copy.wait()
    run_pairs(
        pairs, KINDS[group], own_ref, table, new_ref, 0, oh_own, oh_gh, d_gh, dt_gh, gate_ref,
        radial_any, nw_ref, steps, wm, wmt, wo, wot, nf_s, mx_s, acc_s, gs_s,
        Halves(dot_own, dot_c), {4: Halves(gr_own, gr_c)}, en_s,
    )
    energy_ref[...] = jnp.sum(en_s[...].T, axis=0, keepdims=True)

    fgh_s[...] = jnp.zeros_like(fgh_s)
    src_ref[...] = jnp.zeros_like(src_ref)
    gs0_low = gs0_ref[...].astype(BF16)

    def ghost_finish(step):
        here, rows = ghost_rows(step)
        grad = mm(d_gh[here, :], gs0_low)
        pull, top, rest = finish(
            grad, m0_ref[here, :], nf0_ref[here, :], sum_of((dot_a, dot_b, dot_c), here),
            degree_parts(gr_gh + (gr_c,), here), pre_gh[here, :], unit_gh[here, :], spacing,
            radt_ref, rbft_ref, mixt_ref,
        )
        pull_top = pull.astype(BF16)
        pull_rest = (pull - pull_top.astype(F32)).astype(BF16)
        spread = dt_gh[:, here]
        src_ref[...] += mm(spread, pull_top) + mm(spread, pull_rest)
        onehot = oh_gh[here, :]
        fgh_s[...] += mm(top, onehot) + mm(rest, onehot)

    over_ghost_steps(steps, ghost_finish)
    low, mid = flow_ref.shape[1], fmid_ref.shape[1]
    flow_ref[...] = fgh_s[:, 0:low]
    fmid_ref[...] = fgh_s[:, low : low + mid]
    fhigh_ref[...] = fgh_s[:, low + mid :]


def third_stage(pieces, feats, *rest):
    atoms, feat = feats.shape
    half = atoms * HALF
    sizes = [piece.shape[0] for piece in pieces]
    ghosts = sum(sizes)
    out_shape = (
        struct(atoms, feat, dtype=BF16),
        struct(1, atoms),
        struct(atoms, CH),
    ) + tuple(struct(8, size) for size in sizes) + (struct(half, CH, dtype=BF16),) * 2
    scratch = pair_scratch(atoms, 2 * half, ghosts, 2) + [
        pltpu.VMEM((half, CH), BF16),
        pltpu.VMEM((half, CH), BF16),
        pltpu.VMEM((atoms, CH), F32),
        pltpu.VMEM((8, ghosts), F32),
    ]
    args = tuple(pieces) + (feats,) + rest
    return call(
        third_kernel, "third_group", out_shape, scratch, 1 << 33, args, any_specs(3, len(args)),
        30,
    )


def own_back_kernel(
    oh_own, pre_own, unit_own, radt_ref, rbft_ref, mixt_ref, gs0_ref, src_ref,
    m0_ref, nf0_ref, dot_a, dot_b, dot_c, *refs
):
    gr_own, (force_ref,) = refs[:PARTIALS], refs[PARTIALS:]
    atoms = oh_own.shape[1]
    spacing = spacing_of(atoms, rbft_ref.shape[1])
    grad = tiled(gs0_ref[...])
    src = src_ref[...]
    onto = jnp.zeros((8, atoms), F32)
    for step in range(OWN_STEPS):
        rows = own_rows(step)
        pull, top, rest = finish(
            grad, m0_ref[rows, :], nf0_ref[rows, :], sum_of((dot_a, dot_b, dot_c), rows),
            degree_parts(gr_own, rows), pre_own[rows, :], unit_own[rows, :], spacing, radt_ref,
            rbft_ref, mixt_ref,
        )
        src += jnp.sum(pull.reshape(STEP // atoms, atoms, CH), axis=0)
        onehot = oh_own[rows, :]
        onto += mm(top, onehot) + mm(rest, onehot)
    force_ref[...] = onto - src.T[0:8, :]


def own_back_stage(*args):
    oh_own = args[0]
    out_shape = (struct(8, oh_own.shape[1]),)
    return call(own_back_kernel, "own_back", out_shape, [], 1 << 31, args)[0]


def ring(axis):
    peers = lax.axis_size(axis)
    up = [(i, (i + 1) % peers) for i in range(peers)]
    return up, [(j, i) for i, j in up]


def neighbours_of(block, axis, dim):
    up, down = ring(axis)
    length = block.shape[dim]
    if len(up) == 2 and length == 2:
        other = lax.ppermute(block, axis, up)
        return (
            lax.slice_in_dim(other, length - 1, length, axis=dim),
            lax.slice_in_dim(other, 0, 1, axis=dim),
        )
    before = lax.ppermute(lax.slice_in_dim(block, length - 1, length, axis=dim), axis, up)
    after = lax.ppermute(lax.slice_in_dim(block, 0, 1, axis=dim), axis, down)
    return before, after


def grown(block, axis, dim):
    before, after = neighbours_of(block, axis, dim)
    return jnp.concatenate([before, block, after], axis=dim)


def ghost_pieces(block):
    before, after = neighbours_of(block, "gx", 0)
    return tuple(flat_rows(piece) for piece in (before, block, after))


def flat_rows(piece):
    return piece.reshape(-1, piece.shape[-1])


def fold_kernel(mid_ref, low_ref, high_ref, out_ref):
    lanes = mid_ref.shape[1]
    ext_y = iota(mid_ref.shape, 1) // 32 % 4
    out_ref[...] = (
        mid_ref[...]
        + jnp.where(ext_y == 1, pltpu.roll(low_ref[...], lanes - 64, 1), 0.0)
        + jnp.where(ext_y == 2, pltpu.roll(high_ref[...], 64, 1), 0.0)
    )


def forces_kernel(mid_ref, low_ref, high_ref, own_ref, home_ref, out_ref):
    values = mid_ref[...]
    lanes = values.shape[1]
    ext_z = iota(values.shape, 1) // 8 % 4
    values += jnp.where(ext_z == 1, pltpu.roll(low_ref[...], lanes - 16, 1), 0.0)
    values += jnp.where(ext_z == 2, pltpu.roll(high_ref[...], 16, 1), 0.0)
    first = values.astype(BF16)
    values -= first.astype(F32)
    second = values.astype(BF16)
    third = (values - second.astype(F32)).astype(BF16)
    home = home_ref[...]
    total = own_ref[...] + (mm_nt(first, home) + (mm_nt(second, home) + mm_nt(third, home)))
    for comp in range(3):
        out_ref[comp] = -total[comp : comp + 1, :]


def give_back(low, mid, high, own, home):
    up, down = ring("gx")
    from_low = lax.ppermute(high, "gx", up)
    from_high = lax.ppermute(low, "gx", down)
    from_low, from_high, own = lax.optimization_barrier((from_low, from_high, own))
    mid = mid + jnp.concatenate([from_low, from_high], axis=1)
    up, down = ring("gy")
    from_low = lax.ppermute(mid, "gy", up)
    from_high = lax.ppermute(mid, "gy", down)
    args = (mid, from_low, from_high)
    mid = call(fold_kernel, "fold", (struct(*mid.shape),), [], 1 << 16, args)[0]
    up, down = ring("gz")
    from_low = lax.ppermute(mid, "gz", up)
    from_high = from_low if len(up) == 2 else lax.ppermute(mid, "gz", down)
    args = (mid, from_low, from_high, own, home)
    out_shape = (struct(3, 1, own.shape[1]),)
    return call(forces_kernel, "forces", out_shape, [], 1 << 20, args)[0]


def local(
    features,
    positions,
    neighbours,
    counts,
    cell_atoms,
    rbf_weight,
    radial_weight,
    mix_weight,
    out_weight,
    energy_weight,
    norm_weight,
):
    feats = features[0, 0, 0]
    places = jnp.swapaxes(positions[0, 0], 0, 1)
    cells0, cells12, own_pos, meta = make_cells(
        feats, places, neighbours[0, 0, 0].T, counts[0, 0], cell_atoms[0, 0]
    )
    hold = lax.optimization_barrier
    block0, block12 = (part.reshape(2, 2, 2, 8, part.shape[1]) for part in (cells0, cells12))
    block0 = grown(block0, "gz", 2)
    block0, block12, own_pos, meta = hold((block0, block12, own_pos, meta))
    y_low, y_high = neighbours_of(block0, "gy", 1)
    low_in, high_in = neighbours_of(block0, "gx", 0)
    block12 = grown(block12, "gz", 2)
    oh_own, pre_own, unit_own, radt, rbft, mixt, home, *radial_own = own_stage(
        meta, own_pos, rbf_weight, radial_weight, mix_weight
    )
    y_low, y_high, block12, oh_own = hold((y_low, y_high, block12, oh_own))
    outer = jnp.concatenate([y_low, y_high], axis=1)
    low_out, high_out = neighbours_of(outer, "gx", 0)
    middle = jnp.concatenate([y_low, block0, y_high], axis=1)
    pieces0 = tuple(flat_rows(p) for p in (low_in, low_out, middle, high_in, high_out))
    block1, block2 = block12[..., : GROUP_COLS[1]], block12[..., GROUP_COLS[1] :]
    block1 = grown(block1, "gy", 1)
    (
        new_0, oh_gh, d_gh, dt_gh, pre_gh, unit_gh, gs0, en_0, m0_own, m0_gh, gate_own, gate_gh,
        nf0_own, nf0_gh, *radial_gh,
    ) = start_stage(
        pieces0, feats, own_pos, meta, rbf_weight, radial_weight, mix_weight, out_weight,
        energy_weight[None], oh_own, radial_own[0],
    )
    block1, block2, gate_own = hold((block1, block2, gate_own))
    pieces1 = ghost_pieces(block1)
    block2 = grown(block2, "gy", 1)
    shared = (
        feats, meta, mix_weight, out_weight, norm_weight, oh_own, oh_gh, d_gh, dt_gh, gate_own,
        gate_gh,
    )
    radials = {degree: (radial_own[degree], radial_gh[degree - 1]) for degree in range(1, 5)}
    new_a, en_a, dot_own_a, dot_gh_a, grads_a = pairs_stage(0, 2 * CH, pieces0, shared, radials)
    en_a, block2 = hold((en_a, block2))
    pieces2 = ghost_pieces(block2)
    new_b, en_b, dot_own_b, dot_gh_b, grads_b = pairs_stage(1, 0, pieces1, shared, radials)
    grads = list(grads_a.values()) + list(grads_b.values())
    new, energy, src, low, mid, high, dot_own_c, gr_own_c = third_stage(
        pieces2, *shared, *radials[4], radt, rbft, mixt, gs0, en_0, en_a, en_b, new_0, new_a,
        new_b, pre_gh, unit_gh, m0_gh, nf0_gh, dot_gh_a, dot_gh_b, *[ghost for _, ghost in grads],
    )
    own = own_back_stage(
        oh_own, pre_own, unit_own, radt, rbft, mixt, gs0, src, m0_own, nf0_own, dot_own_a,
        dot_own_b, dot_own_c, *[own for own, _ in grads], gr_own_c,
    )
    forces = give_back(low, mid, high, own, home)
    return (
        new[None, None, None],
        energy[None, None],
        jnp.swapaxes(forces, 0, 1)[None, None],
    )


def solution(mesh):
    split = P("gx", "gy", "gz", None, None)
    flat = P("gx", "gy", "gz", None)
    return jax.shard_map(
        local,
        mesh=mesh,
        in_specs=(split, split, split, flat, flat, P(), P(), P(), P(), P(), P()),
        out_specs=(split, flat, split),
        check_vma=False,
    )
```

```python
import functools
import math

import jax
import jax.numpy as jnp
from jax import lax
from jax.experimental import pallas as pl
from jax.experimental.pallas import tpu as pltpu
from jax.sharding import PartitionSpec as P

F32 = jnp.float32
BF16 = jnp.bfloat16
CH = 128
SLOTS = 32
HALF = 16
STEP = 256
OWN_STEPS = 4
GH_STEPS = 2
MIB = 1024 * 1024
SPACE = pltpu.VMEM
PAIR_DEGREES = (
    (1, 1), (1, 2), (2, 2), (2, 2),
    (3, 3), (3, 3), (3, 3), (3, 4),
    (4, 4), (4, 4), (4, 4), (4, 4),
)
GROUPS = ((0, 3), (3, 8), (8, 12))
KINDS = tuple(sorted({PAIR_DEGREES[pair] for pair in range(*group)}) for group in GROUPS)
DEGREES = tuple(sorted({d for both in kinds for d in both}) for kinds in KINDS)
GROUP_COLS = tuple(2 * CH * (end - begin) for begin, end in GROUPS)


def mm(a, b):
    return jnp.dot(a, b, preferred_element_type=F32)


def mm_nt(a, b):
    return lax.dot_general(a, b, (((1,), (1,)), ((), ())), preferred_element_type=F32)


def iota(shape, dim):
    return lax.broadcasted_iota(jnp.int32, shape, dim)


def flip(w):
    return w.astype(F32).T.astype(BF16)


def pair_cols(pair):
    return slice(CH + pair * 2 * CH, CH + (pair + 1) * 2 * CH)


def struct(*shape, dtype=F32):
    return jax.ShapeDtypeStruct(shape, dtype)


def call(kernel, name, out_shape, scratch, flops, args, specs=None, limit=16):
    size = sum(a.size * a.dtype.itemsize for a in list(args) + list(out_shape))
    return pl.pallas_call(
        kernel,
        out_shape=out_shape,
        in_specs=specs or [pl.BlockSpec(memory_space=SPACE)] * len(args),
        out_specs=tuple(pl.BlockSpec(memory_space=SPACE) for _ in out_shape),
        scratch_shapes=scratch,
        compiler_params=pltpu.CompilerParams(vmem_limit_bytes=limit * MIB),
        cost_estimate=pl.CostEstimate(flops=flops, bytes_accessed=size, transcendentals=0),
        name=name,
    )(*args)


def cells_kernel(
    feat_hbm, pos_hbm, near_hbm, counts_hbm, order_hbm,
    first_ref, own_pos_ref, meta_ref, pick_ref,
    feat_ref, pos_ref, near_ref, counts_ref, order_ref, rows_ref, pos_rows, sems,
):
    args = (pos_hbm, near_hbm, counts_hbm, order_hbm, feat_hbm)
    held = (pos_ref, near_ref, counts_ref, order_ref, feat_ref)
    copies = [
        pltpu.make_async_copy(arg, ref, sems.at[index])
        for index, (arg, ref) in enumerate(zip(args, held))
    ]
    for copy in copies:
        copy.start()
    rows_ref[...] = jnp.zeros_like(rows_ref)
    pos_rows[...] = jnp.zeros_like(pos_rows)
    for copy in copies[:4]:
        copy.wait()
    atoms = feat_ref.shape[0]
    rows_ref[0:SLOTS, :] = near_ref[...].astype(F32)
    rows_ref[SLOTS : SLOTS + 1, :] = counts_ref[...].astype(F32)
    rows_ref[SLOTS + 1 : SLOTS + 2, :] = order_ref[...].astype(F32)
    meta = rows_ref[...].T
    meta_ref[...] = meta
    for comp in range(3):
        places = pos_ref[comp]
        first = places.astype(BF16).astype(F32)
        second = (places - first).astype(BF16).astype(F32)
        pos_rows[comp : comp + 1, :] = first
        pos_rows[4 + comp : 5 + comp, :] = second
        pos_rows[8 + comp : 9 + comp, :] = places - first - second
    pieces = pos_rows[...].astype(BF16)
    lane = iota((atoms, atoms), 1).astype(F32)
    pick = (meta[:, SLOTS + 1 : SLOTS + 2] == lane).astype(F32).astype(BF16)
    same = (iota((atoms, atoms), 0) == iota((atoms, atoms), 1)).astype(F32).astype(BF16)
    own_pos_ref[...] = mm_nt(same, pieces).astype(BF16)
    first_ref[:, CH : 2 * CH] = mm_nt(pick, pieces).astype(BF16)
    pick_ref[...] = pick
    copies[4].wait()
    first_ref[:, 0:CH] = mm(pick, feat_ref[:, 0:CH]).astype(BF16)
    cut = pair_cols(GROUPS[1][0]).start
    first_ref[:, 2 * CH :] = mm(pick, feat_ref[:, CH:cut]).astype(BF16)


def rest_kernel(feat_ref, pick_ref, rest_ref):
    cut = pair_cols(GROUPS[1][0]).start
    rest_ref[...] = mm(pick_ref[...], feat_ref[:, cut:]).astype(BF16)


def make_cells(feats, places, near, counts, order):
    atoms = feats.shape[0]
    out_shape = (
        struct(atoms, 2 * CH + GROUP_COLS[0], dtype=BF16),
        struct(atoms, CH, dtype=BF16),
        struct(atoms, CH),
        struct(atoms, atoms, dtype=BF16),
    )
    args = (feats, places, near, counts, order)
    scratch = [pltpu.VMEM(arg.shape, arg.dtype) for arg in args]
    scratch += [pltpu.VMEM((CH, atoms), F32), pltpu.VMEM((CH, atoms), F32)]
    scratch += [pltpu.SemaphoreType.DMA((5,))]
    specs = [pl.BlockSpec(memory_space=pl.ANY)] * 5
    first, own_pos, meta, pick = call(
        cells_kernel, "cells", out_shape, scratch, 1 << 26, args, specs
    )
    out_shape = (struct(atoms, sum(GROUP_COLS[1:]), dtype=BF16),)
    rest = call(rest_kernel, "cells_rest", out_shape, [], 1 << 26, (feats, pick))[0]
    return first, rest, own_pos, meta


def spacing_of(atoms, nbasis):
    depth = atoms // 16
    return 2.0 * math.sqrt(32.0 + depth * depth) / (nbasis - 1)


def own_onehots(meta_ref, oh_own):
    atoms = meta_ref.shape[0]
    counts = meta_ref[:, SLOTS : SLOTS + 1]
    lane_atom = iota((atoms, atoms), 1).astype(F32)
    for slot in range(HALF):
        hit = jnp.logical_and(meta_ref[:, slot : slot + 1] == lane_atom, counts > slot)
        oh_own[slot * atoms : (slot + 1) * atoms, :] = hit.astype(F32).astype(BF16)


def geometry(near, here):
    diff = near - here
    rel = (diff + pltpu.roll(diff, CH - 4, 1)) + (
        pltpu.roll(diff, CH - 8, 1) + pltpu.roll(diff, CH - 12, 1)
    )
    lane = iota(rel.shape, 1)
    rel = jnp.where(lane < 3, rel, 0.0)
    square = jnp.sum(rel * rel, axis=1, keepdims=True)
    inverse = lax.rsqrt(jnp.where(square > 0.0, square, 1.0))
    dist = square * inverse
    return jnp.where(lane == 3, dist, rel * inverse), dist


def centred_of(dist, spacing, nbasis):
    return dist * (1.0 / spacing) - iota((dist.shape[0], nbasis), 1).astype(F32)


def radial_net(dist, spacing, rbf_ref, rad_ref):
    centred = centred_of(dist, spacing, rbf_ref.shape[0])
    basis = jnp.exp(-0.5 * centred * centred)
    pre = mm(basis.astype(BF16), rbf_ref[...])
    hidden = (pre * jax.nn.sigmoid(pre)).astype(BF16)
    return pre, mm(hidden, rad_ref[...]).astype(BF16)


def own_spread(atoms, size=STEP):
    shape = (atoms, size)
    return (iota(shape, 1) % atoms == iota(shape, 0)).astype(F32).astype(BF16)


def tiled(values, size=STEP):
    return jnp.concatenate([values] * (size // values.shape[0]), axis=0)


def live_ghosts(meta_ref):
    return jnp.maximum(meta_ref[:, SLOTS : SLOTS + 1] - HALF, 0.0)


def step_count(meta_ref):
    total = jnp.sum(live_ghosts(meta_ref)).astype(jnp.int32)
    rows = GH_STEPS * STEP
    return jnp.maximum((total + (rows - 1)) // rows, 1) * GH_STEPS


def own_rows(step, size=STEP):
    return pl.ds(step * size, size)


def ghost_rows(step, size=STEP):
    first = OWN_STEPS * STEP
    if isinstance(step, int):
        return pl.ds(step * size, size), pl.ds(first + step * size, size)
    base = pl.multiple_of(step * size, size)
    return pl.ds(base, size), pl.ds(pl.multiple_of(first + base, size), size)


def over_ghost_steps(steps, body, size=STEP):
    static = GH_STEPS * STEP // size
    for step in range(static):
        body(step)

    def again(step, carry):
        body(step)
        return carry

    lax.fori_loop(static, (steps * STEP + (size - 1)) // size, again, 0)


def block_diagonal(kinds, source, straight=None, across=None):
    zero = jnp.zeros((CH, CH), BF16)
    targets = [ref for ref in (straight, across) if ref is not None]
    for kind, both in enumerate(kinds):
        for ref in targets:
            ref[kind, 0:CH, CH:] = zero
            ref[kind, CH:, 0:CH] = zero
    for degree in sorted({d for both in kinds for d in both}):
        weight = source[degree]
        flipped = flip(weight) if across is not None else None
        for kind, both in enumerate(kinds):
            for side in range(2):
                if both[side] == degree:
                    part = slice(side * CH, side * CH + CH)
                    if straight is not None:
                        straight[kind, part, part] = weight
                    if across is not None:
                        across[kind, part, part] = flipped


def fetch(pieces, cols, table, sems):
    low, high, ghosts = 0, 0, table.shape[0]
    if len(pieces) == 3:
        rows = [(piece, 0, piece.shape[0]) for piece in pieces]
    else:
        low_in, low_out, mid, high_in, high_out = pieces
        half = low_out.shape[0] // 2
        rows = [(low_out, 0, half), (low_in, 0, low_in.shape[0]), (low_out, half, half)]
        rows += [(mid, 0, mid.shape[0])]
        rows += [(high_out, 0, half), (high_in, 0, high_in.shape[0]), (high_out, half, half)]
    copies = []
    at = 0
    for index, (piece, start, count) in enumerate(rows):
        source = piece.at[pl.ds(start, count), cols]
        target = table.at[pl.ds(at, count), :]
        copies.append(pltpu.make_async_copy(source, target, sems.at[index]))
        at += count
    for copy in copies:
        copy.start()
    return copies


def infos_of(group):
    infos = []
    for index, pair in enumerate(range(*GROUPS[group])):
        degrees = PAIR_DEGREES[pair]
        cols = slice(index * 2 * CH, (index + 1) * 2 * CH)
        infos.append((cols, degrees, KINDS[group].index(degrees)))
    return infos


def group_cols(group):
    begin, end = GROUPS[group]
    return slice(pair_cols(begin).start, pair_cols(end - 1).stop)


def twice(values):
    return jnp.concatenate([values, values], axis=1)


def forward(group, rows, onehot, feats, radials, gate_ref, wm, nf_ref, mx_ref):
    near = mm(onehot, feats).astype(BF16)
    nf_ref[rows, :] = near
    gate = twice(gate_ref[rows, :])
    messages = []
    for cols, degrees, kind in infos_of(group):
        radial = jnp.concatenate([radials[d][rows, :] for d in degrees], axis=1)
        mixed = mm(near[:, cols] * radial, wm[kind]).astype(BF16)
        mx_ref[rows, cols] = mixed
        messages.append(mixed * gate)
    return jnp.concatenate(messages, axis=1)


def backward(group, rows, grad, gate_ref, wmt, nf_ref, mx_ref, dot_ref, grad_refs):
    parts = {}
    dots = None
    gate = twice(gate_ref[rows, :])
    for cols, degrees, kind in infos_of(group):
        product = grad[:, cols] * mx_ref[rows, cols]
        dot = (product[:, 0:CH] + product[:, CH:]).astype(F32)
        dots = dot if dots is None else dots + dot
        weighted = mm(grad[:, cols] * gate, wmt[kind]) * nf_ref[rows, cols].astype(F32)
        for side in range(2):
            part = weighted[:, side * CH : (side + 1) * CH]
            degree = degrees[side]
            parts[degree] = parts[degree] + part if degree in parts else part
    dot_ref[rows, :] = dots.astype(dot_ref.dtype)
    for degree, part in parts.items():
        grad_refs[degree][rows, :] = part.astype(grad_refs[degree].dtype)


def own_forward(group, own_ref, oh_own, radials, gate_ref, wm, nf_ref, mx_ref, acc_ref):
    spread = own_spread(own_ref.shape[0])
    feats = own_ref[:, group_cols(group)]
    summed = None
    for step in range(OWN_STEPS):
        rows = own_rows(step)
        message = forward(
            group, rows, oh_own[rows, :], feats, radials, gate_ref, wm, nf_ref, mx_ref
        )
        part = mm(spread, message)
        summed = part if summed is None else summed + part
    acc_ref[...] = summed


def own_backward(group, gs_ref, gate_ref, wmt, nf_ref, mx_ref, dot_ref, grad_refs):
    grad = tiled(gs_ref[...])
    for step in range(OWN_STEPS):
        backward(
            group, own_rows(step), grad, gate_ref, wmt, nf_ref, mx_ref, dot_ref, grad_refs
        )


def ghost_pairs(
    group, own_ref, table, new_ref, new_base, oh_gh, d_gh, dt_gh, gate_ref, radials, nw_ref,
    steps, wm, wmt, wo, wot, nf_s, mx_s, acc_in, acc_s, gs_ref, dot_ref, grad_refs, en_ref,
):
    norm = 1.0 / math.sqrt(SLOTS)
    acc_s[...] = acc_in[...]

    def ghost_forward(step):
        here, _ = ghost_rows(step)
        message = forward(
            group, here, oh_gh[here, :], table[...], radials, gate_ref, wm, nf_s, mx_s
        )
        acc_s[...] += mm(dt_gh[:, here], message)

    over_ghost_steps(steps, ghost_forward)

    begin = group_cols(group).start
    for cols, degrees, kind in infos_of(group):
        summed_low = (acc_s[:, cols] * norm).astype(BF16)
        own = own_ref[:, begin + cols.start : begin + cols.stop]
        updated = own.astype(F32) + mm(summed_low, wo[kind])
        at = begin - new_base + cols.start
        new_ref[:, at : at + 2 * CH] = updated.astype(BF16)
        weight = jnp.concatenate(
            [nw_ref[d - 1 : d, :] * (1.0 / (2 * d + 1)) for d in degrees], axis=1
        )
        scale = weight * updated
        energy = scale * updated
        en_ref[...] += energy[:, 0:CH] + energy[:, CH:]
        gs_ref[:, cols] = (mm((2.0 * scale).astype(BF16), wot[kind]) * norm).astype(BF16)

    def ghost_backward(step):
        here, _ = ghost_rows(step)
        grad = mm(d_gh[here, :], gs_ref[...]).astype(BF16)
        backward(group, here, grad, gate_ref, wmt, nf_s, mx_s, dot_ref, grad_refs)

    over_ghost_steps(steps, ghost_backward)


def pair_scratch(atoms, half, ghosts, group):
    count, width = len(KINDS[group]), GROUP_COLS[group]
    return (
        [pltpu.VMEM((ghosts, width), BF16), pltpu.SemaphoreType.DMA((7,))]
        + [pltpu.VMEM((count, 2 * CH, 2 * CH), BF16) for _ in range(4)]
        + [
            pltpu.VMEM((half, width), BF16),
            pltpu.VMEM((half, width), BF16),
            pltpu.VMEM((atoms, width), F32),
        ]
    )


def own_kernel(
    meta_ref, own_pos_ref, rbf_ref, rad_ref, mix_ref,
    oh_own, pre_ref, unit_ref, radt_ref, rbft_ref, mixt_ref, home_ref, *radial_refs
):
    atoms = meta_ref.shape[0]
    nbasis = rbf_ref.shape[0]
    spacing = spacing_of(atoms, nbasis)
    own_onehots(meta_ref, oh_own)
    here = tiled(own_pos_ref[...].astype(F32))
    for step in range(OWN_STEPS):
        rows = own_rows(step)
        unit, dist = geometry(mm(oh_own[rows, :], own_pos_ref[...]), here)
        unit_ref[rows, :] = unit
        pre, radial = radial_net(dist, spacing, rbf_ref, rad_ref)
        pre_ref[rows, :] = pre.astype(BF16)
        for degree, ref in enumerate(radial_refs):
            ref[rows, :] = radial[:, degree * CH : (degree + 1) * CH]
    for degree in range(5):
        part = slice(degree * CH, (degree + 1) * CH)
        radt_ref[part, :] = flip(rad_ref[:, part])
    for index in range(nbasis // CH):
        part = slice(index * CH, (index + 1) * CH)
        rbft_ref[:, part] = flip(rbf_ref[part, :])
    mixt_ref[...] = flip(mix_ref[0])
    lanes = home_ref.shape[1]
    lane = iota((atoms, lanes), 1)
    ext_x, ext_y, ext_z = lane // 128, lane // 32 % 4, lane // 8 % 4
    slot = ((2 * ext_x + ext_y - 1) * 2 + ext_z - 1) * 8 + lane % 8
    inside = jnp.logical_and(
        jnp.logical_or(ext_y == 1, ext_y == 2), jnp.logical_or(ext_z == 1, ext_z == 2)
    )
    to_slot = jnp.logical_and(iota((atoms, lanes), 0) == slot, inside)
    to_slot = to_slot.astype(F32).astype(BF16)
    order = meta_ref[:, SLOTS + 1 : SLOTS + 2]
    to_atom = (order == iota((atoms, atoms), 1).astype(F32)).astype(F32)
    home_ref[...] = mm(to_atom.T.astype(BF16), to_slot).astype(BF16)


def own_stage(meta, own_pos, rbf, rad, mix):
    atoms = meta.shape[0]
    edges = atoms * HALF
    out_shape = (
        struct(edges, atoms, dtype=BF16),
        struct(edges, CH, dtype=BF16),
        struct(edges, CH),
        struct(*rad.shape[::-1], dtype=BF16),
        struct(*rbf.shape[::-1], dtype=BF16),
        struct(CH, CH, dtype=BF16),
        struct(atoms, 256, dtype=BF16),
    ) + (struct(edges, CH, dtype=BF16),) * 5
    args = (meta, own_pos, rbf, rad, mix)
    return call(own_kernel, "own_edges", out_shape, [], 1 << 31, args)


def scalar_forward(rows, near, radial, mix_ref, m0_ref, gate_ref, nf0_ref):
    near = near.astype(BF16)
    nf0_ref[rows, :] = near
    mixed = mm(near * radial, mix_ref[0])
    m0_ref[rows, :] = mixed.astype(BF16)
    gate = jax.nn.sigmoid(mixed)
    gate_ref[rows, :] = gate.astype(BF16)
    return (mixed * gate).astype(BF16)


def own_forward_kernel(groups, scalar, *refs):
    own_ref, mix_ref, oh_own, refs = *refs[:3], refs[3:]
    radial0, radials = refs[0], dict(enumerate(refs[1:5], start=1))
    refs = refs[5:]
    if scalar:
        m0_ref, gate_ref, nf0_ref, acc0_ref = refs[:4]
        refs = refs[4:]
        spread = own_spread(own_ref.shape[0])
        feats = own_ref[:, 0:CH]
        summed = None
        for step in range(OWN_STEPS):
            rows = own_rows(step)
            message = scalar_forward(
                rows, mm(oh_own[rows, :], feats), radial0[rows, :], mix_ref, m0_ref, gate_ref,
                nf0_ref,
            )
            part = mm(spread, message)
            summed = part if summed is None else summed + part
        acc0_ref[...] = summed
    else:
        gate_ref, refs = refs[0], refs[1:]
    outs, weights = refs[: 3 * len(groups)], refs[3 * len(groups) :]
    for index, group in enumerate(groups):
        block_diagonal(KINDS[group], mix_ref, weights[index])
        nf_ref, mx_ref, acc_ref = outs[3 * index : 3 * index + 3]
        own_forward(
            group, own_ref, oh_own, radials, gate_ref, weights[index], nf_ref, mx_ref, acc_ref
        )


def own_forward_stage(groups, feats, mix, oh_own, radial_own, gate=None):
    atoms = feats.shape[0]
    half = atoms * HALF
    out_shape = ()
    if gate is None:
        out_shape += (struct(half, CH, dtype=BF16),) * 3 + (struct(atoms, CH),)
    for group in groups:
        width = GROUP_COLS[group]
        out_shape += (struct(half, width, dtype=BF16),) * 2 + (struct(atoms, width),)
    args = (feats, mix, oh_own, *radial_own) + (() if gate is None else (gate,))
    scratch = [pltpu.VMEM((len(KINDS[group]), 2 * CH, 2 * CH), BF16) for group in groups]
    name = "own_forward_" + "".join("abc"[group] for group in groups)
    kernel = functools.partial(own_forward_kernel, groups, gate is None)
    outs = call(kernel, name, out_shape, scratch, 1 << 32, args)
    first = len(outs) - 3 * len(groups)
    return outs[:first], [outs[first + 3 * i : first + 3 * i + 3] for i in range(len(groups))]


def start_kernel(
    p0, p1, p2, p3, p4, own_ref, own_pos_ref, meta_ref, rbf_ref, rad_ref, mix_ref, out_ref,
    ew_ref, acc0_ref,
    new_ref, oh_gh, d_gh, dt_gh, pre_ref, unit_ref, gs0_ref, en_ref, m0_gh, gate_gh, nf0_gh,
    radial_gh1, radial_gh2, radial_gh3, radial_gh4,
    table, sems, ghpos, acc_s,
):
    radial_gh = (None, radial_gh1, radial_gh2, radial_gh3, radial_gh4)
    copies = fetch((p0, p1, p2, p3, p4), slice(0, 2 * CH), table, sems)
    atoms = own_ref.shape[0]
    ghosts = table.shape[0]
    spacing = spacing_of(atoms, rbf_ref.shape[0])
    norm = 1.0 / math.sqrt(SLOTS)

    live = live_ghosts(meta_ref)
    sub_atom = iota((atoms, atoms), 0)
    lane_atom = iota((atoms, atoms), 1)
    live_b = jnp.broadcast_to(live, (atoms, atoms))
    end_row = jnp.sum(jnp.where(sub_atom <= lane_atom, live_b, 0.0), axis=0, keepdims=True)
    live_row = jnp.sum(jnp.where(sub_atom == lane_atom, live_b, 0.0), axis=0, keepdims=True)
    start_row = end_row - live_row
    row_b = jnp.broadcast_to(live_row, (atoms, atoms))
    end_col = jnp.sum(jnp.where(lane_atom <= sub_atom, row_b, 0.0), axis=1, keepdims=True)
    start_col = end_col - live
    total = jnp.sum(live)
    steps = step_count(meta_ref)
    ghost_row = meta_ref[:, HALF:SLOTS] - atoms
    high_part = jnp.floor(ghost_row * (1.0 / 16.0))
    row_high = high_part.astype(BF16)
    row_low = (ghost_row - 16.0 * high_part).astype(BF16)

    row = iota((ghosts, CH), 0)
    lane = iota((ghosts, CH), 1)
    zcells = atoms // 32
    per_y = (zcells + 2) * 8
    ext_x = row // (4 * per_y)
    ext_y = row // per_y % 4
    ext_z = row // 8 % (zcells + 2)

    def side_of(ext, last, size):
        return jnp.where(ext == 0, -size, jnp.where(ext == last, size, 0.0))

    shift = jnp.where(lane == 12, side_of(ext_x, 3, 4.0), 0.0)
    shift = jnp.where(lane == 13, side_of(ext_y, 3, 4.0), shift)
    shift = jnp.where(lane == 14, side_of(ext_z, zcells + 1, 2.0 * zcells), shift)
    own0 = own_ref[:, 0:CH]
    acc_s[...] = acc0_ref[...]
    for copy in copies:
        copy.wait()
    ghpos[...] = (table[:, CH:].astype(F32) + shift).astype(BF16)

    def ghost_start(step):
        here, _ = ghost_rows(step)
        base = step * STEP
        edge = (iota((STEP, atoms), 0) + base).astype(F32)
        mine = jnp.logical_and(edge >= start_row, edge < end_row).astype(F32)
        source = mine.astype(BF16)
        d_gh[here, :] = source
        edge_t = (iota((atoms, STEP), 1) + base).astype(F32)
        mine_t = jnp.logical_and(edge_t >= start_col, edge_t < end_col)
        spread = mine_t.astype(F32).astype(BF16)
        dt_gh[:, here] = spread
        edge_col = edge[:, 0:1]
        slot = edge_col - jnp.sum(mine * start_row, axis=1, keepdims=True)
        listed = mm(source, row_high) * 16.0 + mm(source, row_low)
        at_slot = iota((STEP, HALF), 1).astype(F32) == slot
        which = jnp.sum(jnp.where(at_slot, listed, 0.0), axis=1, keepdims=True)
        which = jnp.where(edge_col < total, which, -1.0)
        onehot = (iota((STEP, ghosts), 1).astype(F32) == which).astype(F32).astype(BF16)
        oh_gh[here, :] = onehot
        unit, dist = geometry(mm(onehot, ghpos[...]), mm(source, own_pos_ref[...]))
        unit_ref[here, :] = unit
        pre, radial = radial_net(dist, spacing, rbf_ref, rad_ref)
        pre_ref[here, :] = pre.astype(BF16)
        for degree in range(1, 5):
            radial_gh[degree][here, :] = radial[:, degree * CH : (degree + 1) * CH]
        message = scalar_forward(
            here, mm(onehot, table[:, 0:CH]), radial[:, 0:CH], mix_ref, m0_gh, gate_gh, nf0_gh
        )
        acc_s[...] += mm(spread, message)

    over_ghost_steps(steps, ghost_start)

    low0 = (acc_s[...] * norm).astype(BF16)
    updated0 = own0.astype(F32) + mm(low0, out_ref[0])
    new_ref[:, 0:CH] = updated0.astype(BF16)
    logistic = jax.nn.sigmoid(updated0)
    weight0 = ew_ref[...]
    en_ref[...] = weight0 * updated0 * logistic
    grad0 = (weight0 * logistic * (1.0 + updated0 * (1.0 - logistic))).astype(BF16)
    gs0_ref[...] = mm_nt(grad0, out_ref[0]) * norm


def any_specs(count, total):
    return [pl.BlockSpec(memory_space=pl.ANY)] * count + [
        pl.BlockSpec(memory_space=SPACE)
    ] * (total - count)


def start_stage(pieces, feats, *rest):
    atoms = feats.shape[0]
    half = atoms * HALF
    ghosts = sum(piece.shape[0] for piece in pieces)
    out_shape = (
        struct(atoms, CH, dtype=BF16),
        struct(half, ghosts, dtype=BF16),
        struct(half, atoms, dtype=BF16),
        struct(atoms, half, dtype=BF16),
        struct(half, CH, dtype=BF16),
        struct(half, CH),
        struct(atoms, CH),
        struct(atoms, CH),
    ) + (struct(half, CH, dtype=BF16),) * 7
    scratch = [
        pltpu.VMEM((ghosts, 2 * CH), BF16),
        pltpu.SemaphoreType.DMA((7,)),
        pltpu.VMEM((ghosts, CH), BF16),
        pltpu.VMEM((atoms, CH), F32),
    ]
    args = tuple(pieces) + (feats,) + rest
    return call(
        start_kernel, "ghost_start", out_shape, scratch, 1 << 31, args,
        any_specs(len(pieces), len(args)), 24,
    )


def pairs_kernel(group, count, skip, *refs):
    pieces, refs = refs[:count], refs[count:]
    own_ref, meta_ref, mix_ref, out_ref, nw_ref, oh_gh, d_gh, dt_gh, gate_gh = refs[:9]
    gate_own, nf_own, mx_own, acc_own = refs[9:13]
    refs = refs[13:]
    degrees = DEGREES[group]
    radials, refs = dict(zip(degrees, refs)), refs[len(degrees) :]
    new_ref, en_ref, gs_ref, dot_gh = refs[:4]
    grads, refs = dict(zip(degrees, refs[4:])), refs[4 + len(degrees) :]
    if group == 0:
        dot_own, refs = refs[0], refs[1:]
        grads_own, refs = dict(zip(degrees, refs)), refs[len(degrees) :]
    table, sems, wm, wmt, wo, wot, nf_s, mx_s, acc_s = refs
    copies = fetch(pieces, slice(skip, skip + GROUP_COLS[group]), table, sems)
    block_diagonal(KINDS[group], mix_ref, wm, wmt)
    block_diagonal(KINDS[group], out_ref, wo, wot)
    en_ref[...] = jnp.zeros_like(en_ref)
    for copy in copies:
        copy.wait()
    ghost_pairs(
        group, own_ref, table, new_ref, group_cols(group).start, oh_gh, d_gh, dt_gh, gate_gh,
        radials, nw_ref, step_count(meta_ref), wm, wmt, wo, wot, nf_s, mx_s, acc_own, acc_s,
        gs_ref, dot_gh, grads, en_ref,
    )
    if group == 0:
        own_backward(group, gs_ref, gate_own, wmt, nf_own, mx_own, dot_own, grads_own)


def pairs_stage(group, skip, pieces, shared, own_parts, radial_gh):
    feats = shared[0]
    atoms = feats.shape[0]
    half = atoms * HALF
    ghosts = sum(piece.shape[0] for piece in pieces)
    degrees = DEGREES[group]
    sides = 2 if group == 0 else 1
    out_shape = (
        struct(atoms, GROUP_COLS[group], dtype=BF16),
        struct(atoms, CH),
        struct(atoms, GROUP_COLS[group], dtype=BF16),
    ) + (struct(half, CH, dtype=BF16),) * (sides * (1 + len(degrees)))
    args = tuple(pieces) + tuple(shared) + tuple(own_parts)
    args += tuple(radial_gh[degree - 1] for degree in degrees)
    new, energy, gs, *rest = call(
        functools.partial(pairs_kernel, group, len(pieces), skip), "pairs_" + "abc"[group],
        out_shape, pair_scratch(atoms, half, ghosts, group), 1 << 33, args,
        any_specs(len(pieces), len(args)), 24,
    )
    return new, energy, gs, rest[: 1 + len(degrees)], rest[1 + len(degrees) :]


def own_backward_kernel(group, mix_ref, gs_ref, gate_ref, nf_ref, mx_ref, *refs):
    dot_ref, grads, wmt = refs[0], dict(zip(DEGREES[group], refs[1:-1])), refs[-1]
    block_diagonal(KINDS[group], mix_ref, None, wmt)
    own_backward(group, gs_ref, gate_ref, wmt, nf_ref, mx_ref, dot_ref, grads)


def own_backward_stage(group, mix, gs, gate, nf, mx):
    half = nf.shape[0]
    out_shape = (struct(half, CH, dtype=BF16),) * (1 + len(DEGREES[group]))
    scratch = [pltpu.VMEM((len(KINDS[group]), 2 * CH, 2 * CH), BF16)]
    kernel = functools.partial(own_backward_kernel, group)
    name = "own_backward_" + "abc"[group]
    return call(kernel, name, out_shape, scratch, 1 << 32, (mix, gs, gate, nf, mx))


def finish(
    grad, mixed, near, dots, parts, pre, unit, spacing, radt_ref, rbft_ref, mixt_ref
):
    mixed = mixed.astype(F32)
    gate = jax.nn.sigmoid(mixed)
    first = grad * gate * (1.0 + mixed * (1.0 - gate)) + dots * gate * (1.0 - gate)
    weighted = mm(first.astype(BF16), mixt_ref[...]) * near.astype(F32)
    radial_grad = jnp.concatenate([weighted.astype(BF16)] + parts, axis=1)
    hidden_grad = mm(radial_grad, radt_ref[...])
    pre = pre.astype(F32)
    logistic = jax.nn.sigmoid(pre)
    pre_grad = (hidden_grad * logistic * (1.0 + pre * (1.0 - logistic))).astype(BF16)
    centred = centred_of(unit[:, 3:4], spacing, rbft_ref.shape[1])
    slope = jnp.exp(-0.5 * centred * centred) * centred
    basis_grad = mm(pre_grad, rbft_ref[...])
    dist_grad = jnp.sum(basis_grad * slope, axis=1, keepdims=True) * (-1.0 / spacing)
    pull = unit * dist_grad
    across = pull.T[0:8, :]
    top = across.astype(BF16)
    rest = (across - top.astype(F32)).astype(BF16)
    return pull, top, rest


def sum_of(refs, rows):
    total = refs[0][rows, :].astype(F32)
    for ref in refs[1:]:
        total += ref[rows, :].astype(F32)
    return total


def degree_parts(refs, rows):
    by_degree = {}
    refs = list(refs)
    for degrees in DEGREES:
        for degree in degrees:
            by_degree.setdefault(degree, []).append(refs.pop(0))
    return [sum_of(by_degree[degree], rows).astype(BF16) for degree in range(1, 5)]


PARTIALS = sum(len(degrees) for degrees in DEGREES)


def third_kernel(
    low_ref, mid_ref, high_ref, own_ref, meta_ref, mix_ref, out_ref, nw_ref, oh_gh, d_gh, dt_gh,
    gate_gh, acc_own, radial_gh4,
    radt_ref, rbft_ref, mixt_ref, gs0_ref, en_0, en_a, en_b, new_0, new_a, new_b, pre_gh, unit_gh,
    m0_ref, nf0_ref, dot_a, dot_b, *refs
):
    gr_gh, refs = refs[: PARTIALS - 1], refs[PARTIALS - 1 :]
    (
        new_ref, energy_ref, src_ref, flow_ref, fmid_ref, fhigh_ref, gs_ref,
        table, sems, wm, wmt, wo, wot, nf_s, mx_s, acc_s, dot_c, gr_c, en_s, fgh_s,
    ) = refs
    group = 2
    copies = fetch((low_ref, mid_ref, high_ref), slice(0, GROUP_COLS[group]), table, sems)
    atoms = own_ref.shape[0]
    spacing = spacing_of(atoms, rbft_ref.shape[1])
    block_diagonal(KINDS[group], mix_ref, wm, wmt)
    block_diagonal(KINDS[group], out_ref, wo, wot)
    en_s[...] = en_0[...] + en_a[...] + en_b[...]
    at = 0
    for part in (new_0, new_a, new_b):
        new_ref[:, at : at + part.shape[1]] = part[...]
        at += part.shape[1]
    steps = step_count(meta_ref)

    for copy in copies:
        copy.wait()
    ghost_pairs(
        group, own_ref, table, new_ref, 0, oh_gh, d_gh, dt_gh, gate_gh, {4: radial_gh4}, nw_ref,
        steps, wm, wmt, wo, wot, nf_s, mx_s, acc_own, acc_s, gs_ref, dot_c, {4: gr_c}, en_s,
    )
    energy_ref[...] = jnp.sum(en_s[...].T, axis=0, keepdims=True)

    fgh_s[...] = jnp.zeros_like(fgh_s)
    src_ref[...] = jnp.zeros_like(src_ref)
    gs0_low = gs0_ref[...].astype(BF16)

    def ghost_finish(step):
        here, _ = ghost_rows(step)
        grad = mm(d_gh[here, :], gs0_low)
        pull, top, rest = finish(
            grad, m0_ref[here, :], nf0_ref[here, :], sum_of((dot_a, dot_b, dot_c), here),
            degree_parts(gr_gh + (gr_c,), here), pre_gh[here, :], unit_gh[here, :], spacing,
            radt_ref, rbft_ref, mixt_ref,
        )
        pull_top = pull.astype(BF16)
        pull_rest = (pull - pull_top.astype(F32)).astype(BF16)
        spread = dt_gh[:, here]
        src_ref[...] += mm(spread, pull_top) + mm(spread, pull_rest)
        onehot = oh_gh[here, :]
        fgh_s[...] += mm(top, onehot) + mm(rest, onehot)

    over_ghost_steps(steps, ghost_finish)
    low, mid = flow_ref.shape[1], fmid_ref.shape[1]
    flow_ref[...] = fgh_s[:, 0:low]
    fmid_ref[...] = fgh_s[:, low : low + mid]
    fhigh_ref[...] = fgh_s[:, low + mid :]


def third_stage(pieces, feats, *rest):
    atoms, feat = feats.shape
    half = atoms * HALF
    sizes = [piece.shape[0] for piece in pieces]
    ghosts = sum(sizes)
    out_shape = (
        struct(atoms, feat, dtype=BF16),
        struct(1, atoms),
        struct(atoms, CH),
    ) + tuple(struct(8, size) for size in sizes) + (
        struct(atoms, GROUP_COLS[2], dtype=BF16),
    )
    scratch = pair_scratch(atoms, half, ghosts, 2) + [
        pltpu.VMEM((half, CH), BF16),
        pltpu.VMEM((half, CH), BF16),
        pltpu.VMEM((atoms, CH), F32),
        pltpu.VMEM((8, ghosts), F32),
    ]
    args = tuple(pieces) + (feats,) + rest
    return call(
        third_kernel, "third_group", out_shape, scratch, 1 << 33, args, any_specs(3, len(args)),
        24,
    )


def own_back_kernel(
    oh_own, pre_own, unit_own, radt_ref, rbft_ref, mixt_ref, gs0_ref, src_ref,
    m0_ref, nf0_ref, dot_a, dot_b, dot_c, *refs
):
    gr_own, (force_ref,) = refs[:PARTIALS], refs[PARTIALS:]
    atoms = oh_own.shape[1]
    spacing = spacing_of(atoms, rbft_ref.shape[1])
    grad = tiled(gs0_ref[...])
    src = src_ref[...]
    onto = jnp.zeros((8, atoms), F32)
    for step in range(OWN_STEPS):
        rows = own_rows(step)
        pull, top, rest = finish(
            grad, m0_ref[rows, :], nf0_ref[rows, :], sum_of((dot_a, dot_b, dot_c), rows),
            degree_parts(gr_own, rows), pre_own[rows, :], unit_own[rows, :], spacing, radt_ref,
            rbft_ref, mixt_ref,
        )
        src += jnp.sum(pull.reshape(STEP // atoms, atoms, CH), axis=0)
        onehot = oh_own[rows, :]
        onto += mm(top, onehot) + mm(rest, onehot)
    force_ref[...] = onto - src.T[0:8, :]


def own_back_stage(*args):
    oh_own = args[0]
    out_shape = (struct(8, oh_own.shape[1]),)
    return call(own_back_kernel, "own_back", out_shape, [], 1 << 31, args)[0]


def ring(axis):
    peers = lax.axis_size(axis)
    up = [(i, (i + 1) % peers) for i in range(peers)]
    return up, [(j, i) for i, j in up]


def neighbours_of(block, axis, dim):
    up, down = ring(axis)
    length = block.shape[dim]
    if len(up) == 2 and length == 2:
        other = lax.ppermute(block, axis, up)
        return (
            lax.slice_in_dim(other, length - 1, length, axis=dim),
            lax.slice_in_dim(other, 0, 1, axis=dim),
        )
    before = lax.ppermute(lax.slice_in_dim(block, length - 1, length, axis=dim), axis, up)
    after = lax.ppermute(lax.slice_in_dim(block, 0, 1, axis=dim), axis, down)
    return before, after


def grown(block, axis, dim):
    before, after = neighbours_of(block, axis, dim)
    return jnp.concatenate([before, block, after], axis=dim)


def ghost_pieces(block):
    before, after = neighbours_of(block, "gx", 0)
    return tuple(flat_rows(piece) for piece in (before, block, after))


def flat_rows(piece):
    return piece.reshape(-1, piece.shape[-1])


def fold_kernel(mid_ref, low_ref, high_ref, out_ref):
    lanes = mid_ref.shape[1]
    ext_y = iota(mid_ref.shape, 1) // 32 % 4
    out_ref[...] = (
        mid_ref[...]
        + jnp.where(ext_y == 1, pltpu.roll(low_ref[...], lanes - 64, 1), 0.0)
        + jnp.where(ext_y == 2, pltpu.roll(high_ref[...], 64, 1), 0.0)
    )


def forces_kernel(mid_ref, low_ref, high_ref, own_ref, home_ref, out_ref):
    values = mid_ref[...]
    lanes = values.shape[1]
    ext_z = iota(values.shape, 1) // 8 % 4
    values += jnp.where(ext_z == 1, pltpu.roll(low_ref[...], lanes - 16, 1), 0.0)
    values += jnp.where(ext_z == 2, pltpu.roll(high_ref[...], 16, 1), 0.0)
    first = values.astype(BF16)
    values -= first.astype(F32)
    second = values.astype(BF16)
    third = (values - second.astype(F32)).astype(BF16)
    home = home_ref[...]
    total = own_ref[...] + (mm_nt(first, home) + (mm_nt(second, home) + mm_nt(third, home)))
    for comp in range(3):
        out_ref[comp] = -total[comp : comp + 1, :]


def give_back_x(low, mid, high):
    up, down = ring("gx")
    from_low = lax.ppermute(high, "gx", up)
    from_high = lax.ppermute(low, "gx", down)
    return mid, jnp.concatenate([from_low, from_high], axis=1)


def give_back_y(mid):
    up, down = ring("gy")
    return mid, lax.ppermute(mid, "gy", up), lax.ppermute(mid, "gy", down)


def fold(*args):
    return call(fold_kernel, "fold", (struct(*args[0].shape),), [], 1 << 16, args)[0]


def give_back_z(mid):
    up, down = ring("gz")
    from_low = lax.ppermute(mid, "gz", up)
    return mid, from_low, from_low if len(up) == 2 else lax.ppermute(mid, "gz", down)


def local(
    features,
    positions,
    neighbours,
    counts,
    cell_atoms,
    rbf_weight,
    radial_weight,
    mix_weight,
    out_weight,
    energy_weight,
    norm_weight,
):
    feats = features[0, 0, 0]
    places = jnp.swapaxes(positions[0, 0], 0, 1)
    cells0, cells12, own_pos, meta = make_cells(
        feats, places, neighbours[0, 0, 0].T, counts[0, 0], cell_atoms[0, 0]
    )
    hold = lax.optimization_barrier
    block0, block12 = (part.reshape(2, 2, 2, 8, part.shape[1]) for part in (cells0, cells12))
    block0 = grown(block0, "gz", 2)
    oh_own, pre_own, unit_own, radt, rbft, mixt, home, *radial_own = own_stage(
        meta, own_pos, rbf_weight, radial_weight, mix_weight
    )
    block0, oh_own = hold((block0, oh_own))
    y_low, y_high = neighbours_of(block0, "gy", 1)
    low_in, high_in = neighbours_of(block0, "gx", 0)
    block12 = grown(block12, "gz", 2)
    (m0_own, gate_own, nf0_own, acc0), (own_a, own_b) = own_forward_stage(
        (0, 1), feats, mix_weight, oh_own, radial_own
    )
    y_low, y_high, block12, gate_own = hold((y_low, y_high, block12, gate_own))
    outer = jnp.concatenate([y_low, y_high], axis=1)
    low_out, high_out = neighbours_of(outer, "gx", 0)
    middle = jnp.concatenate([y_low, block0, y_high], axis=1)
    pieces0 = tuple(flat_rows(p) for p in (low_in, low_out, middle, high_in, high_out))
    block1, block2 = block12[..., : GROUP_COLS[1]], block12[..., GROUP_COLS[1] :]
    block1 = grown(block1, "gy", 1)
    _, (own_c,) = own_forward_stage((2,), feats, mix_weight, oh_own, radial_own, gate_own)
    pieces0, acc_c = hold((pieces0, own_c[2]))
    (
        new_0, oh_gh, d_gh, dt_gh, pre_gh, unit_gh, gs0, en_0, m0_gh, gate_gh, nf0_gh, *radial_gh,
    ) = start_stage(
        pieces0, feats, own_pos, meta, rbf_weight, radial_weight, mix_weight, out_weight,
        energy_weight[None], acc0,
    )
    block1, block2, gate_gh = hold((block1, block2, gate_gh))
    pieces1 = ghost_pieces(block1)
    block2 = grown(block2, "gy", 1)
    shared = (feats, meta, mix_weight, out_weight, norm_weight, oh_gh, d_gh, dt_gh, gate_gh)
    new_a, en_a, _, (dot_gh_a, *gr_gh_a), (dot_own_a, *gr_own_a) = pairs_stage(
        0, 2 * CH, pieces0, shared, (gate_own, *own_a), radial_gh
    )
    en_a, block2 = hold((en_a, block2))
    pieces2 = ghost_pieces(block2)
    new_b, en_b, gs_b, (dot_gh_b, *gr_gh_b), _ = pairs_stage(
        1, 0, pieces1, shared, (gate_own, *own_b), radial_gh
    )
    new, energy, src, low, mid, high, gs_c = third_stage(
        pieces2, *shared, acc_c, radial_gh[3], radt, rbft, mixt, gs0, en_0, en_a, en_b, new_0,
        new_a, new_b, pre_gh, unit_gh, m0_gh, nf0_gh, dot_gh_a, dot_gh_b, *gr_gh_a, *gr_gh_b,
    )
    mid, arrived = give_back_x(low, mid, high)
    dot_own_c, *gr_own_c = own_backward_stage(2, mix_weight, gs_c, gate_own, *own_c[:2])
    arrived, gs_b, dot_own_c = hold((arrived, gs_b, dot_own_c))
    mid, from_low, from_high = give_back_y(mid + arrived)
    dot_own_b, *gr_own_b = own_backward_stage(1, mix_weight, gs_b, gate_own, *own_b[:2])
    from_low, from_high, gs0, dot_own_b = hold((from_low, from_high, gs0, dot_own_b))
    folded = give_back_z(fold(mid, from_low, from_high))
    own = own_back_stage(
        oh_own, pre_own, unit_own, radt, rbft, mixt, gs0, src, m0_own, nf0_own, dot_own_a,
        dot_own_b, dot_own_c, *gr_own_a, *gr_own_b, *gr_own_c,
    )
    args = (*folded, own, home)
    out_shape = (struct(3, 1, own.shape[1]),)
    forces = call(forces_kernel, "forces", out_shape, [], 1 << 20, args)[0]
    return (
        new[None, None, None],
        energy[None, None],
        jnp.swapaxes(forces, 0, 1)[None, None],
    )


def solution(mesh):
    split = P("gx", "gy", "gz", None, None)
    flat = P("gx", "gy", "gz", None)
    return jax.shard_map(
        local,
        mesh=mesh,
        in_specs=(split, split, split, flat, flat, P(), P(), P(), P(), P(), P()),
        out_specs=(split, flat, split),
        check_vma=False,
    )
```

```python
import functools
import math

import jax
import jax.numpy as jnp
from jax import lax
from jax.experimental import pallas as pl
from jax.experimental.pallas import tpu as pltpu
from jax.sharding import PartitionSpec as P

F32 = jnp.float32
BF16 = jnp.bfloat16
CH = 128
SLOTS = 32
HALF = 16
STEP = 256
OWN_STEPS = 4
GH_STEPS = 2
MIB = 1024 * 1024
SPACE = pltpu.VMEM
PAIR_DEGREES = (
    (1, 1), (1, 2), (2, 2), (2, 2),
    (3, 3), (3, 3), (3, 3), (3, 4),
    (4, 4), (4, 4), (4, 4), (4, 4),
)
GROUPS = ((0, 3), (3, 12))
KINDS = tuple(sorted({PAIR_DEGREES[pair] for pair in range(*group)}) for group in GROUPS)
DEGREES = tuple(sorted({d for both in kinds for d in both}) for kinds in KINDS)
GROUP_COLS = tuple(2 * CH * (end - begin) for begin, end in GROUPS)


def mm(a, b):
    return jnp.dot(a, b, preferred_element_type=F32)


def mm_nt(a, b):
    return lax.dot_general(a, b, (((1,), (1,)), ((), ())), preferred_element_type=F32)


def iota(shape, dim):
    return lax.broadcasted_iota(jnp.int32, shape, dim)


def flip(w):
    return w.astype(F32).T.astype(BF16)


def pair_cols(pair):
    return slice(CH + pair * 2 * CH, CH + (pair + 1) * 2 * CH)


def struct(*shape, dtype=F32):
    return jax.ShapeDtypeStruct(shape, dtype)


def call(kernel, name, out_shape, scratch, flops, args, specs=None, limit=16):
    size = sum(a.size * a.dtype.itemsize for a in list(args) + list(out_shape))
    return pl.pallas_call(
        kernel,
        out_shape=out_shape,
        in_specs=specs or [pl.BlockSpec(memory_space=SPACE)] * len(args),
        out_specs=tuple(pl.BlockSpec(memory_space=SPACE) for _ in out_shape),
        scratch_shapes=scratch,
        compiler_params=pltpu.CompilerParams(vmem_limit_bytes=limit * MIB),
        cost_estimate=pl.CostEstimate(flops=flops, bytes_accessed=size, transcendentals=0),
        name=name,
    )(*args)


def cells_kernel(
    feat_ref, pos_ref, near_ref, counts_ref, order_ref,
    first_ref, own_pos_ref, meta_ref, pick_ref, rows_ref, pos_rows,
):
    rows_ref[...] = jnp.zeros_like(rows_ref)
    pos_rows[...] = jnp.zeros_like(pos_rows)
    atoms = feat_ref.shape[0]
    rows_ref[0:SLOTS, :] = near_ref[...].astype(F32)
    rows_ref[SLOTS : SLOTS + 1, :] = counts_ref[...].astype(F32)
    rows_ref[SLOTS + 1 : SLOTS + 2, :] = order_ref[...].astype(F32)
    meta = rows_ref[...].T
    meta_ref[...] = meta
    for comp in range(3):
        places = pos_ref[comp]
        first = places.astype(BF16).astype(F32)
        second = (places - first).astype(BF16).astype(F32)
        pos_rows[comp : comp + 1, :] = first
        pos_rows[4 + comp : 5 + comp, :] = second
        pos_rows[8 + comp : 9 + comp, :] = places - first - second
    pieces = pos_rows[...].astype(BF16)
    lane = iota((atoms, atoms), 1).astype(F32)
    pick = (meta[:, SLOTS + 1 : SLOTS + 2] == lane).astype(F32).astype(BF16)
    same = (iota((atoms, atoms), 0) == iota((atoms, atoms), 1)).astype(F32).astype(BF16)
    own_pos_ref[...] = mm_nt(same, pieces).astype(BF16)
    first_ref[:, CH : 2 * CH] = mm_nt(pick, pieces).astype(BF16)
    pick_ref[...] = pick
    first_ref[:, 0:CH] = mm(pick, feat_ref[:, 0:CH]).astype(BF16)
    cut = pair_cols(GROUPS[1][0]).start
    first_ref[:, 2 * CH :] = mm(pick, feat_ref[:, CH:cut]).astype(BF16)


def rest_kernel(feat_ref, pick_ref, rest_ref):
    cut = pair_cols(GROUPS[1][0]).start
    rest_ref[...] = mm(pick_ref[...], feat_ref[:, cut:]).astype(BF16)


def make_cells(feats, places, near, counts, order):
    atoms = feats.shape[0]
    out_shape = (
        struct(atoms, 2 * CH + GROUP_COLS[0], dtype=BF16),
        struct(atoms, CH, dtype=BF16),
        struct(atoms, CH),
        struct(atoms, atoms, dtype=BF16),
    )
    args = (feats, places, near, counts, order)
    scratch = [pltpu.VMEM((CH, atoms), F32), pltpu.VMEM((CH, atoms), F32)]
    first, own_pos, meta, pick = call(cells_kernel, "cells", out_shape, scratch, 1 << 26, args)
    out_shape = (struct(atoms, sum(GROUP_COLS[1:]), dtype=BF16),)
    rest = call(rest_kernel, "cells_rest", out_shape, [], 1 << 26, (feats, pick))[0]
    return first, rest, own_pos, meta


def spacing_of(atoms, nbasis):
    depth = atoms // 16
    return 2.0 * math.sqrt(32.0 + depth * depth) / (nbasis - 1)


def own_onehots(meta_ref, oh_own):
    atoms = meta_ref.shape[0]
    counts = meta_ref[:, SLOTS : SLOTS + 1]
    lane_atom = iota((atoms, atoms), 1).astype(F32)
    for slot in range(HALF):
        hit = jnp.logical_and(meta_ref[:, slot : slot + 1] == lane_atom, counts > slot)
        oh_own[slot * atoms : (slot + 1) * atoms, :] = hit.astype(F32).astype(BF16)


def geometry(near, here):
    diff = near - here
    rel = (diff + pltpu.roll(diff, CH - 4, 1)) + (
        pltpu.roll(diff, CH - 8, 1) + pltpu.roll(diff, CH - 12, 1)
    )
    lane = iota(rel.shape, 1)
    rel = jnp.where(lane < 3, rel, 0.0)
    square = jnp.sum(rel * rel, axis=1, keepdims=True)
    inverse = lax.rsqrt(jnp.where(square > 0.0, square, 1.0))
    dist = square * inverse
    return jnp.where(lane == 3, dist, rel * inverse), dist


def centred_of(dist, spacing, nbasis):
    return dist * (1.0 / spacing) - iota((dist.shape[0], nbasis), 1).astype(F32)


def radial_net(dist, spacing, rbf_ref, rad_ref):
    centred = centred_of(dist, spacing, rbf_ref.shape[0])
    basis = jnp.exp(-0.5 * centred * centred)
    pre = mm(basis.astype(BF16), rbf_ref[...])
    hidden = (pre * jax.nn.sigmoid(pre)).astype(BF16)
    return pre, mm(hidden, rad_ref[...]).astype(BF16)


def own_spread(atoms, size=STEP):
    shape = (atoms, size)
    return (iota(shape, 1) % atoms == iota(shape, 0)).astype(F32).astype(BF16)


def tiled(values, size=STEP):
    return jnp.concatenate([values] * (size // values.shape[0]), axis=0)


def live_ghosts(meta_ref):
    return jnp.maximum(meta_ref[:, SLOTS : SLOTS + 1] - HALF, 0.0)


def step_count(meta_ref):
    total = jnp.sum(live_ghosts(meta_ref)).astype(jnp.int32)
    rows = GH_STEPS * STEP
    return jnp.maximum((total + (rows - 1)) // rows, 1) * GH_STEPS


def own_rows(step, size=STEP):
    return pl.ds(step * size, size)


def ghost_rows(step, size=STEP):
    first = OWN_STEPS * STEP
    if isinstance(step, int):
        return pl.ds(step * size, size), pl.ds(first + step * size, size)
    base = pl.multiple_of(step * size, size)
    return pl.ds(base, size), pl.ds(pl.multiple_of(first + base, size), size)


def over_ghost_steps(steps, body, size=STEP):
    static = GH_STEPS * STEP // size
    for step in range(static):
        body(step)

    def again(step, carry):
        body(step)
        return carry

    lax.fori_loop(static, (steps * STEP + (size - 1)) // size, again, 0)


def block_diagonal(kinds, source, straight=None, across=None):
    zero = jnp.zeros((CH, CH), BF16)
    targets = [ref for ref in (straight, across) if ref is not None]
    for kind, both in enumerate(kinds):
        for ref in targets:
            ref[kind, 0:CH, CH:] = zero
            ref[kind, CH:, 0:CH] = zero
    for degree in sorted({d for both in kinds for d in both}):
        weight = source[degree]
        flipped = flip(weight) if across is not None else None
        for kind, both in enumerate(kinds):
            for side in range(2):
                if both[side] == degree:
                    part = slice(side * CH, side * CH + CH)
                    if straight is not None:
                        straight[kind, part, part] = weight
                    if across is not None:
                        across[kind, part, part] = flipped


def fetch(pieces, cols, table, sems):
    low, high, ghosts = 0, 0, table.shape[0]
    if len(pieces) == 3:
        rows = [(piece, 0, piece.shape[0]) for piece in pieces]
    else:
        low_in, low_out, mid, high_in, high_out = pieces
        half = low_out.shape[0] // 2
        rows = [(low_out, 0, half), (low_in, 0, low_in.shape[0]), (low_out, half, half)]
        rows += [(mid, 0, mid.shape[0])]
        rows += [(high_out, 0, half), (high_in, 0, high_in.shape[0]), (high_out, half, half)]
    copies = []
    at = 0
    for index, (piece, start, count) in enumerate(rows):
        source = piece.at[pl.ds(start, count), cols]
        target = table.at[pl.ds(at, count), :]
        copies.append(pltpu.make_async_copy(source, target, sems.at[index]))
        at += count
    for copy in copies:
        copy.start()
    return copies


def infos_of(group):
    infos = []
    for index, pair in enumerate(range(*GROUPS[group])):
        degrees = PAIR_DEGREES[pair]
        cols = slice(index * 2 * CH, (index + 1) * 2 * CH)
        infos.append((cols, degrees, KINDS[group].index(degrees)))
    return infos


def group_cols(group):
    begin, end = GROUPS[group]
    return slice(pair_cols(begin).start, pair_cols(end - 1).stop)


def twice(values):
    return jnp.concatenate([values, values], axis=1)


def forward(group, rows, onehot, feats, radials, gate_ref, wm, nf_ref, mx_ref):
    near = mm(onehot, feats).astype(BF16)
    nf_ref[rows, :] = near
    gate = twice(gate_ref[rows, :])
    messages = []
    for cols, degrees, kind in infos_of(group):
        radial = jnp.concatenate([radials[d][rows, :] for d in degrees], axis=1)
        mixed = mm(near[:, cols] * radial, wm[kind]).astype(BF16)
        mx_ref[rows, cols] = mixed
        messages.append(mixed * gate)
    return jnp.concatenate(messages, axis=1)


def backward(group, rows, grad, gate_ref, wmt, nf_ref, mx_ref, dot_ref, grad_refs):
    parts = {}
    dots = None
    gate = twice(gate_ref[rows, :])
    for cols, degrees, kind in infos_of(group):
        product = grad[:, cols] * mx_ref[rows, cols]
        dot = (product[:, 0:CH] + product[:, CH:]).astype(F32)
        dots = dot if dots is None else dots + dot
        weighted = mm(grad[:, cols] * gate, wmt[kind]) * nf_ref[rows, cols].astype(F32)
        for side in range(2):
            part = weighted[:, side * CH : (side + 1) * CH]
            degree = degrees[side]
            parts[degree] = parts[degree] + part if degree in parts else part
    dot_ref[rows, :] = dots.astype(dot_ref.dtype)
    for degree, part in parts.items():
        grad_refs[degree][rows, :] = part.astype(grad_refs[degree].dtype)


def own_forward(group, own_ref, oh_own, radials, gate_ref, wm, nf_ref, mx_ref, acc_ref):
    spread = own_spread(own_ref.shape[0])
    feats = own_ref[:, group_cols(group)]
    summed = None
    for step in range(OWN_STEPS):
        rows = own_rows(step)
        message = forward(
            group, rows, oh_own[rows, :], feats, radials, gate_ref, wm, nf_ref, mx_ref
        )
        part = mm(spread, message)
        summed = part if summed is None else summed + part
    acc_ref[...] = summed


def own_backward(group, gs_ref, gate_ref, wmt, nf_ref, mx_ref, dot_ref, grad_refs):
    grad = tiled(gs_ref[...])
    for step in range(OWN_STEPS):
        backward(
            group, own_rows(step), grad, gate_ref, wmt, nf_ref, mx_ref, dot_ref, grad_refs
        )


def ghost_pairs(
    group, own_ref, table, new_ref, new_base, oh_gh, d_gh, dt_gh, gate_ref, radials, nw_ref,
    steps, wm, wmt, wo, wot, nf_s, mx_s, acc_in, acc_s, gs_ref, dot_ref, grad_refs, en_ref,
):
    norm = 1.0 / math.sqrt(SLOTS)
    acc_s[...] = acc_in[...]

    def ghost_forward(step):
        here, _ = ghost_rows(step)
        message = forward(
            group, here, oh_gh[here, :], table[...], radials, gate_ref, wm, nf_s, mx_s
        )
        acc_s[...] += mm(dt_gh[:, here], message)

    over_ghost_steps(steps, ghost_forward)

    begin = group_cols(group).start
    for cols, degrees, kind in infos_of(group):
        summed_low = (acc_s[:, cols] * norm).astype(BF16)
        own = own_ref[:, begin + cols.start : begin + cols.stop]
        updated = own.astype(F32) + mm(summed_low, wo[kind])
        at = begin - new_base + cols.start
        new_ref[:, at : at + 2 * CH] = updated.astype(BF16)
        weight = jnp.concatenate(
            [nw_ref[d - 1 : d, :] * (1.0 / (2 * d + 1)) for d in degrees], axis=1
        )
        scale = weight * updated
        energy = scale * updated
        en_ref[...] += energy[:, 0:CH] + energy[:, CH:]
        gs_ref[:, cols] = (mm((2.0 * scale).astype(BF16), wot[kind]) * norm).astype(BF16)

    def ghost_backward(step):
        here, _ = ghost_rows(step)
        grad = mm(d_gh[here, :], gs_ref[...]).astype(BF16)
        backward(group, here, grad, gate_ref, wmt, nf_s, mx_s, dot_ref, grad_refs)

    over_ghost_steps(steps, ghost_backward)


def pair_scratch(atoms, half, ghosts, group):
    count, width = len(KINDS[group]), GROUP_COLS[group]
    return (
        [pltpu.VMEM((ghosts, width), BF16), pltpu.SemaphoreType.DMA((7,))]
        + [pltpu.VMEM((count, 2 * CH, 2 * CH), BF16) for _ in range(4)]
        + [
            pltpu.VMEM((half, width), BF16),
            pltpu.VMEM((half, width), BF16),
            pltpu.VMEM((atoms, width), F32),
        ]
    )


def own_kernel(
    meta_ref, own_pos_ref, rbf_ref, rad_ref, mix_ref,
    oh_own, pre_ref, unit_ref, radt_ref, rbft_ref, mixt_ref, home_ref, *radial_refs
):
    atoms = meta_ref.shape[0]
    nbasis = rbf_ref.shape[0]
    spacing = spacing_of(atoms, nbasis)
    own_onehots(meta_ref, oh_own)
    here = tiled(own_pos_ref[...].astype(F32))
    for step in range(OWN_STEPS):
        rows = own_rows(step)
        unit, dist = geometry(mm(oh_own[rows, :], own_pos_ref[...]), here)
        unit_ref[rows, :] = unit
        pre, radial = radial_net(dist, spacing, rbf_ref, rad_ref)
        pre_ref[rows, :] = pre.astype(BF16)
        for degree, ref in enumerate(radial_refs):
            ref[rows, :] = radial[:, degree * CH : (degree + 1) * CH]
    for degree in range(5):
        part = slice(degree * CH, (degree + 1) * CH)
        radt_ref[part, :] = flip(rad_ref[:, part])
    for index in range(nbasis // CH):
        part = slice(index * CH, (index + 1) * CH)
        rbft_ref[:, part] = flip(rbf_ref[part, :])
    mixt_ref[...] = flip(mix_ref[0])
    lanes = home_ref.shape[1]
    lane = iota((atoms, lanes), 1)
    ext_x, ext_y, ext_z = lane // 128, lane // 32 % 4, lane // 8 % 4
    slot = ((2 * ext_x + ext_y - 1) * 2 + ext_z - 1) * 8 + lane % 8
    inside = jnp.logical_and(
        jnp.logical_or(ext_y == 1, ext_y == 2), jnp.logical_or(ext_z == 1, ext_z == 2)
    )
    to_slot = jnp.logical_and(iota((atoms, lanes), 0) == slot, inside)
    to_slot = to_slot.astype(F32).astype(BF16)
    order = meta_ref[:, SLOTS + 1 : SLOTS + 2]
    to_atom = (order == iota((atoms, atoms), 1).astype(F32)).astype(F32)
    home_ref[...] = mm(to_atom.T.astype(BF16), to_slot).astype(BF16)


def own_stage(meta, own_pos, rbf, rad, mix):
    atoms = meta.shape[0]
    edges = atoms * HALF
    out_shape = (
        struct(edges, atoms, dtype=BF16),
        struct(edges, CH, dtype=BF16),
        struct(edges, CH),
        struct(*rad.shape[::-1], dtype=BF16),
        struct(*rbf.shape[::-1], dtype=BF16),
        struct(CH, CH, dtype=BF16),
        struct(atoms, 256, dtype=BF16),
    ) + (struct(edges, CH, dtype=BF16),) * 5
    args = (meta, own_pos, rbf, rad, mix)
    return call(own_kernel, "own_edges", out_shape, [], 1 << 31, args)


def scalar_forward(rows, near, radial, mix_ref, m0_ref, gate_ref, nf0_ref):
    near = near.astype(BF16)
    nf0_ref[rows, :] = near
    mixed = mm(near * radial, mix_ref[0])
    m0_ref[rows, :] = mixed.astype(BF16)
    gate = jax.nn.sigmoid(mixed)
    gate_ref[rows, :] = gate.astype(BF16)
    return (mixed * gate).astype(BF16)


def own_forward_kernel(groups, scalar, *refs):
    own_ref, mix_ref, oh_own, refs = *refs[:3], refs[3:]
    radial0, radials = refs[0], dict(enumerate(refs[1:5], start=1))
    refs = refs[5:]
    if scalar:
        m0_ref, gate_ref, nf0_ref, acc0_ref = refs[:4]
        refs = refs[4:]
        spread = own_spread(own_ref.shape[0])
        feats = own_ref[:, 0:CH]
        summed = None
        for step in range(OWN_STEPS):
            rows = own_rows(step)
            message = scalar_forward(
                rows, mm(oh_own[rows, :], feats), radial0[rows, :], mix_ref, m0_ref, gate_ref,
                nf0_ref,
            )
            part = mm(spread, message)
            summed = part if summed is None else summed + part
        acc0_ref[...] = summed
    else:
        gate_ref, refs = refs[0], refs[1:]
    outs, weights = refs[: 3 * len(groups)], refs[3 * len(groups) :]
    for index, group in enumerate(groups):
        block_diagonal(KINDS[group], mix_ref, weights[index])
        nf_ref, mx_ref, acc_ref = outs[3 * index : 3 * index + 3]
        own_forward(
            group, own_ref, oh_own, radials, gate_ref, weights[index], nf_ref, mx_ref, acc_ref
        )


def own_forward_stage(groups, feats, mix, oh_own, radial_own, gate=None):
    atoms = feats.shape[0]
    half = atoms * HALF
    out_shape = ()
    if gate is None:
        out_shape += (struct(half, CH, dtype=BF16),) * 3 + (struct(atoms, CH),)
    for group in groups:
        width = GROUP_COLS[group]
        out_shape += (struct(half, width, dtype=BF16),) * 2 + (struct(atoms, width),)
    args = (feats, mix, oh_own, *radial_own) + (() if gate is None else (gate,))
    scratch = [pltpu.VMEM((len(KINDS[group]), 2 * CH, 2 * CH), BF16) for group in groups]
    name = "own_forward_" + "".join("abc"[group] for group in groups)
    kernel = functools.partial(own_forward_kernel, groups, gate is None)
    outs = call(kernel, name, out_shape, scratch, 1 << 32, args)
    first = len(outs) - 3 * len(groups)
    return outs[:first], [outs[first + 3 * i : first + 3 * i + 3] for i in range(len(groups))]


def start_kernel(
    p0, p1, p2, p3, p4, own_ref, own_pos_ref, meta_ref, rbf_ref, rad_ref, mix_ref, out_ref,
    ew_ref, acc0_ref,
    new_ref, oh_gh, d_gh, dt_gh, pre_ref, unit_ref, gs0_ref, en_ref, m0_gh, gate_gh, nf0_gh,
    radial_gh1, radial_gh2, radial_gh3, radial_gh4,
    table, sems, ghpos, acc_s,
):
    radial_gh = (None, radial_gh1, radial_gh2, radial_gh3, radial_gh4)
    copies = fetch((p0, p1, p2, p3, p4), slice(0, 2 * CH), table, sems)
    atoms = own_ref.shape[0]
    ghosts = table.shape[0]
    spacing = spacing_of(atoms, rbf_ref.shape[0])
    norm = 1.0 / math.sqrt(SLOTS)

    live = live_ghosts(meta_ref)
    sub_atom = iota((atoms, atoms), 0)
    lane_atom = iota((atoms, atoms), 1)
    live_b = jnp.broadcast_to(live, (atoms, atoms))
    end_row = jnp.sum(jnp.where(sub_atom <= lane_atom, live_b, 0.0), axis=0, keepdims=True)
    live_row = jnp.sum(jnp.where(sub_atom == lane_atom, live_b, 0.0), axis=0, keepdims=True)
    start_row = end_row - live_row
    row_b = jnp.broadcast_to(live_row, (atoms, atoms))
    end_col = jnp.sum(jnp.where(lane_atom <= sub_atom, row_b, 0.0), axis=1, keepdims=True)
    start_col = end_col - live
    total = jnp.sum(live)
    steps = step_count(meta_ref)
    ghost_row = meta_ref[:, HALF:SLOTS] - atoms
    high_part = jnp.floor(ghost_row * (1.0 / 16.0))
    row_high = high_part.astype(BF16)
    row_low = (ghost_row - 16.0 * high_part).astype(BF16)

    row = iota((ghosts, CH), 0)
    lane = iota((ghosts, CH), 1)
    zcells = atoms // 32
    per_y = (zcells + 2) * 8
    ext_x = row // (4 * per_y)
    ext_y = row // per_y % 4
    ext_z = row // 8 % (zcells + 2)

    def side_of(ext, last, size):
        return jnp.where(ext == 0, -size, jnp.where(ext == last, size, 0.0))

    shift = jnp.where(lane == 12, side_of(ext_x, 3, 4.0), 0.0)
    shift = jnp.where(lane == 13, side_of(ext_y, 3, 4.0), shift)
    shift = jnp.where(lane == 14, side_of(ext_z, zcells + 1, 2.0 * zcells), shift)
    own0 = own_ref[:, 0:CH]
    acc_s[...] = acc0_ref[...]
    for copy in copies:
        copy.wait()
    ghpos[...] = (table[:, CH:].astype(F32) + shift).astype(BF16)

    def ghost_start(step):
        here, _ = ghost_rows(step)
        base = step * STEP
        edge = (iota((STEP, atoms), 0) + base).astype(F32)
        mine = jnp.logical_and(edge >= start_row, edge < end_row).astype(F32)
        source = mine.astype(BF16)
        d_gh[here, :] = source
        edge_t = (iota((atoms, STEP), 1) + base).astype(F32)
        mine_t = jnp.logical_and(edge_t >= start_col, edge_t < end_col)
        spread = mine_t.astype(F32).astype(BF16)
        dt_gh[:, here] = spread
        edge_col = edge[:, 0:1]
        slot = edge_col - jnp.sum(mine * start_row, axis=1, keepdims=True)
        listed = mm(source, row_high) * 16.0 + mm(source, row_low)
        at_slot = iota((STEP, HALF), 1).astype(F32) == slot
        which = jnp.sum(jnp.where(at_slot, listed, 0.0), axis=1, keepdims=True)
        which = jnp.where(edge_col < total, which, -1.0)
        onehot = (iota((STEP, ghosts), 1).astype(F32) == which).astype(F32).astype(BF16)
        oh_gh[here, :] = onehot
        unit, dist = geometry(mm(onehot, ghpos[...]), mm(source, own_pos_ref[...]))
        unit_ref[here, :] = unit
        pre, radial = radial_net(dist, spacing, rbf_ref, rad_ref)
        pre_ref[here, :] = pre.astype(BF16)
        for degree in range(1, 5):
            radial_gh[degree][here, :] = radial[:, degree * CH : (degree + 1) * CH]
        message = scalar_forward(
            here, mm(onehot, table[:, 0:CH]), radial[:, 0:CH], mix_ref, m0_gh, gate_gh, nf0_gh
        )
        acc_s[...] += mm(spread, message)

    over_ghost_steps(steps, ghost_start)

    low0 = (acc_s[...] * norm).astype(BF16)
    updated0 = own0.astype(F32) + mm(low0, out_ref[0])
    new_ref[:, 0:CH] = updated0.astype(BF16)
    logistic = jax.nn.sigmoid(updated0)
    weight0 = ew_ref[...]
    en_ref[...] = weight0 * updated0 * logistic
    grad0 = (weight0 * logistic * (1.0 + updated0 * (1.0 - logistic))).astype(BF16)
    gs0_ref[...] = mm_nt(grad0, out_ref[0]) * norm


def any_specs(count, total):
    return [pl.BlockSpec(memory_space=pl.ANY)] * count + [
        pl.BlockSpec(memory_space=SPACE)
    ] * (total - count)


def start_stage(pieces, feats, *rest):
    atoms = feats.shape[0]
    half = atoms * HALF
    ghosts = sum(piece.shape[0] for piece in pieces)
    out_shape = (
        struct(atoms, CH, dtype=BF16),
        struct(half, ghosts, dtype=BF16),
        struct(half, atoms, dtype=BF16),
        struct(atoms, half, dtype=BF16),
        struct(half, CH, dtype=BF16),
        struct(half, CH),
        struct(atoms, CH),
        struct(atoms, CH),
    ) + (struct(half, CH, dtype=BF16),) * 7
    scratch = [
        pltpu.VMEM((ghosts, 2 * CH), BF16),
        pltpu.SemaphoreType.DMA((7,)),
        pltpu.VMEM((ghosts, CH), BF16),
        pltpu.VMEM((atoms, CH), F32),
    ]
    args = tuple(pieces) + (feats,) + rest
    return call(
        start_kernel, "ghost_start", out_shape, scratch, 1 << 31, args,
        any_specs(len(pieces), len(args)), 24,
    )


def pairs_kernel(group, count, skip, *refs):
    pieces, refs = refs[:count], refs[count:]
    own_ref, meta_ref, mix_ref, out_ref, nw_ref, oh_gh, d_gh, dt_gh, gate_gh = refs[:9]
    gate_own, nf_own, mx_own, acc_own = refs[9:13]
    refs = refs[13:]
    degrees = DEGREES[group]
    radials, refs = dict(zip(degrees, refs)), refs[len(degrees) :]
    new_ref, en_ref, gs_ref, dot_gh = refs[:4]
    grads, refs = dict(zip(degrees, refs[4:])), refs[4 + len(degrees) :]
    if group == 0:
        dot_own, refs = refs[0], refs[1:]
        grads_own, refs = dict(zip(degrees, refs)), refs[len(degrees) :]
    table, sems, wm, wmt, wo, wot, nf_s, mx_s, acc_s = refs
    copies = fetch(pieces, slice(skip, skip + GROUP_COLS[group]), table, sems)
    block_diagonal(KINDS[group], mix_ref, wm, wmt)
    block_diagonal(KINDS[group], out_ref, wo, wot)
    en_ref[...] = jnp.zeros_like(en_ref)
    for copy in copies:
        copy.wait()
    ghost_pairs(
        group, own_ref, table, new_ref, group_cols(group).start, oh_gh, d_gh, dt_gh, gate_gh,
        radials, nw_ref, step_count(meta_ref), wm, wmt, wo, wot, nf_s, mx_s, acc_own, acc_s,
        gs_ref, dot_gh, grads, en_ref,
    )
    if group == 0:
        own_backward(group, gs_ref, gate_own, wmt, nf_own, mx_own, dot_own, grads_own)


def pairs_stage(group, skip, pieces, shared, own_parts, radial_gh):
    feats = shared[0]
    atoms = feats.shape[0]
    half = atoms * HALF
    ghosts = sum(piece.shape[0] for piece in pieces)
    degrees = DEGREES[group]
    sides = 2 if group == 0 else 1
    out_shape = (
        struct(atoms, GROUP_COLS[group], dtype=BF16),
        struct(atoms, CH),
        struct(atoms, GROUP_COLS[group], dtype=BF16),
    ) + (struct(half, CH, dtype=BF16),) * (sides * (1 + len(degrees)))
    args = tuple(pieces) + tuple(shared) + tuple(own_parts)
    args += tuple(radial_gh[degree - 1] for degree in degrees)
    new, energy, gs, *rest = call(
        functools.partial(pairs_kernel, group, len(pieces), skip), "pairs_" + "abc"[group],
        out_shape, pair_scratch(atoms, half, ghosts, group), 1 << 33, args,
        any_specs(len(pieces), len(args)), 24,
    )
    return new, energy, gs, rest[: 1 + len(degrees)], rest[1 + len(degrees) :]


def own_backward_kernel(group, mix_ref, gs_ref, gate_ref, nf_ref, mx_ref, *refs):
    dot_ref, grads, wmt = refs[0], dict(zip(DEGREES[group], refs[1:-1])), refs[-1]
    block_diagonal(KINDS[group], mix_ref, None, wmt)
    own_backward(group, gs_ref, gate_ref, wmt, nf_ref, mx_ref, dot_ref, grads)


def own_backward_stage(group, mix, gs, gate, nf, mx):
    half = nf.shape[0]
    out_shape = (struct(half, CH, dtype=BF16),) * (1 + len(DEGREES[group]))
    scratch = [pltpu.VMEM((len(KINDS[group]), 2 * CH, 2 * CH), BF16)]
    kernel = functools.partial(own_backward_kernel, group)
    name = "own_backward_" + "abc"[group]
    return call(kernel, name, out_shape, scratch, 1 << 32, (mix, gs, gate, nf, mx))


def finish(
    grad, mixed, near, dots, parts, pre, unit, spacing, radt_ref, rbft_ref, mixt_ref
):
    mixed = mixed.astype(F32)
    gate = jax.nn.sigmoid(mixed)
    first = grad * gate * (1.0 + mixed * (1.0 - gate)) + dots * gate * (1.0 - gate)
    weighted = mm(first.astype(BF16), mixt_ref[...]) * near.astype(F32)
    radial_grad = jnp.concatenate([weighted.astype(BF16)] + parts, axis=1)
    hidden_grad = mm(radial_grad, radt_ref[...])
    pre = pre.astype(F32)
    logistic = jax.nn.sigmoid(pre)
    pre_grad = (hidden_grad * logistic * (1.0 + pre * (1.0 - logistic))).astype(BF16)
    centred = centred_of(unit[:, 3:4], spacing, rbft_ref.shape[1])
    slope = jnp.exp(-0.5 * centred * centred) * centred
    basis_grad = mm(pre_grad, rbft_ref[...])
    dist_grad = jnp.sum(basis_grad * slope, axis=1, keepdims=True) * (-1.0 / spacing)
    pull = unit * dist_grad
    across = pull.T[0:8, :]
    top = across.astype(BF16)
    rest = (across - top.astype(F32)).astype(BF16)
    return pull, top, rest


def sum_of(refs, rows):
    total = refs[0][rows, :].astype(F32)
    for ref in refs[1:]:
        total += ref[rows, :].astype(F32)
    return total


def degree_parts(refs, rows):
    by_degree = {}
    refs = list(refs)
    for degrees in DEGREES:
        for degree in degrees:
            by_degree.setdefault(degree, []).append(refs.pop(0))
    return [sum_of(by_degree[degree], rows).astype(BF16) for degree in range(1, 5)]


PARTIALS = sum(len(degrees) for degrees in DEGREES)


def third_kernel(
    p0, p1, p2, p3, p4, own_ref, meta_ref, mix_ref, out_ref, nw_ref, oh_gh, d_gh, dt_gh, gate_gh,
    acc_own, radial_gh2, radial_gh3, radial_gh4,
    radt_ref, rbft_ref, mixt_ref, gs0_ref, en_0, en_a, new_0, new_a, pre_gh, unit_gh,
    m0_ref, nf0_ref, dot_a, gr1_a, gr2_a,
    new_ref, energy_ref, src_ref, flow_ref, fmid_ref, fhigh_ref, gs_ref,
    table, sems, wm, wmt, wo, wot, nf_s, mx_s, acc_s, dot_c, gr2_c, gr3_c, gr4_c, en_s, fgh_s,
):
    group = 1
    radials = {2: radial_gh2, 3: radial_gh3, 4: radial_gh4}
    grads = {2: gr2_c, 3: gr3_c, 4: gr4_c}
    copies = fetch((p0, p1, p2, p3, p4), slice(0, GROUP_COLS[group]), table, sems)
    atoms = own_ref.shape[0]
    spacing = spacing_of(atoms, rbft_ref.shape[1])
    block_diagonal(KINDS[group], mix_ref, wm, wmt)
    block_diagonal(KINDS[group], out_ref, wo, wot)
    en_s[...] = en_0[...] + en_a[...]
    at = 0
    for part in (new_0, new_a):
        new_ref[:, at : at + part.shape[1]] = part[...]
        at += part.shape[1]
    steps = step_count(meta_ref)

    for copy in copies:
        copy.wait()
    ghost_pairs(
        group, own_ref, table, new_ref, 0, oh_gh, d_gh, dt_gh, gate_gh, radials, nw_ref,
        steps, wm, wmt, wo, wot, nf_s, mx_s, acc_own, acc_s, gs_ref, dot_c, grads, en_s,
    )
    energy_ref[...] = jnp.sum(en_s[...].T, axis=0, keepdims=True)

    fgh_s[...] = jnp.zeros_like(fgh_s)
    src_ref[...] = jnp.zeros_like(src_ref)
    gs0_low = gs0_ref[...].astype(BF16)

    def ghost_finish(step):
        here, _ = ghost_rows(step)
        grad = mm(d_gh[here, :], gs0_low)
        pull, top, rest = finish(
            grad, m0_ref[here, :], nf0_ref[here, :], sum_of((dot_a, dot_c), here),
            degree_parts((gr1_a, gr2_a, gr2_c, gr3_c, gr4_c), here), pre_gh[here, :], unit_gh[here, :], spacing,
            radt_ref, rbft_ref, mixt_ref,
        )
        pull_top = pull.astype(BF16)
        pull_rest = (pull - pull_top.astype(F32)).astype(BF16)
        spread = dt_gh[:, here]
        src_ref[...] += mm(spread, pull_top) + mm(spread, pull_rest)
        onehot = oh_gh[here, :]
        fgh_s[...] += mm(top, onehot) + mm(rest, onehot)

    over_ghost_steps(steps, ghost_finish)
    low, mid = flow_ref.shape[1], fmid_ref.shape[1]
    flow_ref[...] = fgh_s[:, 0:low]
    fmid_ref[...] = fgh_s[:, low : low + mid]
    fhigh_ref[...] = fgh_s[:, low + mid :]


def third_stage(pieces, feats, *rest):
    atoms, feat = feats.shape
    half = atoms * HALF
    ghosts = sum(piece.shape[0] for piece in pieces)
    sizes = (ghosts // 4, ghosts // 2, ghosts // 4)
    out_shape = (
        struct(atoms, feat, dtype=BF16),
        struct(1, atoms),
        struct(atoms, CH),
    ) + tuple(struct(8, size) for size in sizes) + (
        struct(atoms, GROUP_COLS[1], dtype=BF16),
    )
    scratch = pair_scratch(atoms, half, ghosts, 1) + [
        pltpu.VMEM((half, CH), BF16),
        pltpu.VMEM((half, CH), BF16),
        pltpu.VMEM((half, CH), BF16),
        pltpu.VMEM((half, CH), BF16),
        pltpu.VMEM((atoms, CH), F32),
        pltpu.VMEM((8, ghosts), F32),
    ]
    args = tuple(pieces) + (feats,) + rest
    return call(
        third_kernel, "third_group", out_shape, scratch, 1 << 33, args,
        any_specs(len(pieces), len(args)), 28,
    )


def own_back_kernel(
    oh_own, pre_own, unit_own, radt_ref, rbft_ref, mixt_ref, gs0_ref, src_ref,
    m0_ref, nf0_ref, dot_a, dot_c, *refs
):
    gr_own, (force_ref,) = refs[:PARTIALS], refs[PARTIALS:]
    atoms = oh_own.shape[1]
    spacing = spacing_of(atoms, rbft_ref.shape[1])
    grad = tiled(gs0_ref[...])
    src = src_ref[...]
    onto = jnp.zeros((8, atoms), F32)
    for step in range(OWN_STEPS):
        rows = own_rows(step)
        pull, top, rest = finish(
            grad, m0_ref[rows, :], nf0_ref[rows, :], sum_of((dot_a, dot_c), rows),
            degree_parts(gr_own, rows), pre_own[rows, :], unit_own[rows, :], spacing, radt_ref,
            rbft_ref, mixt_ref,
        )
        src += jnp.sum(pull.reshape(STEP // atoms, atoms, CH), axis=0)
        onehot = oh_own[rows, :]
        onto += mm(top, onehot) + mm(rest, onehot)
    force_ref[...] = onto - src.T[0:8, :]


def own_back_stage(*args):
    oh_own = args[0]
    out_shape = (struct(8, oh_own.shape[1]),)
    return call(own_back_kernel, "own_back", out_shape, [], 1 << 31, args)[0]


def ring(axis):
    peers = lax.axis_size(axis)
    up = [(i, (i + 1) % peers) for i in range(peers)]
    return up, [(j, i) for i, j in up]


def neighbours_of(block, axis, dim):
    up, down = ring(axis)
    length = block.shape[dim]
    if len(up) == 2 and length == 2:
        other = lax.ppermute(block, axis, up)
        return (
            lax.slice_in_dim(other, length - 1, length, axis=dim),
            lax.slice_in_dim(other, 0, 1, axis=dim),
        )
    before = lax.ppermute(lax.slice_in_dim(block, length - 1, length, axis=dim), axis, up)
    after = lax.ppermute(lax.slice_in_dim(block, 0, 1, axis=dim), axis, down)
    return before, after


def grown(block, axis, dim):
    before, after = neighbours_of(block, axis, dim)
    return jnp.concatenate([before, block, after], axis=dim)


def ghost_pieces(along_y, block, along_x):
    outer = jnp.concatenate(along_y, axis=1)
    low_out, high_out = neighbours_of(outer, "gx", 0)
    low_in, high_in = along_x
    middle = jnp.concatenate([along_y[0], block, along_y[1]], axis=1)
    return tuple(flat_rows(piece) for piece in (low_in, low_out, middle, high_in, high_out))


def flat_rows(piece):
    return piece.reshape(-1, piece.shape[-1])


def fold_kernel(mid_ref, low_ref, high_ref, out_ref):
    lanes = mid_ref.shape[1]
    ext_y = iota(mid_ref.shape, 1) // 32 % 4
    out_ref[...] = (
        mid_ref[...]
        + jnp.where(ext_y == 1, pltpu.roll(low_ref[...], lanes - 64, 1), 0.0)
        + jnp.where(ext_y == 2, pltpu.roll(high_ref[...], 64, 1), 0.0)
    )


def forces_kernel(mid_ref, low_ref, high_ref, own_ref, home_ref, out_ref):
    values = mid_ref[...]
    lanes = values.shape[1]
    ext_z = iota(values.shape, 1) // 8 % 4
    values += jnp.where(ext_z == 1, pltpu.roll(low_ref[...], lanes - 16, 1), 0.0)
    values += jnp.where(ext_z == 2, pltpu.roll(high_ref[...], 16, 1), 0.0)
    first = values.astype(BF16)
    values -= first.astype(F32)
    second = values.astype(BF16)
    third = (values - second.astype(F32)).astype(BF16)
    home = home_ref[...]
    total = own_ref[...] + (mm_nt(first, home) + (mm_nt(second, home) + mm_nt(third, home)))
    for comp in range(3):
        out_ref[comp] = -total[comp : comp + 1, :]


def give_back_x(low, mid, high):
    up, down = ring("gx")
    from_low = lax.ppermute(high, "gx", up)
    from_high = lax.ppermute(low, "gx", down)
    return mid, jnp.concatenate([from_low, from_high], axis=1)


def give_back_y(mid):
    up, down = ring("gy")
    return mid, lax.ppermute(mid, "gy", up), lax.ppermute(mid, "gy", down)


def fold(*args):
    return call(fold_kernel, "fold", (struct(*args[0].shape),), [], 1 << 16, args)[0]


def give_back_z(mid):
    up, down = ring("gz")
    from_low = lax.ppermute(mid, "gz", up)
    return mid, from_low, from_low if len(up) == 2 else lax.ppermute(mid, "gz", down)


def local(
    features,
    positions,
    neighbours,
    counts,
    cell_atoms,
    rbf_weight,
    radial_weight,
    mix_weight,
    out_weight,
    energy_weight,
    norm_weight,
):
    feats = features[0, 0, 0]
    places = jnp.swapaxes(positions[0, 0], 0, 1)
    cells0, cells1, own_pos, meta = make_cells(
        feats, places, neighbours[0, 0, 0].T, counts[0, 0], cell_atoms[0, 0]
    )
    hold = lax.optimization_barrier
    block0, block1 = (part.reshape(2, 2, 2, 8, part.shape[1]) for part in (cells0, cells1))
    block0 = grown(block0, "gz", 2)
    block0, own_pos, meta = hold((block0, own_pos, meta))
    y0 = neighbours_of(block0, "gy", 1)
    x0_in = neighbours_of(block0, "gx", 0)
    oh_own, pre_own, unit_own, radt, rbft, mixt, home, *radial_own = own_stage(
        meta, own_pos, rbf_weight, radial_weight, mix_weight
    )
    block1 = grown(block1, "gz", 2)
    y1 = neighbours_of(block1, "gy", 1)
    y0, block1, oh_own = hold((y0, block1, oh_own))
    pieces0 = ghost_pieces(y0, block0, x0_in)
    x1_in = neighbours_of(block1, "gx", 0)
    (m0_own, gate_own, nf0_own, acc0), (own_a,) = own_forward_stage(
        (0,), feats, mix_weight, oh_own, radial_own
    )
    (
        new_0, oh_gh, d_gh, dt_gh, pre_gh, unit_gh, gs0, en_0, m0_gh, gate_gh, nf0_gh, *radial_gh,
    ) = start_stage(
        pieces0, feats, own_pos, meta, rbf_weight, radial_weight, mix_weight, out_weight,
        energy_weight[None], acc0,
    )
    y1, gate_gh = hold((y1, gate_gh))
    pieces1 = ghost_pieces(y1, block1, x1_in)
    shared = (feats, meta, mix_weight, out_weight, norm_weight, oh_gh, d_gh, dt_gh, gate_gh)
    new_a, en_a, _, (dot_gh_a, *gr_gh_a), (dot_own_a, *gr_own_a) = pairs_stage(
        0, 2 * CH, pieces0, shared, (gate_own, *own_a), radial_gh
    )
    en_a, gate_own = hold((en_a, gate_own))
    _, (own_b,) = own_forward_stage((1,), feats, mix_weight, oh_own, radial_own, gate_own)
    new, energy, src, low, mid, high, gs_b = third_stage(
        pieces1, *shared, own_b[2], *radial_gh[1:], radt, rbft, mixt, gs0, en_0, en_a, new_0,
        new_a, pre_gh, unit_gh, m0_gh, nf0_gh, dot_gh_a, *gr_gh_a,
    )
    mid, arrived = give_back_x(low, mid, high)
    dot_own_b, *gr_own_b = own_backward_stage(1, mix_weight, gs_b, gate_own, *own_b[:2])
    arrived, gs0, dot_own_b = hold((arrived, gs0, dot_own_b))
    mid, from_low, from_high = give_back_y(mid + arrived)
    own = own_back_stage(
        oh_own, pre_own, unit_own, radt, rbft, mixt, gs0, src, m0_own, nf0_own, dot_own_a,
        dot_own_b, *gr_own_a, *gr_own_b,
    )
    from_low, from_high, own = hold((from_low, from_high, own))
    folded = give_back_z(fold(mid, from_low, from_high))
    args = (*folded, own, home)
    out_shape = (struct(3, 1, own.shape[1]),)
    forces = call(forces_kernel, "forces", out_shape, [], 1 << 20, args)[0]
    return (
        new[None, None, None],
        energy[None, None],
        jnp.swapaxes(forces, 0, 1)[None, None],
    )


def solution(mesh):
    split = P("gx", "gy", "gz", None, None)
    flat = P("gx", "gy", "gz", None)
    return jax.shard_map(
        local,
        mesh=mesh,
        in_specs=(split, split, split, flat, flat, P(), P(), P(), P(), P(), P()),
        out_specs=(split, flat, split),
        check_vma=False,
    )
```

```python
import functools
import math

import jax
import jax.numpy as jnp
from jax import lax
from jax.experimental import pallas as pl
from jax.experimental.pallas import tpu as pltpu
from jax.sharding import PartitionSpec as P

F32 = jnp.float32
BF16 = jnp.bfloat16
CH = 128
SLOTS = 32
HALF = 16
STEP = 256
OWN_STEPS = 4
GH_STEPS = 2
MIB = 1024 * 1024
SPACE = pltpu.VMEM
PAIR_DEGREES = (
    (1, 1), (1, 2), (2, 2), (2, 2),
    (3, 3), (3, 3), (3, 3), (3, 4),
    (4, 4), (4, 4), (4, 4), (4, 4),
)
GROUPS = ((0, 4), (4, 12))
KINDS = tuple(sorted({PAIR_DEGREES[pair] for pair in range(*group)}) for group in GROUPS)
DEGREES = tuple(sorted({d for both in kinds for d in both}) for kinds in KINDS)
GROUP_COLS = tuple(2 * CH * (end - begin) for begin, end in GROUPS)


def mm(a, b):
    return jnp.dot(a, b, preferred_element_type=F32)


def mm_nt(a, b):
    return lax.dot_general(a, b, (((1,), (1,)), ((), ())), preferred_element_type=F32)


def iota(shape, dim):
    return lax.broadcasted_iota(jnp.int32, shape, dim)


def flip(w):
    return w.astype(F32).T.astype(BF16)


def pair_cols(pair):
    return slice(CH + pair * 2 * CH, CH + (pair + 1) * 2 * CH)


def struct(*shape, dtype=F32):
    return jax.ShapeDtypeStruct(shape, dtype)


def call(kernel, name, out_shape, scratch, args, specs=None, limit=16):
    return pl.pallas_call(
        kernel,
        out_shape=out_shape,
        in_specs=specs or [pl.BlockSpec(memory_space=SPACE)] * len(args),
        out_specs=tuple(pl.BlockSpec(memory_space=SPACE) for _ in out_shape),
        scratch_shapes=scratch,
        compiler_params=pltpu.CompilerParams(vmem_limit_bytes=limit * MIB),
        cost_estimate=pl.CostEstimate(flops=1024, bytes_accessed=1024, transcendentals=0),
        name=name,
    )(*args)


def cells_kernel(
    feat_ref, pos_ref, near_ref, counts_ref, order_ref,
    first_ref, own_pos_ref, meta_ref, pick_ref, rows_ref, pos_rows,
):
    rows_ref[...] = jnp.zeros_like(rows_ref)
    pos_rows[...] = jnp.zeros_like(pos_rows)
    atoms = feat_ref.shape[0]
    rows_ref[0:SLOTS, :] = near_ref[...].astype(F32)
    rows_ref[SLOTS : SLOTS + 1, :] = counts_ref[...].astype(F32)
    rows_ref[SLOTS + 1 : SLOTS + 2, :] = order_ref[...].astype(F32)
    meta = rows_ref[...].T
    meta_ref[...] = meta
    for comp in range(3):
        places = pos_ref[comp]
        first = places.astype(BF16).astype(F32)
        second = (places - first).astype(BF16).astype(F32)
        pos_rows[comp : comp + 1, :] = first
        pos_rows[4 + comp : 5 + comp, :] = second
        pos_rows[8 + comp : 9 + comp, :] = places - first - second
    pieces = pos_rows[...].astype(BF16)
    lane = iota((atoms, atoms), 1).astype(F32)
    pick = (meta[:, SLOTS + 1 : SLOTS + 2] == lane).astype(F32).astype(BF16)
    same = (iota((atoms, atoms), 0) == iota((atoms, atoms), 1)).astype(F32).astype(BF16)
    own_pos_ref[...] = mm_nt(same, pieces).astype(BF16)
    first_ref[:, CH : 2 * CH] = mm_nt(pick, pieces).astype(BF16)
    pick_ref[...] = pick
    first_ref[:, 0:CH] = mm(pick, feat_ref[:, 0:CH]).astype(BF16)
    cut = pair_cols(GROUPS[1][0]).start
    first_ref[:, 2 * CH :] = mm(pick, feat_ref[:, CH:cut]).astype(BF16)


def rest_kernel(feat_ref, pick_ref, rest_ref):
    cut = pair_cols(GROUPS[1][0]).start
    rest_ref[...] = mm(pick_ref[...], feat_ref[:, cut:]).astype(BF16)


def make_cells(feats, places, near, counts, order):
    atoms = feats.shape[0]
    out_shape = (
        struct(atoms, 2 * CH + GROUP_COLS[0], dtype=BF16),
        struct(atoms, CH, dtype=BF16),
        struct(atoms, CH),
        struct(atoms, atoms, dtype=BF16),
    )
    args = (feats, places, near, counts, order)
    scratch = [pltpu.VMEM((CH, atoms), F32), pltpu.VMEM((CH, atoms), F32)]
    first, own_pos, meta, pick = call(
        cells_kernel, "cells", out_shape, scratch, args, limit=60
    )
    out_shape = (struct(atoms, sum(GROUP_COLS[1:]), dtype=BF16),)
    rest = call(rest_kernel, "cells_rest", out_shape, [], (feats, pick), limit=60)[0]
    return first, rest, own_pos, meta


def spacing_of(atoms, nbasis):
    depth = atoms // 16
    return 2.0 * math.sqrt(32.0 + depth * depth) / (nbasis - 1)


def own_onehots(meta_ref, oh_own):
    atoms = meta_ref.shape[0]
    counts = meta_ref[:, SLOTS : SLOTS + 1]
    lane_atom = iota((atoms, atoms), 1).astype(F32)
    for slot in range(HALF):
        hit = jnp.logical_and(meta_ref[:, slot : slot + 1] == lane_atom, counts > slot)
        oh_own[slot * atoms : (slot + 1) * atoms, :] = hit.astype(F32).astype(BF16)


def geometry(near, here):
    diff = near - here
    rel = (diff + pltpu.roll(diff, CH - 4, 1)) + (
        pltpu.roll(diff, CH - 8, 1) + pltpu.roll(diff, CH - 12, 1)
    )
    lane = iota(rel.shape, 1)
    rel = jnp.where(lane < 3, rel, 0.0)
    square = jnp.sum(rel * rel, axis=1, keepdims=True)
    inverse = lax.rsqrt(jnp.where(square > 0.0, square, 1.0))
    dist = square * inverse
    return jnp.where(lane == 3, dist, rel * inverse), dist


def centred_of(dist, spacing, nbasis):
    return dist * (1.0 / spacing) - iota((dist.shape[0], nbasis), 1).astype(F32)


def radial_net(dist, spacing, rbf_ref, rad_ref):
    centred = centred_of(dist, spacing, rbf_ref.shape[0])
    basis = jnp.exp(-0.5 * centred * centred)
    pre = mm(basis.astype(BF16), rbf_ref[...])
    hidden = (pre * jax.nn.sigmoid(pre)).astype(BF16)
    return pre, mm(hidden, rad_ref[...]).astype(BF16)


def own_spread(atoms, size=STEP):
    shape = (atoms, size)
    return (iota(shape, 1) % atoms == iota(shape, 0)).astype(F32).astype(BF16)


def tiled(values, size=STEP):
    return jnp.concatenate([values] * (size // values.shape[0]), axis=0)


def live_ghosts(meta_ref):
    return jnp.maximum(meta_ref[:, SLOTS : SLOTS + 1] - HALF, 0.0)


def step_count(meta_ref):
    total = jnp.sum(live_ghosts(meta_ref)).astype(jnp.int32)
    rows = GH_STEPS * STEP
    return jnp.maximum((total + (rows - 1)) // rows, 1) * GH_STEPS


def own_rows(step, size=STEP):
    return pl.ds(step * size, size)


def ghost_rows(step, size=STEP):
    first = OWN_STEPS * STEP
    if isinstance(step, int):
        return pl.ds(step * size, size), pl.ds(first + step * size, size)
    base = pl.multiple_of(step * size, size)
    return pl.ds(base, size), pl.ds(pl.multiple_of(first + base, size), size)


def over_ghost_steps(steps, body, size=STEP):
    static = GH_STEPS * STEP // size
    for step in range(static):
        body(step)

    def again(step, carry):
        body(step)
        return carry

    lax.fori_loop(static, (steps * STEP + (size - 1)) // size, again, 0)


def block_diagonal(kinds, source, straight=None, across=None):
    zero = jnp.zeros((CH, CH), BF16)
    targets = [ref for ref in (straight, across) if ref is not None]
    for kind, both in enumerate(kinds):
        for ref in targets:
            ref[kind, 0:CH, CH:] = zero
            ref[kind, CH:, 0:CH] = zero
    for degree in sorted({d for both in kinds for d in both}):
        weight = source[degree]
        flipped = flip(weight) if across is not None else None
        for kind, both in enumerate(kinds):
            for side in range(2):
                if both[side] == degree:
                    part = slice(side * CH, side * CH + CH)
                    if straight is not None:
                        straight[kind, part, part] = weight
                    if across is not None:
                        across[kind, part, part] = flipped


def fetch(pieces, cols, table, sems):
    low, high, ghosts = 0, 0, table.shape[0]
    if len(pieces) == 3:
        rows = [(piece, 0, piece.shape[0]) for piece in pieces]
    else:
        low_in, low_out, mid, high_in, high_out = pieces
        half = low_out.shape[0] // 2
        rows = [(low_out, 0, half), (low_in, 0, low_in.shape[0]), (low_out, half, half)]
        rows += [(mid, 0, mid.shape[0])]
        rows += [(high_out, 0, half), (high_in, 0, high_in.shape[0]), (high_out, half, half)]
    copies = []
    at = 0
    for index, (piece, start, count) in enumerate(rows):
        source = piece.at[pl.ds(start, count), cols]
        target = table.at[pl.ds(at, count), :]
        copies.append(pltpu.make_async_copy(source, target, sems.at[index]))
        at += count
    for copy in copies:
        copy.start()
    return copies


def infos_of(group):
    infos = []
    for index, pair in enumerate(range(*GROUPS[group])):
        degrees = PAIR_DEGREES[pair]
        cols = slice(index * 2 * CH, (index + 1) * 2 * CH)
        infos.append((cols, degrees, KINDS[group].index(degrees)))
    return infos


def group_cols(group):
    begin, end = GROUPS[group]
    return slice(pair_cols(begin).start, pair_cols(end - 1).stop)


def twice(values):
    return jnp.concatenate([values, values], axis=1)


def forward(group, rows, onehot, feats, radials, gate_ref, wm, nf_ref, mx_ref):
    near = mm(onehot, feats).astype(BF16)
    nf_ref[rows, :] = near
    gate = twice(gate_ref[rows, :])
    messages = []
    for cols, degrees, kind in infos_of(group):
        radial = jnp.concatenate([radials[d][rows, :] for d in degrees], axis=1)
        mixed = mm(near[:, cols] * radial, wm[kind]).astype(BF16)
        mx_ref[rows, cols] = mixed
        messages.append(mixed * gate)
    return jnp.concatenate(messages, axis=1)


def backward(group, rows, grad, gate_ref, wmt, nf_ref, mx_ref, dot_ref, grad_refs):
    parts = {}
    dots = None
    gate = twice(gate_ref[rows, :])
    for cols, degrees, kind in infos_of(group):
        product = grad[:, cols] * mx_ref[rows, cols]
        dot = (product[:, 0:CH] + product[:, CH:]).astype(F32)
        dots = dot if dots is None else dots + dot
        weighted = mm(grad[:, cols] * gate, wmt[kind]) * nf_ref[rows, cols].astype(F32)
        for side in range(2):
            part = weighted[:, side * CH : (side + 1) * CH]
            degree = degrees[side]
            parts[degree] = parts[degree] + part if degree in parts else part
    dot_ref[rows, :] = dots.astype(dot_ref.dtype)
    for degree, part in parts.items():
        grad_refs[degree][rows, :] = part.astype(grad_refs[degree].dtype)


def own_forward(group, own_ref, oh_own, radials, gate_ref, wm, nf_ref, mx_ref, acc_ref):
    spread = own_spread(own_ref.shape[0])
    feats = own_ref[:, group_cols(group)]
    summed = None
    for step in range(OWN_STEPS):
        rows = own_rows(step)
        message = forward(
            group, rows, oh_own[rows, :], feats, radials, gate_ref, wm, nf_ref, mx_ref
        )
        part = mm(spread, message)
        summed = part if summed is None else summed + part
    acc_ref[...] = summed


def own_backward(group, gs_ref, gate_ref, wmt, nf_ref, mx_ref, dot_ref, grad_refs):
    grad = tiled(gs_ref[...])
    for step in range(OWN_STEPS):
        backward(
            group, own_rows(step), grad, gate_ref, wmt, nf_ref, mx_ref, dot_ref, grad_refs
        )


def ghost_pairs(
    group, own_ref, table, new_ref, new_base, oh_gh, d_gh, dt_gh, gate_ref, radials, nw_ref,
    steps, wm, wmt, wo, wot, nf_s, mx_s, acc_in, acc_s, gs_ref, dot_ref, grad_refs, en_ref,
):
    norm = 1.0 / math.sqrt(SLOTS)
    acc_s[...] = acc_in[...]

    def ghost_forward(step):
        here, _ = ghost_rows(step)
        message = forward(
            group, here, oh_gh[here, :], table[...], radials, gate_ref, wm, nf_s, mx_s
        )
        acc_s[...] += mm(dt_gh[:, here], message)

    over_ghost_steps(steps, ghost_forward)

    begin = group_cols(group).start
    for cols, degrees, kind in infos_of(group):
        summed_low = (acc_s[:, cols] * norm).astype(BF16)
        own = own_ref[:, begin + cols.start : begin + cols.stop]
        updated = own.astype(F32) + mm(summed_low, wo[kind])
        at = begin - new_base + cols.start
        new_ref[:, at : at + 2 * CH] = updated.astype(BF16)
        weight = jnp.concatenate(
            [nw_ref[d - 1 : d, :] * (1.0 / (2 * d + 1)) for d in degrees], axis=1
        )
        scale = weight * updated
        energy = scale * updated
        en_ref[...] += energy[:, 0:CH] + energy[:, CH:]
        gs_ref[:, cols] = (mm((2.0 * scale).astype(BF16), wot[kind]) * norm).astype(BF16)

    def ghost_backward(step):
        here, _ = ghost_rows(step)
        grad = mm(d_gh[here, :], gs_ref[...]).astype(BF16)
        backward(group, here, grad, gate_ref, wmt, nf_s, mx_s, dot_ref, grad_refs)

    over_ghost_steps(steps, ghost_backward)


def pair_scratch(atoms, half, ghosts, group):
    count, width = len(KINDS[group]), GROUP_COLS[group]
    return (
        [pltpu.VMEM((ghosts, width), BF16), pltpu.SemaphoreType.DMA((7,))]
        + [pltpu.VMEM((count, 2 * CH, 2 * CH), BF16) for _ in range(4)]
        + [
            pltpu.VMEM((half, width), BF16),
            pltpu.VMEM((half, width), BF16),
            pltpu.VMEM((atoms, width), F32),
        ]
    )


def own_kernel(
    meta_ref, own_pos_ref, rbf_ref, rad_ref,
    oh_own, pre_ref, unit_ref, radt_ref, rbft_ref, home_ref, *radial_refs
):
    atoms = meta_ref.shape[0]
    nbasis = rbf_ref.shape[0]
    spacing = spacing_of(atoms, nbasis)
    own_onehots(meta_ref, oh_own)
    here = tiled(own_pos_ref[...].astype(F32))
    for step in range(OWN_STEPS):
        rows = own_rows(step)
        unit, dist = geometry(mm(oh_own[rows, :], own_pos_ref[...]), here)
        unit_ref[rows, :] = unit
        pre, radial = radial_net(dist, spacing, rbf_ref, rad_ref)
        pre_ref[rows, :] = pre.astype(BF16)
        for degree, ref in enumerate(radial_refs):
            ref[rows, :] = radial[:, degree * CH : (degree + 1) * CH]
    for degree in range(5):
        part = slice(degree * CH, (degree + 1) * CH)
        radt_ref[part, :] = flip(rad_ref[:, part])
    for index in range(nbasis // CH):
        part = slice(index * CH, (index + 1) * CH)
        rbft_ref[:, part] = flip(rbf_ref[part, :])
    lanes = home_ref.shape[1]
    lane = iota((atoms, lanes), 1)
    ext_x, ext_y, ext_z = lane // 128, lane // 32 % 4, lane // 8 % 4
    slot = ((2 * ext_x + ext_y - 1) * 2 + ext_z - 1) * 8 + lane % 8
    inside = jnp.logical_and(
        jnp.logical_or(ext_y == 1, ext_y == 2), jnp.logical_or(ext_z == 1, ext_z == 2)
    )
    to_slot = jnp.logical_and(iota((atoms, lanes), 0) == slot, inside)
    to_slot = to_slot.astype(F32).astype(BF16)
    order = meta_ref[:, SLOTS + 1 : SLOTS + 2]
    to_atom = (order == iota((atoms, atoms), 1).astype(F32)).astype(F32)
    home_ref[...] = mm(to_atom.T.astype(BF16), to_slot).astype(BF16)


def own_stage(meta, own_pos, rbf, rad):
    atoms = meta.shape[0]
    edges = atoms * HALF
    out_shape = (
        struct(edges, atoms, dtype=BF16),
        struct(edges, CH, dtype=BF16),
        struct(edges, CH),
        struct(*rad.shape[::-1], dtype=BF16),
        struct(*rbf.shape[::-1], dtype=BF16),
        struct(atoms, 256, dtype=BF16),
    ) + (struct(edges, CH, dtype=BF16),) * 5
    args = (meta, own_pos, rbf, rad)
    return call(own_kernel, "own_edges", out_shape, [], args, limit=60)


def scalar_forward(rows, near, radial, mix_ref, m0_ref, gate_ref, nf0_ref):
    near = near.astype(BF16)
    nf0_ref[rows, :] = near
    mixed = mm(near * radial, mix_ref[0])
    m0_ref[rows, :] = mixed.astype(BF16)
    gate = jax.nn.sigmoid(mixed)
    gate_ref[rows, :] = gate.astype(BF16)
    return (mixed * gate).astype(BF16)


def own_forward_kernel(groups, scalar, *refs):
    own_ref, mix_ref, oh_own, refs = *refs[:3], refs[3:]
    radial0, radials = refs[0], dict(enumerate(refs[1:5], start=1))
    refs = refs[5:]
    if scalar:
        m0_ref, gate_ref, nf0_ref, acc0_ref = refs[:4]
        refs = refs[4:]
        spread = own_spread(own_ref.shape[0])
        feats = own_ref[:, 0:CH]
        summed = None
        for step in range(OWN_STEPS):
            rows = own_rows(step)
            message = scalar_forward(
                rows, mm(oh_own[rows, :], feats), radial0[rows, :], mix_ref, m0_ref, gate_ref,
                nf0_ref,
            )
            part = mm(spread, message)
            summed = part if summed is None else summed + part
        acc0_ref[...] = summed
    else:
        gate_ref, refs = refs[0], refs[1:]
    outs, weights = refs[: 3 * len(groups)], refs[3 * len(groups) :]
    for index, group in enumerate(groups):
        block_diagonal(KINDS[group], mix_ref, weights[index])
        nf_ref, mx_ref, acc_ref = outs[3 * index : 3 * index + 3]
        own_forward(
            group, own_ref, oh_own, radials, gate_ref, weights[index], nf_ref, mx_ref, acc_ref
        )


def own_forward_stage(groups, feats, mix, oh_own, radial_own, gate=None):
    atoms = feats.shape[0]
    half = atoms * HALF
    out_shape = ()
    if gate is None:
        out_shape += (struct(half, CH, dtype=BF16),) * 3 + (struct(atoms, CH),)
    for group in groups:
        width = GROUP_COLS[group]
        out_shape += (struct(half, width, dtype=BF16),) * 2 + (struct(atoms, width),)
    args = (feats, mix, oh_own, *radial_own) + (() if gate is None else (gate,))
    scratch = [pltpu.VMEM((len(KINDS[group]), 2 * CH, 2 * CH), BF16) for group in groups]
    name = "own_forward_" + "".join("abc"[group] for group in groups)
    kernel = functools.partial(own_forward_kernel, groups, gate is None)
    outs = call(kernel, name, out_shape, scratch, args)
    first = len(outs) - 3 * len(groups)
    return outs[:first], [outs[first + 3 * i : first + 3 * i + 3] for i in range(len(groups))]


def start_kernel(
    p0, p1, p2, p3, p4, own_ref, own_pos_ref, meta_ref, rbf_ref, rad_ref, mix_ref, out_ref,
    ew_ref, acc0_ref,
    new_ref, oh_gh, d_gh, dt_gh, pre_ref, unit_ref, gs0_ref, en_ref, m0_gh, gate_gh, nf0_gh,
    radial_gh1, radial_gh2, radial_gh3, radial_gh4,
    table, sems, ghpos, acc_s,
):
    radial_gh = (None, radial_gh1, radial_gh2, radial_gh3, radial_gh4)
    copies = fetch((p0, p1, p2, p3, p4), slice(0, 2 * CH), table, sems)
    atoms = own_ref.shape[0]
    ghosts = table.shape[0]
    spacing = spacing_of(atoms, rbf_ref.shape[0])
    norm = 1.0 / math.sqrt(SLOTS)

    live = live_ghosts(meta_ref)
    sub_atom = iota((atoms, atoms), 0)
    lane_atom = iota((atoms, atoms), 1)
    live_b = jnp.broadcast_to(live, (atoms, atoms))
    end_row = jnp.sum(jnp.where(sub_atom <= lane_atom, live_b, 0.0), axis=0, keepdims=True)
    live_row = jnp.sum(jnp.where(sub_atom == lane_atom, live_b, 0.0), axis=0, keepdims=True)
    start_row = end_row - live_row
    row_b = jnp.broadcast_to(live_row, (atoms, atoms))
    end_col = jnp.sum(jnp.where(lane_atom <= sub_atom, row_b, 0.0), axis=1, keepdims=True)
    start_col = end_col - live
    total = jnp.sum(live)
    steps = step_count(meta_ref)
    ghost_row = meta_ref[:, HALF:SLOTS] - atoms
    high_part = jnp.floor(ghost_row * (1.0 / 16.0))
    row_high = high_part.astype(BF16)
    row_low = (ghost_row - 16.0 * high_part).astype(BF16)

    row = iota((ghosts, CH), 0)
    lane = iota((ghosts, CH), 1)
    zcells = atoms // 32
    per_y = (zcells + 2) * 8
    ext_x = row // (4 * per_y)
    ext_y = row // per_y % 4
    ext_z = row // 8 % (zcells + 2)

    def side_of(ext, last, size):
        return jnp.where(ext == 0, -size, jnp.where(ext == last, size, 0.0))

    shift = jnp.where(lane == 12, side_of(ext_x, 3, 4.0), 0.0)
    shift = jnp.where(lane == 13, side_of(ext_y, 3, 4.0), shift)
    shift = jnp.where(lane == 14, side_of(ext_z, zcells + 1, 2.0 * zcells), shift)
    own0 = own_ref[:, 0:CH]
    acc_s[...] = acc0_ref[...]
    for copy in copies:
        copy.wait()
    ghpos[...] = (table[:, CH:].astype(F32) + shift).astype(BF16)

    def ghost_start(step):
        here, _ = ghost_rows(step)
        base = step * STEP
        edge = (iota((STEP, atoms), 0) + base).astype(F32)
        mine = jnp.logical_and(edge >= start_row, edge < end_row).astype(F32)
        source = mine.astype(BF16)
        d_gh[here, :] = source
        edge_t = (iota((atoms, STEP), 1) + base).astype(F32)
        mine_t = jnp.logical_and(edge_t >= start_col, edge_t < end_col)
        spread = mine_t.astype(F32).astype(BF16)
        dt_gh[:, here] = spread
        edge_col = edge[:, 0:1]
        slot = edge_col - jnp.sum(mine * start_row, axis=1, keepdims=True)
        listed = mm(source, row_high) * 16.0 + mm(source, row_low)
        at_slot = iota((STEP, HALF), 1).astype(F32) == slot
        which = jnp.sum(jnp.where(at_slot, listed, 0.0), axis=1, keepdims=True)
        which = jnp.where(edge_col < total, which, -1.0)
        onehot = (iota((STEP, ghosts), 1).astype(F32) == which).astype(F32).astype(BF16)
        oh_gh[here, :] = onehot
        unit, dist = geometry(mm(onehot, ghpos[...]), mm(source, own_pos_ref[...]))
        unit_ref[here, :] = unit
        pre, radial = radial_net(dist, spacing, rbf_ref, rad_ref)
        pre_ref[here, :] = pre.astype(BF16)
        for degree in range(1, 5):
            radial_gh[degree][here, :] = radial[:, degree * CH : (degree + 1) * CH]
        message = scalar_forward(
            here, mm(onehot, table[:, 0:CH]), radial[:, 0:CH], mix_ref, m0_gh, gate_gh, nf0_gh
        )
        acc_s[...] += mm(spread, message)

    over_ghost_steps(steps, ghost_start)

    low0 = (acc_s[...] * norm).astype(BF16)
    updated0 = own0.astype(F32) + mm(low0, out_ref[0])
    new_ref[:, 0:CH] = updated0.astype(BF16)
    logistic = jax.nn.sigmoid(updated0)
    weight0 = ew_ref[...]
    en_ref[...] = weight0 * updated0 * logistic
    grad0 = (weight0 * logistic * (1.0 + updated0 * (1.0 - logistic))).astype(BF16)
    gs0_ref[...] = mm_nt(grad0, out_ref[0]) * norm


def any_specs(count, total):
    return [pl.BlockSpec(memory_space=pl.ANY)] * count + [
        pl.BlockSpec(memory_space=SPACE)
    ] * (total - count)


def start_stage(pieces, feats, *rest):
    atoms = feats.shape[0]
    half = atoms * HALF
    ghosts = sum(piece.shape[0] for piece in pieces)
    out_shape = (
        struct(atoms, CH, dtype=BF16),
        struct(half, ghosts, dtype=BF16),
        struct(half, atoms, dtype=BF16),
        struct(atoms, half, dtype=BF16),
        struct(half, CH, dtype=BF16),
        struct(half, CH),
        struct(atoms, CH),
        struct(atoms, CH),
    ) + (struct(half, CH, dtype=BF16),) * 7
    scratch = [
        pltpu.VMEM((ghosts, 2 * CH), BF16),
        pltpu.SemaphoreType.DMA((7,)),
        pltpu.VMEM((ghosts, CH), BF16),
        pltpu.VMEM((atoms, CH), F32),
    ]
    args = tuple(pieces) + (feats,) + rest
    return call(
        start_kernel, "ghost_start", out_shape, scratch, args,
        any_specs(len(pieces), len(args)), 24,
    )


def pairs_kernel(group, count, skip, *refs):
    pieces, refs = refs[:count], refs[count:]
    own_ref, meta_ref, mix_ref, out_ref, nw_ref, oh_gh, d_gh, dt_gh, gate_gh = refs[:9]
    gate_own, nf_own, mx_own, acc_own = refs[9:13]
    refs = refs[13:]
    degrees = DEGREES[group]
    radials, refs = dict(zip(degrees, refs)), refs[len(degrees) :]
    new_ref, en_ref, gs_ref, dot_gh = refs[:4]
    grads, refs = dict(zip(degrees, refs[4:])), refs[4 + len(degrees) :]
    if group == 0:
        dot_own, refs = refs[0], refs[1:]
        grads_own, refs = dict(zip(degrees, refs)), refs[len(degrees) :]
    table, sems, wm, wmt, wo, wot, nf_s, mx_s, acc_s = refs
    copies = fetch(pieces, slice(skip, skip + GROUP_COLS[group]), table, sems)
    block_diagonal(KINDS[group], mix_ref, wm, wmt)
    block_diagonal(KINDS[group], out_ref, wo, wot)
    en_ref[...] = jnp.zeros_like(en_ref)
    for copy in copies:
        copy.wait()
    ghost_pairs(
        group, own_ref, table, new_ref, group_cols(group).start, oh_gh, d_gh, dt_gh, gate_gh,
        radials, nw_ref, step_count(meta_ref), wm, wmt, wo, wot, nf_s, mx_s, acc_own, acc_s,
        gs_ref, dot_gh, grads, en_ref,
    )
    if group == 0:
        own_backward(group, gs_ref, gate_own, wmt, nf_own, mx_own, dot_own, grads_own)


def pairs_stage(group, skip, pieces, shared, own_parts, radial_gh):
    feats = shared[0]
    atoms = feats.shape[0]
    half = atoms * HALF
    ghosts = sum(piece.shape[0] for piece in pieces)
    degrees = DEGREES[group]
    sides = 2 if group == 0 else 1
    out_shape = (
        struct(atoms, GROUP_COLS[group], dtype=BF16),
        struct(atoms, CH),
        struct(atoms, GROUP_COLS[group], dtype=BF16),
    ) + (struct(half, CH, dtype=BF16),) * (sides * (1 + len(degrees)))
    args = tuple(pieces) + tuple(shared) + tuple(own_parts)
    args += tuple(radial_gh[degree - 1] for degree in degrees)
    new, energy, gs, *rest = call(
        functools.partial(pairs_kernel, group, len(pieces), skip), "pairs_" + "abc"[group],
        out_shape, pair_scratch(atoms, half, ghosts, group), args,
        any_specs(len(pieces), len(args)), 24,
    )
    return new, energy, gs, rest[: 1 + len(degrees)], rest[1 + len(degrees) :]


def own_backward_kernel(group, mix_ref, gs_ref, gate_ref, nf_ref, mx_ref, *refs):
    dot_ref, grads, wmt = refs[0], dict(zip(DEGREES[group], refs[1:-1])), refs[-1]
    block_diagonal(KINDS[group], mix_ref, None, wmt)
    own_backward(group, gs_ref, gate_ref, wmt, nf_ref, mx_ref, dot_ref, grads)


def own_backward_stage(group, mix, gs, gate, nf, mx):
    half = nf.shape[0]
    out_shape = (struct(half, CH, dtype=BF16),) * (1 + len(DEGREES[group]))
    scratch = [pltpu.VMEM((len(KINDS[group]), 2 * CH, 2 * CH), BF16)]
    kernel = functools.partial(own_backward_kernel, group)
    name = "own_backward_" + "abc"[group]
    return call(kernel, name, out_shape, scratch, (mix, gs, gate, nf, mx))


def finish(
    grad, mixed, near, dots, parts, pre, unit, spacing, radt_ref, rbft_ref, mix_t
):
    mixed = mixed.astype(F32)
    gate = jax.nn.sigmoid(mixed)
    first = grad * gate * (1.0 + mixed * (1.0 - gate)) + dots * gate * (1.0 - gate)
    weighted = mm(first.astype(BF16), mix_t) * near.astype(F32)
    radial_grad = jnp.concatenate([weighted.astype(BF16)] + parts, axis=1)
    hidden_grad = mm(radial_grad, radt_ref[...])
    pre = pre.astype(F32)
    logistic = jax.nn.sigmoid(pre)
    pre_grad = (hidden_grad * logistic * (1.0 + pre * (1.0 - logistic))).astype(BF16)
    centred = centred_of(unit[:, 3:4], spacing, rbft_ref.shape[1])
    slope = jnp.exp(-0.5 * centred * centred) * centred
    basis_grad = mm(pre_grad, rbft_ref[...])
    dist_grad = jnp.sum(basis_grad * slope, axis=1, keepdims=True) * (-1.0 / spacing)
    pull = unit * dist_grad
    across = pull.T[0:8, :]
    top = across.astype(BF16)
    rest = (across - top.astype(F32)).astype(BF16)
    return pull, top, rest


def sum_of(refs, rows):
    total = refs[0][rows, :].astype(F32)
    for ref in refs[1:]:
        total += ref[rows, :].astype(F32)
    return total


def degree_parts(refs, rows):
    by_degree = {}
    refs = list(refs)
    for degrees in DEGREES:
        for degree in degrees:
            by_degree.setdefault(degree, []).append(refs.pop(0))
    return [sum_of(by_degree[degree], rows).astype(BF16) for degree in range(1, 5)]


PARTIALS = sum(len(degrees) for degrees in DEGREES)


def third_kernel(
    p0, p1, p2, p3, p4, own_ref, meta_ref, mix_ref, out_ref, nw_ref, oh_gh, d_gh, dt_gh, gate_gh,
    acc_own, radt_ref, rbft_ref, gs0_ref, en_0, en_a, new_0, new_a, pre_gh, unit_gh,
    m0_ref, nf0_ref, dot_a, *refs
):
    group = 1
    before, degrees = len(DEGREES[0]), DEGREES[group]
    gr_a, refs = refs[:before], refs[before:]
    radials, refs = dict(zip(degrees, refs)), refs[len(degrees) :]
    new_ref, energy_ref, src_ref, flow_ref, fmid_ref, fhigh_ref, gs_ref = refs[:7]
    table, sems, wm, wmt, wo, wot, nf_s, mx_s, acc_s, dot_c, en_s, fgh_s = refs[7:19]
    grads = dict(zip(degrees, refs[19:]))
    copies = fetch((p0, p1, p2, p3, p4), slice(0, GROUP_COLS[group]), table, sems)
    atoms = own_ref.shape[0]
    spacing = spacing_of(atoms, rbft_ref.shape[1])
    block_diagonal(KINDS[group], mix_ref, wm, wmt)
    block_diagonal(KINDS[group], out_ref, wo, wot)
    en_s[...] = en_0[...] + en_a[...]
    at = 0
    for part in (new_0, new_a):
        new_ref[:, at : at + part.shape[1]] = part[...]
        at += part.shape[1]
    steps = step_count(meta_ref)

    for copy in copies:
        copy.wait()
    ghost_pairs(
        group, own_ref, table, new_ref, 0, oh_gh, d_gh, dt_gh, gate_gh, radials, nw_ref,
        steps, wm, wmt, wo, wot, nf_s, mx_s, acc_own, acc_s, gs_ref, dot_c, grads, en_s,
    )
    energy_ref[...] = jnp.sum(en_s[...].T, axis=0, keepdims=True)

    fgh_s[...] = jnp.zeros_like(fgh_s)
    src_ref[...] = jnp.zeros_like(src_ref)
    gs0_low = gs0_ref[...].astype(BF16)
    mix_t = flip(mix_ref[0])

    def ghost_finish(step):
        here, _ = ghost_rows(step)
        grad = mm(d_gh[here, :], gs0_low)
        pull, top, rest = finish(
            grad, m0_ref[here, :], nf0_ref[here, :], sum_of((dot_a, dot_c), here),
            degree_parts(gr_a + refs[19:], here), pre_gh[here, :], unit_gh[here, :], spacing,
            radt_ref, rbft_ref, mix_t,
        )
        pull_top = pull.astype(BF16)
        pull_rest = (pull - pull_top.astype(F32)).astype(BF16)
        spread = dt_gh[:, here]
        src_ref[...] += mm(spread, pull_top) + mm(spread, pull_rest)
        onehot = oh_gh[here, :]
        fgh_s[...] += mm(top, onehot) + mm(rest, onehot)

    over_ghost_steps(steps, ghost_finish)
    low, mid = flow_ref.shape[1], fmid_ref.shape[1]
    flow_ref[...] = fgh_s[:, 0:low]
    fmid_ref[...] = fgh_s[:, low : low + mid]
    fhigh_ref[...] = fgh_s[:, low + mid :]


def third_stage(pieces, feats, *rest):
    atoms, feat = feats.shape
    half = atoms * HALF
    ghosts = sum(piece.shape[0] for piece in pieces)
    sizes = (ghosts // 4, ghosts // 2, ghosts // 4)
    out_shape = (
        struct(atoms, feat, dtype=BF16),
        struct(1, atoms),
        struct(atoms, CH),
    ) + tuple(struct(8, size) for size in sizes) + (
        struct(atoms, GROUP_COLS[1], dtype=BF16),
    )
    scratch = pair_scratch(atoms, half, ghosts, 1) + [
        pltpu.VMEM((half, CH), BF16),
        pltpu.VMEM((atoms, CH), F32),
        pltpu.VMEM((8, ghosts), F32),
    ]
    scratch += [pltpu.VMEM((half, CH), BF16)] * len(DEGREES[1])
    args = tuple(pieces) + (feats,) + rest
    return call(
        third_kernel, "third_group", out_shape, scratch, args,
        any_specs(len(pieces), len(args)), 28,
    )


def own_back_kernel(
    oh_own, pre_own, unit_own, radt_ref, rbft_ref, mix_ref, gs0_ref, src_ref,
    m0_ref, nf0_ref, dot_a, dot_c, *refs
):
    gr_own, (force_ref,) = refs[:PARTIALS], refs[PARTIALS:]
    atoms = oh_own.shape[1]
    spacing = spacing_of(atoms, rbft_ref.shape[1])
    grad = tiled(gs0_ref[...])
    mix_t = flip(mix_ref[0])
    src = src_ref[...]
    onto = jnp.zeros((8, atoms), F32)
    for step in range(OWN_STEPS):
        rows = own_rows(step)
        pull, top, rest = finish(
            grad, m0_ref[rows, :], nf0_ref[rows, :], sum_of((dot_a, dot_c), rows),
            degree_parts(gr_own, rows), pre_own[rows, :], unit_own[rows, :], spacing, radt_ref,
            rbft_ref, mix_t,
        )
        src += jnp.sum(pull.reshape(STEP // atoms, atoms, CH), axis=0)
        onehot = oh_own[rows, :]
        onto += mm(top, onehot) + mm(rest, onehot)
    force_ref[...] = onto - src.T[0:8, :]


def own_back_stage(*args):
    oh_own = args[0]
    out_shape = (struct(8, oh_own.shape[1]),)
    return call(own_back_kernel, "own_back", out_shape, [], args)[0]


def ring(axis):
    peers = lax.axis_size(axis)
    up = [(i, (i + 1) % peers) for i in range(peers)]
    return up, [(j, i) for i, j in up]


def neighbours_of(block, axis, dim):
    up, down = ring(axis)
    length = block.shape[dim]
    if len(up) == 2 and length == 2:
        other = lax.ppermute(block, axis, up)
        return (
            lax.slice_in_dim(other, length - 1, length, axis=dim),
            lax.slice_in_dim(other, 0, 1, axis=dim),
        )
    before = lax.ppermute(lax.slice_in_dim(block, length - 1, length, axis=dim), axis, up)
    after = lax.ppermute(lax.slice_in_dim(block, 0, 1, axis=dim), axis, down)
    return before, after


def grown(block, axis, dim):
    before, after = neighbours_of(block, axis, dim)
    return jnp.concatenate([before, block, after], axis=dim)


def ghost_pieces(along_y, block, along_x):
    outer = jnp.concatenate(along_y, axis=1)
    low_out, high_out = neighbours_of(outer, "gx", 0)
    low_in, high_in = along_x
    middle = jnp.concatenate([along_y[0], block, along_y[1]], axis=1)
    return tuple(flat_rows(piece) for piece in (low_in, low_out, middle, high_in, high_out))


def flat_rows(piece):
    return piece.reshape(-1, piece.shape[-1])


def fold_kernel(mid_ref, low_ref, high_ref, out_ref):
    lanes = mid_ref.shape[1]
    ext_y = iota(mid_ref.shape, 1) // 32 % 4
    out_ref[...] = (
        mid_ref[...]
        + jnp.where(ext_y == 1, pltpu.roll(low_ref[...], lanes - 64, 1), 0.0)
        + jnp.where(ext_y == 2, pltpu.roll(high_ref[...], 64, 1), 0.0)
    )


def forces_kernel(mid_ref, low_ref, high_ref, own_ref, home_ref, out_ref):
    values = mid_ref[...]
    lanes = values.shape[1]
    ext_z = iota(values.shape, 1) // 8 % 4
    values += jnp.where(ext_z == 1, pltpu.roll(low_ref[...], lanes - 16, 1), 0.0)
    values += jnp.where(ext_z == 2, pltpu.roll(high_ref[...], 16, 1), 0.0)
    first = values.astype(BF16)
    values -= first.astype(F32)
    second = values.astype(BF16)
    third = (values - second.astype(F32)).astype(BF16)
    home = home_ref[...]
    total = own_ref[...] + (mm_nt(first, home) + (mm_nt(second, home) + mm_nt(third, home)))
    for comp in range(3):
        out_ref[comp] = -total[comp : comp + 1, :]


def give_back_x(low, mid, high):
    up, down = ring("gx")
    from_low = lax.ppermute(high, "gx", up)
    from_high = lax.ppermute(low, "gx", down)
    return mid, jnp.concatenate([from_low, from_high], axis=1)


def give_back_y(mid):
    up, down = ring("gy")
    return mid, lax.ppermute(mid, "gy", up), lax.ppermute(mid, "gy", down)


def fold(*args):
    return call(fold_kernel, "fold", (struct(*args[0].shape),), [], args)[0]


def give_back_z(mid):
    up, down = ring("gz")
    from_low = lax.ppermute(mid, "gz", up)
    return mid, from_low, from_low if len(up) == 2 else lax.ppermute(mid, "gz", down)


def local(
    features,
    positions,
    neighbours,
    counts,
    cell_atoms,
    rbf_weight,
    radial_weight,
    mix_weight,
    out_weight,
    energy_weight,
    norm_weight,
):
    feats = features[0, 0, 0]
    places = jnp.swapaxes(positions[0, 0], 0, 1)
    cells0, cells1, own_pos, meta = make_cells(
        feats, places, neighbours[0, 0, 0].T, counts[0, 0], cell_atoms[0, 0]
    )
    hold = lax.optimization_barrier
    block0, block1 = (part.reshape(2, 2, 2, 8, part.shape[1]) for part in (cells0, cells1))
    block0 = grown(block0, "gz", 2)
    block0, own_pos, meta = hold((block0, own_pos, meta))
    y0 = neighbours_of(block0, "gy", 1)
    x0_in = neighbours_of(block0, "gx", 0)
    oh_own, pre_own, unit_own, radt, rbft, home, *radial_own = own_stage(
        meta, own_pos, rbf_weight, radial_weight
    )
    block1 = grown(block1, "gz", 2)
    y1 = neighbours_of(block1, "gy", 1)
    y0, x0_in, block1, oh_own = hold((y0, x0_in, block1, oh_own))
    pieces0 = ghost_pieces(y0, block0, x0_in)
    x1_in = neighbours_of(block1, "gx", 0)
    (m0_own, gate_own, nf0_own, acc0), (own_a,) = own_forward_stage(
        (0,), feats, mix_weight, oh_own, radial_own
    )
    (
        new_0, oh_gh, d_gh, dt_gh, pre_gh, unit_gh, gs0, en_0, m0_gh, gate_gh, nf0_gh, *radial_gh,
    ) = start_stage(
        pieces0, feats, own_pos, meta, rbf_weight, radial_weight, mix_weight, out_weight,
        energy_weight[None], acc0,
    )
    y1, gate_gh = hold((y1, gate_gh))
    pieces1 = ghost_pieces(y1, block1, x1_in)
    shared = (feats, meta, mix_weight, out_weight, norm_weight, oh_gh, d_gh, dt_gh, gate_gh)
    new_a, en_a, _, (dot_gh_a, *gr_gh_a), (dot_own_a, *gr_own_a) = pairs_stage(
        0, 2 * CH, pieces0, shared, (gate_own, *own_a), radial_gh
    )
    en_a, gate_own = hold((en_a, gate_own))
    _, (own_b,) = own_forward_stage((1,), feats, mix_weight, oh_own, radial_own, gate_own)
    new, energy, src, low, mid, high, gs_b = third_stage(
        pieces1, *shared, own_b[2], radt, rbft, gs0, en_0, en_a, new_0, new_a, pre_gh,
        unit_gh, m0_gh, nf0_gh, dot_gh_a, *gr_gh_a,
        *[radial_gh[degree - 1] for degree in DEGREES[1]],
    )
    mid, arrived = give_back_x(low, mid, high)
    dot_own_b, *gr_own_b = own_backward_stage(1, mix_weight, gs_b, gate_own, *own_b[:2])
    arrived, gs0, dot_own_b = hold((arrived, gs0, dot_own_b))
    mid, from_low, from_high = give_back_y(mid + arrived)
    own = own_back_stage(
        oh_own, pre_own, unit_own, radt, rbft, mix_weight, gs0, src, m0_own, nf0_own, dot_own_a,
        dot_own_b, *gr_own_a, *gr_own_b,
    )
    from_low, from_high, own = hold((from_low, from_high, own))
    folded = give_back_z(fold(mid, from_low, from_high))
    args = (*folded, own, home)
    out_shape = (struct(3, 1, own.shape[1]),)
    forces = call(forces_kernel, "forces", out_shape, [], args)[0]
    return (
        new[None, None, None],
        energy[None, None],
        jnp.swapaxes(forces, 0, 1)[None, None],
    )


def solution(mesh):
    split = P("gx", "gy", "gz", None, None)
    flat = P("gx", "gy", "gz", None)
    return jax.shard_map(
        local,
        mesh=mesh,
        in_specs=(split, split, split, flat, flat, P(), P(), P(), P(), P(), P()),
        out_specs=(split, flat, split),
        check_vma=False,
    )
```

```python
import functools
import math

import jax
import jax.numpy as jnp
from jax import lax
from jax.experimental import pallas as pl
from jax.experimental.pallas import tpu as pltpu
from jax.sharding import PartitionSpec as P

F32 = jnp.float32
BF16 = jnp.bfloat16
CH = 128
SLOTS = 32
HALF = 16
STEP = 256
OWN_STEPS = 4
GH_STEPS = 2
MIB = 1024 * 1024
SPACE = pltpu.VMEM
PAIR_DEGREES = (
    (1, 1), (1, 2), (2, 2), (2, 2),
    (3, 3), (3, 3), (3, 3), (3, 4),
    (4, 4), (4, 4), (4, 4), (4, 4),
)
GROUPS = ((0, 4), (4, 12))
KINDS = tuple(sorted({PAIR_DEGREES[pair] for pair in range(*group)}) for group in GROUPS)
DEGREES = tuple(sorted({d for both in kinds for d in both}) for kinds in KINDS)
GROUP_COLS = tuple(2 * CH * (end - begin) for begin, end in GROUPS)


def mm(a, b):
    return jnp.dot(a, b, preferred_element_type=F32)


def mm_nt(a, b):
    return lax.dot_general(a, b, (((1,), (1,)), ((), ())), preferred_element_type=F32)


def iota(shape, dim):
    return lax.broadcasted_iota(jnp.int32, shape, dim)


def flip(w):
    return w.astype(F32).T.astype(BF16)


def pair_cols(pair):
    return slice(CH + pair * 2 * CH, CH + (pair + 1) * 2 * CH)


def struct(*shape, dtype=F32):
    return jax.ShapeDtypeStruct(shape, dtype)


def call(kernel, name, out_shape, scratch, args, specs=None, limit=16):
    return pl.pallas_call(
        kernel,
        out_shape=out_shape,
        in_specs=specs or [pl.BlockSpec(memory_space=SPACE)] * len(args),
        out_specs=tuple(pl.BlockSpec(memory_space=SPACE) for _ in out_shape),
        scratch_shapes=scratch,
        compiler_params=pltpu.CompilerParams(vmem_limit_bytes=limit * MIB),
        cost_estimate=pl.CostEstimate(flops=1024, bytes_accessed=1024, transcendentals=0),
        name=name,
    )(*args)


def cells_kernel(
    feat_ref, pos_ref, lists_ref,
    first_ref, own_pos_ref, meta_ref, pick_ref, rows_ref, pos_rows,
):
    rows_ref[...] = jnp.zeros_like(rows_ref)
    pos_rows[...] = jnp.zeros_like(pos_rows)
    atoms = feat_ref.shape[0]
    rows_ref[0 : SLOTS + 2, :] = lists_ref[...].astype(F32)
    meta = rows_ref[...].T
    meta_ref[...] = meta
    for comp in range(3):
        places = pos_ref[comp]
        first = places.astype(BF16).astype(F32)
        second = (places - first).astype(BF16).astype(F32)
        pos_rows[comp : comp + 1, :] = first
        pos_rows[4 + comp : 5 + comp, :] = second
        pos_rows[8 + comp : 9 + comp, :] = places - first - second
    pieces = pos_rows[...].astype(BF16)
    lane = iota((atoms, atoms), 1).astype(F32)
    pick = (meta[:, SLOTS + 1 : SLOTS + 2] == lane).astype(F32).astype(BF16)
    same = (iota((atoms, atoms), 0) == iota((atoms, atoms), 1)).astype(F32).astype(BF16)
    own_pos_ref[...] = mm_nt(same, pieces).astype(BF16)
    first_ref[:, CH : 2 * CH] = mm_nt(pick, pieces).astype(BF16)
    pick_ref[...] = pick
    first_ref[:, 0:CH] = mm(pick, feat_ref[:, 0:CH]).astype(BF16)
    cut = pair_cols(GROUPS[1][0]).start
    first_ref[:, 2 * CH :] = mm(pick, feat_ref[:, CH:cut]).astype(BF16)


def rest_kernel(feat_ref, pick_ref, rest_ref):
    cut = pair_cols(GROUPS[1][0]).start
    rest_ref[...] = mm(pick_ref[...], feat_ref[:, cut:]).astype(BF16)


def make_cells(feats, places, lists):
    atoms = feats.shape[0]
    out_shape = (
        struct(atoms, 2 * CH + GROUP_COLS[0], dtype=BF16),
        struct(atoms, CH, dtype=BF16),
        struct(atoms, CH),
        struct(atoms, atoms, dtype=BF16),
    )
    args = (feats, places, lists)
    scratch = [pltpu.VMEM((CH, atoms), F32), pltpu.VMEM((CH, atoms), F32)]
    first, own_pos, meta, pick = call(cells_kernel, "cells", out_shape, scratch, args)
    out_shape = (struct(atoms, sum(GROUP_COLS[1:]), dtype=BF16),)
    rest = call(rest_kernel, "cells_rest", out_shape, [], (feats, pick))[0]
    return first, rest, own_pos, meta


def spacing_of(atoms, nbasis):
    depth = atoms // 16
    return 2.0 * math.sqrt(32.0 + depth * depth) / (nbasis - 1)


def own_onehots(meta_ref, oh_own):
    atoms = meta_ref.shape[0]
    counts = meta_ref[:, SLOTS : SLOTS + 1]
    lane_atom = iota((atoms, atoms), 1).astype(F32)
    for slot in range(HALF):
        hit = jnp.logical_and(meta_ref[:, slot : slot + 1] == lane_atom, counts > slot)
        oh_own[slot * atoms : (slot + 1) * atoms, :] = hit.astype(F32).astype(BF16)


def geometry(near, here):
    diff = near - here
    rel = (diff + pltpu.roll(diff, CH - 4, 1)) + (
        pltpu.roll(diff, CH - 8, 1) + pltpu.roll(diff, CH - 12, 1)
    )
    lane = iota(rel.shape, 1)
    rel = jnp.where(lane < 3, rel, 0.0)
    square = jnp.sum(rel * rel, axis=1, keepdims=True)
    inverse = lax.rsqrt(jnp.where(square > 0.0, square, 1.0))
    dist = square * inverse
    return jnp.where(lane == 3, dist, rel * inverse), dist


def centred_of(dist, spacing, nbasis):
    return dist * (1.0 / spacing) - iota((dist.shape[0], nbasis), 1).astype(F32)


def radial_net(dist, spacing, nets_ref):
    nbasis = nets_ref.shape[0] - 5 * CH
    centred = centred_of(dist, spacing, nbasis)
    basis = jnp.exp(-0.5 * centred * centred)
    pre = mm(basis.astype(BF16), nets_ref[0:nbasis, :])
    hidden = (pre * jax.nn.sigmoid(pre)).astype(BF16)
    weight = [nets_ref[nbasis + d * CH : nbasis + (d + 1) * CH, :] for d in range(5)]
    return pre, mm(hidden, jnp.concatenate(weight, axis=1)).astype(BF16)


def tiled(values, size=STEP):
    return jnp.concatenate([values] * (size // values.shape[0]), axis=0)


def live_ghosts(meta_ref):
    return jnp.maximum(meta_ref[:, SLOTS : SLOTS + 1] - HALF, 0.0)


def step_count(meta_ref):
    total = jnp.sum(live_ghosts(meta_ref)).astype(jnp.int32)
    rows = GH_STEPS * STEP
    return jnp.maximum((total + (rows - 1)) // rows, 1) * GH_STEPS


def own_rows(step, size=STEP):
    return pl.ds(step * size, size)


def ghost_rows(step, size=STEP):
    first = OWN_STEPS * STEP
    if isinstance(step, int):
        return pl.ds(step * size, size), pl.ds(first + step * size, size)
    base = pl.multiple_of(step * size, size)
    return pl.ds(base, size), pl.ds(pl.multiple_of(first + base, size), size)


def over_ghost_steps(steps, body, size=STEP):
    static = GH_STEPS * STEP // size
    for step in range(static):
        body(step)

    def again(step, carry):
        body(step)
        return carry

    lax.fori_loop(static, (steps * STEP + (size - 1)) // size, again, 0)


def block_diagonal(kinds, source, straight=None, across=None):
    zero = jnp.zeros((CH, CH), BF16)
    targets = [ref for ref in (straight, across) if ref is not None]
    for kind, both in enumerate(kinds):
        for ref in targets:
            ref[kind, 0:CH, CH:] = zero
            ref[kind, CH:, 0:CH] = zero
    for degree in sorted({d for both in kinds for d in both}):
        weight = source[degree]
        flipped = flip(weight) if across is not None else None
        for kind, both in enumerate(kinds):
            for side in range(2):
                if both[side] == degree:
                    part = slice(side * CH, side * CH + CH)
                    if straight is not None:
                        straight[kind, part, part] = weight
                    if across is not None:
                        across[kind, part, part] = flipped


def fetch(pieces, cols, table, sems):
    low, high, ghosts = 0, 0, table.shape[0]
    if len(pieces) == 3:
        rows = [(piece, 0, piece.shape[0]) for piece in pieces]
    else:
        low_in, low_out, mid, high_in, high_out = pieces
        half = low_out.shape[0] // 2
        rows = [(low_out, 0, half), (low_in, 0, low_in.shape[0]), (low_out, half, half)]
        rows += [(mid, 0, mid.shape[0])]
        rows += [(high_out, 0, half), (high_in, 0, high_in.shape[0]), (high_out, half, half)]
    copies = []
    at = 0
    for index, (piece, start, count) in enumerate(rows):
        source = piece.at[pl.ds(start, count), cols]
        target = table.at[pl.ds(at, count), :]
        copies.append(pltpu.make_async_copy(source, target, sems.at[index]))
        at += count
    for copy in copies:
        copy.start()
    return copies


def infos_of(group):
    infos = []
    for index, pair in enumerate(range(*GROUPS[group])):
        degrees = PAIR_DEGREES[pair]
        cols = slice(index * 2 * CH, (index + 1) * 2 * CH)
        infos.append((cols, degrees, KINDS[group].index(degrees)))
    return infos


def group_cols(group):
    begin, end = GROUPS[group]
    return slice(pair_cols(begin).start, pair_cols(end - 1).stop)


def twice(values):
    return jnp.concatenate([values, values], axis=1)


def forward(group, rows, onehot, feats, radials, gate_ref, wm, nf_ref, mx_ref, slots):
    near = mm(onehot, feats).astype(BF16)
    nf_ref[rows, :] = near
    gate = twice(gate_ref[rows, :])
    wide = gate.astype(F32) if slots else None
    messages = []
    for cols, degrees, kind in infos_of(group):
        radial = jnp.concatenate([radials[d][rows, :] for d in degrees], axis=1)
        mixed = mm(near[:, cols] * radial, wm[kind])
        low = mixed.astype(BF16)
        mx_ref[rows, cols] = low
        messages.append(mixed * wide if slots else low * gate)
    return messages


def backward(group, rows, grad, gate_ref, wmt, nf_ref, mx_ref, dot_ref, grad_refs):
    parts = {}
    dots = None
    gate = twice(gate_ref[rows, :])
    for cols, degrees, kind in infos_of(group):
        product = grad[:, cols] * mx_ref[rows, cols]
        dot = (product[:, 0:CH] + product[:, CH:]).astype(F32)
        dots = dot if dots is None else dots + dot
        weighted = mm(grad[:, cols] * gate, wmt[kind]) * nf_ref[rows, cols].astype(F32)
        for side in range(2):
            part = weighted[:, side * CH : (side + 1) * CH]
            degree = degrees[side]
            parts[degree] = parts[degree] + part if degree in parts else part
    dot_ref[rows, :] = dots.astype(dot_ref.dtype)
    for degree, part in parts.items():
        grad_refs[degree][rows, :] = part.astype(grad_refs[degree].dtype)


def over_slots(values, atoms):
    return jnp.sum(values.reshape(-1, atoms, values.shape[1]), axis=0)


def own_forward(group, own_ref, oh_own, radials, gate_ref, wm, nf_ref, mx_ref, acc_ref):
    atoms = own_ref.shape[0]
    feats = own_ref[:, group_cols(group)]
    for step in range(OWN_STEPS):
        rows = own_rows(step)
        messages = forward(
            group, rows, oh_own[rows, :], feats, radials, gate_ref, wm, nf_ref, mx_ref, True
        )
        for (cols, _, _), message in zip(infos_of(group), messages):
            part = over_slots(message, atoms)
            acc_ref[:, cols] = part if step == 0 else acc_ref[:, cols] + part


def own_backward(group, gs_ref, gate_ref, wmt, nf_ref, mx_ref, dot_ref, grad_refs):
    grad = tiled(gs_ref[...])
    for step in range(OWN_STEPS):
        backward(
            group, own_rows(step), grad, gate_ref, wmt, nf_ref, mx_ref, dot_ref, grad_refs
        )


def ghost_pairs(
    group, own_ref, table, new_ref, new_base, oh_gh, d_gh, dt_gh, gate_ref, radials, nw_ref,
    steps, wm, wmt, wo, wot, nf_s, mx_s, acc_in, acc_s, gs_ref, dot_ref, grad_refs, en_ref,
):
    norm = 1.0 / math.sqrt(SLOTS)
    acc_s[...] = acc_in[...]

    def ghost_forward(step):
        here, _ = ghost_rows(step)
        messages = forward(
            group, here, oh_gh[here, :], table[...], radials, gate_ref, wm, nf_s, mx_s, False
        )
        acc_s[...] += mm(dt_gh[:, here], jnp.concatenate(messages, axis=1))

    over_ghost_steps(steps, ghost_forward)

    begin = group_cols(group).start
    for cols, degrees, kind in infos_of(group):
        summed_low = (acc_s[:, cols] * norm).astype(BF16)
        own = own_ref[:, begin + cols.start : begin + cols.stop]
        updated = own.astype(F32) + mm(summed_low, wo[kind])
        at = begin - new_base + cols.start
        new_ref[:, at : at + 2 * CH] = updated.astype(BF16)
        weight = jnp.concatenate(
            [nw_ref[d - 1 : d, :] * (1.0 / (2 * d + 1)) for d in degrees], axis=1
        )
        scale = weight * updated
        energy = scale * updated
        en_ref[...] += energy[:, 0:CH] + energy[:, CH:]
        gs_ref[:, cols] = (mm((2.0 * scale).astype(BF16), wot[kind]) * norm).astype(BF16)

    def ghost_backward(step):
        here, _ = ghost_rows(step)
        grad = mm(d_gh[here, :], gs_ref[...]).astype(BF16)
        backward(group, here, grad, gate_ref, wmt, nf_s, mx_s, dot_ref, grad_refs)

    over_ghost_steps(steps, ghost_backward)


def pair_scratch(atoms, half, ghosts, group):
    count, width = len(KINDS[group]), GROUP_COLS[group]
    return (
        [pltpu.VMEM((ghosts, width), BF16), pltpu.SemaphoreType.DMA((7,))]
        + [pltpu.VMEM((count, 2 * CH, 2 * CH), BF16) for _ in range(4)]
        + [
            pltpu.VMEM((half, width), BF16),
            pltpu.VMEM((half, width), BF16),
            pltpu.VMEM((atoms, width), F32),
        ]
    )


def own_kernel(
    meta_ref, own_pos_ref, nets_ref,
    oh_own, pre_ref, unit_ref, radt_ref, rbft_ref, home_ref, *radial_refs
):
    atoms = meta_ref.shape[0]
    nbasis = rbft_ref.shape[1]
    spacing = spacing_of(atoms, nbasis)
    own_onehots(meta_ref, oh_own)
    here = tiled(own_pos_ref[...].astype(F32))
    for step in range(OWN_STEPS):
        rows = own_rows(step)
        unit, dist = geometry(mm(oh_own[rows, :], own_pos_ref[...]), here)
        unit_ref[rows, :] = unit
        pre, radial = radial_net(dist, spacing, nets_ref)
        pre_ref[rows, :] = pre.astype(BF16)
        for degree, ref in enumerate(radial_refs):
            ref[rows, :] = radial[:, degree * CH : (degree + 1) * CH]
    for degree in range(5):
        part = slice(degree * CH, (degree + 1) * CH)
        radt_ref[part, :] = flip(nets_ref[nbasis + part.start : nbasis + part.stop, :])
    for index in range(nbasis // CH):
        part = slice(index * CH, (index + 1) * CH)
        rbft_ref[:, part] = flip(nets_ref[part, :])
    lanes = home_ref.shape[1]
    lane = iota((atoms, lanes), 1)
    ext_x, ext_y, ext_z = lane // 128, lane // 32 % 4, lane // 8 % 4
    slot = ((2 * ext_x + ext_y - 1) * 2 + ext_z - 1) * 8 + lane % 8
    inside = jnp.logical_and(
        jnp.logical_or(ext_y == 1, ext_y == 2), jnp.logical_or(ext_z == 1, ext_z == 2)
    )
    to_slot = jnp.logical_and(iota((atoms, lanes), 0) == slot, inside)
    to_slot = to_slot.astype(F32).astype(BF16)
    order = meta_ref[:, SLOTS + 1 : SLOTS + 2]
    to_atom = (order == iota((atoms, atoms), 1).astype(F32)).astype(F32)
    home_ref[...] = mm(to_atom.T.astype(BF16), to_slot).astype(BF16)


def own_stage(meta, own_pos, nets):
    atoms = meta.shape[0]
    edges = atoms * HALF
    out_shape = (
        struct(edges, atoms, dtype=BF16),
        struct(edges, CH, dtype=BF16),
        struct(edges, CH),
        struct(5 * CH, CH, dtype=BF16),
        struct(CH, nets.shape[0] - 5 * CH, dtype=BF16),
        struct(atoms, 256, dtype=BF16),
    ) + (struct(edges, CH, dtype=BF16),) * 5
    return call(own_kernel, "own_edges", out_shape, [], (meta, own_pos, nets))


def scalar_forward(rows, near, radial, mix_ref, m0_ref, gate_ref, nf0_ref):
    near = near.astype(BF16)
    nf0_ref[rows, :] = near
    mixed = mm(near * radial, mix_ref[0])
    m0_ref[rows, :] = mixed.astype(BF16)
    gate = jax.nn.sigmoid(mixed)
    gate_ref[rows, :] = gate.astype(BF16)
    return mixed * gate


def own_forward_kernel(groups, scalar, *refs):
    own_ref, mix_ref, oh_own, refs = *refs[:3], refs[3:]
    radial0, radials = refs[0], dict(enumerate(refs[1:5], start=1))
    refs = refs[5:]
    if scalar:
        m0_ref, gate_ref, nf0_ref, acc0_ref = refs[:4]
        refs = refs[4:]
        atoms = own_ref.shape[0]
        feats = own_ref[:, 0:CH]
        summed = None
        for step in range(OWN_STEPS):
            rows = own_rows(step)
            message = scalar_forward(
                rows, mm(oh_own[rows, :], feats), radial0[rows, :], mix_ref, m0_ref, gate_ref,
                nf0_ref,
            )
            part = over_slots(message, atoms)
            summed = part if summed is None else summed + part
        acc0_ref[...] = summed
    else:
        gate_ref, refs = refs[0], refs[1:]
    outs, weights = refs[: 3 * len(groups)], refs[3 * len(groups) :]
    for index, group in enumerate(groups):
        block_diagonal(KINDS[group], mix_ref, weights[index])
        nf_ref, mx_ref, acc_ref = outs[3 * index : 3 * index + 3]
        own_forward(
            group, own_ref, oh_own, radials, gate_ref, weights[index], nf_ref, mx_ref, acc_ref
        )


def own_forward_stage(groups, feats, mix, oh_own, radial_own, gate=None):
    atoms = feats.shape[0]
    half = atoms * HALF
    out_shape = ()
    if gate is None:
        out_shape += (struct(half, CH, dtype=BF16),) * 3 + (struct(atoms, CH),)
    for group in groups:
        width = GROUP_COLS[group]
        out_shape += (struct(half, width, dtype=BF16),) * 2 + (struct(atoms, width),)
    args = (feats, mix, oh_own, *radial_own) + (() if gate is None else (gate,))
    scratch = [pltpu.VMEM((len(KINDS[group]), 2 * CH, 2 * CH), BF16) for group in groups]
    name = "own_forward_" + "".join("abc"[group] for group in groups)
    kernel = functools.partial(own_forward_kernel, groups, gate is None)
    outs = call(kernel, name, out_shape, scratch, args)
    first = len(outs) - 3 * len(groups)
    return outs[:first], [outs[first + 3 * i : first + 3 * i + 3] for i in range(len(groups))]


def start_kernel(
    p0, p1, p2, own_ref, own_pos_ref, meta_ref, nets_ref, mix_ref, out_ref, ew_ref, acc0_ref,
    new_ref, oh_gh, d_gh, dt_gh, pre_ref, unit_ref, gs0_ref, en_ref, m0_gh, gate_gh, nf0_gh,
    radial_gh1, radial_gh2, radial_gh3, radial_gh4,
    table, sems, ghpos, acc_s,
):
    radial_gh = (None, radial_gh1, radial_gh2, radial_gh3, radial_gh4)
    copies = fetch((p0, p1, p2), slice(0, 2 * CH), table, sems)
    atoms = own_ref.shape[0]
    ghosts = table.shape[0]
    spacing = spacing_of(atoms, nets_ref.shape[0] - 5 * CH)
    norm = 1.0 / math.sqrt(SLOTS)

    live = live_ghosts(meta_ref)
    sub_atom = iota((atoms, atoms), 0)
    lane_atom = iota((atoms, atoms), 1)
    live_b = jnp.broadcast_to(live, (atoms, atoms))
    end_row = jnp.sum(jnp.where(sub_atom <= lane_atom, live_b, 0.0), axis=0, keepdims=True)
    live_row = jnp.sum(jnp.where(sub_atom == lane_atom, live_b, 0.0), axis=0, keepdims=True)
    start_row = end_row - live_row
    row_b = jnp.broadcast_to(live_row, (atoms, atoms))
    end_col = jnp.sum(jnp.where(lane_atom <= sub_atom, row_b, 0.0), axis=1, keepdims=True)
    start_col = end_col - live
    total = jnp.sum(live)
    steps = step_count(meta_ref)
    ghost_row = meta_ref[:, HALF:SLOTS] - atoms
    high_part = jnp.floor(ghost_row * (1.0 / 16.0))
    row_high = high_part.astype(BF16)
    row_low = (ghost_row - 16.0 * high_part).astype(BF16)

    row = iota((ghosts, CH), 0)
    lane = iota((ghosts, CH), 1)
    zcells = atoms // 32
    per_y = (zcells + 2) * 8
    ext_x = row // (4 * per_y)
    ext_y = row // per_y % 4
    ext_z = row // 8 % (zcells + 2)

    def side_of(ext, last, size):
        return jnp.where(ext == 0, -size, jnp.where(ext == last, size, 0.0))

    shift = jnp.where(lane == 12, side_of(ext_x, 3, 4.0), 0.0)
    shift = jnp.where(lane == 13, side_of(ext_y, 3, 4.0), shift)
    shift = jnp.where(lane == 14, side_of(ext_z, zcells + 1, 2.0 * zcells), shift)
    own0 = own_ref[:, 0:CH]
    acc_s[...] = acc0_ref[...]
    for copy in copies:
        copy.wait()
    ghpos[...] = (table[:, CH:].astype(F32) + shift).astype(BF16)

    def ghost_start(step):
        here, _ = ghost_rows(step)
        base = step * STEP
        edge = (iota((STEP, atoms), 0) + base).astype(F32)
        mine = jnp.logical_and(edge >= start_row, edge < end_row).astype(F32)
        source = mine.astype(BF16)
        d_gh[here, :] = source
        edge_t = (iota((atoms, STEP), 1) + base).astype(F32)
        mine_t = jnp.logical_and(edge_t >= start_col, edge_t < end_col)
        spread = mine_t.astype(F32).astype(BF16)
        dt_gh[:, here] = spread
        edge_col = edge[:, 0:1]
        slot = edge_col - jnp.sum(mine * start_row, axis=1, keepdims=True)
        listed = mm(source, row_high) * 16.0 + mm(source, row_low)
        at_slot = iota((STEP, HALF), 1).astype(F32) == slot
        which = jnp.sum(jnp.where(at_slot, listed, 0.0), axis=1, keepdims=True)
        which = jnp.where(edge_col < total, which, -1.0)
        onehot = (iota((STEP, ghosts), 1).astype(F32) == which).astype(F32).astype(BF16)
        oh_gh[here, :] = onehot
        unit, dist = geometry(mm(onehot, ghpos[...]), mm(source, own_pos_ref[...]))
        unit_ref[here, :] = unit
        pre, radial = radial_net(dist, spacing, nets_ref)
        pre_ref[here, :] = pre.astype(BF16)
        for degree in range(1, 5):
            radial_gh[degree][here, :] = radial[:, degree * CH : (degree + 1) * CH]
        message = scalar_forward(
            here, mm(onehot, table[:, 0:CH]), radial[:, 0:CH], mix_ref, m0_gh, gate_gh, nf0_gh
        )
        acc_s[...] += mm(spread, message.astype(BF16))

    over_ghost_steps(steps, ghost_start)

    low0 = (acc_s[...] * norm).astype(BF16)
    updated0 = own0.astype(F32) + mm(low0, out_ref[0])
    new_ref[:, 0:CH] = updated0.astype(BF16)
    logistic = jax.nn.sigmoid(updated0)
    weight0 = ew_ref[...]
    en_ref[...] = weight0 * updated0 * logistic
    grad0 = (weight0 * logistic * (1.0 + updated0 * (1.0 - logistic))).astype(BF16)
    gs0_ref[...] = mm_nt(grad0, out_ref[0]) * norm


def any_specs(count, total):
    return [pl.BlockSpec(memory_space=pl.ANY)] * count + [
        pl.BlockSpec(memory_space=SPACE)
    ] * (total - count)


def start_stage(pieces, feats, *rest):
    atoms = feats.shape[0]
    half = atoms * HALF
    ghosts = sum(piece.shape[0] for piece in pieces)
    out_shape = (
        struct(atoms, CH, dtype=BF16),
        struct(half, ghosts, dtype=BF16),
        struct(half, atoms, dtype=BF16),
        struct(atoms, half, dtype=BF16),
        struct(half, CH, dtype=BF16),
        struct(half, CH),
        struct(atoms, CH),
        struct(atoms, CH),
    ) + (struct(half, CH, dtype=BF16),) * 7
    scratch = [
        pltpu.VMEM((ghosts, 2 * CH), BF16),
        pltpu.SemaphoreType.DMA((7,)),
        pltpu.VMEM((ghosts, CH), BF16),
        pltpu.VMEM((atoms, CH), F32),
    ]
    args = tuple(pieces) + (feats,) + rest
    return call(
        start_kernel, "ghost_start", out_shape, scratch, args,
        any_specs(len(pieces), len(args)), 24,
    )


def pairs_kernel(group, count, skip, *refs):
    pieces, refs = refs[:count], refs[count:]
    own_ref, meta_ref, mix_ref, out_ref, nw_ref, oh_gh, d_gh, dt_gh, gate_gh = refs[:9]
    gate_own, nf_own, mx_own, acc_own = refs[9:13]
    refs = refs[13:]
    degrees = DEGREES[group]
    radials, refs = dict(zip(degrees, refs)), refs[len(degrees) :]
    new_ref, en_ref, gs_ref, dot_gh = refs[:4]
    grads, refs = dict(zip(degrees, refs[4:])), refs[4 + len(degrees) :]
    if group == 0:
        dot_own, refs = refs[0], refs[1:]
        grads_own, refs = dict(zip(degrees, refs)), refs[len(degrees) :]
    table, sems, wm, wmt, wo, wot, nf_s, mx_s, acc_s = refs
    copies = fetch(pieces, slice(skip, skip + GROUP_COLS[group]), table, sems)
    block_diagonal(KINDS[group], mix_ref, wm, wmt)
    block_diagonal(KINDS[group], out_ref, wo, wot)
    en_ref[...] = jnp.zeros_like(en_ref)
    for copy in copies:
        copy.wait()
    ghost_pairs(
        group, own_ref, table, new_ref, group_cols(group).start, oh_gh, d_gh, dt_gh, gate_gh,
        radials, nw_ref, step_count(meta_ref), wm, wmt, wo, wot, nf_s, mx_s, acc_own, acc_s,
        gs_ref, dot_gh, grads, en_ref,
    )
    if group == 0:
        own_backward(group, gs_ref, gate_own, wmt, nf_own, mx_own, dot_own, grads_own)


def pairs_stage(group, skip, pieces, shared, own_parts, radial_gh):
    feats = shared[0]
    atoms = feats.shape[0]
    half = atoms * HALF
    ghosts = sum(piece.shape[0] for piece in pieces)
    degrees = DEGREES[group]
    sides = 2 if group == 0 else 1
    out_shape = (
        struct(atoms, GROUP_COLS[group], dtype=BF16),
        struct(atoms, CH),
        struct(atoms, GROUP_COLS[group], dtype=BF16),
    ) + (struct(half, CH, dtype=BF16),) * (sides * (1 + len(degrees)))
    args = tuple(pieces) + tuple(shared) + tuple(own_parts)
    args += tuple(radial_gh[degree - 1] for degree in degrees)
    new, energy, gs, *rest = call(
        functools.partial(pairs_kernel, group, len(pieces), skip), "pairs_" + "abc"[group],
        out_shape, pair_scratch(atoms, half, ghosts, group), args,
        any_specs(len(pieces), len(args)), 24,
    )
    return new, energy, gs, rest[: 1 + len(degrees)], rest[1 + len(degrees) :]


def own_backward_kernel(group, mix_ref, gs_ref, gate_ref, nf_ref, mx_ref, *refs):
    dot_ref, grads, wmt = refs[0], dict(zip(DEGREES[group], refs[1:-1])), refs[-1]
    block_diagonal(KINDS[group], mix_ref, None, wmt)
    own_backward(group, gs_ref, gate_ref, wmt, nf_ref, mx_ref, dot_ref, grads)


def own_backward_stage(group, mix, gs, gate, nf, mx):
    half = nf.shape[0]
    out_shape = (struct(half, CH, dtype=BF16),) * (1 + len(DEGREES[group]))
    scratch = [pltpu.VMEM((len(KINDS[group]), 2 * CH, 2 * CH), BF16)]
    kernel = functools.partial(own_backward_kernel, group)
    name = "own_backward_" + "abc"[group]
    return call(kernel, name, out_shape, scratch, (mix, gs, gate, nf, mx))


def finish(
    grad, mixed, near, dots, parts, pre, unit, spacing, radt_ref, rbft_ref, mix_t
):
    mixed = mixed.astype(F32)
    gate = jax.nn.sigmoid(mixed)
    first = grad * gate * (1.0 + mixed * (1.0 - gate)) + dots * gate * (1.0 - gate)
    weighted = mm(first.astype(BF16), mix_t) * near.astype(F32)
    radial_grad = jnp.concatenate([weighted.astype(BF16)] + parts, axis=1)
    hidden_grad = mm(radial_grad, radt_ref[...])
    pre = pre.astype(F32)
    logistic = jax.nn.sigmoid(pre)
    pre_grad = (hidden_grad * logistic * (1.0 + pre * (1.0 - logistic))).astype(BF16)
    centred = centred_of(unit[:, 3:4], spacing, rbft_ref.shape[1])
    slope = jnp.exp(-0.5 * centred * centred) * centred
    basis_grad = mm(pre_grad, rbft_ref[...])
    dist_grad = jnp.sum(basis_grad * slope, axis=1, keepdims=True) * (-1.0 / spacing)
    pull = unit * dist_grad
    across = pull.T[0:8, :]
    top = across.astype(BF16)
    rest = (across - top.astype(F32)).astype(BF16)
    return pull, top, rest


def sum_of(refs, rows):
    total = refs[0][rows, :].astype(F32)
    for ref in refs[1:]:
        total += ref[rows, :].astype(F32)
    return total


def degree_parts(refs, rows):
    by_degree = {}
    refs = list(refs)
    for degrees in DEGREES:
        for degree in degrees:
            by_degree.setdefault(degree, []).append(refs.pop(0))
    return [sum_of(by_degree[degree], rows).astype(BF16) for degree in range(1, 5)]


PARTIALS = sum(len(degrees) for degrees in DEGREES)


def third_kernel(
    p0, p1, p2, p3, p4, own_ref, meta_ref, mix_ref, out_ref, nw_ref, oh_gh, d_gh, dt_gh, gate_gh,
    acc_own, radt_ref, rbft_ref, gs0_ref, en_0, en_a, new_0, new_a, pre_gh, unit_gh,
    m0_ref, nf0_ref, dot_a, *refs
):
    group = 1
    before, degrees = len(DEGREES[0]), DEGREES[group]
    gr_a, refs = refs[:before], refs[before:]
    radials, refs = dict(zip(degrees, refs)), refs[len(degrees) :]
    new_ref, energy_ref, src_ref, onto_ref, flow_ref, fmid_ref, fhigh_ref, gs_ref = refs[:8]
    table, sems, wm, wmt, wo, wot, nf_s, mx_s, acc_s, dot_c, en_s, fgh_s = refs[8:20]
    grads = dict(zip(degrees, refs[20:]))
    copies = fetch((p0, p1, p2, p3, p4), slice(0, GROUP_COLS[group]), table, sems)
    atoms = own_ref.shape[0]
    spacing = spacing_of(atoms, rbft_ref.shape[1])
    block_diagonal(KINDS[group], mix_ref, wm, wmt)
    block_diagonal(KINDS[group], out_ref, wo, wot)
    en_s[...] = en_0[...] + en_a[...]
    at = 0
    for part in (new_0, new_a):
        new_ref[:, at : at + part.shape[1]] = part[...]
        at += part.shape[1]
    steps = step_count(meta_ref)

    for copy in copies:
        copy.wait()
    ghost_pairs(
        group, own_ref, table, new_ref, 0, oh_gh, d_gh, dt_gh, gate_gh, radials, nw_ref,
        steps, wm, wmt, wo, wot, nf_s, mx_s, acc_own, acc_s, gs_ref, dot_c, grads, en_s,
    )
    energy_ref[...] = jnp.sum(en_s[...].T, axis=0, keepdims=True)

    fgh_s[...] = jnp.zeros_like(fgh_s)
    src_ref[...] = jnp.zeros_like(src_ref)
    onto_ref[...] = jnp.zeros_like(onto_ref)
    gs0_low = gs0_ref[...].astype(BF16)
    mix_t = flip(mix_ref[0])

    def ghost_finish(step):
        here, _ = ghost_rows(step)
        grad = mm(d_gh[here, :], gs0_low)
        pull, top, rest = finish(
            grad, m0_ref[here, :], nf0_ref[here, :], sum_of((dot_a, dot_c), here),
            degree_parts(gr_a + refs[20:], here), pre_gh[here, :], unit_gh[here, :], spacing,
            radt_ref, rbft_ref, mix_t,
        )
        pull_top = pull.astype(BF16)
        pull_rest = (pull - pull_top.astype(F32)).astype(BF16)
        spread = dt_gh[:, here]
        src_ref[...] += mm(spread, pull_top) + mm(spread, pull_rest)
        onehot = oh_gh[here, :]
        fgh_s[...] += mm(top, onehot) + mm(rest, onehot)

    over_ghost_steps(steps, ghost_finish)
    low, mid = flow_ref.shape[1], fmid_ref.shape[1]
    flow_ref[...] = fgh_s[:, 0:low]
    fmid_ref[...] = fgh_s[:, low : low + mid]
    fhigh_ref[...] = fgh_s[:, low + mid :]


def third_stage(pieces, feats, *rest):
    atoms, feat = feats.shape
    half = atoms * HALF
    ghosts = sum(piece.shape[0] for piece in pieces)
    sizes = (ghosts // 4, ghosts // 2, ghosts // 4)
    out_shape = (
        struct(atoms, feat, dtype=BF16),
        struct(1, atoms),
        struct(atoms, CH),
        struct(8, atoms),
    ) + tuple(struct(8, size) for size in sizes) + (
        struct(atoms, GROUP_COLS[1], dtype=BF16),
    )
    scratch = pair_scratch(atoms, half, ghosts, 1) + [
        pltpu.VMEM((half, CH), BF16),
        pltpu.VMEM((atoms, CH), F32),
        pltpu.VMEM((8, ghosts), F32),
    ]
    scratch += [pltpu.VMEM((half, CH), BF16)] * len(DEGREES[1])
    args = tuple(pieces) + (feats,) + rest
    return call(
        third_kernel, "third_group", out_shape, scratch, args,
        any_specs(len(pieces), len(args)), 28,
    )


def own_back_kernel(
    steps, oh_own, pre_own, unit_own, radt_ref, rbft_ref, mix_ref, gs0_ref,
    m0_ref, nf0_ref, dot_a, dot_c, *refs
):
    gr_own, (src_in, onto_in, src_out, onto_out) = refs[:PARTIALS], refs[PARTIALS:]
    atoms = oh_own.shape[1]
    spacing = spacing_of(atoms, rbft_ref.shape[1])
    grad = tiled(gs0_ref[...])
    mix_t = flip(mix_ref[0])
    src = src_in[...]
    onto = onto_in[...]
    for step in steps:
        rows = own_rows(step)
        pull, top, rest = finish(
            grad, m0_ref[rows, :], nf0_ref[rows, :], sum_of((dot_a, dot_c), rows),
            degree_parts(gr_own, rows), pre_own[rows, :], unit_own[rows, :], spacing, radt_ref,
            rbft_ref, mix_t,
        )
        src += over_slots(pull, atoms)
        onehot = oh_own[rows, :]
        onto += mm(top, onehot) + mm(rest, onehot)
    src_out[...] = src
    onto_out[...] = onto


def own_back_stage(steps, *args):
    atoms = args[0].shape[1]
    out_shape = (struct(atoms, CH), struct(8, atoms))
    kernel = functools.partial(own_back_kernel, tuple(steps))
    return call(kernel, "own_back", out_shape, [], args)


def ring(axis):
    peers = lax.axis_size(axis)
    up = [(i, (i + 1) % peers) for i in range(peers)]
    return up, [(j, i) for i, j in up]


def neighbours_of(block, axis, dim):
    up, down = ring(axis)
    length = block.shape[dim]
    if len(up) == 2 and length == 2:
        other = lax.ppermute(block, axis, up)
        return (
            lax.slice_in_dim(other, length - 1, length, axis=dim),
            lax.slice_in_dim(other, 0, 1, axis=dim),
        )
    before = lax.ppermute(lax.slice_in_dim(block, length - 1, length, axis=dim), axis, up)
    after = lax.ppermute(lax.slice_in_dim(block, 0, 1, axis=dim), axis, down)
    return before, after


def grown(block, axis, dim):
    before, after = neighbours_of(block, axis, dim)
    return jnp.concatenate([before, block, after], axis=dim)


def ghost_pieces(along_y, block, along_x):
    outer = jnp.concatenate(along_y, axis=1)
    low_out, high_out = neighbours_of(outer, "gx", 0)
    low_in, high_in = along_x
    middle = jnp.concatenate([along_y[0], block, along_y[1]], axis=1)
    return tuple(flat_rows(piece) for piece in (low_in, low_out, middle, high_in, high_out))


def flat_rows(piece):
    return piece.reshape(-1, piece.shape[-1])


def fold_kernel(mid_ref, low_ref, high_ref, out_ref):
    lanes = mid_ref.shape[1]
    ext_y = iota(mid_ref.shape, 1) // 32 % 4
    out_ref[...] = (
        mid_ref[...]
        + jnp.where(ext_y == 1, pltpu.roll(low_ref[...], lanes - 64, 1), 0.0)
        + jnp.where(ext_y == 2, pltpu.roll(high_ref[...], 64, 1), 0.0)
    )


def forces_kernel(mid_ref, low_ref, high_ref, src_ref, onto_ref, home_ref, out_ref):
    values = mid_ref[...]
    lanes = values.shape[1]
    ext_z = iota(values.shape, 1) // 8 % 4
    values += jnp.where(ext_z == 1, pltpu.roll(low_ref[...], lanes - 16, 1), 0.0)
    values += jnp.where(ext_z == 2, pltpu.roll(high_ref[...], 16, 1), 0.0)
    first = values.astype(BF16)
    values -= first.astype(F32)
    second = values.astype(BF16)
    third = (values - second.astype(F32)).astype(BF16)
    home = home_ref[...]
    total = onto_ref[...] - src_ref[...].T[0:8, :]
    total += (mm_nt(first, home) + (mm_nt(second, home) + mm_nt(third, home)))
    for comp in range(3):
        out_ref[comp] = -total[comp : comp + 1, :]


def give_back_x(low, mid, high):
    up, down = ring("gx")
    from_low = lax.ppermute(high, "gx", up)
    from_high = lax.ppermute(low, "gx", down)
    return mid, jnp.concatenate([from_low, from_high], axis=1)


def give_back_y(mid):
    up, down = ring("gy")
    return mid, lax.ppermute(mid, "gy", up), lax.ppermute(mid, "gy", down)


def fold(*args):
    return call(fold_kernel, "fold", (struct(*args[0].shape),), [], args)[0]


def give_back_z(mid):
    up, down = ring("gz")
    from_low = lax.ppermute(mid, "gz", up)
    return mid, from_low, from_low if len(up) == 2 else lax.ppermute(mid, "gz", down)


def local(
    features,
    positions,
    neighbours,
    counts,
    cell_atoms,
    rbf_weight,
    radial_weight,
    mix_weight,
    out_weight,
    energy_weight,
    norm_weight,
):
    feats = features[0, 0, 0]
    places = jnp.swapaxes(positions[0, 0], 0, 1)
    lists = jnp.concatenate([neighbours[0, 0, 0].T, counts[0, 0], cell_atoms[0, 0]], axis=0)
    cells0, cells1, own_pos, meta = make_cells(feats, places, lists)
    hold = lax.optimization_barrier
    block0, block1 = (part.reshape(2, 2, 2, 8, part.shape[1]) for part in (cells0, cells1))
    block0 = grown(block0, "gz", 2)
    block0, own_pos, meta = hold((block0, own_pos, meta))
    nets = jnp.concatenate(
        [rbf_weight] + [radial_weight[:, d * CH : (d + 1) * CH] for d in range(5)], axis=0
    )
    y0 = neighbours_of(block0, "gy", 1)
    oh_own, pre_own, unit_own, radt, rbft, home, *radial_own = own_stage(
        meta, own_pos, nets
    )
    block1 = grown(block1, "gz", 2)
    y1 = neighbours_of(block1, "gy", 1)
    y0, block1, oh_own = hold((y0, block1, oh_own))
    middle = jnp.concatenate([y0[0], block0, y0[1]], axis=1)
    low, high = neighbours_of(middle, "gx", 0)
    pieces0 = tuple(flat_rows(piece) for piece in (low, middle, high))
    x1_in = neighbours_of(block1, "gx", 0)
    (m0_own, gate_own, nf0_own, acc0), (own_a,) = own_forward_stage(
        (0,), feats, mix_weight, oh_own, radial_own
    )
    (
        new_0, oh_gh, d_gh, dt_gh, pre_gh, unit_gh, gs0, en_0, m0_gh, gate_gh, nf0_gh, *radial_gh,
    ) = start_stage(
        pieces0, feats, own_pos, meta, nets, mix_weight, out_weight, energy_weight[None], acc0,
    )
    y1, gate_gh = hold((y1, gate_gh))
    pieces1 = ghost_pieces(y1, block1, x1_in)
    shared = (feats, meta, mix_weight, out_weight, norm_weight, oh_gh, d_gh, dt_gh, gate_gh)
    new_a, en_a, _, (dot_gh_a, *gr_gh_a), (dot_own_a, *gr_own_a) = pairs_stage(
        0, 2 * CH, pieces0, shared, (gate_own, *own_a), radial_gh
    )
    en_a, gate_own = hold((en_a, gate_own))
    _, (own_b,) = own_forward_stage((1,), feats, mix_weight, oh_own, radial_own, gate_own)
    new, energy, src, onto, low, mid, high, gs_b = third_stage(
        pieces1, *shared, own_b[2], radt, rbft, gs0, en_0, en_a, new_0, new_a, pre_gh,
        unit_gh, m0_gh, nf0_gh, dot_gh_a, *gr_gh_a,
        *[radial_gh[degree - 1] for degree in DEGREES[1]],
    )
    mid, arrived = give_back_x(low, mid, high)
    dot_own_b, *gr_own_b = own_backward_stage(1, mix_weight, gs_b, gate_own, *own_b[:2])
    arrived, gs0, dot_own_b = hold((arrived, gs0, dot_own_b))
    mid, from_low, from_high = give_back_y(mid + arrived)
    back = (oh_own, pre_own, unit_own, radt, rbft, mix_weight, gs0, m0_own, nf0_own)
    back += (dot_own_a, dot_own_b, *gr_own_a, *gr_own_b)
    src, onto = own_back_stage(range(2), *back, src, onto)
    from_low, from_high, src = hold((from_low, from_high, src))
    folded = give_back_z(fold(mid, from_low, from_high))
    src, onto = own_back_stage(range(2, 4), *back, src, onto)
    args = (*folded, src, onto, home)
    out_shape = (struct(3, 1, src.shape[0]),)
    forces = call(forces_kernel, "forces", out_shape, [], args)[0]
    return (
        new[None, None, None],
        energy[None, None],
        jnp.swapaxes(forces, 0, 1)[None, None],
    )


def solution(mesh):
    split = P("gx", "gy", "gz", None, None)
    flat = P("gx", "gy", "gz", None)
    return jax.shard_map(
        local,
        mesh=mesh,
        in_specs=(split, split, split, flat, flat, P(), P(), P(), P(), P(), P()),
        out_specs=(split, flat, split),
        check_vma=False,
    )
```

```python
import functools
import math

import jax
import jax.numpy as jnp
from jax import lax
from jax.experimental import pallas as pl
from jax.experimental.pallas import tpu as pltpu
from jax.sharding import PartitionSpec as P

F32 = jnp.float32
BF16 = jnp.bfloat16
CH = 128
SLOTS = 32
HALF = 16
STEP = 256
OWN_STEPS = 4
GH_STEPS = 2
MIB = 1024 * 1024
SPACE = pltpu.VMEM
PAIR_DEGREES = (
    (1, 1), (1, 2), (2, 2), (2, 2),
    (3, 3), (3, 3), (3, 3), (3, 4),
    (4, 4), (4, 4), (4, 4), (4, 4),
)
GROUPS = ((0, 4), (4, 12))
KINDS = tuple(sorted({PAIR_DEGREES[pair] for pair in range(*group)}) for group in GROUPS)
DEGREES = tuple(sorted({d for both in kinds for d in both}) for kinds in KINDS)
GROUP_COLS = tuple(2 * CH * (end - begin) for begin, end in GROUPS)


def mm(a, b):
    return jnp.dot(a, b, preferred_element_type=F32)


def mm_nt(a, b):
    return lax.dot_general(a, b, (((1,), (1,)), ((), ())), preferred_element_type=F32)


def iota(shape, dim):
    return lax.broadcasted_iota(jnp.int32, shape, dim)


def flip(w):
    return w.astype(F32).T.astype(BF16)


def pair_cols(pair):
    return slice(CH + pair * 2 * CH, CH + (pair + 1) * 2 * CH)


def struct(*shape, dtype=F32):
    return jax.ShapeDtypeStruct(shape, dtype)


def call(kernel, name, out_shape, scratch, args, specs=None, limit=16):
    return pl.pallas_call(
        kernel,
        out_shape=out_shape,
        in_specs=specs or [pl.BlockSpec(memory_space=SPACE)] * len(args),
        out_specs=tuple(pl.BlockSpec(memory_space=SPACE) for _ in out_shape),
        scratch_shapes=scratch,
        compiler_params=pltpu.CompilerParams(vmem_limit_bytes=limit * MIB),
        cost_estimate=pl.CostEstimate(flops=1024, bytes_accessed=1024, transcendentals=0),
        name=name,
    )(*args)


def cells_kernel(
    feat_ref, pos_ref, lists_ref,
    out_ref, own_pos_ref, meta_ref, rows_ref, pos_rows,
):
    rows_ref[...] = jnp.zeros_like(rows_ref)
    pos_rows[...] = jnp.zeros_like(pos_rows)
    atoms = feat_ref.shape[0]
    rows_ref[0 : SLOTS + 2, :] = lists_ref[...].astype(F32)
    meta = rows_ref[...].T
    meta_ref[...] = meta
    for comp in range(3):
        places = pos_ref[comp]
        first = places.astype(BF16).astype(F32)
        second = (places - first).astype(BF16).astype(F32)
        pos_rows[comp : comp + 1, :] = first
        pos_rows[4 + comp : 5 + comp, :] = second
        pos_rows[8 + comp : 9 + comp, :] = places - first - second
    pieces = pos_rows[...].astype(BF16)
    lane = iota((atoms, atoms), 1).astype(F32)
    pick = (meta[:, SLOTS + 1 : SLOTS + 2] == lane).astype(F32).astype(BF16)
    same = (iota((atoms, atoms), 0) == iota((atoms, atoms), 1)).astype(F32).astype(BF16)
    own_pos_ref[...] = mm_nt(same, pieces).astype(BF16)
    out_ref[:, CH : 2 * CH] = mm_nt(pick, pieces).astype(BF16)
    out_ref[:, 0:CH] = mm(pick, feat_ref[:, 0:CH]).astype(BF16)
    out_ref[:, 2 * CH :] = mm(pick, feat_ref[:, CH:]).astype(BF16)


def make_cells(feats, places, lists):
    atoms, feat = feats.shape
    out_shape = (
        struct(atoms, feat + CH, dtype=BF16),
        struct(atoms, CH, dtype=BF16),
        struct(atoms, CH),
    )
    scratch = [pltpu.VMEM((CH, atoms), F32), pltpu.VMEM((CH, atoms), F32)]
    return call(cells_kernel, "cells", out_shape, scratch, (feats, places, lists))


def spacing_of(atoms, nbasis):
    depth = atoms // 16
    return 2.0 * math.sqrt(32.0 + depth * depth) / (nbasis - 1)


def own_onehots(meta_ref, oh_own):
    atoms = meta_ref.shape[0]
    counts = meta_ref[:, SLOTS : SLOTS + 1]
    lane_atom = iota((atoms, atoms), 1).astype(F32)
    for slot in range(HALF):
        hit = jnp.logical_and(meta_ref[:, slot : slot + 1] == lane_atom, counts > slot)
        oh_own[slot * atoms : (slot + 1) * atoms, :] = hit.astype(F32).astype(BF16)


def geometry(near, here):
    diff = near - here
    rel = (diff + pltpu.roll(diff, CH - 4, 1)) + (
        pltpu.roll(diff, CH - 8, 1) + pltpu.roll(diff, CH - 12, 1)
    )
    lane = iota(rel.shape, 1)
    rel = jnp.where(lane < 3, rel, 0.0)
    square = jnp.sum(rel * rel, axis=1, keepdims=True)
    inverse = lax.rsqrt(jnp.where(square > 0.0, square, 1.0))
    dist = square * inverse
    return jnp.where(lane == 3, dist, rel * inverse), dist


def centred_of(dist, spacing, nbasis):
    return dist * (1.0 / spacing) - iota((dist.shape[0], nbasis), 1).astype(F32)


def radial_net(dist, spacing, rbf_ref, rad_ref):
    centred = centred_of(dist, spacing, rbf_ref.shape[0])
    basis = jnp.exp(-0.5 * centred * centred)
    pre = mm(basis.astype(BF16), rbf_ref[...])
    hidden = (pre * jax.nn.sigmoid(pre)).astype(BF16)
    return pre, mm(hidden, rad_ref[...]).astype(BF16)


def tiled(values, size=STEP):
    return jnp.concatenate([values] * (size // values.shape[0]), axis=0)


def live_ghosts(meta_ref):
    return jnp.maximum(meta_ref[:, SLOTS : SLOTS + 1] - HALF, 0.0)


def step_count(meta_ref):
    total = jnp.sum(live_ghosts(meta_ref)).astype(jnp.int32)
    rows = GH_STEPS * STEP
    return jnp.maximum((total + (rows - 1)) // rows, 1) * GH_STEPS


def own_rows(step, size=STEP):
    return pl.ds(step * size, size)


def ghost_rows(step, size=STEP):
    first = OWN_STEPS * STEP
    if isinstance(step, int):
        return pl.ds(step * size, size), pl.ds(first + step * size, size)
    base = pl.multiple_of(step * size, size)
    return pl.ds(base, size), pl.ds(pl.multiple_of(first + base, size), size)


def over_ghost_steps(steps, body, size=STEP):
    static = GH_STEPS * STEP // size
    for step in range(static):
        body(step)

    def again(step, carry):
        body(step)
        return carry

    lax.fori_loop(static, (steps * STEP + (size - 1)) // size, again, 0)


def block_diagonal(kinds, source, straight=None, across=None):
    zero = jnp.zeros((CH, CH), BF16)
    targets = [ref for ref in (straight, across) if ref is not None]
    for kind, both in enumerate(kinds):
        for ref in targets:
            ref[kind, 0:CH, CH:] = zero
            ref[kind, CH:, 0:CH] = zero
    for degree in sorted({d for both in kinds for d in both}):
        weight = source[degree]
        flipped = flip(weight) if across is not None else None
        for kind, both in enumerate(kinds):
            for side in range(2):
                if both[side] == degree:
                    part = slice(side * CH, side * CH + CH)
                    if straight is not None:
                        straight[kind, part, part] = weight
                    if across is not None:
                        across[kind, part, part] = flipped


def fetch(pieces, cols, table, sems):
    low, high, ghosts = 0, 0, table.shape[0]
    if len(pieces) == 3:
        rows = [(piece, 0, piece.shape[0]) for piece in pieces]
    else:
        low_in, low_out, mid, high_in, high_out = pieces
        half = low_out.shape[0] // 2
        rows = [(low_out, 0, half), (low_in, 0, low_in.shape[0]), (low_out, half, half)]
        rows += [(mid, 0, mid.shape[0])]
        rows += [(high_out, 0, half), (high_in, 0, high_in.shape[0]), (high_out, half, half)]
    copies = []
    at = 0
    for index, (piece, start, count) in enumerate(rows):
        source = piece.at[pl.ds(start, count), cols]
        target = table.at[pl.ds(at, count), :]
        copies.append(pltpu.make_async_copy(source, target, sems.at[index]))
        at += count
    for copy in copies:
        copy.start()
    return copies


def infos_of(group):
    infos = []
    for index, pair in enumerate(range(*GROUPS[group])):
        degrees = PAIR_DEGREES[pair]
        cols = slice(index * 2 * CH, (index + 1) * 2 * CH)
        infos.append((cols, degrees, KINDS[group].index(degrees)))
    return infos


def group_cols(group):
    begin, end = GROUPS[group]
    return slice(pair_cols(begin).start, pair_cols(end - 1).stop)


def twice(values):
    return jnp.concatenate([values, values], axis=1)


def forward(group, rows, onehot, feats, radials, gate_ref, wm, nf_ref, mx_ref, slots):
    near = mm(onehot, feats).astype(BF16)
    nf_ref[rows, :] = near
    gate = twice(gate_ref[rows, :])
    wide = gate.astype(F32) if slots else None
    messages = []
    for cols, degrees, kind in infos_of(group):
        radial = jnp.concatenate([radials[d][rows, :] for d in degrees], axis=1)
        mixed = mm(near[:, cols] * radial, wm[kind])
        low = mixed.astype(BF16)
        mx_ref[rows, cols] = low
        messages.append(mixed * wide if slots else low * gate)
    return messages


def backward(group, rows, grad, gate_ref, wmt, nf_ref, mx_ref, dot_ref, grad_refs):
    parts = {}
    dots = None
    gate = twice(gate_ref[rows, :])
    for cols, degrees, kind in infos_of(group):
        product = grad[:, cols] * mx_ref[rows, cols]
        dot = (product[:, 0:CH] + product[:, CH:]).astype(F32)
        dots = dot if dots is None else dots + dot
        weighted = mm(grad[:, cols] * gate, wmt[kind]) * nf_ref[rows, cols].astype(F32)
        for side in range(2):
            part = weighted[:, side * CH : (side + 1) * CH]
            degree = degrees[side]
            parts[degree] = parts[degree] + part if degree in parts else part
    dot_ref[rows, :] = dots.astype(dot_ref.dtype)
    for degree, part in parts.items():
        grad_refs[degree][rows, :] = part.astype(grad_refs[degree].dtype)


def over_slots(values, atoms):
    return jnp.sum(values.reshape(-1, atoms, values.shape[1]), axis=0)


def own_forward(group, own_ref, oh_own, radials, gate_ref, wm, nf_ref, mx_ref, acc_ref):
    atoms = own_ref.shape[0]
    feats = own_ref[:, group_cols(group)]
    for step in range(OWN_STEPS):
        rows = own_rows(step)
        messages = forward(
            group, rows, oh_own[rows, :], feats, radials, gate_ref, wm, nf_ref, mx_ref, True
        )
        for (cols, _, _), message in zip(infos_of(group), messages):
            part = over_slots(message, atoms)
            acc_ref[:, cols] = part if step == 0 else acc_ref[:, cols] + part


def own_backward(group, gs_ref, gate_ref, wmt, nf_ref, mx_ref, dot_ref, grad_refs):
    grad = tiled(gs_ref[...])
    for step in range(OWN_STEPS):
        backward(
            group, own_rows(step), grad, gate_ref, wmt, nf_ref, mx_ref, dot_ref, grad_refs
        )


def ghost_pairs(
    group, own_ref, table, new_ref, new_base, oh_gh, d_gh, dt_gh, gate_ref, radials, nw_ref,
    steps, wm, wmt, wo, wot, nf_s, mx_s, acc_in, acc_s, gs_ref, dot_ref, grad_refs, en_ref,
):
    norm = 1.0 / math.sqrt(SLOTS)
    acc_s[...] = acc_in[...]

    def ghost_forward(step):
        here, _ = ghost_rows(step)
        messages = forward(
            group, here, oh_gh[here, :], table[...], radials, gate_ref, wm, nf_s, mx_s, False
        )
        acc_s[...] += mm(dt_gh[:, here], jnp.concatenate(messages, axis=1))

    over_ghost_steps(steps, ghost_forward)

    begin = group_cols(group).start
    for cols, degrees, kind in infos_of(group):
        summed_low = (acc_s[:, cols] * norm).astype(BF16)
        own = own_ref[:, begin + cols.start : begin + cols.stop]
        updated = own.astype(F32) + mm(summed_low, wo[kind])
        at = begin - new_base + cols.start
        new_ref[:, at : at + 2 * CH] = updated.astype(BF16)
        weight = jnp.concatenate(
            [nw_ref[d - 1 : d, :] * (1.0 / (2 * d + 1)) for d in degrees], axis=1
        )
        scale = weight * updated
        energy = scale * updated
        en_ref[...] += energy[:, 0:CH] + energy[:, CH:]
        gs_ref[:, cols] = (mm((2.0 * scale).astype(BF16), wot[kind]) * norm).astype(BF16)

    def ghost_backward(step):
        here, _ = ghost_rows(step)
        grad = mm(d_gh[here, :], gs_ref[...]).astype(BF16)
        backward(group, here, grad, gate_ref, wmt, nf_s, mx_s, dot_ref, grad_refs)

    over_ghost_steps(steps, ghost_backward)


def pair_scratch(atoms, half, ghosts, group):
    count, width = len(KINDS[group]), GROUP_COLS[group]
    return (
        [pltpu.VMEM((ghosts, width), BF16), pltpu.SemaphoreType.DMA((7,))]
        + [pltpu.VMEM((count, 2 * CH, 2 * CH), BF16) for _ in range(4)]
        + [
            pltpu.VMEM((half, width), BF16),
            pltpu.VMEM((half, width), BF16),
            pltpu.VMEM((atoms, width), F32),
        ]
    )


def own_kernel(
    meta_ref, own_pos_ref, rbf_ref, rad_ref,
    oh_own, pre_ref, unit_ref, radt_ref, rbft_ref, home_ref, *radial_refs
):
    atoms = meta_ref.shape[0]
    nbasis = rbft_ref.shape[1]
    spacing = spacing_of(atoms, nbasis)
    own_onehots(meta_ref, oh_own)
    here = tiled(own_pos_ref[...].astype(F32))
    for step in range(OWN_STEPS):
        rows = own_rows(step)
        unit, dist = geometry(mm(oh_own[rows, :], own_pos_ref[...]), here)
        unit_ref[rows, :] = unit
        pre, radial = radial_net(dist, spacing, rbf_ref, rad_ref)
        pre_ref[rows, :] = pre.astype(BF16)
        for degree, ref in enumerate(radial_refs):
            ref[rows, :] = radial[:, degree * CH : (degree + 1) * CH]
    for degree in range(5):
        part = slice(degree * CH, (degree + 1) * CH)
        radt_ref[part, :] = flip(rad_ref[:, part])
    for index in range(nbasis // CH):
        part = slice(index * CH, (index + 1) * CH)
        rbft_ref[:, part] = flip(rbf_ref[part, :])
    lanes = home_ref.shape[1]
    lane = iota((atoms, lanes), 1)
    ext_x, ext_y, ext_z = lane // 128, lane // 32 % 4, lane // 8 % 4
    slot = ((2 * ext_x + ext_y - 1) * 2 + ext_z - 1) * 8 + lane % 8
    inside = jnp.logical_and(
        jnp.logical_or(ext_y == 1, ext_y == 2), jnp.logical_or(ext_z == 1, ext_z == 2)
    )
    to_slot = jnp.logical_and(iota((atoms, lanes), 0) == slot, inside)
    to_slot = to_slot.astype(F32).astype(BF16)
    order = meta_ref[:, SLOTS + 1 : SLOTS + 2]
    to_atom = (order == iota((atoms, atoms), 1).astype(F32)).astype(F32)
    home_ref[...] = mm(to_atom.T.astype(BF16), to_slot).astype(BF16)


def own_stage(meta, own_pos, rbf, rad):
    atoms = meta.shape[0]
    edges = atoms * HALF
    out_shape = (
        struct(edges, atoms, dtype=BF16),
        struct(edges, CH, dtype=BF16),
        struct(edges, CH),
        struct(5 * CH, CH, dtype=BF16),
        struct(CH, rbf.shape[0], dtype=BF16),
        struct(atoms, 256, dtype=BF16),
    ) + (struct(edges, CH, dtype=BF16),) * 5
    return call(own_kernel, "own_edges", out_shape, [], (meta, own_pos, rbf, rad))


def scalar_forward(rows, near, radial, mix_ref, m0_ref, gate_ref, nf0_ref):
    near = near.astype(BF16)
    nf0_ref[rows, :] = near
    mixed = mm(near * radial, mix_ref[0])
    m0_ref[rows, :] = mixed.astype(BF16)
    gate = jax.nn.sigmoid(mixed)
    gate_ref[rows, :] = gate.astype(BF16)
    return mixed * gate


def own_forward_kernel(groups, scalar, *refs):
    own_ref, mix_ref, oh_own, refs = *refs[:3], refs[3:]
    radial0, radials = refs[0], dict(enumerate(refs[1:5], start=1))
    refs = refs[5:]
    if scalar:
        m0_ref, gate_ref, nf0_ref, acc0_ref = refs[:4]
        refs = refs[4:]
        atoms = own_ref.shape[0]
        feats = own_ref[:, 0:CH]
        summed = None
        for step in range(OWN_STEPS):
            rows = own_rows(step)
            message = scalar_forward(
                rows, mm(oh_own[rows, :], feats), radial0[rows, :], mix_ref, m0_ref, gate_ref,
                nf0_ref,
            )
            part = over_slots(message, atoms)
            summed = part if summed is None else summed + part
        acc0_ref[...] = summed
    else:
        gate_ref, refs = refs[0], refs[1:]
    outs, weights = refs[: 3 * len(groups)], refs[3 * len(groups) :]
    for index, group in enumerate(groups):
        block_diagonal(KINDS[group], mix_ref, weights[index])
        nf_ref, mx_ref, acc_ref = outs[3 * index : 3 * index + 3]
        own_forward(
            group, own_ref, oh_own, radials, gate_ref, weights[index], nf_ref, mx_ref, acc_ref
        )


def own_forward_stage(groups, feats, mix, oh_own, radial_own, gate=None):
    atoms = feats.shape[0]
    half = atoms * HALF
    out_shape = ()
    if gate is None:
        out_shape += (struct(half, CH, dtype=BF16),) * 3 + (struct(atoms, CH),)
    for group in groups:
        width = GROUP_COLS[group]
        out_shape += (struct(half, width, dtype=BF16),) * 2 + (struct(atoms, width),)
    args = (feats, mix, oh_own, *radial_own) + (() if gate is None else (gate,))
    scratch = [pltpu.VMEM((len(KINDS[group]), 2 * CH, 2 * CH), BF16) for group in groups]
    name = "own_forward_" + "".join("abc"[group] for group in groups)
    kernel = functools.partial(own_forward_kernel, groups, gate is None)
    outs = call(kernel, name, out_shape, scratch, args)
    first = len(outs) - 3 * len(groups)
    return outs[:first], [outs[first + 3 * i : first + 3 * i + 3] for i in range(len(groups))]


def start_kernel(
    p0, p1, p2, own_ref, own_pos_ref, meta_ref, rbf_ref, rad_ref, mix_ref, out_ref, ew_ref,
    acc0_ref,
    new_ref, oh_gh, d_gh, dt_gh, pre_ref, unit_ref, gs0_ref, en_ref, m0_gh, gate_gh, nf0_gh,
    radial_gh1, radial_gh2, radial_gh3, radial_gh4,
    table, sems, ghpos, acc_s,
):
    radial_gh = (None, radial_gh1, radial_gh2, radial_gh3, radial_gh4)
    copies = fetch((p0, p1, p2), slice(0, 2 * CH), table, sems)
    atoms = own_ref.shape[0]
    ghosts = table.shape[0]
    spacing = spacing_of(atoms, rbf_ref.shape[0])
    norm = 1.0 / math.sqrt(SLOTS)

    live = live_ghosts(meta_ref)
    sub_atom = iota((atoms, atoms), 0)
    lane_atom = iota((atoms, atoms), 1)
    live_b = jnp.broadcast_to(live, (atoms, atoms))
    end_row = jnp.sum(jnp.where(sub_atom <= lane_atom, live_b, 0.0), axis=0, keepdims=True)
    live_row = jnp.sum(jnp.where(sub_atom == lane_atom, live_b, 0.0), axis=0, keepdims=True)
    start_row = end_row - live_row
    row_b = jnp.broadcast_to(live_row, (atoms, atoms))
    end_col = jnp.sum(jnp.where(lane_atom <= sub_atom, row_b, 0.0), axis=1, keepdims=True)
    start_col = end_col - live
    total = jnp.sum(live)
    steps = step_count(meta_ref)
    ghost_row = meta_ref[:, HALF:SLOTS] - atoms
    high_part = jnp.floor(ghost_row * (1.0 / 16.0))
    row_high = high_part.astype(BF16)
    row_low = (ghost_row - 16.0 * high_part).astype(BF16)

    row = iota((ghosts, CH), 0)
    lane = iota((ghosts, CH), 1)
    zcells = atoms // 32
    per_y = (zcells + 2) * 8
    ext_x = row // (4 * per_y)
    ext_y = row // per_y % 4
    ext_z = row // 8 % (zcells + 2)

    def side_of(ext, last, size):
        return jnp.where(ext == 0, -size, jnp.where(ext == last, size, 0.0))

    shift = jnp.where(lane == 12, side_of(ext_x, 3, 4.0), 0.0)
    shift = jnp.where(lane == 13, side_of(ext_y, 3, 4.0), shift)
    shift = jnp.where(lane == 14, side_of(ext_z, zcells + 1, 2.0 * zcells), shift)
    own0 = own_ref[:, 0:CH]
    acc_s[...] = acc0_ref[...]
    for copy in copies:
        copy.wait()
    ghpos[...] = (table[:, CH:].astype(F32) + shift).astype(BF16)

    def ghost_start(step):
        here, _ = ghost_rows(step)
        base = step * STEP
        edge = (iota((STEP, atoms), 0) + base).astype(F32)
        mine = jnp.logical_and(edge >= start_row, edge < end_row).astype(F32)
        source = mine.astype(BF16)
        d_gh[here, :] = source
        edge_t = (iota((atoms, STEP), 1) + base).astype(F32)
        mine_t = jnp.logical_and(edge_t >= start_col, edge_t < end_col)
        spread = mine_t.astype(F32).astype(BF16)
        dt_gh[:, here] = spread
        edge_col = edge[:, 0:1]
        slot = edge_col - jnp.sum(mine * start_row, axis=1, keepdims=True)
        listed = mm(source, row_high) * 16.0 + mm(source, row_low)
        at_slot = iota((STEP, HALF), 1).astype(F32) == slot
        which = jnp.sum(jnp.where(at_slot, listed, 0.0), axis=1, keepdims=True)
        which = jnp.where(edge_col < total, which, -1.0)
        onehot = (iota((STEP, ghosts), 1).astype(F32) == which).astype(F32).astype(BF16)
        oh_gh[here, :] = onehot
        unit, dist = geometry(mm(onehot, ghpos[...]), mm(source, own_pos_ref[...]))
        unit_ref[here, :] = unit
        pre, radial = radial_net(dist, spacing, rbf_ref, rad_ref)
        pre_ref[here, :] = pre.astype(BF16)
        for degree in range(1, 5):
            radial_gh[degree][here, :] = radial[:, degree * CH : (degree + 1) * CH]
        message = scalar_forward(
            here, mm(onehot, table[:, 0:CH]), radial[:, 0:CH], mix_ref, m0_gh, gate_gh, nf0_gh
        )
        acc_s[...] += mm(spread, message.astype(BF16))

    over_ghost_steps(steps, ghost_start)

    low0 = (acc_s[...] * norm).astype(BF16)
    updated0 = own0.astype(F32) + mm(low0, out_ref[0])
    new_ref[:, 0:CH] = updated0.astype(BF16)
    logistic = jax.nn.sigmoid(updated0)
    weight0 = ew_ref[...]
    en_ref[...] = weight0 * updated0 * logistic
    grad0 = (weight0 * logistic * (1.0 + updated0 * (1.0 - logistic))).astype(BF16)
    gs0_ref[...] = mm_nt(grad0, out_ref[0]) * norm


def any_specs(count, total):
    return [pl.BlockSpec(memory_space=pl.ANY)] * count + [
        pl.BlockSpec(memory_space=SPACE)
    ] * (total - count)


def start_stage(pieces, feats, *rest):
    atoms = feats.shape[0]
    half = atoms * HALF
    ghosts = sum(piece.shape[0] for piece in pieces)
    out_shape = (
        struct(atoms, CH, dtype=BF16),
        struct(half, ghosts, dtype=BF16),
        struct(half, atoms, dtype=BF16),
        struct(atoms, half, dtype=BF16),
        struct(half, CH, dtype=BF16),
        struct(half, CH),
        struct(atoms, CH),
        struct(atoms, CH),
    ) + (struct(half, CH, dtype=BF16),) * 7
    scratch = [
        pltpu.VMEM((ghosts, 2 * CH), BF16),
        pltpu.SemaphoreType.DMA((7,)),
        pltpu.VMEM((ghosts, CH), BF16),
        pltpu.VMEM((atoms, CH), F32),
    ]
    args = tuple(pieces) + (feats,) + rest
    return call(
        start_kernel, "ghost_start", out_shape, scratch, args,
        any_specs(len(pieces), len(args)), 24,
    )


def pairs_kernel(group, count, skip, *refs):
    pieces, refs = refs[:count], refs[count:]
    own_ref, meta_ref, mix_ref, out_ref, nw_ref, oh_gh, d_gh, dt_gh, gate_gh = refs[:9]
    gate_own, nf_own, mx_own, acc_own = refs[9:13]
    refs = refs[13:]
    degrees = DEGREES[group]
    radials, refs = dict(zip(degrees, refs)), refs[len(degrees) :]
    new_ref, en_ref, gs_ref, dot_gh = refs[:4]
    grads, refs = dict(zip(degrees, refs[4:])), refs[4 + len(degrees) :]
    if group == 0:
        dot_own, refs = refs[0], refs[1:]
        grads_own, refs = dict(zip(degrees, refs)), refs[len(degrees) :]
    table, sems, wm, wmt, wo, wot, nf_s, mx_s, acc_s = refs
    copies = fetch(pieces, slice(skip, skip + GROUP_COLS[group]), table, sems)
    block_diagonal(KINDS[group], mix_ref, wm, wmt)
    block_diagonal(KINDS[group], out_ref, wo, wot)
    en_ref[...] = jnp.zeros_like(en_ref)
    for copy in copies:
        copy.wait()
    ghost_pairs(
        group, own_ref, table, new_ref, group_cols(group).start, oh_gh, d_gh, dt_gh, gate_gh,
        radials, nw_ref, step_count(meta_ref), wm, wmt, wo, wot, nf_s, mx_s, acc_own, acc_s,
        gs_ref, dot_gh, grads, en_ref,
    )
    if group == 0:
        own_backward(group, gs_ref, gate_own, wmt, nf_own, mx_own, dot_own, grads_own)


def pairs_stage(group, skip, pieces, shared, own_parts, radial_gh):
    feats = shared[0]
    atoms = feats.shape[0]
    half = atoms * HALF
    ghosts = sum(piece.shape[0] for piece in pieces)
    degrees = DEGREES[group]
    sides = 2 if group == 0 else 1
    out_shape = (
        struct(atoms, GROUP_COLS[group], dtype=BF16),
        struct(atoms, CH),
        struct(atoms, GROUP_COLS[group], dtype=BF16),
    ) + (struct(half, CH, dtype=BF16),) * (sides * (1 + len(degrees)))
    args = tuple(pieces) + tuple(shared) + tuple(own_parts)
    args += tuple(radial_gh[degree - 1] for degree in degrees)
    new, energy, gs, *rest = call(
        functools.partial(pairs_kernel, group, len(pieces), skip), "pairs_" + "abc"[group],
        out_shape, pair_scratch(atoms, half, ghosts, group), args,
        any_specs(len(pieces), len(args)), 24,
    )
    return new, energy, gs, rest[: 1 + len(degrees)], rest[1 + len(degrees) :]


def own_backward_kernel(group, mix_ref, gs_ref, gate_ref, nf_ref, mx_ref, *refs):
    dot_ref, grads, wmt = refs[0], dict(zip(DEGREES[group], refs[1:-1])), refs[-1]
    block_diagonal(KINDS[group], mix_ref, None, wmt)
    own_backward(group, gs_ref, gate_ref, wmt, nf_ref, mx_ref, dot_ref, grads)


def own_backward_stage(group, mix, gs, gate, nf, mx):
    half = nf.shape[0]
    out_shape = (struct(half, CH, dtype=BF16),) * (1 + len(DEGREES[group]))
    scratch = [pltpu.VMEM((len(KINDS[group]), 2 * CH, 2 * CH), BF16)]
    kernel = functools.partial(own_backward_kernel, group)
    name = "own_backward_" + "abc"[group]
    return call(kernel, name, out_shape, scratch, (mix, gs, gate, nf, mx))


def finish(
    grad, mixed, near, dots, parts, pre, unit, spacing, radt_ref, rbft_ref, mix_t
):
    mixed = mixed.astype(F32)
    gate = jax.nn.sigmoid(mixed)
    first = grad * gate * (1.0 + mixed * (1.0 - gate)) + dots * gate * (1.0 - gate)
    weighted = mm(first.astype(BF16), mix_t) * near.astype(F32)
    radial_grad = jnp.concatenate([weighted.astype(BF16)] + parts, axis=1)
    hidden_grad = mm(radial_grad, radt_ref[...])
    pre = pre.astype(F32)
    logistic = jax.nn.sigmoid(pre)
    pre_grad = (hidden_grad * logistic * (1.0 + pre * (1.0 - logistic))).astype(BF16)
    centred = centred_of(unit[:, 3:4], spacing, rbft_ref.shape[1])
    slope = jnp.exp(-0.5 * centred * centred) * centred
    basis_grad = mm(pre_grad, rbft_ref[...])
    dist_grad = jnp.sum(basis_grad * slope, axis=1, keepdims=True) * (-1.0 / spacing)
    pull = unit * dist_grad
    across = pull.T[0:8, :]
    top = across.astype(BF16)
    rest = (across - top.astype(F32)).astype(BF16)
    return pull, top, rest


def sum_of(refs, rows):
    total = refs[0][rows, :].astype(F32)
    for ref in refs[1:]:
        total += ref[rows, :].astype(F32)
    return total


def degree_parts(refs, rows):
    by_degree = {}
    refs = list(refs)
    for degrees in DEGREES:
        for degree in degrees:
            by_degree.setdefault(degree, []).append(refs.pop(0))
    return [sum_of(by_degree[degree], rows).astype(BF16) for degree in range(1, 5)]


PARTIALS = sum(len(degrees) for degrees in DEGREES)


def third_kernel(
    p0, p1, p2, p3, p4, own_ref, meta_ref, mix_ref, out_ref, nw_ref, oh_gh, d_gh, dt_gh, gate_gh,
    acc_own, radt_ref, rbft_ref, gs0_ref, en_0, en_a, new_0, new_a, pre_gh, unit_gh,
    m0_ref, nf0_ref, dot_a, *refs
):
    group = 1
    before, degrees = len(DEGREES[0]), DEGREES[group]
    gr_a, refs = refs[:before], refs[before:]
    radials, refs = dict(zip(degrees, refs)), refs[len(degrees) :]
    new_ref, energy_ref, src_ref, onto_ref, flow_ref, fmid_ref, fhigh_ref, gs_ref = refs[:8]
    table, sems, wm, wmt, wo, wot, nf_s, mx_s, acc_s, dot_c, en_s, fgh_s = refs[8:20]
    grads = dict(zip(degrees, refs[20:]))
    copies = fetch((p0, p1, p2, p3, p4), slice(0, GROUP_COLS[group]), table, sems)
    atoms = own_ref.shape[0]
    spacing = spacing_of(atoms, rbft_ref.shape[1])
    block_diagonal(KINDS[group], mix_ref, wm, wmt)
    block_diagonal(KINDS[group], out_ref, wo, wot)
    en_s[...] = en_0[...] + en_a[...]
    at = 0
    for part in (new_0, new_a):
        new_ref[:, at : at + part.shape[1]] = part[...]
        at += part.shape[1]
    steps = step_count(meta_ref)

    for copy in copies:
        copy.wait()
    ghost_pairs(
        group, own_ref, table, new_ref, 0, oh_gh, d_gh, dt_gh, gate_gh, radials, nw_ref,
        steps, wm, wmt, wo, wot, nf_s, mx_s, acc_own, acc_s, gs_ref, dot_c, grads, en_s,
    )
    energy_ref[...] = jnp.sum(en_s[...].T, axis=0, keepdims=True)

    fgh_s[...] = jnp.zeros_like(fgh_s)
    src_ref[...] = jnp.zeros_like(src_ref)
    onto_ref[...] = jnp.zeros_like(onto_ref)
    gs0_low = gs0_ref[...].astype(BF16)
    mix_t = flip(mix_ref[0])

    def ghost_finish(step):
        here, _ = ghost_rows(step)
        grad = mm(d_gh[here, :], gs0_low)
        pull, top, rest = finish(
            grad, m0_ref[here, :], nf0_ref[here, :], sum_of((dot_a, dot_c), here),
            degree_parts(gr_a + refs[20:], here), pre_gh[here, :], unit_gh[here, :], spacing,
            radt_ref, rbft_ref, mix_t,
        )
        pull_top = pull.astype(BF16)
        pull_rest = (pull - pull_top.astype(F32)).astype(BF16)
        spread = dt_gh[:, here]
        src_ref[...] += mm(spread, pull_top) + mm(spread, pull_rest)
        onehot = oh_gh[here, :]
        fgh_s[...] += mm(top, onehot) + mm(rest, onehot)

    over_ghost_steps(steps, ghost_finish)
    low, mid = flow_ref.shape[1], fmid_ref.shape[1]
    flow_ref[...] = fgh_s[:, 0:low]
    fmid_ref[...] = fgh_s[:, low : low + mid]
    fhigh_ref[...] = fgh_s[:, low + mid :]


def third_stage(pieces, feats, *rest):
    atoms, feat = feats.shape
    half = atoms * HALF
    ghosts = sum(piece.shape[0] for piece in pieces)
    sizes = (ghosts // 4, ghosts // 2, ghosts // 4)
    out_shape = (
        struct(atoms, feat, dtype=BF16),
        struct(1, atoms),
        struct(atoms, CH),
        struct(8, atoms),
    ) + tuple(struct(8, size) for size in sizes) + (
        struct(atoms, GROUP_COLS[1], dtype=BF16),
    )
    scratch = pair_scratch(atoms, half, ghosts, 1) + [
        pltpu.VMEM((half, CH), BF16),
        pltpu.VMEM((atoms, CH), F32),
        pltpu.VMEM((8, ghosts), F32),
    ]
    scratch += [pltpu.VMEM((half, CH), BF16)] * len(DEGREES[1])
    args = tuple(pieces) + (feats,) + rest
    return call(
        third_kernel, "third_group", out_shape, scratch, args,
        any_specs(len(pieces), len(args)), 28,
    )


def own_back_kernel(
    steps, oh_own, pre_own, unit_own, radt_ref, rbft_ref, mix_ref, gs0_ref,
    m0_ref, nf0_ref, dot_a, dot_c, *refs
):
    gr_own, (src_in, onto_in, src_out, onto_out) = refs[:PARTIALS], refs[PARTIALS:]
    atoms = oh_own.shape[1]
    spacing = spacing_of(atoms, rbft_ref.shape[1])
    grad = tiled(gs0_ref[...])
    mix_t = flip(mix_ref[0])
    src = src_in[...]
    onto = onto_in[...]
    for step in steps:
        rows = own_rows(step)
        pull, top, rest = finish(
            grad, m0_ref[rows, :], nf0_ref[rows, :], sum_of((dot_a, dot_c), rows),
            degree_parts(gr_own, rows), pre_own[rows, :], unit_own[rows, :], spacing, radt_ref,
            rbft_ref, mix_t,
        )
        src += over_slots(pull, atoms)
        onehot = oh_own[rows, :]
        onto += mm(top, onehot) + mm(rest, onehot)
    src_out[...] = src
    onto_out[...] = onto


def own_back_stage(steps, *args):
    atoms = args[0].shape[1]
    out_shape = (struct(atoms, CH), struct(8, atoms))
    kernel = functools.partial(own_back_kernel, tuple(steps))
    return call(kernel, "own_back", out_shape, [], args)


def ring(axis):
    peers = lax.axis_size(axis)
    up = [(i, (i + 1) % peers) for i in range(peers)]
    return up, [(j, i) for i, j in up]


def neighbours_of(block, axis, dim):
    up, down = ring(axis)
    length = block.shape[dim]
    if len(up) == 2 and length == 2:
        other = lax.ppermute(block, axis, up)
        return (
            lax.slice_in_dim(other, length - 1, length, axis=dim),
            lax.slice_in_dim(other, 0, 1, axis=dim),
        )
    before = lax.ppermute(lax.slice_in_dim(block, length - 1, length, axis=dim), axis, up)
    after = lax.ppermute(lax.slice_in_dim(block, 0, 1, axis=dim), axis, down)
    return before, after


def grown(block, axis, dim):
    before, after = neighbours_of(block, axis, dim)
    return jnp.concatenate([before, block, after], axis=dim)


def ghost_pieces(along_y, block, along_x):
    outer = jnp.concatenate(along_y, axis=1)
    low_out, high_out = neighbours_of(outer, "gx", 0)
    low_in, high_in = along_x
    middle = jnp.concatenate([along_y[0], block, along_y[1]], axis=1)
    return tuple(flat_rows(piece) for piece in (low_in, low_out, middle, high_in, high_out))


def flat_rows(piece):
    return piece.reshape(-1, piece.shape[-1])


def fold_kernel(mid_ref, low_ref, high_ref, out_ref):
    lanes = mid_ref.shape[1]
    ext_y = iota(mid_ref.shape, 1) // 32 % 4
    out_ref[...] = (
        mid_ref[...]
        + jnp.where(ext_y == 1, pltpu.roll(low_ref[...], lanes - 64, 1), 0.0)
        + jnp.where(ext_y == 2, pltpu.roll(high_ref[...], 64, 1), 0.0)
    )


def forces_kernel(mid_ref, low_ref, high_ref, src_ref, onto_ref, home_ref, out_ref):
    values = mid_ref[...]
    lanes = values.shape[1]
    ext_z = iota(values.shape, 1) // 8 % 4
    values += jnp.where(ext_z == 1, pltpu.roll(low_ref[...], lanes - 16, 1), 0.0)
    values += jnp.where(ext_z == 2, pltpu.roll(high_ref[...], 16, 1), 0.0)
    first = values.astype(BF16)
    values -= first.astype(F32)
    second = values.astype(BF16)
    third = (values - second.astype(F32)).astype(BF16)
    home = home_ref[...]
    total = onto_ref[...] - src_ref[...].T[0:8, :]
    total += (mm_nt(first, home) + (mm_nt(second, home) + mm_nt(third, home)))
    for comp in range(3):
        out_ref[comp] = -total[comp : comp + 1, :]


def give_back_x(low, mid, high):
    up, down = ring("gx")
    from_low = lax.ppermute(high, "gx", up)
    from_high = lax.ppermute(low, "gx", down)
    return mid, jnp.concatenate([from_low, from_high], axis=1)


def give_back_y(mid):
    up, down = ring("gy")
    return mid, lax.ppermute(mid, "gy", up), lax.ppermute(mid, "gy", down)


def fold(*args):
    return call(fold_kernel, "fold", (struct(*args[0].shape),), [], args)[0]


def give_back_z(mid):
    up, down = ring("gz")
    from_low = lax.ppermute(mid, "gz", up)
    return mid, from_low, from_low if len(up) == 2 else lax.ppermute(mid, "gz", down)


def local(
    features,
    positions,
    neighbours,
    counts,
    cell_atoms,
    rbf_weight,
    radial_weight,
    mix_weight,
    out_weight,
    energy_weight,
    norm_weight,
):
    feats = features[0, 0, 0]
    places = jnp.swapaxes(positions[0, 0], 0, 1)
    lists = jnp.concatenate([neighbours[0, 0, 0].T, counts[0, 0], cell_atoms[0, 0]], axis=0)
    cells, own_pos, meta = make_cells(feats, places, lists)
    hold = lax.optimization_barrier
    block = cells.reshape(2, 2, 2, 8, cells.shape[1])
    cut = 2 * CH + GROUP_COLS[0]
    z = neighbours_of(block, "gz", 2)
    y1_in = neighbours_of(block[..., cut:], "gy", 1)
    oh_own, pre_own, unit_own, radt, rbft, home, *radial_own = own_stage(
        meta, own_pos, rbf_weight, radial_weight
    )
    (m0_own, gate_own, nf0_own, acc0), (own_a,) = own_forward_stage(
        (0,), feats, mix_weight, oh_own, radial_own
    )
    z, y1_in, gate_own = hold((z, y1_in, gate_own))
    block = jnp.concatenate([z[0], block, z[1]], axis=2)
    block0, block1 = block[..., :cut], block[..., cut:]
    y0 = neighbours_of(block0, "gy", 1)
    x1_in = neighbours_of(block1, "gx", 0)
    _, (own_b,) = own_forward_stage((1,), feats, mix_weight, oh_own, radial_own, gate_own)
    y0, x1_in, z1, acc_b = hold((y0, x1_in, [part[..., cut:] for part in z], own_b[2]))
    middle = jnp.concatenate([y0[0], block0, y0[1]], axis=1)
    low, high = neighbours_of(middle, "gx", 0)
    y1_out = neighbours_of(jnp.concatenate(z1, axis=2), "gy", 1)
    low, high, y1_out = hold((low, high, y1_out))
    y1 = [
        jnp.concatenate([out[:, :, 0:1], inner, out[:, :, 1:2]], axis=2)
        for out, inner in zip(y1_out, y1_in)
    ]
    pieces0 = tuple(flat_rows(piece) for piece in (low, middle, high))
    pieces1 = ghost_pieces(y1, block1, x1_in)
    (
        new_0, oh_gh, d_gh, dt_gh, pre_gh, unit_gh, gs0, en_0, m0_gh, gate_gh, nf0_gh, *radial_gh,
    ) = start_stage(
        pieces0, feats, own_pos, meta, rbf_weight, radial_weight, mix_weight, out_weight,
        energy_weight[None], acc0,
    )
    shared = (feats, meta, mix_weight, out_weight, norm_weight, oh_gh, d_gh, dt_gh, gate_gh)
    new_a, en_a, _, (dot_gh_a, *gr_gh_a), (dot_own_a, *gr_own_a) = pairs_stage(
        0, 2 * CH, pieces0, shared, (gate_own, *own_a), radial_gh
    )
    new, energy, src, onto, low, mid, high, gs_b = third_stage(
        pieces1, *shared, acc_b, radt, rbft, gs0, en_0, en_a, new_0, new_a, pre_gh,
        unit_gh, m0_gh, nf0_gh, dot_gh_a, *gr_gh_a,
        *[radial_gh[degree - 1] for degree in DEGREES[1]],
    )
    mid, arrived = give_back_x(low, mid, high)
    dot_own_b, *gr_own_b = own_backward_stage(1, mix_weight, gs_b, gate_own, *own_b[:2])
    arrived, gs0, dot_own_b = hold((arrived, gs0, dot_own_b))
    mid, from_low, from_high = give_back_y(mid + arrived)
    back = (oh_own, pre_own, unit_own, radt, rbft, mix_weight, gs0, m0_own, nf0_own)
    back += (dot_own_a, dot_own_b, *gr_own_a, *gr_own_b)
    src, onto = own_back_stage(range(2), *back, src, onto)
    from_low, from_high, src = hold((from_low, from_high, src))
    folded = give_back_z(fold(mid, from_low, from_high))
    src, onto = own_back_stage(range(2, 4), *back, src, onto)
    args = (*folded, src, onto, home)
    out_shape = (struct(3, 1, src.shape[0]),)
    forces = call(forces_kernel, "forces", out_shape, [], args)[0]
    return (
        new[None, None, None],
        energy[None, None],
        jnp.swapaxes(forces, 0, 1)[None, None],
    )


def solution(mesh):
    split = P("gx", "gy", "gz", None, None)
    flat = P("gx", "gy", "gz", None)
    return jax.shard_map(
        local,
        mesh=mesh,
        in_specs=(split, split, split, flat, flat, P(), P(), P(), P(), P(), P()),
        out_specs=(split, flat, split),
        check_vma=False,
    )
```

```python
import functools
import math

import jax
import jax.numpy as jnp
from jax import lax
from jax.experimental import pallas as pl
from jax.experimental.pallas import tpu as pltpu
from jax.sharding import PartitionSpec as P

F32 = jnp.float32
BF16 = jnp.bfloat16
CH = 128
SLOTS = 32
HALF = 16
STEP = 256
OWN_STEPS = 4
GH_STEPS = 2
MIB = 1024 * 1024
SPACE = pltpu.VMEM
PAIR_DEGREES = (
    (1, 1), (1, 2), (2, 2), (2, 2),
    (3, 3), (3, 3), (3, 3), (3, 4),
    (4, 4), (4, 4), (4, 4), (4, 4),
)
GROUPS = ((0, 4), (4, 12))
KINDS = tuple(sorted({PAIR_DEGREES[pair] for pair in range(*group)}) for group in GROUPS)
DEGREES = tuple(sorted({d for both in kinds for d in both}) for kinds in KINDS)
GROUP_COLS = tuple(2 * CH * (end - begin) for begin, end in GROUPS)


def mm(a, b):
    return jnp.dot(a, b, preferred_element_type=F32)


def mm_nt(a, b):
    return lax.dot_general(a, b, (((1,), (1,)), ((), ())), preferred_element_type=F32)


def iota(shape, dim):
    return lax.broadcasted_iota(jnp.int32, shape, dim)


def flip(w):
    return w.astype(F32).T.astype(BF16)


def pair_cols(pair):
    return slice(CH + pair * 2 * CH, CH + (pair + 1) * 2 * CH)


def struct(*shape, dtype=F32):
    return jax.ShapeDtypeStruct(shape, dtype)


def call(kernel, name, out_shape, scratch, args, specs=None, limit=16):
    return pl.pallas_call(
        kernel,
        out_shape=out_shape,
        in_specs=specs or [pl.BlockSpec(memory_space=SPACE)] * len(args),
        out_specs=tuple(pl.BlockSpec(memory_space=SPACE) for _ in out_shape),
        scratch_shapes=scratch,
        compiler_params=pltpu.CompilerParams(vmem_limit_bytes=limit * MIB),
        cost_estimate=pl.CostEstimate(flops=1024, bytes_accessed=1024, transcendentals=0),
        name=name,
    )(*args)


def cells_kernel(
    feat_ref, pos_ref, lists_ref,
    out_ref, own_pos_ref, meta_ref, pick_ref, rows_ref, pos_rows,
):
    rows_ref[...] = jnp.zeros_like(rows_ref)
    pos_rows[...] = jnp.zeros_like(pos_rows)
    atoms = feat_ref.shape[0]
    rows_ref[0 : SLOTS + 2, :] = lists_ref[...].astype(F32)
    meta = rows_ref[...].T
    meta_ref[...] = meta
    for comp in range(3):
        places = pos_ref[comp]
        first = places.astype(BF16).astype(F32)
        second = (places - first).astype(BF16).astype(F32)
        pos_rows[comp : comp + 1, :] = first
        pos_rows[4 + comp : 5 + comp, :] = second
        pos_rows[8 + comp : 9 + comp, :] = places - first - second
    pieces = pos_rows[...].astype(BF16)
    lane = iota((atoms, atoms), 1).astype(F32)
    pick = (meta[:, SLOTS + 1 : SLOTS + 2] == lane).astype(F32).astype(BF16)
    same = (iota((atoms, atoms), 0) == iota((atoms, atoms), 1)).astype(F32).astype(BF16)
    own_pos_ref[...] = mm_nt(same, pieces).astype(BF16)
    out_ref[:, CH : 2 * CH] = mm_nt(pick, pieces).astype(BF16)
    pick_ref[...] = pick
    out_ref[:, 0:CH] = mm(pick, feat_ref[:, 0:CH]).astype(BF16)
    cut = pair_cols(GROUPS[1][0]).start
    out_ref[:, 2 * CH :] = mm(pick, feat_ref[:, CH:cut]).astype(BF16)


def rest_kernel(feat_ref, pick_ref, rest_ref):
    cut = pair_cols(GROUPS[1][0]).start
    rest_ref[...] = mm(pick_ref[...], feat_ref[:, cut:]).astype(BF16)


def make_cells(feats, places, lists):
    atoms = feats.shape[0]
    out_shape = (
        struct(atoms, 2 * CH + GROUP_COLS[0], dtype=BF16),
        struct(atoms, CH, dtype=BF16),
        struct(atoms, CH),
        struct(atoms, atoms, dtype=BF16),
    )
    args = (feats, places, lists)
    scratch = [pltpu.VMEM((CH, atoms), F32), pltpu.VMEM((CH, atoms), F32)]
    first, own_pos, meta, pick = call(cells_kernel, "cells", out_shape, scratch, args)
    out_shape = (struct(atoms, GROUP_COLS[1], dtype=BF16),)
    rest = call(rest_kernel, "cells_rest", out_shape, [], (feats, pick))[0]
    return first, rest, own_pos, meta


def spacing_of(atoms, nbasis):
    depth = atoms // 16
    return 2.0 * math.sqrt(32.0 + depth * depth) / (nbasis - 1)


def own_onehots(meta_ref, oh_own):
    atoms = meta_ref.shape[0]
    counts = meta_ref[:, SLOTS : SLOTS + 1]
    lane_atom = iota((atoms, atoms), 1).astype(F32)
    for slot in range(HALF):
        hit = jnp.logical_and(meta_ref[:, slot : slot + 1] == lane_atom, counts > slot)
        oh_own[slot * atoms : (slot + 1) * atoms, :] = hit.astype(F32).astype(BF16)


def geometry(near, here):
    diff = near - here
    rel = (diff + pltpu.roll(diff, CH - 4, 1)) + (
        pltpu.roll(diff, CH - 8, 1) + pltpu.roll(diff, CH - 12, 1)
    )
    lane = iota(rel.shape, 1)
    rel = jnp.where(lane < 3, rel, 0.0)
    square = jnp.sum(rel * rel, axis=1, keepdims=True)
    inverse = lax.rsqrt(jnp.where(square > 0.0, square, 1.0))
    dist = square * inverse
    return jnp.where(lane == 3, dist, rel * inverse), dist


def centred_of(dist, spacing, nbasis):
    return dist * (1.0 / spacing) - iota((dist.shape[0], nbasis), 1).astype(F32)


def radial_net(dist, spacing, rbf_ref, rad_ref):
    centred = centred_of(dist, spacing, rbf_ref.shape[0])
    basis = jnp.exp(-0.5 * centred * centred)
    pre = mm(basis.astype(BF16), rbf_ref[...])
    hidden = (pre * jax.nn.sigmoid(pre)).astype(BF16)
    return pre, mm(hidden, rad_ref[...]).astype(BF16)


def tiled(values, size=STEP):
    return jnp.concatenate([values] * (size // values.shape[0]), axis=0)


def live_ghosts(meta_ref):
    return jnp.maximum(meta_ref[:, SLOTS : SLOTS + 1] - HALF, 0.0)


def step_count(meta_ref):
    total = jnp.sum(live_ghosts(meta_ref)).astype(jnp.int32)
    rows = GH_STEPS * STEP
    return jnp.maximum((total + (rows - 1)) // rows, 1) * GH_STEPS


def own_rows(step, size=STEP):
    return pl.ds(step * size, size)


def ghost_rows(step, size=STEP):
    first = OWN_STEPS * STEP
    if isinstance(step, int):
        return pl.ds(step * size, size), pl.ds(first + step * size, size)
    base = pl.multiple_of(step * size, size)
    return pl.ds(base, size), pl.ds(pl.multiple_of(first + base, size), size)


def over_ghost_steps(steps, body, size=STEP):
    static = GH_STEPS * STEP // size
    for step in range(static):
        body(step)

    def again(step, carry):
        body(step)
        return carry

    lax.fori_loop(static, (steps * STEP + (size - 1)) // size, again, 0)


def block_diagonal(kinds, source, straight=None, across=None):
    zero = jnp.zeros((CH, CH), BF16)
    targets = [ref for ref in (straight, across) if ref is not None]
    for kind, both in enumerate(kinds):
        for ref in targets:
            ref[kind, 0:CH, CH:] = zero
            ref[kind, CH:, 0:CH] = zero
    for degree in sorted({d for both in kinds for d in both}):
        weight = source[degree]
        flipped = flip(weight) if across is not None else None
        for kind, both in enumerate(kinds):
            for side in range(2):
                if both[side] == degree:
                    part = slice(side * CH, side * CH + CH)
                    if straight is not None:
                        straight[kind, part, part] = weight
                    if across is not None:
                        across[kind, part, part] = flipped


def fetch(pieces, cols, table, sems):
    low, high, ghosts = 0, 0, table.shape[0]
    if len(pieces) == 3:
        rows = [(piece, 0, piece.shape[0]) for piece in pieces]
    else:
        low_in, low_out, mid, high_in, high_out = pieces
        half = low_out.shape[0] // 2
        rows = [(low_out, 0, half), (low_in, 0, low_in.shape[0]), (low_out, half, half)]
        rows += [(mid, 0, mid.shape[0])]
        rows += [(high_out, 0, half), (high_in, 0, high_in.shape[0]), (high_out, half, half)]
    copies = []
    at = 0
    for index, (piece, start, count) in enumerate(rows):
        source = piece.at[pl.ds(start, count), cols]
        target = table.at[pl.ds(at, count), :]
        copies.append(pltpu.make_async_copy(source, target, sems.at[index]))
        at += count
    for copy in copies:
        copy.start()
    return copies


def infos_of(group):
    infos = []
    for index, pair in enumerate(range(*GROUPS[group])):
        degrees = PAIR_DEGREES[pair]
        cols = slice(index * 2 * CH, (index + 1) * 2 * CH)
        infos.append((cols, degrees, KINDS[group].index(degrees)))
    return infos


def group_cols(group):
    begin, end = GROUPS[group]
    return slice(pair_cols(begin).start, pair_cols(end - 1).stop)


def twice(values):
    return jnp.concatenate([values, values], axis=1)


def forward(group, rows, onehot, feats, radials, gate_ref, wm, nf_ref, mx_ref, slots):
    near = mm(onehot, feats).astype(BF16)
    nf_ref[rows, :] = near
    gate = twice(gate_ref[rows, :])
    wide = gate.astype(F32) if slots else None
    messages = []
    for cols, degrees, kind in infos_of(group):
        radial = jnp.concatenate([radials[d][rows, :] for d in degrees], axis=1)
        mixed = mm(near[:, cols] * radial, wm[kind])
        low = mixed.astype(BF16)
        mx_ref[rows, cols] = low
        messages.append(mixed * wide if slots else low * gate)
    return messages


def backward(group, rows, grad, gate_ref, wmt, nf_ref, mx_ref, dot_ref, grad_refs):
    parts = {}
    dots = None
    gate = twice(gate_ref[rows, :])
    for cols, degrees, kind in infos_of(group):
        product = grad[:, cols] * mx_ref[rows, cols]
        dot = (product[:, 0:CH] + product[:, CH:]).astype(F32)
        dots = dot if dots is None else dots + dot
        weighted = mm(grad[:, cols] * gate, wmt[kind]) * nf_ref[rows, cols].astype(F32)
        for side in range(2):
            part = weighted[:, side * CH : (side + 1) * CH]
            degree = degrees[side]
            parts[degree] = parts[degree] + part if degree in parts else part
    dot_ref[rows, :] = dots.astype(dot_ref.dtype)
    for degree, part in parts.items():
        grad_refs[degree][rows, :] = part.astype(grad_refs[degree].dtype)


def over_slots(values, atoms):
    return jnp.sum(values.reshape(-1, atoms, values.shape[1]), axis=0)


def own_forward(group, own_ref, oh_own, radials, gate_ref, wm, nf_ref, mx_ref, acc_ref):
    atoms = own_ref.shape[0]
    feats = own_ref[:, group_cols(group)]
    for step in range(OWN_STEPS):
        rows = own_rows(step)
        messages = forward(
            group, rows, oh_own[rows, :], feats, radials, gate_ref, wm, nf_ref, mx_ref, True
        )
        for (cols, _, _), message in zip(infos_of(group), messages):
            part = over_slots(message, atoms)
            acc_ref[:, cols] = part if step == 0 else acc_ref[:, cols] + part


def own_backward(group, gs_ref, gate_ref, wmt, nf_ref, mx_ref, dot_ref, grad_refs):
    grad = tiled(gs_ref[...])
    for step in range(OWN_STEPS):
        backward(
            group, own_rows(step), grad, gate_ref, wmt, nf_ref, mx_ref, dot_ref, grad_refs
        )


def ghost_pairs(
    group, own_ref, table, new_ref, new_base, oh_gh, d_gh, dt_gh, gate_ref, radials, nw_ref,
    steps, wm, wmt, wo, wot, nf_s, mx_s, acc_in, acc_s, gs_ref, dot_ref, grad_refs, en_ref,
):
    norm = 1.0 / math.sqrt(SLOTS)
    acc_s[...] = acc_in[...]

    def ghost_forward(step):
        here, _ = ghost_rows(step)
        messages = forward(
            group, here, oh_gh[here, :], table[...], radials, gate_ref, wm, nf_s, mx_s, False
        )
        acc_s[...] += mm(dt_gh[:, here], jnp.concatenate(messages, axis=1))

    over_ghost_steps(steps, ghost_forward)

    begin = group_cols(group).start
    for cols, degrees, kind in infos_of(group):
        summed_low = (acc_s[:, cols] * norm).astype(BF16)
        own = own_ref[:, begin + cols.start : begin + cols.stop]
        updated = own.astype(F32) + mm(summed_low, wo[kind])
        at = begin - new_base + cols.start
        new_ref[:, at : at + 2 * CH] = updated.astype(BF16)
        weight = jnp.concatenate(
            [nw_ref[d - 1 : d, :] * (1.0 / (2 * d + 1)) for d in degrees], axis=1
        )
        scale = weight * updated
        energy = scale * updated
        en_ref[...] += energy[:, 0:CH] + energy[:, CH:]
        gs_ref[:, cols] = (mm((2.0 * scale).astype(BF16), wot[kind]) * norm).astype(BF16)

    def ghost_backward(step):
        here, _ = ghost_rows(step)
        grad = mm(d_gh[here, :], gs_ref[...]).astype(BF16)
        backward(group, here, grad, gate_ref, wmt, nf_s, mx_s, dot_ref, grad_refs)

    over_ghost_steps(steps, ghost_backward)


def pair_scratch(atoms, half, ghosts, group):
    count, width = len(KINDS[group]), GROUP_COLS[group]
    return (
        [pltpu.VMEM((ghosts, width), BF16), pltpu.SemaphoreType.DMA((7,))]
        + [pltpu.VMEM((count, 2 * CH, 2 * CH), BF16) for _ in range(4)]
        + [
            pltpu.VMEM((half, width), BF16),
            pltpu.VMEM((half, width), BF16),
            pltpu.VMEM((atoms, width), F32),
        ]
    )


def own_kernel(
    meta_ref, own_pos_ref, rbf_ref, rad_ref,
    oh_own, pre_ref, unit_ref, radt_ref, rbft_ref, home_ref, *radial_refs
):
    atoms = meta_ref.shape[0]
    nbasis = rbft_ref.shape[1]
    spacing = spacing_of(atoms, nbasis)
    own_onehots(meta_ref, oh_own)
    here = tiled(own_pos_ref[...].astype(F32))
    for step in range(OWN_STEPS):
        rows = own_rows(step)
        unit, dist = geometry(mm(oh_own[rows, :], own_pos_ref[...]), here)
        unit_ref[rows, :] = unit
        pre, radial = radial_net(dist, spacing, rbf_ref, rad_ref)
        pre_ref[rows, :] = pre.astype(BF16)
        for degree, ref in enumerate(radial_refs):
            ref[rows, :] = radial[:, degree * CH : (degree + 1) * CH]
    for degree in range(5):
        part = slice(degree * CH, (degree + 1) * CH)
        radt_ref[part, :] = flip(rad_ref[:, part])
    for index in range(nbasis // CH):
        part = slice(index * CH, (index + 1) * CH)
        rbft_ref[:, part] = flip(rbf_ref[part, :])
    lanes = home_ref.shape[1]
    lane = iota((atoms, lanes), 1)
    ext_x, ext_y, ext_z = lane // 128, lane // 32 % 4, lane // 8 % 4
    slot = ((2 * ext_x + ext_y - 1) * 2 + ext_z - 1) * 8 + lane % 8
    inside = jnp.logical_and(
        jnp.logical_or(ext_y == 1, ext_y == 2), jnp.logical_or(ext_z == 1, ext_z == 2)
    )
    to_slot = jnp.logical_and(iota((atoms, lanes), 0) == slot, inside)
    to_slot = to_slot.astype(F32).astype(BF16)
    order = meta_ref[:, SLOTS + 1 : SLOTS + 2]
    to_atom = (order == iota((atoms, atoms), 1).astype(F32)).astype(F32)
    home_ref[...] = mm(to_atom.T.astype(BF16), to_slot).astype(BF16)


def own_stage(meta, own_pos, rbf, rad):
    atoms = meta.shape[0]
    edges = atoms * HALF
    out_shape = (
        struct(edges, atoms, dtype=BF16),
        struct(edges, CH, dtype=BF16),
        struct(edges, CH),
        struct(5 * CH, CH, dtype=BF16),
        struct(CH, rbf.shape[0], dtype=BF16),
        struct(atoms, 256, dtype=BF16),
    ) + (struct(edges, CH, dtype=BF16),) * 5
    return call(own_kernel, "own_edges", out_shape, [], (meta, own_pos, rbf, rad))


def scalar_forward(rows, near, radial, mix_ref, m0_ref, gate_ref, nf0_ref):
    near = near.astype(BF16)
    nf0_ref[rows, :] = near
    mixed = mm(near * radial, mix_ref[0])
    m0_ref[rows, :] = mixed.astype(BF16)
    gate = jax.nn.sigmoid(mixed)
    gate_ref[rows, :] = gate.astype(BF16)
    return mixed * gate


def own_forward_kernel(groups, scalar, *refs):
    own_ref, mix_ref, oh_own, refs = *refs[:3], refs[3:]
    radial0, radials = refs[0], dict(enumerate(refs[1:5], start=1))
    refs = refs[5:]
    if scalar:
        m0_ref, gate_ref, nf0_ref, acc0_ref = refs[:4]
        refs = refs[4:]
        atoms = own_ref.shape[0]
        feats = own_ref[:, 0:CH]
        summed = None
        for step in range(OWN_STEPS):
            rows = own_rows(step)
            message = scalar_forward(
                rows, mm(oh_own[rows, :], feats), radial0[rows, :], mix_ref, m0_ref, gate_ref,
                nf0_ref,
            )
            part = over_slots(message, atoms)
            summed = part if summed is None else summed + part
        acc0_ref[...] = summed
    else:
        gate_ref, refs = refs[0], refs[1:]
    outs, weights = refs[: 3 * len(groups)], refs[3 * len(groups) :]
    for index, group in enumerate(groups):
        block_diagonal(KINDS[group], mix_ref, weights[index])
        nf_ref, mx_ref, acc_ref = outs[3 * index : 3 * index + 3]
        own_forward(
            group, own_ref, oh_own, radials, gate_ref, weights[index], nf_ref, mx_ref, acc_ref
        )


def own_forward_stage(groups, feats, mix, oh_own, radial_own, gate=None):
    atoms = feats.shape[0]
    half = atoms * HALF
    out_shape = ()
    if gate is None:
        out_shape += (struct(half, CH, dtype=BF16),) * 3 + (struct(atoms, CH),)
    for group in groups:
        width = GROUP_COLS[group]
        out_shape += (struct(half, width, dtype=BF16),) * 2 + (struct(atoms, width),)
    args = (feats, mix, oh_own, *radial_own) + (() if gate is None else (gate,))
    scratch = [pltpu.VMEM((len(KINDS[group]), 2 * CH, 2 * CH), BF16) for group in groups]
    name = "own_forward_" + "".join("abc"[group] for group in groups)
    kernel = functools.partial(own_forward_kernel, groups, gate is None)
    outs = call(kernel, name, out_shape, scratch, args)
    first = len(outs) - 3 * len(groups)
    return outs[:first], [outs[first + 3 * i : first + 3 * i + 3] for i in range(len(groups))]


def start_kernel(
    p0, p1, p2, p3, p4, own_ref, own_pos_ref, meta_ref, rbf_ref, rad_ref, mix_ref, out_ref, ew_ref,
    acc0_ref,
    new_ref, oh_gh, d_gh, dt_gh, pre_ref, unit_ref, gs0_ref, en_ref, m0_gh, gate_gh, nf0_gh,
    radial_gh1, radial_gh2, radial_gh3, radial_gh4,
    table, sems, ghpos, acc_s,
):
    radial_gh = (None, radial_gh1, radial_gh2, radial_gh3, radial_gh4)
    copies = fetch((p0, p1, p2, p3, p4), slice(0, 2 * CH), table, sems)
    atoms = own_ref.shape[0]
    ghosts = table.shape[0]
    spacing = spacing_of(atoms, rbf_ref.shape[0])
    norm = 1.0 / math.sqrt(SLOTS)

    live = live_ghosts(meta_ref)
    sub_atom = iota((atoms, atoms), 0)
    lane_atom = iota((atoms, atoms), 1)
    live_b = jnp.broadcast_to(live, (atoms, atoms))
    end_row = jnp.sum(jnp.where(sub_atom <= lane_atom, live_b, 0.0), axis=0, keepdims=True)
    live_row = jnp.sum(jnp.where(sub_atom == lane_atom, live_b, 0.0), axis=0, keepdims=True)
    start_row = end_row - live_row
    row_b = jnp.broadcast_to(live_row, (atoms, atoms))
    end_col = jnp.sum(jnp.where(lane_atom <= sub_atom, row_b, 0.0), axis=1, keepdims=True)
    start_col = end_col - live
    total = jnp.sum(live)
    steps = step_count(meta_ref)
    ghost_row = meta_ref[:, HALF:SLOTS] - atoms
    high_part = jnp.floor(ghost_row * (1.0 / 16.0))
    row_high = high_part.astype(BF16)
    row_low = (ghost_row - 16.0 * high_part).astype(BF16)

    row = iota((ghosts, CH), 0)
    lane = iota((ghosts, CH), 1)
    zcells = atoms // 32
    per_y = (zcells + 2) * 8
    ext_x = row // (4 * per_y)
    ext_y = row // per_y % 4
    ext_z = row // 8 % (zcells + 2)

    def side_of(ext, last, size):
        return jnp.where(ext == 0, -size, jnp.where(ext == last, size, 0.0))

    shift = jnp.where(lane == 12, side_of(ext_x, 3, 4.0), 0.0)
    shift = jnp.where(lane == 13, side_of(ext_y, 3, 4.0), shift)
    shift = jnp.where(lane == 14, side_of(ext_z, zcells + 1, 2.0 * zcells), shift)
    own0 = own_ref[:, 0:CH]
    acc_s[...] = acc0_ref[...]
    for copy in copies:
        copy.wait()
    ghpos[...] = (table[:, CH:].astype(F32) + shift).astype(BF16)

    def ghost_start(step):
        here, _ = ghost_rows(step)
        base = step * STEP
        edge = (iota((STEP, atoms), 0) + base).astype(F32)
        mine = jnp.logical_and(edge >= start_row, edge < end_row).astype(F32)
        source = mine.astype(BF16)
        d_gh[here, :] = source
        edge_t = (iota((atoms, STEP), 1) + base).astype(F32)
        mine_t = jnp.logical_and(edge_t >= start_col, edge_t < end_col)
        spread = mine_t.astype(F32).astype(BF16)
        dt_gh[:, here] = spread
        edge_col = edge[:, 0:1]
        slot = edge_col - jnp.sum(mine * start_row, axis=1, keepdims=True)
        listed = mm(source, row_high) * 16.0 + mm(source, row_low)
        at_slot = iota((STEP, HALF), 1).astype(F32) == slot
        which = jnp.sum(jnp.where(at_slot, listed, 0.0), axis=1, keepdims=True)
        which = jnp.where(edge_col < total, which, -1.0)
        onehot = (iota((STEP, ghosts), 1).astype(F32) == which).astype(F32).astype(BF16)
        oh_gh[here, :] = onehot
        unit, dist = geometry(mm(onehot, ghpos[...]), mm(source, own_pos_ref[...]))
        unit_ref[here, :] = unit
        pre, radial = radial_net(dist, spacing, rbf_ref, rad_ref)
        pre_ref[here, :] = pre.astype(BF16)
        for degree in range(1, 5):
            radial_gh[degree][here, :] = radial[:, degree * CH : (degree + 1) * CH]
        message = scalar_forward(
            here, mm(onehot, table[:, 0:CH]), radial[:, 0:CH], mix_ref, m0_gh, gate_gh, nf0_gh
        )
        acc_s[...] += mm(spread, message.astype(BF16))

    over_ghost_steps(steps, ghost_start)

    low0 = (acc_s[...] * norm).astype(BF16)
    updated0 = own0.astype(F32) + mm(low0, out_ref[0])
    new_ref[:, 0:CH] = updated0.astype(BF16)
    logistic = jax.nn.sigmoid(updated0)
    weight0 = ew_ref[...]
    en_ref[...] = weight0 * updated0 * logistic
    grad0 = (weight0 * logistic * (1.0 + updated0 * (1.0 - logistic))).astype(BF16)
    gs0_ref[...] = mm_nt(grad0, out_ref[0]) * norm


def any_specs(count, total):
    return [pl.BlockSpec(memory_space=pl.ANY)] * count + [
        pl.BlockSpec(memory_space=SPACE)
    ] * (total - count)


def start_stage(pieces, feats, *rest):
    atoms = feats.shape[0]
    half = atoms * HALF
    ghosts = sum(piece.shape[0] for piece in pieces)
    out_shape = (
        struct(atoms, CH, dtype=BF16),
        struct(half, ghosts, dtype=BF16),
        struct(half, atoms, dtype=BF16),
        struct(atoms, half, dtype=BF16),
        struct(half, CH, dtype=BF16),
        struct(half, CH),
        struct(atoms, CH),
        struct(atoms, CH),
    ) + (struct(half, CH, dtype=BF16),) * 7
    scratch = [
        pltpu.VMEM((ghosts, 2 * CH), BF16),
        pltpu.SemaphoreType.DMA((7,)),
        pltpu.VMEM((ghosts, CH), BF16),
        pltpu.VMEM((atoms, CH), F32),
    ]
    args = tuple(pieces) + (feats,) + rest
    return call(
        start_kernel, "ghost_start", out_shape, scratch, args,
        any_specs(len(pieces), len(args)), 24,
    )


def pairs_kernel(group, count, skip, *refs):
    pieces, refs = refs[:count], refs[count:]
    own_ref, meta_ref, mix_ref, out_ref, nw_ref, oh_gh, d_gh, dt_gh, gate_gh = refs[:9]
    gate_own, nf_own, mx_own, acc_own = refs[9:13]
    refs = refs[13:]
    degrees = DEGREES[group]
    radials, refs = dict(zip(degrees, refs)), refs[len(degrees) :]
    new_ref, en_ref, gs_ref, dot_gh = refs[:4]
    grads, refs = dict(zip(degrees, refs[4:])), refs[4 + len(degrees) :]
    if group == 0:
        dot_own, refs = refs[0], refs[1:]
        grads_own, refs = dict(zip(degrees, refs)), refs[len(degrees) :]
    table, sems, wm, wmt, wo, wot, nf_s, mx_s, acc_s = refs
    copies = fetch(pieces, slice(skip, skip + GROUP_COLS[group]), table, sems)
    block_diagonal(KINDS[group], mix_ref, wm, wmt)
    block_diagonal(KINDS[group], out_ref, wo, wot)
    en_ref[...] = jnp.zeros_like(en_ref)
    for copy in copies:
        copy.wait()
    ghost_pairs(
        group, own_ref, table, new_ref, group_cols(group).start, oh_gh, d_gh, dt_gh, gate_gh,
        radials, nw_ref, step_count(meta_ref), wm, wmt, wo, wot, nf_s, mx_s, acc_own, acc_s,
        gs_ref, dot_gh, grads, en_ref,
    )
    if group == 0:
        own_backward(group, gs_ref, gate_own, wmt, nf_own, mx_own, dot_own, grads_own)


def pairs_stage(group, skip, pieces, shared, own_parts, radial_gh):
    feats = shared[0]
    atoms = feats.shape[0]
    half = atoms * HALF
    ghosts = sum(piece.shape[0] for piece in pieces)
    degrees = DEGREES[group]
    sides = 2 if group == 0 else 1
    out_shape = (
        struct(atoms, GROUP_COLS[group], dtype=BF16),
        struct(atoms, CH),
        struct(atoms, GROUP_COLS[group], dtype=BF16),
    ) + (struct(half, CH, dtype=BF16),) * (sides * (1 + len(degrees)))
    args = tuple(pieces) + tuple(shared) + tuple(own_parts)
    args += tuple(radial_gh[degree - 1] for degree in degrees)
    new, energy, gs, *rest = call(
        functools.partial(pairs_kernel, group, len(pieces), skip), "pairs_" + "abc"[group],
        out_shape, pair_scratch(atoms, half, ghosts, group), args,
        any_specs(len(pieces), len(args)), 24,
    )
    return new, energy, gs, rest[: 1 + len(degrees)], rest[1 + len(degrees) :]


def own_backward_kernel(group, mix_ref, gs_ref, gate_ref, nf_ref, mx_ref, *refs):
    dot_ref, grads, wmt = refs[0], dict(zip(DEGREES[group], refs[1:-1])), refs[-1]
    block_diagonal(KINDS[group], mix_ref, None, wmt)
    own_backward(group, gs_ref, gate_ref, wmt, nf_ref, mx_ref, dot_ref, grads)


def own_backward_stage(group, mix, gs, gate, nf, mx):
    half = nf.shape[0]
    out_shape = (struct(half, CH, dtype=BF16),) * (1 + len(DEGREES[group]))
    scratch = [pltpu.VMEM((len(KINDS[group]), 2 * CH, 2 * CH), BF16)]
    kernel = functools.partial(own_backward_kernel, group)
    name = "own_backward_" + "abc"[group]
    return call(kernel, name, out_shape, scratch, (mix, gs, gate, nf, mx))


def finish(
    grad, mixed, near, dots, parts, pre, unit, spacing, radt_ref, rbft_ref, mix_t
):
    mixed = mixed.astype(F32)
    gate = jax.nn.sigmoid(mixed)
    first = grad * gate * (1.0 + mixed * (1.0 - gate)) + dots * gate * (1.0 - gate)
    weighted = mm(first.astype(BF16), mix_t) * near.astype(F32)
    radial_grad = jnp.concatenate([weighted.astype(BF16)] + parts, axis=1)
    hidden_grad = mm(radial_grad, radt_ref[...])
    pre = pre.astype(F32)
    logistic = jax.nn.sigmoid(pre)
    pre_grad = (hidden_grad * logistic * (1.0 + pre * (1.0 - logistic))).astype(BF16)
    centred = centred_of(unit[:, 3:4], spacing, rbft_ref.shape[1])
    slope = jnp.exp(-0.5 * centred * centred) * centred
    basis_grad = mm(pre_grad, rbft_ref[...])
    dist_grad = jnp.sum(basis_grad * slope, axis=1, keepdims=True) * (-1.0 / spacing)
    pull = unit * dist_grad
    across = pull.T[0:8, :]
    top = across.astype(BF16)
    rest = (across - top.astype(F32)).astype(BF16)
    return pull, top, rest


def sum_of(refs, rows):
    total = refs[0][rows, :].astype(F32)
    for ref in refs[1:]:
        total += ref[rows, :].astype(F32)
    return total


def degree_parts(refs, rows):
    by_degree = {}
    refs = list(refs)
    for degrees in DEGREES:
        for degree in degrees:
            by_degree.setdefault(degree, []).append(refs.pop(0))
    return [sum_of(by_degree[degree], rows).astype(BF16) for degree in range(1, 5)]


PARTIALS = sum(len(degrees) for degrees in DEGREES)


def third_kernel(
    p0, p1, p2, p3, p4, own_ref, meta_ref, mix_ref, out_ref, nw_ref, oh_gh, d_gh, dt_gh, gate_gh,
    acc_own, radt_ref, rbft_ref, gs0_ref, en_0, en_a, new_0, new_a, pre_gh, unit_gh,
    m0_ref, nf0_ref, dot_a, *refs
):
    group = 1
    before, degrees = len(DEGREES[0]), DEGREES[group]
    gr_a, refs = refs[:before], refs[before:]
    radials, refs = dict(zip(degrees, refs)), refs[len(degrees) :]
    new_ref, energy_ref, src_ref, onto_ref, flow_ref, fmid_ref, fhigh_ref, gs_ref = refs[:8]
    table, sems, wm, wmt, wo, wot, nf_s, mx_s, acc_s, dot_c, en_s, fgh_s = refs[8:20]
    grads = dict(zip(degrees, refs[20:]))
    copies = fetch((p0, p1, p2, p3, p4), slice(0, GROUP_COLS[group]), table, sems)
    atoms = own_ref.shape[0]
    spacing = spacing_of(atoms, rbft_ref.shape[1])
    block_diagonal(KINDS[group], mix_ref, wm, wmt)
    block_diagonal(KINDS[group], out_ref, wo, wot)
    en_s[...] = en_0[...] + en_a[...]
    at = 0
    for part in (new_0, new_a):
        new_ref[:, at : at + part.shape[1]] = part[...]
        at += part.shape[1]
    steps = step_count(meta_ref)

    for copy in copies:
        copy.wait()
    ghost_pairs(
        group, own_ref, table, new_ref, 0, oh_gh, d_gh, dt_gh, gate_gh, radials, nw_ref,
        steps, wm, wmt, wo, wot, nf_s, mx_s, acc_own, acc_s, gs_ref, dot_c, grads, en_s,
    )
    energy_ref[...] = jnp.sum(en_s[...].T, axis=0, keepdims=True)

    fgh_s[...] = jnp.zeros_like(fgh_s)
    src_ref[...] = jnp.zeros_like(src_ref)
    onto_ref[...] = jnp.zeros_like(onto_ref)
    gs0_low = gs0_ref[...].astype(BF16)
    mix_t = flip(mix_ref[0])

    def ghost_finish(step):
        here, _ = ghost_rows(step)
        grad = mm(d_gh[here, :], gs0_low)
        pull, top, rest = finish(
            grad, m0_ref[here, :], nf0_ref[here, :], sum_of((dot_a, dot_c), here),
            degree_parts(gr_a + refs[20:], here), pre_gh[here, :], unit_gh[here, :], spacing,
            radt_ref, rbft_ref, mix_t,
        )
        pull_top = pull.astype(BF16)
        pull_rest = (pull - pull_top.astype(F32)).astype(BF16)
        spread = dt_gh[:, here]
        src_ref[...] += mm(spread, pull_top) + mm(spread, pull_rest)
        onehot = oh_gh[here, :]
        fgh_s[...] += mm(top, onehot) + mm(rest, onehot)

    over_ghost_steps(steps, ghost_finish)
    low, mid = flow_ref.shape[1], fmid_ref.shape[1]
    flow_ref[...] = fgh_s[:, 0:low]
    fmid_ref[...] = fgh_s[:, low : low + mid]
    fhigh_ref[...] = fgh_s[:, low + mid :]


def third_stage(pieces, feats, *rest):
    atoms, feat = feats.shape
    half = atoms * HALF
    ghosts = sum(piece.shape[0] for piece in pieces)
    sizes = (ghosts // 4, ghosts // 2, ghosts // 4)
    out_shape = (
        struct(atoms, feat, dtype=BF16),
        struct(1, atoms),
        struct(atoms, CH),
        struct(8, atoms),
    ) + tuple(struct(8, size) for size in sizes) + (
        struct(atoms, GROUP_COLS[1], dtype=BF16),
    )
    scratch = pair_scratch(atoms, half, ghosts, 1) + [
        pltpu.VMEM((half, CH), BF16),
        pltpu.VMEM((atoms, CH), F32),
        pltpu.VMEM((8, ghosts), F32),
    ]
    scratch += [pltpu.VMEM((half, CH), BF16)] * len(DEGREES[1])
    args = tuple(pieces) + (feats,) + rest
    return call(
        third_kernel, "third_group", out_shape, scratch, args,
        any_specs(len(pieces), len(args)), 28,
    )


def own_back_kernel(
    steps, oh_own, pre_own, unit_own, radt_ref, rbft_ref, mix_ref, gs0_ref,
    m0_ref, nf0_ref, dot_a, dot_c, *refs
):
    gr_own, (src_in, onto_in, src_out, onto_out) = refs[:PARTIALS], refs[PARTIALS:]
    atoms = oh_own.shape[1]
    spacing = spacing_of(atoms, rbft_ref.shape[1])
    grad = tiled(gs0_ref[...])
    mix_t = flip(mix_ref[0])
    src = src_in[...]
    onto = onto_in[...]
    for step in steps:
        rows = own_rows(step)
        pull, top, rest = finish(
            grad, m0_ref[rows, :], nf0_ref[rows, :], sum_of((dot_a, dot_c), rows),
            degree_parts(gr_own, rows), pre_own[rows, :], unit_own[rows, :], spacing, radt_ref,
            rbft_ref, mix_t,
        )
        src += over_slots(pull, atoms)
        onehot = oh_own[rows, :]
        onto += mm(top, onehot) + mm(rest, onehot)
    src_out[...] = src
    onto_out[...] = onto


def own_back_stage(steps, *args):
    atoms = args[0].shape[1]
    out_shape = (struct(atoms, CH), struct(8, atoms))
    kernel = functools.partial(own_back_kernel, tuple(steps))
    return call(kernel, "own_back", out_shape, [], args)


def ring(axis):
    peers = lax.axis_size(axis)
    up = [(i, (i + 1) % peers) for i in range(peers)]
    return up, [(j, i) for i, j in up]


def neighbours_of(block, axis, dim):
    up, down = ring(axis)
    length = block.shape[dim]
    if len(up) == 2 and length == 2:
        other = lax.ppermute(block, axis, up)
        return (
            lax.slice_in_dim(other, length - 1, length, axis=dim),
            lax.slice_in_dim(other, 0, 1, axis=dim),
        )
    before = lax.ppermute(lax.slice_in_dim(block, length - 1, length, axis=dim), axis, up)
    after = lax.ppermute(lax.slice_in_dim(block, 0, 1, axis=dim), axis, down)
    return before, after


def grown(block, axis, dim):
    before, after = neighbours_of(block, axis, dim)
    return jnp.concatenate([before, block, after], axis=dim)


def ghost_pieces(along_y, block, along_x):
    outer = jnp.concatenate(along_y, axis=1)
    low_out, high_out = neighbours_of(outer, "gx", 0)
    low_in, high_in = along_x
    middle = jnp.concatenate([along_y[0], block, along_y[1]], axis=1)
    return tuple(flat_rows(piece) for piece in (low_in, low_out, middle, high_in, high_out))


def flat_rows(piece):
    return piece.reshape(-1, piece.shape[-1])


def fold_kernel(mid_ref, low_ref, high_ref, out_ref):
    lanes = mid_ref.shape[1]
    ext_y = iota(mid_ref.shape, 1) // 32 % 4
    out_ref[...] = (
        mid_ref[...]
        + jnp.where(ext_y == 1, pltpu.roll(low_ref[...], lanes - 64, 1), 0.0)
        + jnp.where(ext_y == 2, pltpu.roll(high_ref[...], 64, 1), 0.0)
    )


def forces_kernel(mid_ref, low_ref, high_ref, src_ref, onto_ref, home_ref, out_ref):
    values = mid_ref[...]
    lanes = values.shape[1]
    ext_z = iota(values.shape, 1) // 8 % 4
    values += jnp.where(ext_z == 1, pltpu.roll(low_ref[...], lanes - 16, 1), 0.0)
    values += jnp.where(ext_z == 2, pltpu.roll(high_ref[...], 16, 1), 0.0)
    first = values.astype(BF16)
    values -= first.astype(F32)
    second = values.astype(BF16)
    third = (values - second.astype(F32)).astype(BF16)
    home = home_ref[...]
    total = onto_ref[...] - src_ref[...].T[0:8, :]
    total += (mm_nt(first, home) + (mm_nt(second, home) + mm_nt(third, home)))
    for comp in range(3):
        out_ref[comp] = -total[comp : comp + 1, :]


def give_back_x(low, mid, high):
    up, down = ring("gx")
    from_low = lax.ppermute(high, "gx", up)
    from_high = lax.ppermute(low, "gx", down)
    return mid, jnp.concatenate([from_low, from_high], axis=1)


def give_back_y(mid):
    up, down = ring("gy")
    return mid, lax.ppermute(mid, "gy", up), lax.ppermute(mid, "gy", down)


def fold(*args):
    return call(fold_kernel, "fold", (struct(*args[0].shape),), [], args)[0]


def give_back_z(mid):
    up, down = ring("gz")
    from_low = lax.ppermute(mid, "gz", up)
    return mid, from_low, from_low if len(up) == 2 else lax.ppermute(mid, "gz", down)


def local(
    features,
    positions,
    neighbours,
    counts,
    cell_atoms,
    rbf_weight,
    radial_weight,
    mix_weight,
    out_weight,
    energy_weight,
    norm_weight,
):
    feats = features[0, 0, 0]
    places = jnp.swapaxes(positions[0, 0], 0, 1)
    lists = jnp.concatenate([neighbours[0, 0, 0].T, counts[0, 0], cell_atoms[0, 0]], axis=0)
    cells0, cells1, own_pos, meta = make_cells(feats, places, lists)
    hold = lax.optimization_barrier
    block0, block1 = (part.reshape(2, 2, 2, 8, part.shape[1]) for part in (cells0, cells1))
    z0 = neighbours_of(block0, "gz", 2)
    z1 = neighbours_of(block1, "gz", 2)
    oh_own, pre_own, unit_own, radt, rbft, home, *radial_own = own_stage(
        meta, own_pos, rbf_weight, radial_weight
    )
    z0, oh_own = hold((z0, oh_own))
    block0 = jnp.concatenate([z0[0], block0, z0[1]], axis=2)
    y0 = neighbours_of(block0, "gy", 1)
    x0_in = neighbours_of(block0, "gx", 0)
    (m0_own, gate_own, nf0_own, acc0), (own_a,) = own_forward_stage(
        (0,), feats, mix_weight, oh_own, radial_own
    )
    block1 = jnp.concatenate([z1[0], block1, z1[1]], axis=2)
    y0, x0_in, block1, acc0 = hold((y0, x0_in, block1, acc0))
    x0_out = neighbours_of(jnp.concatenate(y0, axis=1), "gx", 0)
    y1 = neighbours_of(block1, "gy", 1)
    x1_in = neighbours_of(block1, "gx", 0)
    _, (own_b,) = own_forward_stage((1,), feats, mix_weight, oh_own, radial_own, gate_own)
    x0_out, acc_b = hold((x0_out, own_b[2]))
    middle = jnp.concatenate([y0[0], block0, y0[1]], axis=1)
    pieces0 = (x0_in[0], x0_out[0], middle, x0_in[1], x0_out[1])
    pieces0 = tuple(flat_rows(piece) for piece in pieces0)
    (
        new_0, oh_gh, d_gh, dt_gh, pre_gh, unit_gh, gs0, en_0, m0_gh, gate_gh, nf0_gh, *radial_gh,
    ) = start_stage(
        pieces0, feats, own_pos, meta, rbf_weight, radial_weight, mix_weight, out_weight,
        energy_weight[None], acc0,
    )
    y1, gate_gh = hold((y1, gate_gh))
    pieces1 = ghost_pieces(y1, block1, x1_in)
    shared = (feats, meta, mix_weight, out_weight, norm_weight, oh_gh, d_gh, dt_gh, gate_gh)
    new_a, en_a, _, (dot_gh_a, *gr_gh_a), (dot_own_a, *gr_own_a) = pairs_stage(
        0, 2 * CH, pieces0, shared, (gate_own, *own_a), radial_gh
    )
    new, energy, src, onto, low, mid, high, gs_b = third_stage(
        pieces1, *shared, acc_b, radt, rbft, gs0, en_0, en_a, new_0, new_a, pre_gh,
        unit_gh, m0_gh, nf0_gh, dot_gh_a, *gr_gh_a,
        *[radial_gh[degree - 1] for degree in DEGREES[1]],
    )
    mid, arrived = give_back_x(low, mid, high)
    dot_own_b, *gr_own_b = own_backward_stage(1, mix_weight, gs_b, gate_own, *own_b[:2])
    arrived, gs0, dot_own_b = hold((arrived, gs0, dot_own_b))
    mid, from_low, from_high = give_back_y(mid + arrived)
    back = (oh_own, pre_own, unit_own, radt, rbft, mix_weight, gs0, m0_own, nf0_own)
    back += (dot_own_a, dot_own_b, *gr_own_a, *gr_own_b)
    src, onto = own_back_stage(range(2), *back, src, onto)
    from_low, from_high, src = hold((from_low, from_high, src))
    folded = give_back_z(fold(mid, from_low, from_high))
    src, onto = own_back_stage(range(2, 4), *back, src, onto)
    args = (*folded, src, onto, home)
    out_shape = (struct(3, 1, src.shape[0]),)
    forces = call(forces_kernel, "forces", out_shape, [], args)[0]
    return (
        new[None, None, None],
        energy[None, None],
        jnp.swapaxes(forces, 0, 1)[None, None],
    )


def solution(mesh):
    split = P("gx", "gy", "gz", None, None)
    flat = P("gx", "gy", "gz", None)
    return jax.shard_map(
        local,
        mesh=mesh,
        in_specs=(split, split, split, flat, flat, P(), P(), P(), P(), P(), P()),
        out_specs=(split, flat, split),
        check_vma=False,
    )
```

```python
import functools
import math

import jax
import jax.numpy as jnp
from jax import lax
from jax.experimental import pallas as pl
from jax.experimental.pallas import tpu as pltpu
from jax.sharding import PartitionSpec as P

F32 = jnp.float32
BF16 = jnp.bfloat16
CH = 128
SLOTS = 32
HALF = 16
STEP = 256
OWN_STEPS = 4
GH_STEPS = 2
MIB = 1024 * 1024
SPACE = pltpu.VMEM
PAIR_DEGREES = (
    (1, 1), (1, 2), (2, 2), (2, 2),
    (3, 3), (3, 3), (3, 3), (3, 4),
    (4, 4), (4, 4), (4, 4), (4, 4),
)
GROUPS = ((0, 4), (4, 12))
KINDS = tuple(sorted({PAIR_DEGREES[pair] for pair in range(*group)}) for group in GROUPS)
DEGREES = tuple(sorted({d for both in kinds for d in both}) for kinds in KINDS)
GROUP_COLS = tuple(2 * CH * (end - begin) for begin, end in GROUPS)


def mm(a, b):
    return jnp.dot(a, b, preferred_element_type=F32)


def mm_nt(a, b):
    return lax.dot_general(a, b, (((1,), (1,)), ((), ())), preferred_element_type=F32)


def iota(shape, dim):
    return lax.broadcasted_iota(jnp.int32, shape, dim)


def flip(w):
    return w.astype(F32).T.astype(BF16)


def pair_cols(pair):
    return slice(CH + pair * 2 * CH, CH + (pair + 1) * 2 * CH)


def struct(*shape, dtype=F32):
    return jax.ShapeDtypeStruct(shape, dtype)


def call(kernel, name, out_shape, scratch, args, specs=None, limit=16):
    return pl.pallas_call(
        kernel,
        out_shape=out_shape,
        in_specs=specs or [pl.BlockSpec(memory_space=SPACE)] * len(args),
        out_specs=tuple(pl.BlockSpec(memory_space=SPACE) for _ in out_shape),
        scratch_shapes=scratch,
        compiler_params=pltpu.CompilerParams(vmem_limit_bytes=limit * MIB),
        cost_estimate=pl.CostEstimate(flops=1024, bytes_accessed=1024, transcendentals=0),
        name=name,
    )(*args)


def cells_kernel(
    feat_ref, lists_ref,
    out_ref, own_pos_ref, meta_ref, pick_ref, rows_ref, pos_rows,
):
    rows_ref[...] = jnp.zeros_like(rows_ref)
    pos_rows[...] = jnp.zeros_like(pos_rows)
    atoms = feat_ref.shape[0]
    rows_ref[0 : SLOTS + 2, :] = lists_ref[0 : SLOTS + 2, :]
    meta = rows_ref[...].T
    meta_ref[...] = meta
    for comp in range(3):
        places = lists_ref[SLOTS + 2 + comp : SLOTS + 3 + comp, :]
        first = places.astype(BF16).astype(F32)
        second = (places - first).astype(BF16).astype(F32)
        pos_rows[comp : comp + 1, :] = first
        pos_rows[4 + comp : 5 + comp, :] = second
        pos_rows[8 + comp : 9 + comp, :] = places - first - second
    pieces = pos_rows[...].astype(BF16)
    lane = iota((atoms, atoms), 1).astype(F32)
    pick = (meta[:, SLOTS + 1 : SLOTS + 2] == lane).astype(F32).astype(BF16)
    same = (iota((atoms, atoms), 0) == iota((atoms, atoms), 1)).astype(F32).astype(BF16)
    own_pos_ref[...] = mm_nt(same, pieces).astype(BF16)
    out_ref[:, CH : 2 * CH] = mm_nt(pick, pieces).astype(BF16)
    pick_ref[...] = pick
    out_ref[:, 0:CH] = mm(pick, feat_ref[:, 0:CH]).astype(BF16)
    cut = pair_cols(GROUPS[1][0]).start
    out_ref[:, 2 * CH :] = mm(pick, feat_ref[:, CH:cut]).astype(BF16)


def rest_kernel(feat_ref, pick_ref, rest_ref):
    cut = pair_cols(GROUPS[1][0]).start
    rest_ref[...] = mm(pick_ref[...], feat_ref[:, cut:]).astype(BF16)


def make_cells(feats, lists):
    atoms = feats.shape[0]
    out_shape = (
        struct(atoms, 2 * CH + GROUP_COLS[0], dtype=BF16),
        struct(atoms, CH, dtype=BF16),
        struct(atoms, CH),
        struct(atoms, atoms, dtype=BF16),
    )
    args = (feats, lists)
    scratch = [pltpu.VMEM((CH, atoms), F32), pltpu.VMEM((CH, atoms), F32)]
    first, own_pos, meta, pick = call(cells_kernel, "cells", out_shape, scratch, args)
    out_shape = (struct(atoms, GROUP_COLS[1], dtype=BF16),)
    rest = call(rest_kernel, "cells_rest", out_shape, [], (feats, pick))[0]
    return first, rest, own_pos, meta


def spacing_of(atoms, nbasis):
    depth = atoms // 16
    return 2.0 * math.sqrt(32.0 + depth * depth) / (nbasis - 1)


def own_onehots(meta_ref, oh_own):
    atoms = meta_ref.shape[0]
    counts = meta_ref[:, SLOTS : SLOTS + 1]
    lane_atom = iota((atoms, atoms), 1).astype(F32)
    for slot in range(HALF):
        hit = jnp.logical_and(meta_ref[:, slot : slot + 1] == lane_atom, counts > slot)
        oh_own[slot * atoms : (slot + 1) * atoms, :] = hit.astype(F32).astype(BF16)


def geometry(near, here):
    diff = near - here
    rel = (diff + pltpu.roll(diff, CH - 4, 1)) + (
        pltpu.roll(diff, CH - 8, 1) + pltpu.roll(diff, CH - 12, 1)
    )
    lane = iota(rel.shape, 1)
    rel = jnp.where(lane < 3, rel, 0.0)
    square = jnp.sum(rel * rel, axis=1, keepdims=True)
    inverse = lax.rsqrt(jnp.where(square > 0.0, square, 1.0))
    dist = square * inverse
    return jnp.where(lane == 3, dist, rel * inverse), dist


def centred_of(dist, spacing, nbasis):
    return dist * (1.0 / spacing) - iota((dist.shape[0], nbasis), 1).astype(F32)


def radial_net(dist, spacing, rbf_ref, rad_ref):
    centred = centred_of(dist, spacing, rbf_ref.shape[0])
    basis = jnp.exp(-0.5 * centred * centred)
    pre = mm(basis.astype(BF16), rbf_ref[...])
    hidden = (pre * jax.nn.sigmoid(pre)).astype(BF16)
    return pre, mm(hidden, rad_ref[...]).astype(BF16)


def tiled(values, size=STEP):
    return jnp.concatenate([values] * (size // values.shape[0]), axis=0)


def live_ghosts(meta_ref):
    return jnp.maximum(meta_ref[:, SLOTS : SLOTS + 1] - HALF, 0.0)


def step_count(meta_ref):
    total = jnp.sum(live_ghosts(meta_ref)).astype(jnp.int32)
    rows = GH_STEPS * STEP
    return jnp.maximum((total + (rows - 1)) // rows, 1) * GH_STEPS


def own_rows(step, size=STEP):
    return pl.ds(step * size, size)


def ghost_rows(step, size=STEP):
    first = OWN_STEPS * STEP
    if isinstance(step, int):
        return pl.ds(step * size, size), pl.ds(first + step * size, size)
    base = pl.multiple_of(step * size, size)
    return pl.ds(base, size), pl.ds(pl.multiple_of(first + base, size), size)


def over_ghost_steps(steps, body, size=STEP):
    static = GH_STEPS * STEP // size
    for step in range(static):
        body(step)

    def again(step, carry):
        body(step)
        return carry

    lax.fori_loop(static, (steps * STEP + (size - 1)) // size, again, 0)


def block_diagonal(kinds, source, straight=None, across=None):
    zero = jnp.zeros((CH, CH), BF16)
    targets = [ref for ref in (straight, across) if ref is not None]
    for kind, both in enumerate(kinds):
        for ref in targets:
            ref[kind, 0:CH, CH:] = zero
            ref[kind, CH:, 0:CH] = zero
    for degree in sorted({d for both in kinds for d in both}):
        weight = source[degree]
        flipped = flip(weight) if across is not None else None
        for kind, both in enumerate(kinds):
            for side in range(2):
                if both[side] == degree:
                    part = slice(side * CH, side * CH + CH)
                    if straight is not None:
                        straight[kind, part, part] = weight
                    if across is not None:
                        across[kind, part, part] = flipped


def fetch(pieces, cols, table, sems):
    low, high, ghosts = 0, 0, table.shape[0]
    if len(pieces) == 3:
        rows = [(piece, 0, piece.shape[0]) for piece in pieces]
    else:
        low_in, low_out, mid, high_in, high_out = pieces
        half = low_out.shape[0] // 2
        rows = [(low_out, 0, half), (low_in, 0, low_in.shape[0]), (low_out, half, half)]
        rows += [(mid, 0, mid.shape[0])]
        rows += [(high_out, 0, half), (high_in, 0, high_in.shape[0]), (high_out, half, half)]
    copies = []
    at = 0
    for index, (piece, start, count) in enumerate(rows):
        source = piece.at[pl.ds(start, count), cols]
        target = table.at[pl.ds(at, count), :]
        copies.append(pltpu.make_async_copy(source, target, sems.at[index]))
        at += count
    for copy in copies:
        copy.start()
    return copies


def infos_of(group):
    infos = []
    for index, pair in enumerate(range(*GROUPS[group])):
        degrees = PAIR_DEGREES[pair]
        cols = slice(index * 2 * CH, (index + 1) * 2 * CH)
        infos.append((cols, degrees, KINDS[group].index(degrees)))
    return infos


def group_cols(group):
    begin, end = GROUPS[group]
    return slice(pair_cols(begin).start, pair_cols(end - 1).stop)


def twice(values):
    return jnp.concatenate([values, values], axis=1)


def forward(group, rows, onehot, feats, radials, gate_ref, wm, nf_ref, mx_ref, slots):
    near = mm(onehot, feats).astype(BF16)
    nf_ref[rows, :] = near
    gate = twice(gate_ref[rows, :])
    wide = gate.astype(F32) if slots else None
    messages = []
    for cols, degrees, kind in infos_of(group):
        radial = jnp.concatenate([radials[d][rows, :] for d in degrees], axis=1)
        mixed = mm(near[:, cols] * radial, wm[kind])
        low = mixed.astype(BF16)
        mx_ref[rows, cols] = low
        messages.append(mixed * wide if slots else low * gate)
    return messages


def backward(group, rows, grad, gate_ref, wmt, nf_ref, mx_ref, dot_ref, grad_refs):
    parts = {}
    dots = None
    gate = twice(gate_ref[rows, :])
    for cols, degrees, kind in infos_of(group):
        product = grad[:, cols] * mx_ref[rows, cols]
        dot = (product[:, 0:CH] + product[:, CH:]).astype(F32)
        dots = dot if dots is None else dots + dot
        weighted = mm(grad[:, cols] * gate, wmt[kind]) * nf_ref[rows, cols].astype(F32)
        for side in range(2):
            part = weighted[:, side * CH : (side + 1) * CH]
            degree = degrees[side]
            parts[degree] = parts[degree] + part if degree in parts else part
    dot_ref[rows, :] = dots.astype(dot_ref.dtype)
    for degree, part in parts.items():
        grad_refs[degree][rows, :] = part.astype(grad_refs[degree].dtype)


def over_slots(values, atoms):
    return jnp.sum(values.reshape(-1, atoms, values.shape[1]), axis=0)


def own_forward(group, own_ref, oh_own, radials, gate_ref, wm, nf_ref, mx_ref, acc_ref):
    atoms = own_ref.shape[0]
    feats = own_ref[:, group_cols(group)]
    for step in range(OWN_STEPS):
        rows = own_rows(step)
        messages = forward(
            group, rows, oh_own[rows, :], feats, radials, gate_ref, wm, nf_ref, mx_ref, True
        )
        for (cols, _, _), message in zip(infos_of(group), messages):
            part = over_slots(message, atoms)
            acc_ref[:, cols] = part if step == 0 else acc_ref[:, cols] + part


def own_backward(group, gs_ref, gate_ref, wmt, nf_ref, mx_ref, dot_ref, grad_refs):
    grad = tiled(gs_ref[...])
    for step in range(OWN_STEPS):
        backward(
            group, own_rows(step), grad, gate_ref, wmt, nf_ref, mx_ref, dot_ref, grad_refs
        )


def ghost_pairs(
    group, own_ref, table, new_ref, new_base, oh_gh, d_gh, dt_gh, gate_ref, radials, nw_ref,
    steps, wm, wmt, wo, wot, nf_s, mx_s, acc_in, acc_s, gs_ref, dot_ref, grad_refs, en_ref,
):
    norm = 1.0 / math.sqrt(SLOTS)
    acc_s[...] = acc_in[...]

    def ghost_forward(step):
        here, _ = ghost_rows(step)
        messages = forward(
            group, here, oh_gh[here, :], table[...], radials, gate_ref, wm, nf_s, mx_s, False
        )
        acc_s[...] += mm(dt_gh[:, here], jnp.concatenate(messages, axis=1))

    over_ghost_steps(steps, ghost_forward)

    begin = group_cols(group).start
    for cols, degrees, kind in infos_of(group):
        summed_low = (acc_s[:, cols] * norm).astype(BF16)
        own = own_ref[:, begin + cols.start : begin + cols.stop]
        updated = own.astype(F32) + mm(summed_low, wo[kind])
        at = begin - new_base + cols.start
        new_ref[:, at : at + 2 * CH] = updated.astype(BF16)
        weight = jnp.concatenate(
            [nw_ref[d - 1 : d, :] * (1.0 / (2 * d + 1)) for d in degrees], axis=1
        )
        scale = weight * updated
        energy = scale * updated
        en_ref[...] += energy[:, 0:CH] + energy[:, CH:]
        gs_ref[:, cols] = (mm((2.0 * scale).astype(BF16), wot[kind]) * norm).astype(BF16)

    def ghost_backward(step):
        here, _ = ghost_rows(step)
        grad = mm(d_gh[here, :], gs_ref[...]).astype(BF16)
        backward(group, here, grad, gate_ref, wmt, nf_s, mx_s, dot_ref, grad_refs)

    over_ghost_steps(steps, ghost_backward)


def pair_scratch(atoms, half, ghosts, group):
    count, width = len(KINDS[group]), GROUP_COLS[group]
    return (
        [pltpu.VMEM((ghosts, width), BF16), pltpu.SemaphoreType.DMA((7,))]
        + [pltpu.VMEM((count, 2 * CH, 2 * CH), BF16) for _ in range(4)]
        + [
            pltpu.VMEM((half, width), BF16),
            pltpu.VMEM((half, width), BF16),
            pltpu.VMEM((atoms, width), F32),
        ]
    )


def own_kernel(
    meta_ref, own_pos_ref, rbf_ref, rad_ref,
    oh_own, pre_ref, unit_ref, radt_ref, rbft_ref, home_ref, *radial_refs
):
    atoms = meta_ref.shape[0]
    nbasis = rbft_ref.shape[1]
    spacing = spacing_of(atoms, nbasis)
    own_onehots(meta_ref, oh_own)
    here = tiled(own_pos_ref[...].astype(F32))
    for step in range(OWN_STEPS):
        rows = own_rows(step)
        unit, dist = geometry(mm(oh_own[rows, :], own_pos_ref[...]), here)
        unit_ref[rows, :] = unit
        pre, radial = radial_net(dist, spacing, rbf_ref, rad_ref)
        pre_ref[rows, :] = pre.astype(BF16)
        for degree, ref in enumerate(radial_refs):
            ref[rows, :] = radial[:, degree * CH : (degree + 1) * CH]
    for degree in range(5):
        part = slice(degree * CH, (degree + 1) * CH)
        radt_ref[part, :] = flip(rad_ref[:, part])
    for index in range(nbasis // CH):
        part = slice(index * CH, (index + 1) * CH)
        rbft_ref[:, part] = flip(rbf_ref[part, :])
    lanes = home_ref.shape[1]
    lane = iota((atoms, lanes), 1)
    ext_x, ext_y, ext_z = lane // 128, lane // 32 % 4, lane // 8 % 4
    slot = ((2 * ext_x + ext_y - 1) * 2 + ext_z - 1) * 8 + lane % 8
    inside = jnp.logical_and(
        jnp.logical_or(ext_y == 1, ext_y == 2), jnp.logical_or(ext_z == 1, ext_z == 2)
    )
    to_slot = jnp.logical_and(iota((atoms, lanes), 0) == slot, inside)
    to_slot = to_slot.astype(F32).astype(BF16)
    order = meta_ref[:, SLOTS + 1 : SLOTS + 2]
    to_atom = (order == iota((atoms, atoms), 1).astype(F32)).astype(F32)
    home_ref[...] = mm(to_atom.T.astype(BF16), to_slot).astype(BF16)


def own_stage(meta, own_pos, rbf, rad):
    atoms = meta.shape[0]
    edges = atoms * HALF
    out_shape = (
        struct(edges, atoms, dtype=BF16),
        struct(edges, CH, dtype=BF16),
        struct(edges, CH),
        struct(5 * CH, CH, dtype=BF16),
        struct(CH, rbf.shape[0], dtype=BF16),
        struct(atoms, 256, dtype=BF16),
    ) + (struct(edges, CH, dtype=BF16),) * 5
    return call(own_kernel, "own_edges", out_shape, [], (meta, own_pos, rbf, rad))


def scalar_forward(rows, near, radial, mix_ref, m0_ref, gate_ref, nf0_ref):
    near = near.astype(BF16)
    nf0_ref[rows, :] = near
    mixed = mm(near * radial, mix_ref[0])
    m0_ref[rows, :] = mixed.astype(BF16)
    gate = jax.nn.sigmoid(mixed)
    gate_ref[rows, :] = gate.astype(BF16)
    return mixed * gate


def own_forward_kernel(groups, scalar, *refs):
    own_ref, mix_ref, oh_own, refs = *refs[:3], refs[3:]
    radial0, radials = refs[0], dict(enumerate(refs[1:5], start=1))
    refs = refs[5:]
    if scalar:
        m0_ref, gate_ref, nf0_ref, acc0_ref = refs[:4]
        refs = refs[4:]
        atoms = own_ref.shape[0]
        feats = own_ref[:, 0:CH]
        summed = None
        for step in range(OWN_STEPS):
            rows = own_rows(step)
            message = scalar_forward(
                rows, mm(oh_own[rows, :], feats), radial0[rows, :], mix_ref, m0_ref, gate_ref,
                nf0_ref,
            )
            part = over_slots(message, atoms)
            summed = part if summed is None else summed + part
        acc0_ref[...] = summed
    else:
        gate_ref, refs = refs[0], refs[1:]
    outs, weights = refs[: 3 * len(groups)], refs[3 * len(groups) :]
    for index, group in enumerate(groups):
        block_diagonal(KINDS[group], mix_ref, weights[index])
        nf_ref, mx_ref, acc_ref = outs[3 * index : 3 * index + 3]
        own_forward(
            group, own_ref, oh_own, radials, gate_ref, weights[index], nf_ref, mx_ref, acc_ref
        )


def own_forward_stage(groups, feats, mix, oh_own, radial_own, gate=None):
    atoms = feats.shape[0]
    half = atoms * HALF
    out_shape = ()
    if gate is None:
        out_shape += (struct(half, CH, dtype=BF16),) * 3 + (struct(atoms, CH),)
    for group in groups:
        width = GROUP_COLS[group]
        out_shape += (struct(half, width, dtype=BF16),) * 2 + (struct(atoms, width),)
    args = (feats, mix, oh_own, *radial_own) + (() if gate is None else (gate,))
    scratch = [pltpu.VMEM((len(KINDS[group]), 2 * CH, 2 * CH), BF16) for group in groups]
    name = "own_forward_" + "".join("abc"[group] for group in groups)
    kernel = functools.partial(own_forward_kernel, groups, gate is None)
    outs = call(kernel, name, out_shape, scratch, args)
    first = len(outs) - 3 * len(groups)
    return outs[:first], [outs[first + 3 * i : first + 3 * i + 3] for i in range(len(groups))]


def start_kernel(
    p0, p1, p2, own_ref, own_pos_ref, meta_ref, rbf_ref, rad_ref, mix_ref, out_ref, ew_ref,
    acc0_ref,
    new_ref, oh_gh, d_gh, dt_gh, pre_ref, unit_ref, gs0_ref, en_ref, m0_gh, gate_gh, nf0_gh,
    radial_gh1, radial_gh2, radial_gh3, radial_gh4,
    table, sems, ghpos, acc_s,
):
    radial_gh = (None, radial_gh1, radial_gh2, radial_gh3, radial_gh4)
    copies = fetch((p0, p1, p2), slice(0, 2 * CH), table, sems)
    atoms = own_ref.shape[0]
    ghosts = table.shape[0]
    spacing = spacing_of(atoms, rbf_ref.shape[0])
    norm = 1.0 / math.sqrt(SLOTS)

    live = live_ghosts(meta_ref)
    sub_atom = iota((atoms, atoms), 0)
    lane_atom = iota((atoms, atoms), 1)
    live_b = jnp.broadcast_to(live, (atoms, atoms))
    end_row = jnp.sum(jnp.where(sub_atom <= lane_atom, live_b, 0.0), axis=0, keepdims=True)
    live_row = jnp.sum(jnp.where(sub_atom == lane_atom, live_b, 0.0), axis=0, keepdims=True)
    start_row = end_row - live_row
    row_b = jnp.broadcast_to(live_row, (atoms, atoms))
    end_col = jnp.sum(jnp.where(lane_atom <= sub_atom, row_b, 0.0), axis=1, keepdims=True)
    start_col = end_col - live
    total = jnp.sum(live)
    steps = step_count(meta_ref)
    ghost_row = meta_ref[:, HALF:SLOTS] - atoms
    high_part = jnp.floor(ghost_row * (1.0 / 16.0))
    row_high = high_part.astype(BF16)
    row_low = (ghost_row - 16.0 * high_part).astype(BF16)

    row = iota((ghosts, CH), 0)
    lane = iota((ghosts, CH), 1)
    zcells = atoms // 32
    per_y = (zcells + 2) * 8
    ext_x = row // (4 * per_y)
    ext_y = row // per_y % 4
    ext_z = row // 8 % (zcells + 2)

    def side_of(ext, last, size):
        return jnp.where(ext == 0, -size, jnp.where(ext == last, size, 0.0))

    shift = jnp.where(lane == 12, side_of(ext_x, 3, 4.0), 0.0)
    shift = jnp.where(lane == 13, side_of(ext_y, 3, 4.0), shift)
    shift = jnp.where(lane == 14, side_of(ext_z, zcells + 1, 2.0 * zcells), shift)
    own0 = own_ref[:, 0:CH]
    acc_s[...] = acc0_ref[...]
    for copy in copies:
        copy.wait()
    ghpos[...] = (table[:, CH:].astype(F32) + shift).astype(BF16)

    def ghost_start(step):
        here, _ = ghost_rows(step)
        base = step * STEP
        edge = (iota((STEP, atoms), 0) + base).astype(F32)
        mine = jnp.logical_and(edge >= start_row, edge < end_row).astype(F32)
        source = mine.astype(BF16)
        d_gh[here, :] = source
        edge_t = (iota((atoms, STEP), 1) + base).astype(F32)
        mine_t = jnp.logical_and(edge_t >= start_col, edge_t < end_col)
        spread = mine_t.astype(F32).astype(BF16)
        dt_gh[:, here] = spread
        edge_col = edge[:, 0:1]
        slot = edge_col - jnp.sum(mine * start_row, axis=1, keepdims=True)
        listed = mm(source, row_high) * 16.0 + mm(source, row_low)
        at_slot = iota((STEP, HALF), 1).astype(F32) == slot
        which = jnp.sum(jnp.where(at_slot, listed, 0.0), axis=1, keepdims=True)
        which = jnp.where(edge_col < total, which, -1.0)
        onehot = (iota((STEP, ghosts), 1).astype(F32) == which).astype(F32).astype(BF16)
        oh_gh[here, :] = onehot
        unit, dist = geometry(mm(onehot, ghpos[...]), mm(source, own_pos_ref[...]))
        unit_ref[here, :] = unit
        pre, radial = radial_net(dist, spacing, rbf_ref, rad_ref)
        pre_ref[here, :] = pre.astype(BF16)
        for degree in range(1, 5):
            radial_gh[degree][here, :] = radial[:, degree * CH : (degree + 1) * CH]
        message = scalar_forward(
            here, mm(onehot, table[:, 0:CH]), radial[:, 0:CH], mix_ref, m0_gh, gate_gh, nf0_gh
        )
        acc_s[...] += mm(spread, message.astype(BF16))

    over_ghost_steps(steps, ghost_start)

    low0 = (acc_s[...] * norm).astype(BF16)
    updated0 = own0.astype(F32) + mm(low0, out_ref[0])
    new_ref[:, 0:CH] = updated0.astype(BF16)
    logistic = jax.nn.sigmoid(updated0)
    weight0 = ew_ref[...]
    en_ref[...] = weight0 * updated0 * logistic
    grad0 = (weight0 * logistic * (1.0 + updated0 * (1.0 - logistic))).astype(BF16)
    gs0_ref[...] = mm_nt(grad0, out_ref[0]) * norm


def any_specs(count, total):
    return [pl.BlockSpec(memory_space=pl.ANY)] * count + [
        pl.BlockSpec(memory_space=SPACE)
    ] * (total - count)


def start_stage(pieces, feats, *rest):
    atoms = feats.shape[0]
    half = atoms * HALF
    ghosts = sum(piece.shape[0] for piece in pieces)
    out_shape = (
        struct(atoms, CH, dtype=BF16),
        struct(half, ghosts, dtype=BF16),
        struct(half, atoms, dtype=BF16),
        struct(atoms, half, dtype=BF16),
        struct(half, CH, dtype=BF16),
        struct(half, CH),
        struct(atoms, CH),
        struct(atoms, CH),
    ) + (struct(half, CH, dtype=BF16),) * 7
    scratch = [
        pltpu.VMEM((ghosts, 2 * CH), BF16),
        pltpu.SemaphoreType.DMA((7,)),
        pltpu.VMEM((ghosts, CH), BF16),
        pltpu.VMEM((atoms, CH), F32),
    ]
    args = tuple(pieces) + (feats,) + rest
    return call(
        start_kernel, "ghost_start", out_shape, scratch, args,
        any_specs(len(pieces), len(args)), 24,
    )


def pairs_kernel(group, count, skip, *refs):
    pieces, refs = refs[:count], refs[count:]
    own_ref, meta_ref, mix_ref, out_ref, nw_ref, oh_gh, d_gh, dt_gh, gate_gh = refs[:9]
    gate_own, nf_own, mx_own, acc_own = refs[9:13]
    refs = refs[13:]
    degrees = DEGREES[group]
    radials, refs = dict(zip(degrees, refs)), refs[len(degrees) :]
    new_ref, en_ref, gs_ref, dot_gh = refs[:4]
    grads, refs = dict(zip(degrees, refs[4:])), refs[4 + len(degrees) :]
    if group == 0:
        dot_own, refs = refs[0], refs[1:]
        grads_own, refs = dict(zip(degrees, refs)), refs[len(degrees) :]
    table, sems, wm, wmt, wo, wot, nf_s, mx_s, acc_s = refs
    copies = fetch(pieces, slice(skip, skip + GROUP_COLS[group]), table, sems)
    block_diagonal(KINDS[group], mix_ref, wm, wmt)
    block_diagonal(KINDS[group], out_ref, wo, wot)
    en_ref[...] = jnp.zeros_like(en_ref)
    for copy in copies:
        copy.wait()
    ghost_pairs(
        group, own_ref, table, new_ref, group_cols(group).start, oh_gh, d_gh, dt_gh, gate_gh,
        radials, nw_ref, step_count(meta_ref), wm, wmt, wo, wot, nf_s, mx_s, acc_own, acc_s,
        gs_ref, dot_gh, grads, en_ref,
    )
    if group == 0:
        own_backward(group, gs_ref, gate_own, wmt, nf_own, mx_own, dot_own, grads_own)


def pairs_stage(group, skip, pieces, shared, own_parts, radial_gh):
    feats = shared[0]
    atoms = feats.shape[0]
    half = atoms * HALF
    ghosts = sum(piece.shape[0] for piece in pieces)
    degrees = DEGREES[group]
    sides = 2 if group == 0 else 1
    out_shape = (
        struct(atoms, GROUP_COLS[group], dtype=BF16),
        struct(atoms, CH),
        struct(atoms, GROUP_COLS[group], dtype=BF16),
    ) + (struct(half, CH, dtype=BF16),) * (sides * (1 + len(degrees)))
    args = tuple(pieces) + tuple(shared) + tuple(own_parts)
    args += tuple(radial_gh[degree - 1] for degree in degrees)
    new, energy, gs, *rest = call(
        functools.partial(pairs_kernel, group, len(pieces), skip), "pairs_" + "abc"[group],
        out_shape, pair_scratch(atoms, half, ghosts, group), args,
        any_specs(len(pieces), len(args)), 24,
    )
    return new, energy, gs, rest[: 1 + len(degrees)], rest[1 + len(degrees) :]


def own_backward_kernel(group, mix_ref, gs_ref, gate_ref, nf_ref, mx_ref, *refs):
    dot_ref, grads, wmt = refs[0], dict(zip(DEGREES[group], refs[1:-1])), refs[-1]
    block_diagonal(KINDS[group], mix_ref, None, wmt)
    own_backward(group, gs_ref, gate_ref, wmt, nf_ref, mx_ref, dot_ref, grads)


def own_backward_stage(group, mix, gs, gate, nf, mx):
    half = nf.shape[0]
    out_shape = (struct(half, CH, dtype=BF16),) * (1 + len(DEGREES[group]))
    scratch = [pltpu.VMEM((len(KINDS[group]), 2 * CH, 2 * CH), BF16)]
    kernel = functools.partial(own_backward_kernel, group)
    name = "own_backward_" + "abc"[group]
    return call(kernel, name, out_shape, scratch, (mix, gs, gate, nf, mx))


def finish(
    grad, mixed, near, dots, parts, pre, unit, spacing, radt_ref, rbft_ref, mix_t
):
    mixed = mixed.astype(F32)
    gate = jax.nn.sigmoid(mixed)
    first = grad * gate * (1.0 + mixed * (1.0 - gate)) + dots * gate * (1.0 - gate)
    weighted = mm(first.astype(BF16), mix_t) * near.astype(F32)
    radial_grad = jnp.concatenate([weighted.astype(BF16)] + parts, axis=1)
    hidden_grad = mm(radial_grad, radt_ref[...])
    pre = pre.astype(F32)
    logistic = jax.nn.sigmoid(pre)
    pre_grad = (hidden_grad * logistic * (1.0 + pre * (1.0 - logistic))).astype(BF16)
    centred = centred_of(unit[:, 3:4], spacing, rbft_ref.shape[1])
    slope = jnp.exp(-0.5 * centred * centred) * centred
    basis_grad = mm(pre_grad, rbft_ref[...])
    dist_grad = jnp.sum(basis_grad * slope, axis=1, keepdims=True) * (-1.0 / spacing)
    pull = unit * dist_grad
    across = pull.T[0:8, :]
    top = across.astype(BF16)
    rest = (across - top.astype(F32)).astype(BF16)
    return pull, top, rest


def sum_of(refs, rows):
    total = refs[0][rows, :].astype(F32)
    for ref in refs[1:]:
        total += ref[rows, :].astype(F32)
    return total


def degree_parts(refs, rows):
    by_degree = {}
    refs = list(refs)
    for degrees in DEGREES:
        for degree in degrees:
            by_degree.setdefault(degree, []).append(refs.pop(0))
    return [sum_of(by_degree[degree], rows).astype(BF16) for degree in range(1, 5)]


PARTIALS = sum(len(degrees) for degrees in DEGREES)


def third_kernel(
    p0, p1, p2, own_ref, meta_ref, mix_ref, out_ref, nw_ref, oh_gh, d_gh, dt_gh, gate_gh, acc_own,
    radt_ref, rbft_ref, gs0_ref, en_0, en_a, new_0, new_a, pre_gh, unit_gh,
    m0_ref, nf0_ref, dot_a, *refs
):
    group = 1
    before, degrees = len(DEGREES[0]), DEGREES[group]
    gr_a, refs = refs[:before], refs[before:]
    radials, refs = dict(zip(degrees, refs)), refs[len(degrees) :]
    new_ref, energy_ref, src_ref, onto_ref, flow_ref, fmid_ref, fhigh_ref, gs_ref = refs[:8]
    table, sems, wm, wmt, wo, wot, nf_s, mx_s, acc_s, dot_c, en_s, fgh_s = refs[8:20]
    grads = dict(zip(degrees, refs[20:]))
    copies = fetch((p0, p1, p2), slice(0, GROUP_COLS[group]), table, sems)
    atoms = own_ref.shape[0]
    spacing = spacing_of(atoms, rbft_ref.shape[1])
    block_diagonal(KINDS[group], mix_ref, wm, wmt)
    block_diagonal(KINDS[group], out_ref, wo, wot)
    en_s[...] = en_0[...] + en_a[...]
    at = 0
    for part in (new_0, new_a):
        new_ref[:, at : at + part.shape[1]] = part[...]
        at += part.shape[1]
    steps = step_count(meta_ref)

    for copy in copies:
        copy.wait()
    ghost_pairs(
        group, own_ref, table, new_ref, 0, oh_gh, d_gh, dt_gh, gate_gh, radials, nw_ref,
        steps, wm, wmt, wo, wot, nf_s, mx_s, acc_own, acc_s, gs_ref, dot_c, grads, en_s,
    )
    energy_ref[...] = jnp.sum(en_s[...].T, axis=0, keepdims=True)

    fgh_s[...] = jnp.zeros_like(fgh_s)
    src_ref[...] = jnp.zeros_like(src_ref)
    onto_ref[...] = jnp.zeros_like(onto_ref)
    gs0_low = gs0_ref[...].astype(BF16)
    mix_t = flip(mix_ref[0])

    def ghost_finish(step):
        here, _ = ghost_rows(step)
        grad = mm(d_gh[here, :], gs0_low)
        pull, top, rest = finish(
            grad, m0_ref[here, :], nf0_ref[here, :], sum_of((dot_a, dot_c), here),
            degree_parts(gr_a + refs[20:], here), pre_gh[here, :], unit_gh[here, :], spacing,
            radt_ref, rbft_ref, mix_t,
        )
        pull_top = pull.astype(BF16)
        pull_rest = (pull - pull_top.astype(F32)).astype(BF16)
        spread = dt_gh[:, here]
        src_ref[...] += mm(spread, pull_top) + mm(spread, pull_rest)
        onehot = oh_gh[here, :]
        fgh_s[...] += mm(top, onehot) + mm(rest, onehot)

    over_ghost_steps(steps, ghost_finish)
    low, mid = flow_ref.shape[1], fmid_ref.shape[1]
    flow_ref[...] = fgh_s[:, 0:low]
    fmid_ref[...] = fgh_s[:, low : low + mid]
    fhigh_ref[...] = fgh_s[:, low + mid :]


def third_stage(pieces, feats, *rest):
    atoms, feat = feats.shape
    half = atoms * HALF
    ghosts = sum(piece.shape[0] for piece in pieces)
    sizes = (ghosts // 4, ghosts // 2, ghosts // 4)
    out_shape = (
        struct(atoms, feat, dtype=BF16),
        struct(1, atoms),
        struct(atoms, CH),
        struct(8, atoms),
    ) + tuple(struct(8, size) for size in sizes) + (
        struct(atoms, GROUP_COLS[1], dtype=BF16),
    )
    scratch = pair_scratch(atoms, half, ghosts, 1) + [
        pltpu.VMEM((half, CH), BF16),
        pltpu.VMEM((atoms, CH), F32),
        pltpu.VMEM((8, ghosts), F32),
    ]
    scratch += [pltpu.VMEM((half, CH), BF16)] * len(DEGREES[1])
    args = tuple(pieces) + (feats,) + rest
    return call(
        third_kernel, "third_group", out_shape, scratch, args,
        any_specs(len(pieces), len(args)), 28,
    )


def own_back_kernel(
    steps, oh_own, pre_own, unit_own, radt_ref, rbft_ref, mix_ref, gs0_ref,
    m0_ref, nf0_ref, dot_a, dot_c, *refs
):
    gr_own, (src_in, onto_in, src_out, onto_out) = refs[:PARTIALS], refs[PARTIALS:]
    atoms = oh_own.shape[1]
    spacing = spacing_of(atoms, rbft_ref.shape[1])
    grad = tiled(gs0_ref[...])
    mix_t = flip(mix_ref[0])
    src = src_in[...]
    onto = onto_in[...]
    for step in steps:
        rows = own_rows(step)
        pull, top, rest = finish(
            grad, m0_ref[rows, :], nf0_ref[rows, :], sum_of((dot_a, dot_c), rows),
            degree_parts(gr_own, rows), pre_own[rows, :], unit_own[rows, :], spacing, radt_ref,
            rbft_ref, mix_t,
        )
        src += over_slots(pull, atoms)
        onehot = oh_own[rows, :]
        onto += mm(top, onehot) + mm(rest, onehot)
    src_out[...] = src
    onto_out[...] = onto


def own_back_stage(steps, *args):
    atoms = args[0].shape[1]
    out_shape = (struct(atoms, CH), struct(8, atoms))
    kernel = functools.partial(own_back_kernel, tuple(steps))
    return call(kernel, "own_back", out_shape, [], args)


def ring(axis):
    peers = lax.axis_size(axis)
    up = [(i, (i + 1) % peers) for i in range(peers)]
    return up, [(j, i) for i, j in up]


def neighbours_of(block, axis, dim):
    up, down = ring(axis)
    length = block.shape[dim]
    if len(up) == 2 and length == 2:
        other = lax.ppermute(block, axis, up)
        return (
            lax.slice_in_dim(other, length - 1, length, axis=dim),
            lax.slice_in_dim(other, 0, 1, axis=dim),
        )
    before = lax.ppermute(lax.slice_in_dim(block, length - 1, length, axis=dim), axis, up)
    after = lax.ppermute(lax.slice_in_dim(block, 0, 1, axis=dim), axis, down)
    return before, after


def grown(block, axis, dim):
    before, after = neighbours_of(block, axis, dim)
    return jnp.concatenate([before, block, after], axis=dim)


def flat_rows(piece):
    return piece.reshape(-1, piece.shape[-1])


def fold_kernel(mid_ref, low_ref, high_ref, out_ref):
    lanes = mid_ref.shape[1]
    ext_y = iota(mid_ref.shape, 1) // 32 % 4
    out_ref[...] = (
        mid_ref[...]
        + jnp.where(ext_y == 1, pltpu.roll(low_ref[...], lanes - 64, 1), 0.0)
        + jnp.where(ext_y == 2, pltpu.roll(high_ref[...], 64, 1), 0.0)
    )


def forces_kernel(mid_ref, low_ref, high_ref, src_ref, onto_ref, home_ref, out_ref):
    values = mid_ref[...]
    lanes = values.shape[1]
    ext_z = iota(values.shape, 1) // 8 % 4
    values += jnp.where(ext_z == 1, pltpu.roll(low_ref[...], lanes - 16, 1), 0.0)
    values += jnp.where(ext_z == 2, pltpu.roll(high_ref[...], 16, 1), 0.0)
    first = values.astype(BF16)
    values -= first.astype(F32)
    second = values.astype(BF16)
    third = (values - second.astype(F32)).astype(BF16)
    home = home_ref[...]
    total = onto_ref[...] - src_ref[...].T[0:8, :]
    total += (mm_nt(first, home) + (mm_nt(second, home) + mm_nt(third, home)))
    for comp in range(3):
        out_ref[comp] = -total[comp : comp + 1, :]


def give_back_x(low, mid, high):
    up, down = ring("gx")
    from_low = lax.ppermute(high, "gx", up)
    from_high = lax.ppermute(low, "gx", down)
    return mid, jnp.concatenate([from_low, from_high], axis=1)


def give_back_y(mid):
    up, down = ring("gy")
    return mid, lax.ppermute(mid, "gy", up), lax.ppermute(mid, "gy", down)


def fold(*args):
    return call(fold_kernel, "fold", (struct(*args[0].shape),), [], args)[0]


def give_back_z(mid):
    up, down = ring("gz")
    from_low = lax.ppermute(mid, "gz", up)
    return mid, from_low, from_low if len(up) == 2 else lax.ppermute(mid, "gz", down)


def local(
    features,
    positions,
    neighbours,
    counts,
    cell_atoms,
    rbf_weight,
    radial_weight,
    mix_weight,
    out_weight,
    energy_weight,
    norm_weight,
):
    feats = features[0, 0, 0]
    lists = (neighbours[0, 0, 0].T, counts[0, 0], cell_atoms[0, 0])
    lists = jnp.concatenate([*(part.astype(F32) for part in lists), positions[0, 0, 0]], axis=0)
    cells0, cells1, own_pos, meta = make_cells(feats, lists)
    hold = lax.optimization_barrier
    block0, block1 = (part.reshape(2, 2, 2, 8, part.shape[1]) for part in (cells0, cells1))
    z0 = neighbours_of(block0, "gz", 2)
    z1 = neighbours_of(block1, "gz", 2)
    y1_in = neighbours_of(block1, "gy", 1)
    z0, own_pos, meta = hold((z0, own_pos, meta))
    block0 = jnp.concatenate([z0[0], block0, z0[1]], axis=2)
    y0 = neighbours_of(block0, "gy", 1)
    oh_own, pre_own, unit_own, radt, rbft, home, *radial_own = own_stage(
        meta, own_pos, rbf_weight, radial_weight
    )
    y0, z1, y1_in, oh_own = hold((y0, z1, y1_in, oh_own))
    middle = jnp.concatenate([y0[0], block0, y0[1]], axis=1)
    x0 = neighbours_of(middle, "gx", 0)
    y1_out = neighbours_of(jnp.concatenate(z1, axis=2), "gy", 1)
    (m0_own, gate_own, nf0_own, acc0), (own_a,) = own_forward_stage(
        (0,), feats, mix_weight, oh_own, radial_own
    )
    x0, y1_out, acc0 = hold((x0, y1_out, acc0))
    pieces0 = tuple(flat_rows(piece) for piece in (x0[0], middle, x0[1]))
    low, high = [
        jnp.concatenate([out[:, :, 0:1], inner, out[:, :, 1:2]], axis=2)
        for out, inner in zip(y1_out, y1_in)
    ]
    block1 = jnp.concatenate([z1[0], block1, z1[1]], axis=2)
    block1 = jnp.concatenate([low, block1, high], axis=1)
    low, high = neighbours_of(block1, "gx", 0)
    pieces1 = tuple(flat_rows(piece) for piece in (low, block1, high))
    (
        new_0, oh_gh, d_gh, dt_gh, pre_gh, unit_gh, gs0, en_0, m0_gh, gate_gh, nf0_gh, *radial_gh,
    ) = start_stage(
        pieces0, feats, own_pos, meta, rbf_weight, radial_weight, mix_weight, out_weight,
        energy_weight[None], acc0,
    )
    _, (own_b,) = own_forward_stage((1,), feats, mix_weight, oh_own, radial_own, gate_own)
    shared = (feats, meta, mix_weight, out_weight, norm_weight, oh_gh, d_gh, dt_gh, gate_gh)
    new_a, en_a, _, (dot_gh_a, *gr_gh_a), (dot_own_a, *gr_own_a) = pairs_stage(
        0, 2 * CH, pieces0, shared, (gate_own, *own_a), radial_gh
    )
    new, energy, src, onto, low, mid, high, gs_b = third_stage(
        pieces1, *shared, own_b[2], radt, rbft, gs0, en_0, en_a, new_0, new_a, pre_gh,
        unit_gh, m0_gh, nf0_gh, dot_gh_a, *gr_gh_a,
        *[radial_gh[degree - 1] for degree in DEGREES[1]],
    )
    mid, arrived = give_back_x(low, mid, high)
    dot_own_b, *gr_own_b = own_backward_stage(1, mix_weight, gs_b, gate_own, *own_b[:2])
    arrived, gs0, dot_own_b = hold((arrived, gs0, dot_own_b))
    mid, from_low, from_high = give_back_y(mid + arrived)
    back = (oh_own, pre_own, unit_own, radt, rbft, mix_weight, gs0, m0_own, nf0_own)
    back += (dot_own_a, dot_own_b, *gr_own_a, *gr_own_b)
    src, onto = own_back_stage(range(2), *back, src, onto)
    from_low, from_high, src = hold((from_low, from_high, src))
    folded = give_back_z(fold(mid, from_low, from_high))
    src, onto = own_back_stage(range(2, 4), *back, src, onto)
    args = (*folded, src, onto, home)
    out_shape = (struct(3, 1, src.shape[0]),)
    forces = call(forces_kernel, "forces", out_shape, [], args)[0]
    return (
        new[None, None, None],
        energy[None, None],
        jnp.swapaxes(forces, 0, 1)[None, None],
    )


def solution(mesh):
    split = P("gx", "gy", "gz", None, None)
    flat = P("gx", "gy", "gz", None)
    return jax.shard_map(
        local,
        mesh=mesh,
        in_specs=(split, split, split, flat, flat, P(), P(), P(), P(), P(), P()),
        out_specs=(split, flat, split),
        check_vma=False,
    )
```

```python
import functools
import math

import jax
import jax.numpy as jnp
from jax import lax
from jax.experimental import pallas as pl
from jax.experimental.pallas import tpu as pltpu
from jax.sharding import PartitionSpec as P

F32 = jnp.float32
BF16 = jnp.bfloat16
CH = 128
SLOTS = 32
HALF = 16
STEP = 256
OWN_STEPS = 4
GH_STEPS = 2
MIB = 1024 * 1024
SPACE = pltpu.VMEM
PAIR_DEGREES = (
    (1, 1), (1, 2), (2, 2), (2, 2),
    (3, 3), (3, 3), (3, 3), (3, 4),
    (4, 4), (4, 4), (4, 4), (4, 4),
)
GROUPS = ((0, 4), (4, 12))
KINDS = tuple(sorted({PAIR_DEGREES[pair] for pair in range(*group)}) for group in GROUPS)
DEGREES = tuple(sorted({d for both in kinds for d in both}) for kinds in KINDS)
GROUP_COLS = tuple(2 * CH * (end - begin) for begin, end in GROUPS)


def mm(a, b):
    return jnp.dot(a, b, preferred_element_type=F32)


def mm_nt(a, b):
    return lax.dot_general(a, b, (((1,), (1,)), ((), ())), preferred_element_type=F32)


def iota(shape, dim):
    return lax.broadcasted_iota(jnp.int32, shape, dim)


def flip(w):
    return w.astype(F32).T.astype(BF16)


def pair_cols(pair):
    return slice(CH + pair * 2 * CH, CH + (pair + 1) * 2 * CH)


def struct(*shape, dtype=F32):
    return jax.ShapeDtypeStruct(shape, dtype)


def call(kernel, name, out_shape, scratch, args, specs=None, limit=16):
    return pl.pallas_call(
        kernel,
        out_shape=out_shape,
        in_specs=specs or [pl.BlockSpec(memory_space=SPACE)] * len(args),
        out_specs=tuple(pl.BlockSpec(memory_space=SPACE) for _ in out_shape),
        scratch_shapes=scratch,
        compiler_params=pltpu.CompilerParams(vmem_limit_bytes=limit * MIB),
        cost_estimate=pl.CostEstimate(flops=1024, bytes_accessed=1024, transcendentals=0),
        name=name,
    )(*args)


def cells_kernel(
    feat_ref, pos_ref, lists_ref,
    out_ref, own_pos_ref, meta_ref, pick_ref, rows_ref, pos_rows,
):
    rows_ref[...] = jnp.zeros_like(rows_ref)
    pos_rows[...] = jnp.zeros_like(pos_rows)
    atoms = feat_ref.shape[0]
    rows_ref[0 : SLOTS + 2, :] = lists_ref[...].astype(F32)
    meta = rows_ref[...].T
    meta_ref[...] = meta
    for comp in range(3):
        places = pos_ref[comp]
        first = places.astype(BF16).astype(F32)
        second = (places - first).astype(BF16).astype(F32)
        pos_rows[comp : comp + 1, :] = first
        pos_rows[4 + comp : 5 + comp, :] = second
        pos_rows[8 + comp : 9 + comp, :] = places - first - second
    pieces = pos_rows[...].astype(BF16)
    lane = iota((atoms, atoms), 1).astype(F32)
    pick = (meta[:, SLOTS + 1 : SLOTS + 2] == lane).astype(F32).astype(BF16)
    same = (iota((atoms, atoms), 0) == iota((atoms, atoms), 1)).astype(F32).astype(BF16)
    own_pos_ref[...] = mm_nt(same, pieces).astype(BF16)
    out_ref[:, CH : 2 * CH] = mm_nt(pick, pieces).astype(BF16)
    pick_ref[...] = pick
    out_ref[:, 0:CH] = mm(pick, feat_ref[:, 0:CH]).astype(BF16)
    cut = pair_cols(GROUPS[1][0]).start
    out_ref[:, 2 * CH :] = mm(pick, feat_ref[:, CH:cut]).astype(BF16)


def rest_kernel(feat_ref, pick_ref, rest_ref):
    cut = pair_cols(GROUPS[1][0]).start
    rest_ref[...] = mm(pick_ref[...], feat_ref[:, cut:]).astype(BF16)


def make_cells(feats, places, lists):
    atoms = feats.shape[0]
    out_shape = (
        struct(atoms, 2 * CH + GROUP_COLS[0], dtype=BF16),
        struct(atoms, CH, dtype=BF16),
        struct(atoms, CH),
        struct(atoms, atoms, dtype=BF16),
    )
    args = (feats, places, lists)
    scratch = [pltpu.VMEM((CH, atoms), F32), pltpu.VMEM((CH, atoms), F32)]
    first, own_pos, meta, pick = call(cells_kernel, "cells", out_shape, scratch, args)
    out_shape = (struct(atoms, GROUP_COLS[1], dtype=BF16),)
    rest = call(rest_kernel, "cells_rest", out_shape, [], (feats, pick))[0]
    return first, rest, own_pos, meta


def spacing_of(atoms, nbasis):
    depth = atoms // 16
    return 2.0 * math.sqrt(32.0 + depth * depth) / (nbasis - 1)


def own_onehots(meta_ref, oh_own):
    atoms = meta_ref.shape[0]
    counts = meta_ref[:, SLOTS : SLOTS + 1]
    lane_atom = iota((atoms, atoms), 1).astype(F32)
    for slot in range(HALF):
        hit = jnp.logical_and(meta_ref[:, slot : slot + 1] == lane_atom, counts > slot)
        oh_own[slot * atoms : (slot + 1) * atoms, :] = hit.astype(F32).astype(BF16)


def geometry(near, here):
    diff = near - here
    rel = (diff + pltpu.roll(diff, CH - 4, 1)) + (
        pltpu.roll(diff, CH - 8, 1) + pltpu.roll(diff, CH - 12, 1)
    )
    lane = iota(rel.shape, 1)
    rel = jnp.where(lane < 3, rel, 0.0)
    square = jnp.sum(rel * rel, axis=1, keepdims=True)
    inverse = lax.rsqrt(jnp.where(square > 0.0, square, 1.0))
    dist = square * inverse
    return jnp.where(lane == 3, dist, rel * inverse), dist


def centred_of(dist, spacing, nbasis):
    return dist * (1.0 / spacing) - iota((dist.shape[0], nbasis), 1).astype(F32)


def radial_net(dist, spacing, rbf_ref, rad_ref):
    centred = centred_of(dist, spacing, rbf_ref.shape[0])
    basis = jnp.exp(-0.5 * centred * centred)
    pre = mm(basis.astype(BF16), rbf_ref[...])
    hidden = (pre * jax.nn.sigmoid(pre)).astype(BF16)
    return pre, mm(hidden, rad_ref[...]).astype(BF16)


def tiled(values, size=STEP):
    return jnp.concatenate([values] * (size // values.shape[0]), axis=0)


def live_ghosts(meta_ref):
    return jnp.maximum(meta_ref[:, SLOTS : SLOTS + 1] - HALF, 0.0)


def step_count(meta_ref):
    total = jnp.sum(live_ghosts(meta_ref)).astype(jnp.int32)
    rows = GH_STEPS * STEP
    return jnp.maximum((total + (rows - 1)) // rows, 1) * GH_STEPS


def own_rows(step, size=STEP):
    return pl.ds(step * size, size)


def ghost_rows(step, size=STEP):
    first = OWN_STEPS * STEP
    if isinstance(step, int):
        return pl.ds(step * size, size), pl.ds(first + step * size, size)
    base = pl.multiple_of(step * size, size)
    return pl.ds(base, size), pl.ds(pl.multiple_of(first + base, size), size)


def over_ghost_steps(steps, body, size=STEP):
    static = GH_STEPS * STEP // size
    for step in range(static):
        body(step)

    def again(step, carry):
        body(step)
        return carry

    lax.fori_loop(static, (steps * STEP + (size - 1)) // size, again, 0)


def block_diagonal(kinds, source, straight=None, across=None):
    zero = jnp.zeros((CH, CH), BF16)
    targets = [ref for ref in (straight, across) if ref is not None]
    for kind, both in enumerate(kinds):
        for ref in targets:
            ref[kind, 0:CH, CH:] = zero
            ref[kind, CH:, 0:CH] = zero
    for degree in sorted({d for both in kinds for d in both}):
        weight = source[degree]
        flipped = flip(weight) if across is not None else None
        for kind, both in enumerate(kinds):
            for side in range(2):
                if both[side] == degree:
                    part = slice(side * CH, side * CH + CH)
                    if straight is not None:
                        straight[kind, part, part] = weight
                    if across is not None:
                        across[kind, part, part] = flipped


def fetch(pieces, cols, table, sems):
    low, high, ghosts = 0, 0, table.shape[0]
    if len(pieces) == 3:
        rows = [(piece, 0, piece.shape[0]) for piece in pieces]
    else:
        low_in, low_out, mid, high_in, high_out = pieces
        half = low_out.shape[0] // 2
        rows = [(low_out, 0, half), (low_in, 0, low_in.shape[0]), (low_out, half, half)]
        rows += [(mid, 0, mid.shape[0])]
        rows += [(high_out, 0, half), (high_in, 0, high_in.shape[0]), (high_out, half, half)]
    copies = []
    at = 0
    for index, (piece, start, count) in enumerate(rows):
        source = piece.at[pl.ds(start, count), cols]
        target = table.at[pl.ds(at, count), :]
        copies.append(pltpu.make_async_copy(source, target, sems.at[index]))
        at += count
    for copy in copies:
        copy.start()
    return copies


def infos_of(group):
    infos = []
    for index, pair in enumerate(range(*GROUPS[group])):
        degrees = PAIR_DEGREES[pair]
        cols = slice(index * 2 * CH, (index + 1) * 2 * CH)
        infos.append((cols, degrees, KINDS[group].index(degrees)))
    return infos


def group_cols(group):
    begin, end = GROUPS[group]
    return slice(pair_cols(begin).start, pair_cols(end - 1).stop)


def twice(values):
    return jnp.concatenate([values, values], axis=1)


def forward(group, rows, onehot, feats, radials, gate_ref, wm, nf_ref, mx_ref, slots):
    near = mm(onehot, feats).astype(BF16)
    nf_ref[rows, :] = near
    gate = twice(gate_ref[rows, :])
    wide = gate.astype(F32) if slots else None
    messages = []
    for cols, degrees, kind in infos_of(group):
        radial = jnp.concatenate([radials[d][rows, :] for d in degrees], axis=1)
        mixed = mm(near[:, cols] * radial, wm[kind])
        low = mixed.astype(BF16)
        mx_ref[rows, cols] = low
        messages.append(mixed * wide if slots else low * gate)
    return messages


def backward(group, rows, grad, gate_ref, wmt, nf_ref, mx_ref, dot_ref, grad_refs):
    parts = {}
    dots = None
    gate = twice(gate_ref[rows, :])
    for cols, degrees, kind in infos_of(group):
        product = grad[:, cols] * mx_ref[rows, cols]
        dot = (product[:, 0:CH] + product[:, CH:]).astype(F32)
        dots = dot if dots is None else dots + dot
        weighted = mm(grad[:, cols] * gate, wmt[kind]) * nf_ref[rows, cols].astype(F32)
        for side in range(2):
            part = weighted[:, side * CH : (side + 1) * CH]
            degree = degrees[side]
            parts[degree] = parts[degree] + part if degree in parts else part
    dot_ref[rows, :] = dots.astype(dot_ref.dtype)
    for degree, part in parts.items():
        grad_refs[degree][rows, :] = part.astype(grad_refs[degree].dtype)


def over_slots(values, atoms):
    return jnp.sum(values.reshape(-1, atoms, values.shape[1]), axis=0)


def own_forward(group, own_ref, oh_own, radials, gate_ref, wm, nf_ref, mx_ref, acc_ref):
    atoms = own_ref.shape[0]
    feats = own_ref[:, group_cols(group)]
    for step in range(OWN_STEPS):
        rows = own_rows(step)
        messages = forward(
            group, rows, oh_own[rows, :], feats, radials, gate_ref, wm, nf_ref, mx_ref, True
        )
        for (cols, _, _), message in zip(infos_of(group), messages):
            part = over_slots(message, atoms)
            acc_ref[:, cols] = part if step == 0 else acc_ref[:, cols] + part


def own_backward(group, gs_ref, gate_ref, wmt, nf_ref, mx_ref, dot_ref, grad_refs):
    grad = tiled(gs_ref[...])
    for step in range(OWN_STEPS):
        backward(
            group, own_rows(step), grad, gate_ref, wmt, nf_ref, mx_ref, dot_ref, grad_refs
        )


def ghost_pairs(
    group, own_ref, table, new_ref, new_base, oh_gh, d_gh, dt_gh, gate_ref, radials, nw_ref,
    steps, wm, wmt, wo, wot, nf_s, mx_s, acc_in, acc_s, gs_ref, dot_ref, grad_refs, en_ref,
):
    norm = 1.0 / math.sqrt(SLOTS)
    acc_s[...] = acc_in[...]

    def ghost_forward(step):
        here, _ = ghost_rows(step)
        messages = forward(
            group, here, oh_gh[here, :], table[...], radials, gate_ref, wm, nf_s, mx_s, False
        )
        acc_s[...] += mm(dt_gh[:, here], jnp.concatenate(messages, axis=1))

    over_ghost_steps(steps, ghost_forward)

    begin = group_cols(group).start
    for cols, degrees, kind in infos_of(group):
        summed_low = (acc_s[:, cols] * norm).astype(BF16)
        own = own_ref[:, begin + cols.start : begin + cols.stop]
        updated = own.astype(F32) + mm(summed_low, wo[kind])
        at = begin - new_base + cols.start
        new_ref[:, at : at + 2 * CH] = updated.astype(BF16)
        weight = jnp.concatenate(
            [nw_ref[d - 1 : d, :] * (1.0 / (2 * d + 1)) for d in degrees], axis=1
        )
        scale = weight * updated
        energy = scale * updated
        en_ref[...] += energy[:, 0:CH] + energy[:, CH:]
        gs_ref[:, cols] = (mm((2.0 * scale).astype(BF16), wot[kind]) * norm).astype(BF16)

    def ghost_backward(step):
        here, _ = ghost_rows(step)
        grad = mm(d_gh[here, :], gs_ref[...]).astype(BF16)
        backward(group, here, grad, gate_ref, wmt, nf_s, mx_s, dot_ref, grad_refs)

    over_ghost_steps(steps, ghost_backward)


def pair_scratch(atoms, half, ghosts, group):
    count, width = len(KINDS[group]), GROUP_COLS[group]
    return (
        [pltpu.VMEM((ghosts, width), BF16), pltpu.SemaphoreType.DMA((7,))]
        + [pltpu.VMEM((count, 2 * CH, 2 * CH), BF16) for _ in range(4)]
        + [
            pltpu.VMEM((half, width), BF16),
            pltpu.VMEM((half, width), BF16),
            pltpu.VMEM((atoms, width), F32),
        ]
    )


def own_kernel(
    meta_ref, own_pos_ref, rbf_ref, rad_ref,
    oh_own, pre_ref, unit_ref, radt_ref, rbft_ref, home_ref, *radial_refs
):
    atoms = meta_ref.shape[0]
    nbasis = rbft_ref.shape[1]
    spacing = spacing_of(atoms, nbasis)
    own_onehots(meta_ref, oh_own)
    here = tiled(own_pos_ref[...].astype(F32))
    for step in range(OWN_STEPS):
        rows = own_rows(step)
        unit, dist = geometry(mm(oh_own[rows, :], own_pos_ref[...]), here)
        unit_ref[rows, :] = unit
        pre, radial = radial_net(dist, spacing, rbf_ref, rad_ref)
        pre_ref[rows, :] = pre.astype(BF16)
        for degree, ref in enumerate(radial_refs):
            ref[rows, :] = radial[:, degree * CH : (degree + 1) * CH]
    for degree in range(5):
        part = slice(degree * CH, (degree + 1) * CH)
        radt_ref[part, :] = flip(rad_ref[:, part])
    for index in range(nbasis // CH):
        part = slice(index * CH, (index + 1) * CH)
        rbft_ref[:, part] = flip(rbf_ref[part, :])
    lanes = home_ref.shape[1]
    lane = iota((atoms, lanes), 1)
    ext_x, ext_y, ext_z = lane // 128, lane // 32 % 4, lane // 8 % 4
    slot = ((2 * ext_x + ext_y - 1) * 2 + ext_z - 1) * 8 + lane % 8
    inside = jnp.logical_and(
        jnp.logical_or(ext_y == 1, ext_y == 2), jnp.logical_or(ext_z == 1, ext_z == 2)
    )
    to_slot = jnp.logical_and(iota((atoms, lanes), 0) == slot, inside)
    to_slot = to_slot.astype(F32).astype(BF16)
    order = meta_ref[:, SLOTS + 1 : SLOTS + 2]
    to_atom = (order == iota((atoms, atoms), 1).astype(F32)).astype(F32)
    home_ref[...] = mm(to_atom.T.astype(BF16), to_slot).astype(BF16)


def own_stage(meta, own_pos, rbf, rad):
    atoms = meta.shape[0]
    edges = atoms * HALF
    out_shape = (
        struct(edges, atoms, dtype=BF16),
        struct(edges, CH, dtype=BF16),
        struct(edges, CH),
        struct(5 * CH, CH, dtype=BF16),
        struct(CH, rbf.shape[0], dtype=BF16),
        struct(atoms, 256, dtype=BF16),
    ) + (struct(edges, CH, dtype=BF16),) * 5
    return call(own_kernel, "own_edges", out_shape, [], (meta, own_pos, rbf, rad))


def scalar_forward(rows, near, radial, mix_ref, m0_ref, gate_ref, nf0_ref):
    near = near.astype(BF16)
    nf0_ref[rows, :] = near
    mixed = mm(near * radial, mix_ref[0])
    m0_ref[rows, :] = mixed.astype(BF16)
    gate = jax.nn.sigmoid(mixed)
    gate_ref[rows, :] = gate.astype(BF16)
    return mixed * gate


def own_forward_kernel(groups, scalar, *refs):
    own_ref, mix_ref, oh_own, refs = *refs[:3], refs[3:]
    radial0, radials = refs[0], dict(enumerate(refs[1:5], start=1))
    refs = refs[5:]
    if scalar:
        m0_ref, gate_ref, nf0_ref, acc0_ref = refs[:4]
        refs = refs[4:]
        atoms = own_ref.shape[0]
        feats = own_ref[:, 0:CH]
        summed = None
        for step in range(OWN_STEPS):
            rows = own_rows(step)
            message = scalar_forward(
                rows, mm(oh_own[rows, :], feats), radial0[rows, :], mix_ref, m0_ref, gate_ref,
                nf0_ref,
            )
            part = over_slots(message, atoms)
            summed = part if summed is None else summed + part
        acc0_ref[...] = summed
    else:
        gate_ref, refs = refs[0], refs[1:]
    outs, weights = refs[: 3 * len(groups)], refs[3 * len(groups) :]
    for index, group in enumerate(groups):
        block_diagonal(KINDS[group], mix_ref, weights[index])
        nf_ref, mx_ref, acc_ref = outs[3 * index : 3 * index + 3]
        own_forward(
            group, own_ref, oh_own, radials, gate_ref, weights[index], nf_ref, mx_ref, acc_ref
        )


def own_forward_stage(groups, feats, mix, oh_own, radial_own, gate=None):
    atoms = feats.shape[0]
    half = atoms * HALF
    out_shape = ()
    if gate is None:
        out_shape += (struct(half, CH, dtype=BF16),) * 3 + (struct(atoms, CH),)
    for group in groups:
        width = GROUP_COLS[group]
        out_shape += (struct(half, width, dtype=BF16),) * 2 + (struct(atoms, width),)
    args = (feats, mix, oh_own, *radial_own) + (() if gate is None else (gate,))
    scratch = [pltpu.VMEM((len(KINDS[group]), 2 * CH, 2 * CH), BF16) for group in groups]
    name = "own_forward_" + "".join("abc"[group] for group in groups)
    kernel = functools.partial(own_forward_kernel, groups, gate is None)
    outs = call(kernel, name, out_shape, scratch, args)
    first = len(outs) - 3 * len(groups)
    return outs[:first], [outs[first + 3 * i : first + 3 * i + 3] for i in range(len(groups))]


def start_kernel(
    p0, p1, p2, own_ref, own_pos_ref, meta_ref, rbf_ref, rad_ref, mix_ref, out_ref, ew_ref,
    acc0_ref,
    new_ref, oh_gh, d_gh, dt_gh, pre_ref, unit_ref, gs0_ref, en_ref, m0_gh, gate_gh, nf0_gh,
    radial_gh1, radial_gh2, radial_gh3, radial_gh4,
    table, sems, ghpos, acc_s,
):
    radial_gh = (None, radial_gh1, radial_gh2, radial_gh3, radial_gh4)
    copies = fetch((p0, p1, p2), slice(0, 2 * CH), table, sems)
    atoms = own_ref.shape[0]
    ghosts = table.shape[0]
    spacing = spacing_of(atoms, rbf_ref.shape[0])
    norm = 1.0 / math.sqrt(SLOTS)

    live = live_ghosts(meta_ref)
    sub_atom = iota((atoms, atoms), 0)
    lane_atom = iota((atoms, atoms), 1)
    live_b = jnp.broadcast_to(live, (atoms, atoms))
    end_row = jnp.sum(jnp.where(sub_atom <= lane_atom, live_b, 0.0), axis=0, keepdims=True)
    live_row = jnp.sum(jnp.where(sub_atom == lane_atom, live_b, 0.0), axis=0, keepdims=True)
    start_row = end_row - live_row
    row_b = jnp.broadcast_to(live_row, (atoms, atoms))
    end_col = jnp.sum(jnp.where(lane_atom <= sub_atom, row_b, 0.0), axis=1, keepdims=True)
    start_col = end_col - live
    total = jnp.sum(live)
    steps = step_count(meta_ref)
    ghost_row = meta_ref[:, HALF:SLOTS] - atoms
    high_part = jnp.floor(ghost_row * (1.0 / 16.0))
    row_high = high_part.astype(BF16)
    row_low = (ghost_row - 16.0 * high_part).astype(BF16)

    row = iota((ghosts, CH), 0)
    lane = iota((ghosts, CH), 1)
    zcells = atoms // 32
    per_y = (zcells + 2) * 8
    ext_x = row // (4 * per_y)
    ext_y = row // per_y % 4
    ext_z = row // 8 % (zcells + 2)

    def side_of(ext, last, size):
        return jnp.where(ext == 0, -size, jnp.where(ext == last, size, 0.0))

    shift = jnp.where(lane == 12, side_of(ext_x, 3, 4.0), 0.0)
    shift = jnp.where(lane == 13, side_of(ext_y, 3, 4.0), shift)
    shift = jnp.where(lane == 14, side_of(ext_z, zcells + 1, 2.0 * zcells), shift)
    own0 = own_ref[:, 0:CH]
    acc_s[...] = acc0_ref[...]
    for copy in copies:
        copy.wait()
    ghpos[...] = (table[:, CH:].astype(F32) + shift).astype(BF16)

    def ghost_start(step):
        here, _ = ghost_rows(step)
        base = step * STEP
        edge = (iota((STEP, atoms), 0) + base).astype(F32)
        mine = jnp.logical_and(edge >= start_row, edge < end_row).astype(F32)
        source = mine.astype(BF16)
        d_gh[here, :] = source
        edge_t = (iota((atoms, STEP), 1) + base).astype(F32)
        mine_t = jnp.logical_and(edge_t >= start_col, edge_t < end_col)
        spread = mine_t.astype(F32).astype(BF16)
        dt_gh[:, here] = spread
        edge_col = edge[:, 0:1]
        slot = edge_col - jnp.sum(mine * start_row, axis=1, keepdims=True)
        listed = mm(source, row_high) * 16.0 + mm(source, row_low)
        at_slot = iota((STEP, HALF), 1).astype(F32) == slot
        which = jnp.sum(jnp.where(at_slot, listed, 0.0), axis=1, keepdims=True)
        which = jnp.where(edge_col < total, which, -1.0)
        onehot = (iota((STEP, ghosts), 1).astype(F32) == which).astype(F32).astype(BF16)
        oh_gh[here, :] = onehot
        unit, dist = geometry(mm(onehot, ghpos[...]), mm(source, own_pos_ref[...]))
        unit_ref[here, :] = unit
        pre, radial = radial_net(dist, spacing, rbf_ref, rad_ref)
        pre_ref[here, :] = pre.astype(BF16)
        for degree in range(1, 5):
            radial_gh[degree][here, :] = radial[:, degree * CH : (degree + 1) * CH]
        message = scalar_forward(
            here, mm(onehot, table[:, 0:CH]), radial[:, 0:CH], mix_ref, m0_gh, gate_gh, nf0_gh
        )
        acc_s[...] += mm(spread, message.astype(BF16))

    over_ghost_steps(steps, ghost_start)

    low0 = (acc_s[...] * norm).astype(BF16)
    updated0 = own0.astype(F32) + mm(low0, out_ref[0])
    new_ref[:, 0:CH] = updated0.astype(BF16)
    logistic = jax.nn.sigmoid(updated0)
    weight0 = ew_ref[...]
    en_ref[...] = weight0 * updated0 * logistic
    grad0 = (weight0 * logistic * (1.0 + updated0 * (1.0 - logistic))).astype(BF16)
    gs0_ref[...] = mm_nt(grad0, out_ref[0]) * norm


def any_specs(count, total):
    return [pl.BlockSpec(memory_space=pl.ANY)] * count + [
        pl.BlockSpec(memory_space=SPACE)
    ] * (total - count)


def start_stage(pieces, feats, *rest):
    atoms = feats.shape[0]
    half = atoms * HALF
    ghosts = sum(piece.shape[0] for piece in pieces)
    out_shape = (
        struct(atoms, CH, dtype=BF16),
        struct(half, ghosts, dtype=BF16),
        struct(half, atoms, dtype=BF16),
        struct(atoms, half, dtype=BF16),
        struct(half, CH, dtype=BF16),
        struct(half, CH),
        struct(atoms, CH),
        struct(atoms, CH),
    ) + (struct(half, CH, dtype=BF16),) * 7
    scratch = [
        pltpu.VMEM((ghosts, 2 * CH), BF16),
        pltpu.SemaphoreType.DMA((7,)),
        pltpu.VMEM((ghosts, CH), BF16),
        pltpu.VMEM((atoms, CH), F32),
    ]
    args = tuple(pieces) + (feats,) + rest
    return call(
        start_kernel, "ghost_start", out_shape, scratch, args,
        any_specs(len(pieces), len(args)), 24,
    )


def pairs_kernel(group, count, skip, *refs):
    pieces, refs = refs[:count], refs[count:]
    own_ref, meta_ref, mix_ref, out_ref, nw_ref, oh_gh, d_gh, dt_gh, gate_gh = refs[:9]
    gate_own, nf_own, mx_own, acc_own = refs[9:13]
    refs = refs[13:]
    degrees = DEGREES[group]
    radials, refs = dict(zip(degrees, refs)), refs[len(degrees) :]
    new_ref, en_ref, gs_ref, dot_gh = refs[:4]
    grads, refs = dict(zip(degrees, refs[4:])), refs[4 + len(degrees) :]
    if group == 0:
        dot_own, refs = refs[0], refs[1:]
        grads_own, refs = dict(zip(degrees, refs)), refs[len(degrees) :]
    table, sems, wm, wmt, wo, wot, nf_s, mx_s, acc_s = refs
    copies = fetch(pieces, slice(skip, skip + GROUP_COLS[group]), table, sems)
    block_diagonal(KINDS[group], mix_ref, wm, wmt)
    block_diagonal(KINDS[group], out_ref, wo, wot)
    en_ref[...] = jnp.zeros_like(en_ref)
    for copy in copies:
        copy.wait()
    ghost_pairs(
        group, own_ref, table, new_ref, group_cols(group).start, oh_gh, d_gh, dt_gh, gate_gh,
        radials, nw_ref, step_count(meta_ref), wm, wmt, wo, wot, nf_s, mx_s, acc_own, acc_s,
        gs_ref, dot_gh, grads, en_ref,
    )
    if group == 0:
        own_backward(group, gs_ref, gate_own, wmt, nf_own, mx_own, dot_own, grads_own)


def pairs_stage(group, skip, pieces, shared, own_parts, radial_gh):
    feats = shared[0]
    atoms = feats.shape[0]
    half = atoms * HALF
    ghosts = sum(piece.shape[0] for piece in pieces)
    degrees = DEGREES[group]
    sides = 2 if group == 0 else 1
    out_shape = (
        struct(atoms, GROUP_COLS[group], dtype=BF16),
        struct(atoms, CH),
        struct(atoms, GROUP_COLS[group], dtype=BF16),
    ) + (struct(half, CH, dtype=BF16),) * (sides * (1 + len(degrees)))
    args = tuple(pieces) + tuple(shared) + tuple(own_parts)
    args += tuple(radial_gh[degree - 1] for degree in degrees)
    new, energy, gs, *rest = call(
        functools.partial(pairs_kernel, group, len(pieces), skip), "pairs_" + "abc"[group],
        out_shape, pair_scratch(atoms, half, ghosts, group), args,
        any_specs(len(pieces), len(args)), 24,
    )
    return new, energy, gs, rest[: 1 + len(degrees)], rest[1 + len(degrees) :]


def own_backward_kernel(group, mix_ref, gs_ref, gate_ref, nf_ref, mx_ref, *refs):
    dot_ref, grads, wmt = refs[0], dict(zip(DEGREES[group], refs[1:-1])), refs[-1]
    block_diagonal(KINDS[group], mix_ref, None, wmt)
    own_backward(group, gs_ref, gate_ref, wmt, nf_ref, mx_ref, dot_ref, grads)


def own_backward_stage(group, mix, gs, gate, nf, mx):
    half = nf.shape[0]
    out_shape = (struct(half, CH, dtype=BF16),) * (1 + len(DEGREES[group]))
    scratch = [pltpu.VMEM((len(KINDS[group]), 2 * CH, 2 * CH), BF16)]
    kernel = functools.partial(own_backward_kernel, group)
    name = "own_backward_" + "abc"[group]
    return call(kernel, name, out_shape, scratch, (mix, gs, gate, nf, mx))


def finish(
    grad, mixed, near, dots, parts, pre, unit, spacing, radt_ref, rbft_ref, mix_t
):
    mixed = mixed.astype(F32)
    gate = jax.nn.sigmoid(mixed)
    first = grad * gate * (1.0 + mixed * (1.0 - gate)) + dots * gate * (1.0 - gate)
    weighted = mm(first.astype(BF16), mix_t) * near.astype(F32)
    radial_grad = jnp.concatenate([weighted.astype(BF16)] + parts, axis=1)
    hidden_grad = mm(radial_grad, radt_ref[...])
    pre = pre.astype(F32)
    logistic = jax.nn.sigmoid(pre)
    pre_grad = (hidden_grad * logistic * (1.0 + pre * (1.0 - logistic))).astype(BF16)
    centred = centred_of(unit[:, 3:4], spacing, rbft_ref.shape[1])
    slope = jnp.exp(-0.5 * centred * centred) * centred
    basis_grad = mm(pre_grad, rbft_ref[...])
    dist_grad = jnp.sum(basis_grad * slope, axis=1, keepdims=True) * (-1.0 / spacing)
    pull = unit * dist_grad
    across = pull.T[0:8, :]
    top = across.astype(BF16)
    rest = (across - top.astype(F32)).astype(BF16)
    return pull, top, rest


def sum_of(refs, rows):
    total = refs[0][rows, :].astype(F32)
    for ref in refs[1:]:
        total += ref[rows, :].astype(F32)
    return total


def degree_parts(refs, rows):
    by_degree = {}
    refs = list(refs)
    for degrees in DEGREES:
        for degree in degrees:
            by_degree.setdefault(degree, []).append(refs.pop(0))
    return [sum_of(by_degree[degree], rows).astype(BF16) for degree in range(1, 5)]


PARTIALS = sum(len(degrees) for degrees in DEGREES)


def third_kernel(
    p0, p1, p2, p3, p4, own_ref, meta_ref, mix_ref, out_ref, nw_ref, oh_gh, d_gh, dt_gh, gate_gh,
    acc_own, radt_ref, rbft_ref, gs0_ref, en_0, en_a, new_0, new_a, pre_gh, unit_gh,
    m0_ref, nf0_ref, dot_a, *refs
):
    group = 1
    before, degrees = len(DEGREES[0]), DEGREES[group]
    gr_a, refs = refs[:before], refs[before:]
    radials, refs = dict(zip(degrees, refs)), refs[len(degrees) :]
    new_ref, energy_ref, src_ref, onto_ref, flow_ref, fmid_ref, fhigh_ref, gs_ref = refs[:8]
    table, sems, wm, wmt, wo, wot, nf_s, mx_s, acc_s, dot_c, en_s, fgh_s = refs[8:20]
    grads = dict(zip(degrees, refs[20:]))
    copies = fetch((p0, p1, p2, p3, p4), slice(0, GROUP_COLS[group]), table, sems)
    atoms = own_ref.shape[0]
    spacing = spacing_of(atoms, rbft_ref.shape[1])
    block_diagonal(KINDS[group], mix_ref, wm, wmt)
    block_diagonal(KINDS[group], out_ref, wo, wot)
    en_s[...] = en_0[...] + en_a[...]
    at = 0
    for part in (new_0, new_a):
        new_ref[:, at : at + part.shape[1]] = part[...]
        at += part.shape[1]
    steps = step_count(meta_ref)

    for copy in copies:
        copy.wait()
    ghost_pairs(
        group, own_ref, table, new_ref, 0, oh_gh, d_gh, dt_gh, gate_gh, radials, nw_ref,
        steps, wm, wmt, wo, wot, nf_s, mx_s, acc_own, acc_s, gs_ref, dot_c, grads, en_s,
    )
    energy_ref[...] = jnp.sum(en_s[...].T, axis=0, keepdims=True)

    fgh_s[...] = jnp.zeros_like(fgh_s)
    src_ref[...] = jnp.zeros_like(src_ref)
    onto_ref[...] = jnp.zeros_like(onto_ref)
    gs0_low = gs0_ref[...].astype(BF16)
    mix_t = flip(mix_ref[0])

    def ghost_finish(step):
        here, _ = ghost_rows(step)
        grad = mm(d_gh[here, :], gs0_low)
        pull, top, rest = finish(
            grad, m0_ref[here, :], nf0_ref[here, :], sum_of((dot_a, dot_c), here),
            degree_parts(gr_a + refs[20:], here), pre_gh[here, :], unit_gh[here, :], spacing,
            radt_ref, rbft_ref, mix_t,
        )
        pull_top = pull.astype(BF16)
        pull_rest = (pull - pull_top.astype(F32)).astype(BF16)
        spread = dt_gh[:, here]
        src_ref[...] += mm(spread, pull_top) + mm(spread, pull_rest)
        onehot = oh_gh[here, :]
        fgh_s[...] += mm(top, onehot) + mm(rest, onehot)

    over_ghost_steps(steps, ghost_finish)
    low, mid = flow_ref.shape[1], fmid_ref.shape[1]
    flow_ref[...] = fgh_s[:, 0:low]
    fmid_ref[...] = fgh_s[:, low : low + mid]
    fhigh_ref[...] = fgh_s[:, low + mid :]


def third_stage(pieces, feats, *rest):
    atoms, feat = feats.shape
    half = atoms * HALF
    ghosts = sum(piece.shape[0] for piece in pieces)
    sizes = (ghosts // 4, ghosts // 2, ghosts // 4)
    out_shape = (
        struct(atoms, feat, dtype=BF16),
        struct(1, atoms),
        struct(atoms, CH),
        struct(8, atoms),
    ) + tuple(struct(8, size) for size in sizes) + (
        struct(atoms, GROUP_COLS[1], dtype=BF16),
    )
    scratch = pair_scratch(atoms, half, ghosts, 1) + [
        pltpu.VMEM((half, CH), BF16),
        pltpu.VMEM((atoms, CH), F32),
        pltpu.VMEM((8, ghosts), F32),
    ]
    scratch += [pltpu.VMEM((half, CH), BF16)] * len(DEGREES[1])
    args = tuple(pieces) + (feats,) + rest
    return call(
        third_kernel, "third_group", out_shape, scratch, args,
        any_specs(len(pieces), len(args)), 28,
    )


def own_back_kernel(
    steps, oh_own, pre_own, unit_own, radt_ref, rbft_ref, mix_ref, gs0_ref,
    m0_ref, nf0_ref, dot_a, dot_c, *refs
):
    gr_own, (src_in, onto_in, src_out, onto_out) = refs[:PARTIALS], refs[PARTIALS:]
    atoms = oh_own.shape[1]
    spacing = spacing_of(atoms, rbft_ref.shape[1])
    grad = tiled(gs0_ref[...])
    mix_t = flip(mix_ref[0])
    src = src_in[...]
    onto = onto_in[...]
    for step in steps:
        rows = own_rows(step)
        pull, top, rest = finish(
            grad, m0_ref[rows, :], nf0_ref[rows, :], sum_of((dot_a, dot_c), rows),
            degree_parts(gr_own, rows), pre_own[rows, :], unit_own[rows, :], spacing, radt_ref,
            rbft_ref, mix_t,
        )
        src += over_slots(pull, atoms)
        onehot = oh_own[rows, :]
        onto += mm(top, onehot) + mm(rest, onehot)
    src_out[...] = src
    onto_out[...] = onto


def own_back_stage(steps, *args):
    atoms = args[0].shape[1]
    out_shape = (struct(atoms, CH), struct(8, atoms))
    kernel = functools.partial(own_back_kernel, tuple(steps))
    return call(kernel, "own_back", out_shape, [], args)


def ring(axis):
    peers = lax.axis_size(axis)
    up = [(i, (i + 1) % peers) for i in range(peers)]
    return up, [(j, i) for i, j in up]


def neighbours_of(block, axis, dim):
    up, down = ring(axis)
    length = block.shape[dim]
    if len(up) == 2 and length == 2:
        other = lax.ppermute(block, axis, up)
        return (
            lax.slice_in_dim(other, length - 1, length, axis=dim),
            lax.slice_in_dim(other, 0, 1, axis=dim),
        )
    before = lax.ppermute(lax.slice_in_dim(block, length - 1, length, axis=dim), axis, up)
    after = lax.ppermute(lax.slice_in_dim(block, 0, 1, axis=dim), axis, down)
    return before, after


def grown(block, axis, dim):
    before, after = neighbours_of(block, axis, dim)
    return jnp.concatenate([before, block, after], axis=dim)


def flat_rows(piece):
    return piece.reshape(-1, piece.shape[-1])


def fold_kernel(mid_ref, low_ref, high_ref, out_ref):
    lanes = mid_ref.shape[1]
    ext_y = iota(mid_ref.shape, 1) // 32 % 4
    out_ref[...] = (
        mid_ref[...]
        + jnp.where(ext_y == 1, pltpu.roll(low_ref[...], lanes - 64, 1), 0.0)
        + jnp.where(ext_y == 2, pltpu.roll(high_ref[...], 64, 1), 0.0)
    )


def forces_kernel(mid_ref, low_ref, high_ref, src_ref, onto_ref, home_ref, out_ref):
    values = mid_ref[...]
    lanes = values.shape[1]
    ext_z = iota(values.shape, 1) // 8 % 4
    values += jnp.where(ext_z == 1, pltpu.roll(low_ref[...], lanes - 16, 1), 0.0)
    values += jnp.where(ext_z == 2, pltpu.roll(high_ref[...], 16, 1), 0.0)
    first = values.astype(BF16)
    values -= first.astype(F32)
    second = values.astype(BF16)
    third = (values - second.astype(F32)).astype(BF16)
    home = home_ref[...]
    total = onto_ref[...] - src_ref[...].T[0:8, :]
    total += (mm_nt(first, home) + (mm_nt(second, home) + mm_nt(third, home)))
    for comp in range(3):
        out_ref[comp] = -total[comp : comp + 1, :]


def give_back_x(low, mid, high):
    up, down = ring("gx")
    from_low = lax.ppermute(high, "gx", up)
    from_high = lax.ppermute(low, "gx", down)
    return mid, jnp.concatenate([from_low, from_high], axis=1)


def give_back_y(mid):
    up, down = ring("gy")
    return mid, lax.ppermute(mid, "gy", up), lax.ppermute(mid, "gy", down)


def fold(*args):
    return call(fold_kernel, "fold", (struct(*args[0].shape),), [], args)[0]


def give_back_z(mid):
    up, down = ring("gz")
    from_low = lax.ppermute(mid, "gz", up)
    return mid, from_low, from_low if len(up) == 2 else lax.ppermute(mid, "gz", down)


def local(
    features,
    positions,
    neighbours,
    counts,
    cell_atoms,
    rbf_weight,
    radial_weight,
    mix_weight,
    out_weight,
    energy_weight,
    norm_weight,
):
    feats = features[0, 0, 0]
    places = jnp.swapaxes(positions[0, 0], 0, 1)
    lists = jnp.concatenate([neighbours[0, 0, 0].T, counts[0, 0], cell_atoms[0, 0]], axis=0)
    cells0, cells1, own_pos, meta = make_cells(feats, places, lists)
    hold = lax.optimization_barrier
    block0, block1 = (part.reshape(2, 2, 2, 8, part.shape[1]) for part in (cells0, cells1))
    z0 = neighbours_of(block0, "gz", 2)
    z1 = neighbours_of(block1, "gz", 2)
    y1_in = neighbours_of(block1, "gy", 1)
    z0, own_pos, meta = hold((z0, own_pos, meta))
    block0 = jnp.concatenate([z0[0], block0, z0[1]], axis=2)
    y0 = neighbours_of(block0, "gy", 1)
    oh_own, pre_own, unit_own, radt, rbft, home, *radial_own = own_stage(
        meta, own_pos, rbf_weight, radial_weight
    )
    z1, y1_in, oh_own = hold((z1, y1_in, oh_own))
    block1 = jnp.concatenate([z1[0], block1, z1[1]], axis=2)
    x1_in = neighbours_of(block1, "gx", 0)
    y0, z1, oh_own = hold((y0, z1, oh_own))
    middle = jnp.concatenate([y0[0], block0, y0[1]], axis=1)
    x0 = neighbours_of(middle, "gx", 0)
    y1_out = neighbours_of(jnp.concatenate(z1, axis=2), "gy", 1)
    x1_in, oh_own = hold((x1_in, oh_own))
    (m0_own, gate_own, nf0_own, acc0), (own_a,) = own_forward_stage(
        (0,), feats, mix_weight, oh_own, radial_own
    )
    _, (own_b,) = own_forward_stage((1,), feats, mix_weight, oh_own, radial_own, gate_own)
    x0, y1_out, acc0, acc_b = hold((x0, y1_out, acc0, own_b[2]))
    pieces0 = tuple(flat_rows(piece) for piece in (x0[0], middle, x0[1]))
    y1 = [
        jnp.concatenate([out[:, :, 0:1], inner, out[:, :, 1:2]], axis=2)
        for out, inner in zip(y1_out, y1_in)
    ]
    outer = jnp.concatenate(y1, axis=1)
    x1_out = neighbours_of(outer, "gx", 0)
    block1 = jnp.concatenate([y1[0], block1, y1[1]], axis=1)
    pieces1 = (x1_in[0], x1_out[0], block1, x1_in[1], x1_out[1])
    pieces1 = tuple(flat_rows(piece) for piece in pieces1)
    (
        new_0, oh_gh, d_gh, dt_gh, pre_gh, unit_gh, gs0, en_0, m0_gh, gate_gh, nf0_gh, *radial_gh,
    ) = start_stage(
        pieces0, feats, own_pos, meta, rbf_weight, radial_weight, mix_weight, out_weight,
        energy_weight[None], acc0,
    )
    shared = (feats, meta, mix_weight, out_weight, norm_weight, oh_gh, d_gh, dt_gh, gate_gh)
    new_a, en_a, _, (dot_gh_a, *gr_gh_a), (dot_own_a, *gr_own_a) = pairs_stage(
        0, 2 * CH, pieces0, shared, (gate_own, *own_a), radial_gh
    )
    new, energy, src, onto, low, mid, high, gs_b = third_stage(
        pieces1, *shared, acc_b, radt, rbft, gs0, en_0, en_a, new_0, new_a, pre_gh,
        unit_gh, m0_gh, nf0_gh, dot_gh_a, *gr_gh_a,
        *[radial_gh[degree - 1] for degree in DEGREES[1]],
    )
    mid, arrived = give_back_x(low, mid, high)
    dot_own_b, *gr_own_b = own_backward_stage(1, mix_weight, gs_b, gate_own, *own_b[:2])
    arrived, gs0, dot_own_b = hold((arrived, gs0, dot_own_b))
    mid, from_low, from_high = give_back_y(mid + arrived)
    back = (oh_own, pre_own, unit_own, radt, rbft, mix_weight, gs0, m0_own, nf0_own)
    back += (dot_own_a, dot_own_b, *gr_own_a, *gr_own_b)
    src, onto = own_back_stage(range(2), *back, src, onto)
    from_low, from_high, src = hold((from_low, from_high, src))
    folded = give_back_z(fold(mid, from_low, from_high))
    src, onto = own_back_stage(range(2, 4), *back, src, onto)
    args = (*folded, src, onto, home)
    out_shape = (struct(3, 1, src.shape[0]),)
    forces = call(forces_kernel, "forces", out_shape, [], args)[0]
    return (
        new[None, None, None],
        energy[None, None],
        jnp.swapaxes(forces, 0, 1)[None, None],
    )


def solution(mesh):
    split = P("gx", "gy", "gz", None, None)
    flat = P("gx", "gy", "gz", None)
    return jax.shard_map(
        local,
        mesh=mesh,
        in_specs=(split, split, split, flat, flat, P(), P(), P(), P(), P(), P()),
        out_specs=(split, flat, split),
        check_vma=False,
    )
```

```python
import functools
import math

import jax
import jax.numpy as jnp
from jax import lax
from jax.experimental import pallas as pl
from jax.experimental.pallas import tpu as pltpu
from jax.sharding import PartitionSpec as P

F32 = jnp.float32
BF16 = jnp.bfloat16
CH = 128
SLOTS = 32
HALF = 16
STEP = 256
OWN_STEPS = 4
GH_STEPS = 2
MIB = 1024 * 1024
SPACE = pltpu.VMEM
PAIR_DEGREES = (
    (1, 1), (1, 2), (2, 2), (2, 2),
    (3, 3), (3, 3), (3, 3), (3, 4),
    (4, 4), (4, 4), (4, 4), (4, 4),
)
GROUPS = ((0, 3), (3, 12))
KINDS = tuple(sorted({PAIR_DEGREES[pair] for pair in range(*group)}) for group in GROUPS)
DEGREES = tuple(sorted({d for both in kinds for d in both}) for kinds in KINDS)
GROUP_COLS = tuple(2 * CH * (end - begin) for begin, end in GROUPS)


def mm(a, b):
    return jnp.dot(a, b, preferred_element_type=F32)


def mm_nt(a, b):
    return lax.dot_general(a, b, (((1,), (1,)), ((), ())), preferred_element_type=F32)


def iota(shape, dim):
    return lax.broadcasted_iota(jnp.int32, shape, dim)


def flip(w):
    return w.astype(F32).T.astype(BF16)


def pair_cols(pair):
    return slice(CH + pair * 2 * CH, CH + (pair + 1) * 2 * CH)


def struct(*shape, dtype=F32):
    return jax.ShapeDtypeStruct(shape, dtype)


def call(kernel, name, out_shape, scratch, args, specs=None, limit=16):
    return pl.pallas_call(
        kernel,
        out_shape=out_shape,
        in_specs=specs or [pl.BlockSpec(memory_space=SPACE)] * len(args),
        out_specs=tuple(pl.BlockSpec(memory_space=SPACE) for _ in out_shape),
        scratch_shapes=scratch,
        compiler_params=pltpu.CompilerParams(vmem_limit_bytes=limit * MIB),
        cost_estimate=pl.CostEstimate(flops=1024, bytes_accessed=1024, transcendentals=0),
        name=name,
    )(*args)


def cells_kernel(
    feat_ref, pos_ref, lists_ref,
    out_ref, own_pos_ref, meta_ref, pick_ref, rows_ref, pos_rows,
):
    rows_ref[...] = jnp.zeros_like(rows_ref)
    pos_rows[...] = jnp.zeros_like(pos_rows)
    atoms = feat_ref.shape[0]
    rows_ref[0 : SLOTS + 2, :] = lists_ref[...].astype(F32)
    meta = rows_ref[...].T
    meta_ref[...] = meta
    for comp in range(3):
        places = pos_ref[comp]
        first = places.astype(BF16).astype(F32)
        second = (places - first).astype(BF16).astype(F32)
        pos_rows[comp : comp + 1, :] = first
        pos_rows[4 + comp : 5 + comp, :] = second
        pos_rows[8 + comp : 9 + comp, :] = places - first - second
    pieces = pos_rows[...].astype(BF16)
    lane = iota((atoms, atoms), 1).astype(F32)
    pick = (meta[:, SLOTS + 1 : SLOTS + 2] == lane).astype(F32).astype(BF16)
    same = (iota((atoms, atoms), 0) == iota((atoms, atoms), 1)).astype(F32).astype(BF16)
    own_pos_ref[...] = mm_nt(same, pieces).astype(BF16)
    out_ref[:, CH : 2 * CH] = mm_nt(pick, pieces).astype(BF16)
    pick_ref[...] = pick
    out_ref[:, 0:CH] = mm(pick, feat_ref[:, 0:CH]).astype(BF16)
    cut = pair_cols(GROUPS[1][0]).start
    out_ref[:, 2 * CH :] = mm(pick, feat_ref[:, CH:cut]).astype(BF16)


def rest_kernel(feat_ref, pick_ref, rest_ref):
    cut = pair_cols(GROUPS[1][0]).start
    rest_ref[...] = mm(pick_ref[...], feat_ref[:, cut:]).astype(BF16)


def make_cells(feats, places, lists):
    atoms = feats.shape[0]
    out_shape = (
        struct(atoms, 2 * CH + GROUP_COLS[0], dtype=BF16),
        struct(atoms, CH, dtype=BF16),
        struct(atoms, CH),
        struct(atoms, atoms, dtype=BF16),
    )
    args = (feats, places, lists)
    scratch = [pltpu.VMEM((CH, atoms), F32), pltpu.VMEM((CH, atoms), F32)]
    first, own_pos, meta, pick = call(cells_kernel, "cells", out_shape, scratch, args)
    out_shape = (struct(atoms, GROUP_COLS[1], dtype=BF16),)
    rest = call(rest_kernel, "cells_rest", out_shape, [], (feats, pick))[0]
    return first, rest, own_pos, meta


def spacing_of(atoms, nbasis):
    depth = atoms // 16
    return 2.0 * math.sqrt(32.0 + depth * depth) / (nbasis - 1)


def own_onehots(meta_ref, oh_own):
    atoms = meta_ref.shape[0]
    counts = meta_ref[:, SLOTS : SLOTS + 1]
    lane_atom = iota((atoms, atoms), 1).astype(F32)
    for slot in range(HALF):
        hit = jnp.logical_and(meta_ref[:, slot : slot + 1] == lane_atom, counts > slot)
        oh_own[slot * atoms : (slot + 1) * atoms, :] = hit.astype(F32).astype(BF16)


def geometry(near, here):
    diff = near - here
    rel = (diff + pltpu.roll(diff, CH - 4, 1)) + (
        pltpu.roll(diff, CH - 8, 1) + pltpu.roll(diff, CH - 12, 1)
    )
    lane = iota(rel.shape, 1)
    rel = jnp.where(lane < 3, rel, 0.0)
    square = jnp.sum(rel * rel, axis=1, keepdims=True)
    inverse = lax.rsqrt(jnp.where(square > 0.0, square, 1.0))
    dist = square * inverse
    return jnp.where(lane == 3, dist, rel * inverse), dist


def centred_of(dist, spacing, nbasis):
    return dist * (1.0 / spacing) - iota((dist.shape[0], nbasis), 1).astype(F32)


def radial_net(dist, spacing, rbf_ref, rad_ref):
    centred = centred_of(dist, spacing, rbf_ref.shape[0])
    basis = jnp.exp(-0.5 * centred * centred)
    pre = mm(basis.astype(BF16), rbf_ref[...])
    hidden = (pre * jax.nn.sigmoid(pre)).astype(BF16)
    return pre, mm(hidden, rad_ref[...]).astype(BF16)


def tiled(values, size=STEP):
    return jnp.concatenate([values] * (size // values.shape[0]), axis=0)


def live_ghosts(meta_ref):
    return jnp.maximum(meta_ref[:, SLOTS : SLOTS + 1] - HALF, 0.0)


def step_count(meta_ref):
    total = jnp.sum(live_ghosts(meta_ref)).astype(jnp.int32)
    rows = GH_STEPS * STEP
    return jnp.maximum((total + (rows - 1)) // rows, 1) * GH_STEPS


def own_rows(step, size=STEP):
    return pl.ds(step * size, size)


def ghost_rows(step, size=STEP):
    first = OWN_STEPS * STEP
    if isinstance(step, int):
        return pl.ds(step * size, size), pl.ds(first + step * size, size)
    base = pl.multiple_of(step * size, size)
    return pl.ds(base, size), pl.ds(pl.multiple_of(first + base, size), size)


def over_ghost_steps(steps, body, size=STEP):
    static = GH_STEPS * STEP // size
    for step in range(static):
        body(step)

    def again(step, carry):
        body(step)
        return carry

    lax.fori_loop(static, (steps * STEP + (size - 1)) // size, again, 0)


def block_diagonal(kinds, source, straight=None, across=None):
    zero = jnp.zeros((CH, CH), BF16)
    targets = [ref for ref in (straight, across) if ref is not None]
    for kind, both in enumerate(kinds):
        for ref in targets:
            ref[kind, 0:CH, CH:] = zero
            ref[kind, CH:, 0:CH] = zero
    for degree in sorted({d for both in kinds for d in both}):
        weight = source[degree]
        flipped = flip(weight) if across is not None else None
        for kind, both in enumerate(kinds):
            for side in range(2):
                if both[side] == degree:
                    part = slice(side * CH, side * CH + CH)
                    if straight is not None:
                        straight[kind, part, part] = weight
                    if across is not None:
                        across[kind, part, part] = flipped


def fetch(pieces, cols, table, sems):
    low, high, ghosts = 0, 0, table.shape[0]
    if len(pieces) == 3:
        rows = [(piece, 0, piece.shape[0]) for piece in pieces]
    else:
        low_in, low_out, mid, high_in, high_out = pieces
        half = low_out.shape[0] // 2
        rows = [(low_out, 0, half), (low_in, 0, low_in.shape[0]), (low_out, half, half)]
        rows += [(mid, 0, mid.shape[0])]
        rows += [(high_out, 0, half), (high_in, 0, high_in.shape[0]), (high_out, half, half)]
    copies = []
    at = 0
    for index, (piece, start, count) in enumerate(rows):
        source = piece.at[pl.ds(start, count), cols]
        target = table.at[pl.ds(at, count), :]
        copies.append(pltpu.make_async_copy(source, target, sems.at[index]))
        at += count
    for copy in copies:
        copy.start()
    return copies


def infos_of(group):
    infos = []
    for index, pair in enumerate(range(*GROUPS[group])):
        degrees = PAIR_DEGREES[pair]
        cols = slice(index * 2 * CH, (index + 1) * 2 * CH)
        infos.append((cols, degrees, KINDS[group].index(degrees)))
    return infos


def group_cols(group):
    begin, end = GROUPS[group]
    return slice(pair_cols(begin).start, pair_cols(end - 1).stop)


def twice(values):
    return jnp.concatenate([values, values], axis=1)


def forward(group, rows, onehot, feats, radials, gate_ref, wm, nf_ref, mx_ref, slots):
    near = mm(onehot, feats).astype(BF16)
    nf_ref[rows, :] = near
    gate = twice(gate_ref[rows, :])
    wide = gate.astype(F32) if slots else None
    messages = []
    for cols, degrees, kind in infos_of(group):
        radial = jnp.concatenate([radials[d][rows, :] for d in degrees], axis=1)
        mixed = mm(near[:, cols] * radial, wm[kind])
        low = mixed.astype(BF16)
        mx_ref[rows, cols] = low
        messages.append(mixed * wide if slots else low * gate)
    return messages


def backward(group, rows, grad, gate_ref, wmt, nf_ref, mx_ref, dot_ref, grad_refs):
    parts = {}
    dots = None
    gate = twice(gate_ref[rows, :])
    for cols, degrees, kind in infos_of(group):
        product = grad[:, cols] * mx_ref[rows, cols]
        dot = (product[:, 0:CH] + product[:, CH:]).astype(F32)
        dots = dot if dots is None else dots + dot
        weighted = mm(grad[:, cols] * gate, wmt[kind]) * nf_ref[rows, cols].astype(F32)
        for side in range(2):
            part = weighted[:, side * CH : (side + 1) * CH]
            degree = degrees[side]
            parts[degree] = parts[degree] + part if degree in parts else part
    dot_ref[rows, :] = dots.astype(dot_ref.dtype)
    for degree, part in parts.items():
        grad_refs[degree][rows, :] = part.astype(grad_refs[degree].dtype)


def over_slots(values, atoms):
    return jnp.sum(values.reshape(-1, atoms, values.shape[1]), axis=0)


def own_forward(group, own_ref, oh_own, radials, gate_ref, wm, nf_ref, mx_ref, acc_ref):
    atoms = own_ref.shape[0]
    feats = own_ref[:, group_cols(group)]
    for step in range(OWN_STEPS):
        rows = own_rows(step)
        messages = forward(
            group, rows, oh_own[rows, :], feats, radials, gate_ref, wm, nf_ref, mx_ref, True
        )
        for (cols, _, _), message in zip(infos_of(group), messages):
            part = over_slots(message, atoms)
            acc_ref[:, cols] = part if step == 0 else acc_ref[:, cols] + part


def own_backward(group, gs_ref, gate_ref, wmt, nf_ref, mx_ref, dot_ref, grad_refs):
    grad = tiled(gs_ref[...])
    for step in range(OWN_STEPS):
        backward(
            group, own_rows(step), grad, gate_ref, wmt, nf_ref, mx_ref, dot_ref, grad_refs
        )


def ghost_pairs(
    group, own_ref, table, new_ref, new_base, oh_gh, d_gh, dt_gh, gate_ref, radials, nw_ref,
    steps, wm, wmt, wo, wot, nf_s, mx_s, acc_in, acc_s, gs_ref, dot_ref, grad_refs, en_ref,
):
    norm = 1.0 / math.sqrt(SLOTS)
    acc_s[...] = acc_in[...]

    def ghost_forward(step):
        here, _ = ghost_rows(step)
        messages = forward(
            group, here, oh_gh[here, :], table[...], radials, gate_ref, wm, nf_s, mx_s, False
        )
        acc_s[...] += mm(dt_gh[:, here], jnp.concatenate(messages, axis=1))

    over_ghost_steps(steps, ghost_forward)

    begin = group_cols(group).start
    for cols, degrees, kind in infos_of(group):
        summed_low = (acc_s[:, cols] * norm).astype(BF16)
        own = own_ref[:, begin + cols.start : begin + cols.stop]
        updated = own.astype(F32) + mm(summed_low, wo[kind])
        at = begin - new_base + cols.start
        new_ref[:, at : at + 2 * CH] = updated.astype(BF16)
        weight = jnp.concatenate(
            [nw_ref[d - 1 : d, :] * (1.0 / (2 * d + 1)) for d in degrees], axis=1
        )
        scale = weight * updated
        energy = scale * updated
        en_ref[...] += energy[:, 0:CH] + energy[:, CH:]
        gs_ref[:, cols] = (mm((2.0 * scale).astype(BF16), wot[kind]) * norm).astype(BF16)

    def ghost_backward(step):
        here, _ = ghost_rows(step)
        grad = mm(d_gh[here, :], gs_ref[...]).astype(BF16)
        backward(group, here, grad, gate_ref, wmt, nf_s, mx_s, dot_ref, grad_refs)

    over_ghost_steps(steps, ghost_backward)


def pair_scratch(atoms, half, ghosts, group):
    count, width = len(KINDS[group]), GROUP_COLS[group]
    return (
        [pltpu.VMEM((ghosts, width), BF16), pltpu.SemaphoreType.DMA((7,))]
        + [pltpu.VMEM((count, 2 * CH, 2 * CH), BF16) for _ in range(4)]
        + [
            pltpu.VMEM((half, width), BF16),
            pltpu.VMEM((half, width), BF16),
            pltpu.VMEM((atoms, width), F32),
        ]
    )


def own_kernel(
    meta_ref, own_pos_ref, rbf_ref, rad_ref,
    oh_own, pre_ref, unit_ref, radt_ref, rbft_ref, home_ref, *radial_refs
):
    atoms = meta_ref.shape[0]
    nbasis = rbft_ref.shape[1]
    spacing = spacing_of(atoms, nbasis)
    own_onehots(meta_ref, oh_own)
    here = tiled(own_pos_ref[...].astype(F32))
    for step in range(OWN_STEPS):
        rows = own_rows(step)
        unit, dist = geometry(mm(oh_own[rows, :], own_pos_ref[...]), here)
        unit_ref[rows, :] = unit
        pre, radial = radial_net(dist, spacing, rbf_ref, rad_ref)
        pre_ref[rows, :] = pre.astype(BF16)
        for degree, ref in enumerate(radial_refs):
            ref[rows, :] = radial[:, degree * CH : (degree + 1) * CH]
    for degree in range(5):
        part = slice(degree * CH, (degree + 1) * CH)
        radt_ref[part, :] = flip(rad_ref[:, part])
    for index in range(nbasis // CH):
        part = slice(index * CH, (index + 1) * CH)
        rbft_ref[:, part] = flip(rbf_ref[part, :])
    lanes = home_ref.shape[1]
    lane = iota((atoms, lanes), 1)
    ext_x, ext_y, ext_z = lane // 128, lane // 32 % 4, lane // 8 % 4
    slot = ((2 * ext_x + ext_y - 1) * 2 + ext_z - 1) * 8 + lane % 8
    inside = jnp.logical_and(
        jnp.logical_or(ext_y == 1, ext_y == 2), jnp.logical_or(ext_z == 1, ext_z == 2)
    )
    to_slot = jnp.logical_and(iota((atoms, lanes), 0) == slot, inside)
    to_slot = to_slot.astype(F32).astype(BF16)
    order = meta_ref[:, SLOTS + 1 : SLOTS + 2]
    to_atom = (order == iota((atoms, atoms), 1).astype(F32)).astype(F32)
    home_ref[...] = mm(to_atom.T.astype(BF16), to_slot).astype(BF16)


def own_stage(meta, own_pos, rbf, rad):
    atoms = meta.shape[0]
    edges = atoms * HALF
    out_shape = (
        struct(edges, atoms, dtype=BF16),
        struct(edges, CH, dtype=BF16),
        struct(edges, CH),
        struct(5 * CH, CH, dtype=BF16),
        struct(CH, rbf.shape[0], dtype=BF16),
        struct(atoms, 256, dtype=BF16),
    ) + (struct(edges, CH, dtype=BF16),) * 5
    return call(own_kernel, "own_edges", out_shape, [], (meta, own_pos, rbf, rad))


def scalar_forward(rows, near, radial, mix_ref, m0_ref, gate_ref, nf0_ref):
    near = near.astype(BF16)
    nf0_ref[rows, :] = near
    mixed = mm(near * radial, mix_ref[0])
    m0_ref[rows, :] = mixed.astype(BF16)
    gate = jax.nn.sigmoid(mixed)
    gate_ref[rows, :] = gate.astype(BF16)
    return mixed * gate


def own_forward_kernel(groups, scalar, *refs):
    own_ref, mix_ref, oh_own, refs = *refs[:3], refs[3:]
    radial0, radials = refs[0], dict(enumerate(refs[1:5], start=1))
    refs = refs[5:]
    if scalar:
        m0_ref, gate_ref, nf0_ref, acc0_ref = refs[:4]
        refs = refs[4:]
        atoms = own_ref.shape[0]
        feats = own_ref[:, 0:CH]
        summed = None
        for step in range(OWN_STEPS):
            rows = own_rows(step)
            message = scalar_forward(
                rows, mm(oh_own[rows, :], feats), radial0[rows, :], mix_ref, m0_ref, gate_ref,
                nf0_ref,
            )
            part = over_slots(message, atoms)
            summed = part if summed is None else summed + part
        acc0_ref[...] = summed
    else:
        gate_ref, refs = refs[0], refs[1:]
    outs, weights = refs[: 3 * len(groups)], refs[3 * len(groups) :]
    for index, group in enumerate(groups):
        block_diagonal(KINDS[group], mix_ref, weights[index])
        nf_ref, mx_ref, acc_ref = outs[3 * index : 3 * index + 3]
        own_forward(
            group, own_ref, oh_own, radials, gate_ref, weights[index], nf_ref, mx_ref, acc_ref
        )


def own_forward_stage(groups, feats, mix, oh_own, radial_own, gate=None):
    atoms = feats.shape[0]
    half = atoms * HALF
    out_shape = ()
    if gate is None:
        out_shape += (struct(half, CH, dtype=BF16),) * 3 + (struct(atoms, CH),)
    for group in groups:
        width = GROUP_COLS[group]
        out_shape += (struct(half, width, dtype=BF16),) * 2 + (struct(atoms, width),)
    args = (feats, mix, oh_own, *radial_own) + (() if gate is None else (gate,))
    scratch = [pltpu.VMEM((len(KINDS[group]), 2 * CH, 2 * CH), BF16) for group in groups]
    name = "own_forward_" + "".join("abc"[group] for group in groups)
    kernel = functools.partial(own_forward_kernel, groups, gate is None)
    outs = call(kernel, name, out_shape, scratch, args)
    first = len(outs) - 3 * len(groups)
    return outs[:first], [outs[first + 3 * i : first + 3 * i + 3] for i in range(len(groups))]


def start_kernel(
    p0, p1, p2, own_ref, own_pos_ref, meta_ref, rbf_ref, rad_ref, mix_ref, out_ref, ew_ref,
    acc0_ref,
    new_ref, oh_gh, d_gh, dt_gh, pre_ref, unit_ref, gs0_ref, en_ref, m0_gh, gate_gh, nf0_gh,
    radial_gh1, radial_gh2, radial_gh3, radial_gh4,
    table, sems, ghpos, acc_s,
):
    radial_gh = (None, radial_gh1, radial_gh2, radial_gh3, radial_gh4)
    copies = fetch((p0, p1, p2), slice(0, 2 * CH), table, sems)
    atoms = own_ref.shape[0]
    ghosts = table.shape[0]
    spacing = spacing_of(atoms, rbf_ref.shape[0])
    norm = 1.0 / math.sqrt(SLOTS)

    live = live_ghosts(meta_ref)
    sub_atom = iota((atoms, atoms), 0)
    lane_atom = iota((atoms, atoms), 1)
    live_b = jnp.broadcast_to(live, (atoms, atoms))
    end_row = jnp.sum(jnp.where(sub_atom <= lane_atom, live_b, 0.0), axis=0, keepdims=True)
    live_row = jnp.sum(jnp.where(sub_atom == lane_atom, live_b, 0.0), axis=0, keepdims=True)
    start_row = end_row - live_row
    row_b = jnp.broadcast_to(live_row, (atoms, atoms))
    end_col = jnp.sum(jnp.where(lane_atom <= sub_atom, row_b, 0.0), axis=1, keepdims=True)
    start_col = end_col - live
    total = jnp.sum(live)
    steps = step_count(meta_ref)
    ghost_row = meta_ref[:, HALF:SLOTS] - atoms
    high_part = jnp.floor(ghost_row * (1.0 / 16.0))
    row_high = high_part.astype(BF16)
    row_low = (ghost_row - 16.0 * high_part).astype(BF16)

    row = iota((ghosts, CH), 0)
    lane = iota((ghosts, CH), 1)
    zcells = atoms // 32
    per_y = (zcells + 2) * 8
    ext_x = row // (4 * per_y)
    ext_y = row // per_y % 4
    ext_z = row // 8 % (zcells + 2)

    def side_of(ext, last, size):
        return jnp.where(ext == 0, -size, jnp.where(ext == last, size, 0.0))

    shift = jnp.where(lane == 12, side_of(ext_x, 3, 4.0), 0.0)
    shift = jnp.where(lane == 13, side_of(ext_y, 3, 4.0), shift)
    shift = jnp.where(lane == 14, side_of(ext_z, zcells + 1, 2.0 * zcells), shift)
    own0 = own_ref[:, 0:CH]
    acc_s[...] = acc0_ref[...]
    for copy in copies:
        copy.wait()
    ghpos[...] = (table[:, CH:].astype(F32) + shift).astype(BF16)

    def ghost_start(step):
        here, _ = ghost_rows(step)
        base = step * STEP
        edge = (iota((STEP, atoms), 0) + base).astype(F32)
        mine = jnp.logical_and(edge >= start_row, edge < end_row).astype(F32)
        source = mine.astype(BF16)
        d_gh[here, :] = source
        edge_t = (iota((atoms, STEP), 1) + base).astype(F32)
        mine_t = jnp.logical_and(edge_t >= start_col, edge_t < end_col)
        spread = mine_t.astype(F32).astype(BF16)
        dt_gh[:, here] = spread
        edge_col = edge[:, 0:1]
        slot = edge_col - jnp.sum(mine * start_row, axis=1, keepdims=True)
        listed = mm(source, row_high) * 16.0 + mm(source, row_low)
        at_slot = iota((STEP, HALF), 1).astype(F32) == slot
        which = jnp.sum(jnp.where(at_slot, listed, 0.0), axis=1, keepdims=True)
        which = jnp.where(edge_col < total, which, -1.0)
        onehot = (iota((STEP, ghosts), 1).astype(F32) == which).astype(F32).astype(BF16)
        oh_gh[here, :] = onehot
        unit, dist = geometry(mm(onehot, ghpos[...]), mm(source, own_pos_ref[...]))
        unit_ref[here, :] = unit
        pre, radial = radial_net(dist, spacing, rbf_ref, rad_ref)
        pre_ref[here, :] = pre.astype(BF16)
        for degree in range(1, 5):
            radial_gh[degree][here, :] = radial[:, degree * CH : (degree + 1) * CH]
        message = scalar_forward(
            here, mm(onehot, table[:, 0:CH]), radial[:, 0:CH], mix_ref, m0_gh, gate_gh, nf0_gh
        )
        acc_s[...] += mm(spread, message.astype(BF16))

    over_ghost_steps(steps, ghost_start)

    low0 = (acc_s[...] * norm).astype(BF16)
    updated0 = own0.astype(F32) + mm(low0, out_ref[0])
    new_ref[:, 0:CH] = updated0.astype(BF16)
    logistic = jax.nn.sigmoid(updated0)
    weight0 = ew_ref[...]
    en_ref[...] = weight0 * updated0 * logistic
    grad0 = (weight0 * logistic * (1.0 + updated0 * (1.0 - logistic))).astype(BF16)
    gs0_ref[...] = mm_nt(grad0, out_ref[0]) * norm


def any_specs(count, total):
    return [pl.BlockSpec(memory_space=pl.ANY)] * count + [
        pl.BlockSpec(memory_space=SPACE)
    ] * (total - count)


def start_stage(pieces, feats, *rest):
    atoms = feats.shape[0]
    half = atoms * HALF
    ghosts = sum(piece.shape[0] for piece in pieces)
    out_shape = (
        struct(atoms, CH, dtype=BF16),
        struct(half, ghosts, dtype=BF16),
        struct(half, atoms, dtype=BF16),
        struct(atoms, half, dtype=BF16),
        struct(half, CH, dtype=BF16),
        struct(half, CH),
        struct(atoms, CH),
        struct(atoms, CH),
    ) + (struct(half, CH, dtype=BF16),) * 7
    scratch = [
        pltpu.VMEM((ghosts, 2 * CH), BF16),
        pltpu.SemaphoreType.DMA((7,)),
        pltpu.VMEM((ghosts, CH), BF16),
        pltpu.VMEM((atoms, CH), F32),
    ]
    args = tuple(pieces) + (feats,) + rest
    return call(
        start_kernel, "ghost_start", out_shape, scratch, args,
        any_specs(len(pieces), len(args)), 24,
    )


def pairs_kernel(group, count, skip, *refs):
    pieces, refs = refs[:count], refs[count:]
    own_ref, meta_ref, mix_ref, out_ref, nw_ref, oh_gh, d_gh, dt_gh, gate_gh = refs[:9]
    gate_own, nf_own, mx_own, acc_own = refs[9:13]
    refs = refs[13:]
    degrees = DEGREES[group]
    radials, refs = dict(zip(degrees, refs)), refs[len(degrees) :]
    new_ref, en_ref, gs_ref, dot_gh = refs[:4]
    grads, refs = dict(zip(degrees, refs[4:])), refs[4 + len(degrees) :]
    if group == 0:
        dot_own, refs = refs[0], refs[1:]
        grads_own, refs = dict(zip(degrees, refs)), refs[len(degrees) :]
    table, sems, wm, wmt, wo, wot, nf_s, mx_s, acc_s = refs
    copies = fetch(pieces, slice(skip, skip + GROUP_COLS[group]), table, sems)
    block_diagonal(KINDS[group], mix_ref, wm, wmt)
    block_diagonal(KINDS[group], out_ref, wo, wot)
    en_ref[...] = jnp.zeros_like(en_ref)
    for copy in copies:
        copy.wait()
    ghost_pairs(
        group, own_ref, table, new_ref, group_cols(group).start, oh_gh, d_gh, dt_gh, gate_gh,
        radials, nw_ref, step_count(meta_ref), wm, wmt, wo, wot, nf_s, mx_s, acc_own, acc_s,
        gs_ref, dot_gh, grads, en_ref,
    )
    if group == 0:
        own_backward(group, gs_ref, gate_own, wmt, nf_own, mx_own, dot_own, grads_own)


def pairs_stage(group, skip, pieces, shared, own_parts, radial_gh):
    feats = shared[0]
    atoms = feats.shape[0]
    half = atoms * HALF
    ghosts = sum(piece.shape[0] for piece in pieces)
    degrees = DEGREES[group]
    sides = 2 if group == 0 else 1
    out_shape = (
        struct(atoms, GROUP_COLS[group], dtype=BF16),
        struct(atoms, CH),
        struct(atoms, GROUP_COLS[group], dtype=BF16),
    ) + (struct(half, CH, dtype=BF16),) * (sides * (1 + len(degrees)))
    args = tuple(pieces) + tuple(shared) + tuple(own_parts)
    args += tuple(radial_gh[degree - 1] for degree in degrees)
    new, energy, gs, *rest = call(
        functools.partial(pairs_kernel, group, len(pieces), skip), "pairs_" + "abc"[group],
        out_shape, pair_scratch(atoms, half, ghosts, group), args,
        any_specs(len(pieces), len(args)), 24,
    )
    return new, energy, gs, rest[: 1 + len(degrees)], rest[1 + len(degrees) :]


def own_backward_kernel(group, mix_ref, gs_ref, gate_ref, nf_ref, mx_ref, *refs):
    dot_ref, grads, wmt = refs[0], dict(zip(DEGREES[group], refs[1:-1])), refs[-1]
    block_diagonal(KINDS[group], mix_ref, None, wmt)
    own_backward(group, gs_ref, gate_ref, wmt, nf_ref, mx_ref, dot_ref, grads)


def own_backward_stage(group, mix, gs, gate, nf, mx):
    half = nf.shape[0]
    out_shape = (struct(half, CH, dtype=BF16),) * (1 + len(DEGREES[group]))
    scratch = [pltpu.VMEM((len(KINDS[group]), 2 * CH, 2 * CH), BF16)]
    kernel = functools.partial(own_backward_kernel, group)
    name = "own_backward_" + "abc"[group]
    return call(kernel, name, out_shape, scratch, (mix, gs, gate, nf, mx))


def finish(
    grad, mixed, near, dots, parts, pre, unit, spacing, radt_ref, rbft_ref, mix_t
):
    mixed = mixed.astype(F32)
    gate = jax.nn.sigmoid(mixed)
    first = grad * gate * (1.0 + mixed * (1.0 - gate)) + dots * gate * (1.0 - gate)
    weighted = mm(first.astype(BF16), mix_t) * near.astype(F32)
    radial_grad = jnp.concatenate([weighted.astype(BF16)] + parts, axis=1)
    hidden_grad = mm(radial_grad, radt_ref[...])
    pre = pre.astype(F32)
    logistic = jax.nn.sigmoid(pre)
    pre_grad = (hidden_grad * logistic * (1.0 + pre * (1.0 - logistic))).astype(BF16)
    centred = centred_of(unit[:, 3:4], spacing, rbft_ref.shape[1])
    slope = jnp.exp(-0.5 * centred * centred) * centred
    basis_grad = mm(pre_grad, rbft_ref[...])
    dist_grad = jnp.sum(basis_grad * slope, axis=1, keepdims=True) * (-1.0 / spacing)
    pull = unit * dist_grad
    across = pull.T[0:8, :]
    top = across.astype(BF16)
    rest = (across - top.astype(F32)).astype(BF16)
    return pull, top, rest


def sum_of(refs, rows):
    total = refs[0][rows, :].astype(F32)
    for ref in refs[1:]:
        total += ref[rows, :].astype(F32)
    return total


def degree_parts(refs, rows):
    by_degree = {}
    refs = list(refs)
    for degrees in DEGREES:
        for degree in degrees:
            by_degree.setdefault(degree, []).append(refs.pop(0))
    return [sum_of(by_degree[degree], rows).astype(BF16) for degree in range(1, 5)]


PARTIALS = sum(len(degrees) for degrees in DEGREES)


def third_kernel(
    p0, p1, p2, p3, p4, own_ref, meta_ref, mix_ref, out_ref, nw_ref, oh_gh, d_gh, dt_gh, gate_gh,
    acc_own, radt_ref, rbft_ref, gs0_ref, en_0, en_a, new_0, new_a, pre_gh, unit_gh,
    m0_ref, nf0_ref, dot_a, *refs
):
    group = 1
    before, degrees = len(DEGREES[0]), DEGREES[group]
    gr_a, refs = refs[:before], refs[before:]
    radials, refs = dict(zip(degrees, refs)), refs[len(degrees) :]
    new_ref, energy_ref, src_ref, onto_ref, flow_ref, fmid_ref, fhigh_ref, gs_ref = refs[:8]
    table, sems, wm, wmt, wo, wot, nf_s, mx_s, acc_s, dot_c, en_s, fgh_s = refs[8:20]
    grads = dict(zip(degrees, refs[20:]))
    copies = fetch((p0, p1, p2, p3, p4), slice(0, GROUP_COLS[group]), table, sems)
    atoms = own_ref.shape[0]
    spacing = spacing_of(atoms, rbft_ref.shape[1])
    block_diagonal(KINDS[group], mix_ref, wm, wmt)
    block_diagonal(KINDS[group], out_ref, wo, wot)
    en_s[...] = en_0[...] + en_a[...]
    at = 0
    for part in (new_0, new_a):
        new_ref[:, at : at + part.shape[1]] = part[...]
        at += part.shape[1]
    steps = step_count(meta_ref)

    for copy in copies:
        copy.wait()
    ghost_pairs(
        group, own_ref, table, new_ref, 0, oh_gh, d_gh, dt_gh, gate_gh, radials, nw_ref,
        steps, wm, wmt, wo, wot, nf_s, mx_s, acc_own, acc_s, gs_ref, dot_c, grads, en_s,
    )
    energy_ref[...] = jnp.sum(en_s[...].T, axis=0, keepdims=True)

    fgh_s[...] = jnp.zeros_like(fgh_s)
    src_ref[...] = jnp.zeros_like(src_ref)
    onto_ref[...] = jnp.zeros_like(onto_ref)
    gs0_low = gs0_ref[...].astype(BF16)
    mix_t = flip(mix_ref[0])

    def ghost_finish(step):
        here, _ = ghost_rows(step)
        grad = mm(d_gh[here, :], gs0_low)
        pull, top, rest = finish(
            grad, m0_ref[here, :], nf0_ref[here, :], sum_of((dot_a, dot_c), here),
            degree_parts(gr_a + refs[20:], here), pre_gh[here, :], unit_gh[here, :], spacing,
            radt_ref, rbft_ref, mix_t,
        )
        pull_top = pull.astype(BF16)
        pull_rest = (pull - pull_top.astype(F32)).astype(BF16)
        spread = dt_gh[:, here]
        src_ref[...] += mm(spread, pull_top) + mm(spread, pull_rest)
        onehot = oh_gh[here, :]
        fgh_s[...] += mm(top, onehot) + mm(rest, onehot)

    over_ghost_steps(steps, ghost_finish)
    low, mid = flow_ref.shape[1], fmid_ref.shape[1]
    flow_ref[...] = fgh_s[:, 0:low]
    fmid_ref[...] = fgh_s[:, low : low + mid]
    fhigh_ref[...] = fgh_s[:, low + mid :]


def third_stage(pieces, feats, *rest):
    atoms, feat = feats.shape
    half = atoms * HALF
    ghosts = sum(piece.shape[0] for piece in pieces)
    sizes = (ghosts // 4, ghosts // 2, ghosts // 4)
    out_shape = (
        struct(atoms, feat, dtype=BF16),
        struct(1, atoms),
        struct(atoms, CH),
        struct(8, atoms),
    ) + tuple(struct(8, size) for size in sizes) + (
        struct(atoms, GROUP_COLS[1], dtype=BF16),
    )
    scratch = pair_scratch(atoms, half, ghosts, 1) + [
        pltpu.VMEM((half, CH), BF16),
        pltpu.VMEM((atoms, CH), F32),
        pltpu.VMEM((8, ghosts), F32),
    ]
    scratch += [pltpu.VMEM((half, CH), BF16)] * len(DEGREES[1])
    args = tuple(pieces) + (feats,) + rest
    return call(
        third_kernel, "third_group", out_shape, scratch, args,
        any_specs(len(pieces), len(args)), 28,
    )


def own_back_kernel(
    steps, oh_own, pre_own, unit_own, radt_ref, rbft_ref, mix_ref, gs0_ref,
    m0_ref, nf0_ref, dot_a, dot_c, *refs
):
    gr_own, (src_in, onto_in, src_out, onto_out) = refs[:PARTIALS], refs[PARTIALS:]
    atoms = oh_own.shape[1]
    spacing = spacing_of(atoms, rbft_ref.shape[1])
    grad = tiled(gs0_ref[...])
    mix_t = flip(mix_ref[0])
    src = src_in[...]
    onto = onto_in[...]
    for step in steps:
        rows = own_rows(step)
        pull, top, rest = finish(
            grad, m0_ref[rows, :], nf0_ref[rows, :], sum_of((dot_a, dot_c), rows),
            degree_parts(gr_own, rows), pre_own[rows, :], unit_own[rows, :], spacing, radt_ref,
            rbft_ref, mix_t,
        )
        src += over_slots(pull, atoms)
        onehot = oh_own[rows, :]
        onto += mm(top, onehot) + mm(rest, onehot)
    src_out[...] = src
    onto_out[...] = onto


def own_back_stage(steps, *args):
    atoms = args[0].shape[1]
    out_shape = (struct(atoms, CH), struct(8, atoms))
    kernel = functools.partial(own_back_kernel, tuple(steps))
    return call(kernel, "own_back", out_shape, [], args)


def ring(axis):
    peers = lax.axis_size(axis)
    up = [(i, (i + 1) % peers) for i in range(peers)]
    return up, [(j, i) for i, j in up]


def neighbours_of(block, axis, dim):
    up, down = ring(axis)
    length = block.shape[dim]
    if len(up) == 2 and length == 2:
        other = lax.ppermute(block, axis, up)
        return (
            lax.slice_in_dim(other, length - 1, length, axis=dim),
            lax.slice_in_dim(other, 0, 1, axis=dim),
        )
    before = lax.ppermute(lax.slice_in_dim(block, length - 1, length, axis=dim), axis, up)
    after = lax.ppermute(lax.slice_in_dim(block, 0, 1, axis=dim), axis, down)
    return before, after


def grown(block, axis, dim):
    before, after = neighbours_of(block, axis, dim)
    return jnp.concatenate([before, block, after], axis=dim)


def flat_rows(piece):
    return piece.reshape(-1, piece.shape[-1])


def fold_kernel(mid_ref, low_ref, high_ref, out_ref):
    lanes = mid_ref.shape[1]
    ext_y = iota(mid_ref.shape, 1) // 32 % 4
    out_ref[...] = (
        mid_ref[...]
        + jnp.where(ext_y == 1, pltpu.roll(low_ref[...], lanes - 64, 1), 0.0)
        + jnp.where(ext_y == 2, pltpu.roll(high_ref[...], 64, 1), 0.0)
    )


def forces_kernel(mid_ref, low_ref, high_ref, src_ref, onto_ref, home_ref, out_ref):
    values = mid_ref[...]
    lanes = values.shape[1]
    ext_z = iota(values.shape, 1) // 8 % 4
    values += jnp.where(ext_z == 1, pltpu.roll(low_ref[...], lanes - 16, 1), 0.0)
    values += jnp.where(ext_z == 2, pltpu.roll(high_ref[...], 16, 1), 0.0)
    first = values.astype(BF16)
    values -= first.astype(F32)
    second = values.astype(BF16)
    third = (values - second.astype(F32)).astype(BF16)
    home = home_ref[...]
    total = onto_ref[...] - src_ref[...].T[0:8, :]
    total += (mm_nt(first, home) + (mm_nt(second, home) + mm_nt(third, home)))
    for comp in range(3):
        out_ref[comp] = -total[comp : comp + 1, :]


def give_back_x(low, mid, high):
    up, down = ring("gx")
    from_low = lax.ppermute(high, "gx", up)
    from_high = lax.ppermute(low, "gx", down)
    return mid, jnp.concatenate([from_low, from_high], axis=1)


def give_back_y(mid):
    up, down = ring("gy")
    return mid, lax.ppermute(mid, "gy", up), lax.ppermute(mid, "gy", down)


def fold(*args):
    return call(fold_kernel, "fold", (struct(*args[0].shape),), [], args)[0]


def give_back_z(mid):
    up, down = ring("gz")
    from_low = lax.ppermute(mid, "gz", up)
    return mid, from_low, from_low if len(up) == 2 else lax.ppermute(mid, "gz", down)


def local(
    features,
    positions,
    neighbours,
    counts,
    cell_atoms,
    rbf_weight,
    radial_weight,
    mix_weight,
    out_weight,
    energy_weight,
    norm_weight,
):
    feats = features[0, 0, 0]
    places = jnp.swapaxes(positions[0, 0], 0, 1)
    lists = jnp.concatenate([neighbours[0, 0, 0].T, counts[0, 0], cell_atoms[0, 0]], axis=0)
    cells0, cells1, own_pos, meta = make_cells(feats, places, lists)
    hold = lax.optimization_barrier
    block0, block1 = (part.reshape(2, 2, 2, 8, part.shape[1]) for part in (cells0, cells1))
    z0 = neighbours_of(block0, "gz", 2)
    z1 = neighbours_of(block1, "gz", 2)
    y1_in = neighbours_of(block1, "gy", 1)
    z0, own_pos, meta = hold((z0, own_pos, meta))
    block0 = jnp.concatenate([z0[0], block0, z0[1]], axis=2)
    y0 = neighbours_of(block0, "gy", 1)
    oh_own, pre_own, unit_own, radt, rbft, home, *radial_own = own_stage(
        meta, own_pos, rbf_weight, radial_weight
    )
    z1, y1_in, oh_own = hold((z1, y1_in, oh_own))
    block1 = jnp.concatenate([z1[0], block1, z1[1]], axis=2)
    x1_in = neighbours_of(block1, "gx", 0)
    y0, z1, oh_own = hold((y0, z1, oh_own))
    middle = jnp.concatenate([y0[0], block0, y0[1]], axis=1)
    x0 = neighbours_of(middle, "gx", 0)
    y1_out = neighbours_of(jnp.concatenate(z1, axis=2), "gy", 1)
    x1_in, oh_own = hold((x1_in, oh_own))
    (m0_own, gate_own, nf0_own, acc0), (own_a,) = own_forward_stage(
        (0,), feats, mix_weight, oh_own, radial_own
    )
    _, (own_b,) = own_forward_stage((1,), feats, mix_weight, oh_own, radial_own, gate_own)
    x0, y1_out, acc0, acc_b = hold((x0, y1_out, acc0, own_b[2]))
    pieces0 = tuple(flat_rows(piece) for piece in (x0[0], middle, x0[1]))
    y1 = [
        jnp.concatenate([out[:, :, 0:1], inner, out[:, :, 1:2]], axis=2)
        for out, inner in zip(y1_out, y1_in)
    ]
    outer = jnp.concatenate(y1, axis=1)
    x1_out = neighbours_of(outer, "gx", 0)
    block1 = jnp.concatenate([y1[0], block1, y1[1]], axis=1)
    pieces1 = (x1_in[0], x1_out[0], block1, x1_in[1], x1_out[1])
    pieces1 = tuple(flat_rows(piece) for piece in pieces1)
    (
        new_0, oh_gh, d_gh, dt_gh, pre_gh, unit_gh, gs0, en_0, m0_gh, gate_gh, nf0_gh, *radial_gh,
    ) = start_stage(
        pieces0, feats, own_pos, meta, rbf_weight, radial_weight, mix_weight, out_weight,
        energy_weight[None], acc0,
    )
    shared = (feats, meta, mix_weight, out_weight, norm_weight, oh_gh, d_gh, dt_gh, gate_gh)
    new_a, en_a, _, (dot_gh_a, *gr_gh_a), (dot_own_a, *gr_own_a) = pairs_stage(
        0, 2 * CH, pieces0, shared, (gate_own, *own_a), radial_gh
    )
    new, energy, src, onto, low, mid, high, gs_b = third_stage(
        pieces1, *shared, acc_b, radt, rbft, gs0, en_0, en_a, new_0, new_a, pre_gh,
        unit_gh, m0_gh, nf0_gh, dot_gh_a, *gr_gh_a,
        *[radial_gh[degree - 1] for degree in DEGREES[1]],
    )
    mid, arrived = give_back_x(low, mid, high)
    dot_own_b, *gr_own_b = own_backward_stage(1, mix_weight, gs_b, gate_own, *own_b[:2])
    arrived, gs0, dot_own_b = hold((arrived, gs0, dot_own_b))
    mid, from_low, from_high = give_back_y(mid + arrived)
    back = (oh_own, pre_own, unit_own, radt, rbft, mix_weight, gs0, m0_own, nf0_own)
    back += (dot_own_a, dot_own_b, *gr_own_a, *gr_own_b)
    src, onto = own_back_stage(range(2), *back, src, onto)
    from_low, from_high, src = hold((from_low, from_high, src))
    folded = give_back_z(fold(mid, from_low, from_high))
    src, onto = own_back_stage(range(2, 4), *back, src, onto)
    args = (*folded, src, onto, home)
    out_shape = (struct(3, 1, src.shape[0]),)
    forces = call(forces_kernel, "forces", out_shape, [], args)[0]
    return (
        new[None, None, None],
        energy[None, None],
        jnp.swapaxes(forces, 0, 1)[None, None],
    )


def solution(mesh):
    split = P("gx", "gy", "gz", None, None)
    flat = P("gx", "gy", "gz", None)
    return jax.shard_map(
        local,
        mesh=mesh,
        in_specs=(split, split, split, flat, flat, P(), P(), P(), P(), P(), P()),
        out_specs=(split, flat, split),
        check_vma=False,
    )
```

```python
import functools
import math

import jax
import jax.numpy as jnp
from jax import lax
from jax.experimental import pallas as pl
from jax.experimental.pallas import tpu as pltpu
from jax.sharding import PartitionSpec as P

F32 = jnp.float32
BF16 = jnp.bfloat16
CH = 128
SLOTS = 32
HALF = 16
STEP = 256
OWN_STEPS = 4
GH_STEPS = 2
MIB = 1024 * 1024
SPACE = pltpu.VMEM
PAIR_DEGREES = (
    (1, 1), (1, 2), (2, 2), (2, 2),
    (3, 3), (3, 3), (3, 3), (3, 4),
    (4, 4), (4, 4), (4, 4), (4, 4),
)
GROUPS = ((0, 4), (4, 12))
KINDS = tuple(sorted({PAIR_DEGREES[pair] for pair in range(*group)}) for group in GROUPS)
DEGREES = tuple(sorted({d for both in kinds for d in both}) for kinds in KINDS)
GROUP_COLS = tuple(2 * CH * (end - begin) for begin, end in GROUPS)


def mm(a, b):
    return jnp.dot(a, b, preferred_element_type=F32)


def mm_nt(a, b):
    return lax.dot_general(a, b, (((1,), (1,)), ((), ())), preferred_element_type=F32)


def iota(shape, dim):
    return lax.broadcasted_iota(jnp.int32, shape, dim)


def flip(w):
    return w.astype(F32).T.astype(BF16)


def pair_cols(pair):
    return slice(CH + pair * 2 * CH, CH + (pair + 1) * 2 * CH)


def struct(*shape, dtype=F32):
    return jax.ShapeDtypeStruct(shape, dtype)


def call(kernel, name, out_shape, scratch, args, specs=None, limit=16, work=1024):
    return pl.pallas_call(
        kernel,
        out_shape=out_shape,
        in_specs=specs or [pl.BlockSpec(memory_space=SPACE)] * len(args),
        out_specs=tuple(pl.BlockSpec(memory_space=SPACE) for _ in out_shape),
        scratch_shapes=scratch,
        compiler_params=pltpu.CompilerParams(vmem_limit_bytes=limit * MIB),
        cost_estimate=pl.CostEstimate(flops=work, bytes_accessed=1024, transcendentals=0),
        name=name,
    )(*args)


def cells_kernel(
    feat_ref, pos_ref, lists_ref,
    out_ref, own_pos_ref, meta_ref, pick_ref, rows_ref, pos_rows,
):
    rows_ref[...] = jnp.zeros_like(rows_ref)
    pos_rows[...] = jnp.zeros_like(pos_rows)
    atoms = feat_ref.shape[0]
    rows_ref[0 : SLOTS + 2, :] = lists_ref[...].astype(F32)
    meta = rows_ref[...].T
    meta_ref[...] = meta
    for comp in range(3):
        places = pos_ref[comp]
        first = places.astype(BF16).astype(F32)
        second = (places - first).astype(BF16).astype(F32)
        pos_rows[comp : comp + 1, :] = first
        pos_rows[4 + comp : 5 + comp, :] = second
        pos_rows[8 + comp : 9 + comp, :] = places - first - second
    pieces = pos_rows[...].astype(BF16)
    lane = iota((atoms, atoms), 1).astype(F32)
    pick = (meta[:, SLOTS + 1 : SLOTS + 2] == lane).astype(F32).astype(BF16)
    same = (iota((atoms, atoms), 0) == iota((atoms, atoms), 1)).astype(F32).astype(BF16)
    own_pos_ref[...] = mm_nt(same, pieces).astype(BF16)
    out_ref[:, CH : 2 * CH] = mm_nt(pick, pieces).astype(BF16)
    pick_ref[...] = pick
    out_ref[:, 0:CH] = mm(pick, feat_ref[:, 0:CH]).astype(BF16)
    cut = pair_cols(GROUPS[1][0]).start
    out_ref[:, 2 * CH :] = mm(pick, feat_ref[:, CH:cut]).astype(BF16)


def rest_kernel(feat_ref, pick_ref, rest_ref):
    cut = pair_cols(GROUPS[1][0]).start
    rest_ref[...] = mm(pick_ref[...], feat_ref[:, cut:]).astype(BF16)


def make_cells(feats, places, lists):
    atoms = feats.shape[0]
    out_shape = (
        struct(atoms, 2 * CH + GROUP_COLS[0], dtype=BF16),
        struct(atoms, CH, dtype=BF16),
        struct(atoms, CH),
        struct(atoms, atoms, dtype=BF16),
    )
    args = (feats, places, lists)
    scratch = [pltpu.VMEM((CH, atoms), F32), pltpu.VMEM((CH, atoms), F32)]
    first, own_pos, meta, pick = call(cells_kernel, "cells", out_shape, scratch, args)
    out_shape = (struct(atoms, GROUP_COLS[1], dtype=BF16),)
    rest = call(rest_kernel, "cells_rest", out_shape, [], (feats, pick), work=1 << 32)[0]
    return first, rest, own_pos, meta


def spacing_of(atoms, nbasis):
    depth = atoms // 16
    return 2.0 * math.sqrt(32.0 + depth * depth) / (nbasis - 1)


def own_onehots(meta_ref, oh_own):
    atoms = meta_ref.shape[0]
    counts = meta_ref[:, SLOTS : SLOTS + 1]
    lane_atom = iota((atoms, atoms), 1).astype(F32)
    for slot in range(HALF):
        hit = jnp.logical_and(meta_ref[:, slot : slot + 1] == lane_atom, counts > slot)
        oh_own[slot * atoms : (slot + 1) * atoms, :] = hit.astype(F32).astype(BF16)


def geometry(near, here):
    diff = near - here
    rel = (diff + pltpu.roll(diff, CH - 4, 1)) + (
        pltpu.roll(diff, CH - 8, 1) + pltpu.roll(diff, CH - 12, 1)
    )
    lane = iota(rel.shape, 1)
    rel = jnp.where(lane < 3, rel, 0.0)
    square = jnp.sum(rel * rel, axis=1, keepdims=True)
    inverse = lax.rsqrt(jnp.where(square > 0.0, square, 1.0))
    dist = square * inverse
    return jnp.where(lane == 3, dist, rel * inverse), dist


def centred_of(dist, spacing, nbasis):
    return dist * (1.0 / spacing) - iota((dist.shape[0], nbasis), 1).astype(F32)


def radial_net(dist, spacing, rbf_ref, rad_ref):
    centred = centred_of(dist, spacing, rbf_ref.shape[0])
    basis = jnp.exp(-0.5 * centred * centred)
    pre = mm(basis.astype(BF16), rbf_ref[...])
    hidden = (pre * jax.nn.sigmoid(pre)).astype(BF16)
    return pre, mm(hidden, rad_ref[...]).astype(BF16)


def tiled(values, size=STEP):
    return jnp.concatenate([values] * (size // values.shape[0]), axis=0)


def live_ghosts(meta_ref):
    return jnp.maximum(meta_ref[:, SLOTS : SLOTS + 1] - HALF, 0.0)


def step_count(meta_ref):
    total = jnp.sum(live_ghosts(meta_ref)).astype(jnp.int32)
    rows = GH_STEPS * STEP
    return jnp.maximum((total + (rows - 1)) // rows, 1) * GH_STEPS


def own_rows(step, size=STEP):
    return pl.ds(step * size, size)


def ghost_rows(step, size=STEP):
    first = OWN_STEPS * STEP
    if isinstance(step, int):
        return pl.ds(step * size, size), pl.ds(first + step * size, size)
    base = pl.multiple_of(step * size, size)
    return pl.ds(base, size), pl.ds(pl.multiple_of(first + base, size), size)


def over_ghost_steps(steps, body, size=STEP):
    static = GH_STEPS * STEP // size
    for step in range(static):
        body(step)

    def again(step, carry):
        body(step)
        return carry

    lax.fori_loop(static, (steps * STEP + (size - 1)) // size, again, 0)


def block_diagonal(kinds, source, straight=None, across=None):
    zero = jnp.zeros((CH, CH), BF16)
    targets = [ref for ref in (straight, across) if ref is not None]
    for kind, both in enumerate(kinds):
        for ref in targets:
            ref[kind, 0:CH, CH:] = zero
            ref[kind, CH:, 0:CH] = zero
    for degree in sorted({d for both in kinds for d in both}):
        weight = source[degree]
        flipped = flip(weight) if across is not None else None
        for kind, both in enumerate(kinds):
            for side in range(2):
                if both[side] == degree:
                    part = slice(side * CH, side * CH + CH)
                    if straight is not None:
                        straight[kind, part, part] = weight
                    if across is not None:
                        across[kind, part, part] = flipped


def fetch(pieces, cols, table, sems):
    low, high, ghosts = 0, 0, table.shape[0]
    if len(pieces) == 3:
        rows = [(piece, 0, piece.shape[0]) for piece in pieces]
    else:
        low_in, low_out, mid, high_in, high_out = pieces
        half = low_out.shape[0] // 2
        rows = [(low_out, 0, half), (low_in, 0, low_in.shape[0]), (low_out, half, half)]
        rows += [(mid, 0, mid.shape[0])]
        rows += [(high_out, 0, half), (high_in, 0, high_in.shape[0]), (high_out, half, half)]
    copies = []
    at = 0
    for index, (piece, start, count) in enumerate(rows):
        source = piece.at[pl.ds(start, count), cols]
        target = table.at[pl.ds(at, count), :]
        copies.append(pltpu.make_async_copy(source, target, sems.at[index]))
        at += count
    for copy in copies:
        copy.start()
    return copies


def infos_of(group):
    infos = []
    for index, pair in enumerate(range(*GROUPS[group])):
        degrees = PAIR_DEGREES[pair]
        cols = slice(index * 2 * CH, (index + 1) * 2 * CH)
        infos.append((cols, degrees, KINDS[group].index(degrees)))
    return infos


def group_cols(group):
    begin, end = GROUPS[group]
    return slice(pair_cols(begin).start, pair_cols(end - 1).stop)


def twice(values):
    return jnp.concatenate([values, values], axis=1)


def forward(group, rows, onehot, feats, radials, gate_ref, wm, nf_ref, mx_ref, slots):
    near = mm(onehot, feats).astype(BF16)
    nf_ref[rows, :] = near
    gate = twice(gate_ref[rows, :])
    wide = gate.astype(F32) if slots else None
    messages = []
    for cols, degrees, kind in infos_of(group):
        radial = jnp.concatenate([radials[d][rows, :] for d in degrees], axis=1)
        mixed = mm(near[:, cols] * radial, wm[kind])
        low = mixed.astype(BF16)
        mx_ref[rows, cols] = low
        messages.append(mixed * wide if slots else low * gate)
    return messages


def backward(group, rows, grad, gate_ref, wmt, nf_ref, mx_ref, dot_ref, grad_refs):
    parts = {}
    dots = None
    gate = twice(gate_ref[rows, :])
    for cols, degrees, kind in infos_of(group):
        product = grad[:, cols] * mx_ref[rows, cols]
        dot = (product[:, 0:CH] + product[:, CH:]).astype(F32)
        dots = dot if dots is None else dots + dot
        weighted = mm(grad[:, cols] * gate, wmt[kind]) * nf_ref[rows, cols].astype(F32)
        for side in range(2):
            part = weighted[:, side * CH : (side + 1) * CH]
            degree = degrees[side]
            parts[degree] = parts[degree] + part if degree in parts else part
    dot_ref[rows, :] = dots.astype(dot_ref.dtype)
    for degree, part in parts.items():
        grad_refs[degree][rows, :] = part.astype(grad_refs[degree].dtype)


def over_slots(values, atoms):
    return jnp.sum(values.reshape(-1, atoms, values.shape[1]), axis=0)


def own_forward(group, own_ref, oh_own, radials, gate_ref, wm, nf_ref, mx_ref, acc_ref):
    atoms = own_ref.shape[0]
    feats = own_ref[:, group_cols(group)]
    for step in range(OWN_STEPS):
        rows = own_rows(step)
        messages = forward(
            group, rows, oh_own[rows, :], feats, radials, gate_ref, wm, nf_ref, mx_ref, True
        )
        for (cols, _, _), message in zip(infos_of(group), messages):
            part = over_slots(message, atoms)
            acc_ref[:, cols] = part if step == 0 else acc_ref[:, cols] + part


def own_backward(group, gs_ref, gate_ref, wmt, nf_ref, mx_ref, dot_ref, grad_refs):
    grad = tiled(gs_ref[...])
    for step in range(OWN_STEPS):
        backward(
            group, own_rows(step), grad, gate_ref, wmt, nf_ref, mx_ref, dot_ref, grad_refs
        )


def ghost_pairs(
    group, own_ref, table, new_ref, new_base, oh_gh, d_gh, dt_gh, gate_ref, radials, nw_ref,
    steps, wm, wmt, wo, wot, nf_s, mx_s, acc_in, acc_s, gs_ref, dot_ref, grad_refs, en_ref,
):
    norm = 1.0 / math.sqrt(SLOTS)
    acc_s[...] = acc_in[...]

    def ghost_forward(step):
        here, _ = ghost_rows(step)
        messages = forward(
            group, here, oh_gh[here, :], table[...], radials, gate_ref, wm, nf_s, mx_s, False
        )
        acc_s[...] += mm(dt_gh[:, here], jnp.concatenate(messages, axis=1))

    over_ghost_steps(steps, ghost_forward)

    begin = group_cols(group).start
    for cols, degrees, kind in infos_of(group):
        summed_low = (acc_s[:, cols] * norm).astype(BF16)
        own = own_ref[:, begin + cols.start : begin + cols.stop]
        updated = own.astype(F32) + mm(summed_low, wo[kind])
        at = begin - new_base + cols.start
        new_ref[:, at : at + 2 * CH] = updated.astype(BF16)
        weight = jnp.concatenate(
            [nw_ref[d - 1 : d, :] * (1.0 / (2 * d + 1)) for d in degrees], axis=1
        )
        scale = weight * updated
        energy = scale * updated
        en_ref[...] += energy[:, 0:CH] + energy[:, CH:]
        gs_ref[:, cols] = (mm((2.0 * scale).astype(BF16), wot[kind]) * norm).astype(BF16)

    def ghost_backward(step):
        here, _ = ghost_rows(step)
        grad = mm(d_gh[here, :], gs_ref[...]).astype(BF16)
        backward(group, here, grad, gate_ref, wmt, nf_s, mx_s, dot_ref, grad_refs)

    over_ghost_steps(steps, ghost_backward)


def pair_scratch(atoms, half, ghosts, group):
    count, width = len(KINDS[group]), GROUP_COLS[group]
    return (
        [pltpu.VMEM((ghosts, width), BF16), pltpu.SemaphoreType.DMA((7,))]
        + [pltpu.VMEM((count, 2 * CH, 2 * CH), BF16) for _ in range(4)]
        + [
            pltpu.VMEM((half, width), BF16),
            pltpu.VMEM((half, width), BF16),
            pltpu.VMEM((atoms, width), F32),
        ]
    )


def own_kernel(
    meta_ref, own_pos_ref, rbf_ref, rad_ref,
    oh_own, pre_ref, unit_ref, radt_ref, rbft_ref, home_ref, *radial_refs
):
    atoms = meta_ref.shape[0]
    nbasis = rbft_ref.shape[1]
    spacing = spacing_of(atoms, nbasis)
    own_onehots(meta_ref, oh_own)
    here = tiled(own_pos_ref[...].astype(F32))
    for step in range(OWN_STEPS):
        rows = own_rows(step)
        unit, dist = geometry(mm(oh_own[rows, :], own_pos_ref[...]), here)
        unit_ref[rows, :] = unit
        pre, radial = radial_net(dist, spacing, rbf_ref, rad_ref)
        pre_ref[rows, :] = pre.astype(BF16)
        for degree, ref in enumerate(radial_refs):
            ref[rows, :] = radial[:, degree * CH : (degree + 1) * CH]
    for degree in range(5):
        part = slice(degree * CH, (degree + 1) * CH)
        radt_ref[part, :] = flip(rad_ref[:, part])
    for index in range(nbasis // CH):
        part = slice(index * CH, (index + 1) * CH)
        rbft_ref[:, part] = flip(rbf_ref[part, :])
    lanes = home_ref.shape[1]
    lane = iota((atoms, lanes), 1)
    ext_x, ext_y, ext_z = lane // 128, lane // 32 % 4, lane // 8 % 4
    slot = ((2 * ext_x + ext_y - 1) * 2 + ext_z - 1) * 8 + lane % 8
    inside = jnp.logical_and(
        jnp.logical_or(ext_y == 1, ext_y == 2), jnp.logical_or(ext_z == 1, ext_z == 2)
    )
    to_slot = jnp.logical_and(iota((atoms, lanes), 0) == slot, inside)
    to_slot = to_slot.astype(F32).astype(BF16)
    order = meta_ref[:, SLOTS + 1 : SLOTS + 2]
    to_atom = (order == iota((atoms, atoms), 1).astype(F32)).astype(F32)
    home_ref[...] = mm(to_atom.T.astype(BF16), to_slot).astype(BF16)


def own_stage(meta, own_pos, rbf, rad):
    atoms = meta.shape[0]
    edges = atoms * HALF
    out_shape = (
        struct(edges, atoms, dtype=BF16),
        struct(edges, CH, dtype=BF16),
        struct(edges, CH),
        struct(5 * CH, CH, dtype=BF16),
        struct(CH, rbf.shape[0], dtype=BF16),
        struct(atoms, 256, dtype=BF16),
    ) + (struct(edges, CH, dtype=BF16),) * 5
    return call(own_kernel, "own_edges", out_shape, [], (meta, own_pos, rbf, rad))


def scalar_forward(rows, near, radial, mix_ref, m0_ref, gate_ref, nf0_ref):
    near = near.astype(BF16)
    nf0_ref[rows, :] = near
    mixed = mm(near * radial, mix_ref[0])
    m0_ref[rows, :] = mixed.astype(BF16)
    gate = jax.nn.sigmoid(mixed)
    gate_ref[rows, :] = gate.astype(BF16)
    return mixed * gate


def own_forward_kernel(groups, scalar, *refs):
    own_ref, mix_ref, oh_own, refs = *refs[:3], refs[3:]
    radial0, radials = refs[0], dict(enumerate(refs[1:5], start=1))
    refs = refs[5:]
    if scalar:
        m0_ref, gate_ref, nf0_ref, acc0_ref = refs[:4]
        refs = refs[4:]
        atoms = own_ref.shape[0]
        feats = own_ref[:, 0:CH]
        summed = None
        for step in range(OWN_STEPS):
            rows = own_rows(step)
            message = scalar_forward(
                rows, mm(oh_own[rows, :], feats), radial0[rows, :], mix_ref, m0_ref, gate_ref,
                nf0_ref,
            )
            part = over_slots(message, atoms)
            summed = part if summed is None else summed + part
        acc0_ref[...] = summed
    else:
        gate_ref, refs = refs[0], refs[1:]
    outs, weights = refs[: 3 * len(groups)], refs[3 * len(groups) :]
    for index, group in enumerate(groups):
        block_diagonal(KINDS[group], mix_ref, weights[index])
        nf_ref, mx_ref, acc_ref = outs[3 * index : 3 * index + 3]
        own_forward(
            group, own_ref, oh_own, radials, gate_ref, weights[index], nf_ref, mx_ref, acc_ref
        )


def own_forward_stage(groups, feats, mix, oh_own, radial_own, gate=None):
    atoms = feats.shape[0]
    half = atoms * HALF
    out_shape = ()
    if gate is None:
        out_shape += (struct(half, CH, dtype=BF16),) * 3 + (struct(atoms, CH),)
    for group in groups:
        width = GROUP_COLS[group]
        out_shape += (struct(half, width, dtype=BF16),) * 2 + (struct(atoms, width),)
    args = (feats, mix, oh_own, *radial_own) + (() if gate is None else (gate,))
    scratch = [pltpu.VMEM((len(KINDS[group]), 2 * CH, 2 * CH), BF16) for group in groups]
    name = "own_forward_" + "".join("abc"[group] for group in groups)
    kernel = functools.partial(own_forward_kernel, groups, gate is None)
    outs = call(kernel, name, out_shape, scratch, args)
    first = len(outs) - 3 * len(groups)
    return outs[:first], [outs[first + 3 * i : first + 3 * i + 3] for i in range(len(groups))]


def start_kernel(
    p0, p1, p2, own_ref, own_pos_ref, meta_ref, rbf_ref, rad_ref, mix_ref, out_ref, ew_ref,
    acc0_ref,
    new_ref, oh_gh, d_gh, dt_gh, pre_ref, unit_ref, gs0_ref, en_ref, m0_gh, gate_gh, nf0_gh,
    radial_gh1, radial_gh2, radial_gh3, radial_gh4,
    table, sems, ghpos, acc_s,
):
    radial_gh = (None, radial_gh1, radial_gh2, radial_gh3, radial_gh4)
    copies = fetch((p0, p1, p2), slice(0, 2 * CH), table, sems)
    atoms = own_ref.shape[0]
    ghosts = table.shape[0]
    spacing = spacing_of(atoms, rbf_ref.shape[0])
    norm = 1.0 / math.sqrt(SLOTS)

    live = live_ghosts(meta_ref)
    sub_atom = iota((atoms, atoms), 0)
    lane_atom = iota((atoms, atoms), 1)
    live_b = jnp.broadcast_to(live, (atoms, atoms))
    end_row = jnp.sum(jnp.where(sub_atom <= lane_atom, live_b, 0.0), axis=0, keepdims=True)
    live_row = jnp.sum(jnp.where(sub_atom == lane_atom, live_b, 0.0), axis=0, keepdims=True)
    start_row = end_row - live_row
    row_b = jnp.broadcast_to(live_row, (atoms, atoms))
    end_col = jnp.sum(jnp.where(lane_atom <= sub_atom, row_b, 0.0), axis=1, keepdims=True)
    start_col = end_col - live
    total = jnp.sum(live)
    steps = step_count(meta_ref)
    ghost_row = meta_ref[:, HALF:SLOTS] - atoms
    high_part = jnp.floor(ghost_row * (1.0 / 16.0))
    row_high = high_part.astype(BF16)
    row_low = (ghost_row - 16.0 * high_part).astype(BF16)

    row = iota((ghosts, CH), 0)
    lane = iota((ghosts, CH), 1)
    zcells = atoms // 32
    per_y = (zcells + 2) * 8
    ext_x = row // (4 * per_y)
    ext_y = row // per_y % 4
    ext_z = row // 8 % (zcells + 2)

    def side_of(ext, last, size):
        return jnp.where(ext == 0, -size, jnp.where(ext == last, size, 0.0))

    shift = jnp.where(lane == 12, side_of(ext_x, 3, 4.0), 0.0)
    shift = jnp.where(lane == 13, side_of(ext_y, 3, 4.0), shift)
    shift = jnp.where(lane == 14, side_of(ext_z, zcells + 1, 2.0 * zcells), shift)
    own0 = own_ref[:, 0:CH]
    acc_s[...] = acc0_ref[...]
    for copy in copies:
        copy.wait()
    ghpos[...] = (table[:, CH:].astype(F32) + shift).astype(BF16)

    def ghost_start(step):
        here, _ = ghost_rows(step)
        base = step * STEP
        edge = (iota((STEP, atoms), 0) + base).astype(F32)
        mine = jnp.logical_and(edge >= start_row, edge < end_row).astype(F32)
        source = mine.astype(BF16)
        d_gh[here, :] = source
        edge_t = (iota((atoms, STEP), 1) + base).astype(F32)
        mine_t = jnp.logical_and(edge_t >= start_col, edge_t < end_col)
        spread = mine_t.astype(F32).astype(BF16)
        dt_gh[:, here] = spread
        edge_col = edge[:, 0:1]
        slot = edge_col - jnp.sum(mine * start_row, axis=1, keepdims=True)
        listed = mm(source, row_high) * 16.0 + mm(source, row_low)
        at_slot = iota((STEP, HALF), 1).astype(F32) == slot
        which = jnp.sum(jnp.where(at_slot, listed, 0.0), axis=1, keepdims=True)
        which = jnp.where(edge_col < total, which, -1.0)
        onehot = (iota((STEP, ghosts), 1).astype(F32) == which).astype(F32).astype(BF16)
        oh_gh[here, :] = onehot
        unit, dist = geometry(mm(onehot, ghpos[...]), mm(source, own_pos_ref[...]))
        unit_ref[here, :] = unit
        pre, radial = radial_net(dist, spacing, rbf_ref, rad_ref)
        pre_ref[here, :] = pre.astype(BF16)
        for degree in range(1, 5):
            radial_gh[degree][here, :] = radial[:, degree * CH : (degree + 1) * CH]
        message = scalar_forward(
            here, mm(onehot, table[:, 0:CH]), radial[:, 0:CH], mix_ref, m0_gh, gate_gh, nf0_gh
        )
        acc_s[...] += mm(spread, message.astype(BF16))

    over_ghost_steps(steps, ghost_start)

    low0 = (acc_s[...] * norm).astype(BF16)
    updated0 = own0.astype(F32) + mm(low0, out_ref[0])
    new_ref[:, 0:CH] = updated0.astype(BF16)
    logistic = jax.nn.sigmoid(updated0)
    weight0 = ew_ref[...]
    en_ref[...] = weight0 * updated0 * logistic
    grad0 = (weight0 * logistic * (1.0 + updated0 * (1.0 - logistic))).astype(BF16)
    gs0_ref[...] = mm_nt(grad0, out_ref[0]) * norm


def any_specs(count, total):
    return [pl.BlockSpec(memory_space=pl.ANY)] * count + [
        pl.BlockSpec(memory_space=SPACE)
    ] * (total - count)


def start_stage(pieces, feats, *rest):
    atoms = feats.shape[0]
    half = atoms * HALF
    ghosts = sum(piece.shape[0] for piece in pieces)
    out_shape = (
        struct(atoms, CH, dtype=BF16),
        struct(half, ghosts, dtype=BF16),
        struct(half, atoms, dtype=BF16),
        struct(atoms, half, dtype=BF16),
        struct(half, CH, dtype=BF16),
        struct(half, CH),
        struct(atoms, CH),
        struct(atoms, CH),
    ) + (struct(half, CH, dtype=BF16),) * 7
    scratch = [
        pltpu.VMEM((ghosts, 2 * CH), BF16),
        pltpu.SemaphoreType.DMA((7,)),
        pltpu.VMEM((ghosts, CH), BF16),
        pltpu.VMEM((atoms, CH), F32),
    ]
    args = tuple(pieces) + (feats,) + rest
    return call(
        start_kernel, "ghost_start", out_shape, scratch, args,
        any_specs(len(pieces), len(args)), 24,
    )


def pairs_kernel(group, count, skip, *refs):
    pieces, refs = refs[:count], refs[count:]
    own_ref, meta_ref, mix_ref, out_ref, nw_ref, oh_gh, d_gh, dt_gh, gate_gh = refs[:9]
    gate_own, nf_own, mx_own, acc_own = refs[9:13]
    refs = refs[13:]
    degrees = DEGREES[group]
    radials, refs = dict(zip(degrees, refs)), refs[len(degrees) :]
    new_ref, en_ref, gs_ref, dot_gh = refs[:4]
    grads, refs = dict(zip(degrees, refs[4:])), refs[4 + len(degrees) :]
    if group == 0:
        dot_own, refs = refs[0], refs[1:]
        grads_own, refs = dict(zip(degrees, refs)), refs[len(degrees) :]
    table, sems, wm, wmt, wo, wot, nf_s, mx_s, acc_s = refs
    copies = fetch(pieces, slice(skip, skip + GROUP_COLS[group]), table, sems)
    block_diagonal(KINDS[group], mix_ref, wm, wmt)
    block_diagonal(KINDS[group], out_ref, wo, wot)
    en_ref[...] = jnp.zeros_like(en_ref)
    for copy in copies:
        copy.wait()
    ghost_pairs(
        group, own_ref, table, new_ref, group_cols(group).start, oh_gh, d_gh, dt_gh, gate_gh,
        radials, nw_ref, step_count(meta_ref), wm, wmt, wo, wot, nf_s, mx_s, acc_own, acc_s,
        gs_ref, dot_gh, grads, en_ref,
    )
    if group == 0:
        own_backward(group, gs_ref, gate_own, wmt, nf_own, mx_own, dot_own, grads_own)


def pairs_stage(group, skip, pieces, shared, own_parts, radial_gh):
    feats = shared[0]
    atoms = feats.shape[0]
    half = atoms * HALF
    ghosts = sum(piece.shape[0] for piece in pieces)
    degrees = DEGREES[group]
    sides = 2 if group == 0 else 1
    out_shape = (
        struct(atoms, GROUP_COLS[group], dtype=BF16),
        struct(atoms, CH),
        struct(atoms, GROUP_COLS[group], dtype=BF16),
    ) + (struct(half, CH, dtype=BF16),) * (sides * (1 + len(degrees)))
    args = tuple(pieces) + tuple(shared) + tuple(own_parts)
    args += tuple(radial_gh[degree - 1] for degree in degrees)
    new, energy, gs, *rest = call(
        functools.partial(pairs_kernel, group, len(pieces), skip), "pairs_" + "abc"[group],
        out_shape, pair_scratch(atoms, half, ghosts, group), args,
        any_specs(len(pieces), len(args)), 24,
    )
    return new, energy, gs, rest[: 1 + len(degrees)], rest[1 + len(degrees) :]


def own_backward_kernel(group, mix_ref, gs_ref, gate_ref, nf_ref, mx_ref, *refs):
    dot_ref, grads, wmt = refs[0], dict(zip(DEGREES[group], refs[1:-1])), refs[-1]
    block_diagonal(KINDS[group], mix_ref, None, wmt)
    own_backward(group, gs_ref, gate_ref, wmt, nf_ref, mx_ref, dot_ref, grads)


def own_backward_stage(group, mix, gs, gate, nf, mx):
    half = nf.shape[0]
    out_shape = (struct(half, CH, dtype=BF16),) * (1 + len(DEGREES[group]))
    scratch = [pltpu.VMEM((len(KINDS[group]), 2 * CH, 2 * CH), BF16)]
    kernel = functools.partial(own_backward_kernel, group)
    name = "own_backward_" + "abc"[group]
    return call(kernel, name, out_shape, scratch, (mix, gs, gate, nf, mx))


def finish(
    grad, mixed, near, dots, parts, pre, unit, spacing, radt_ref, rbft_ref, mix_t
):
    mixed = mixed.astype(F32)
    gate = jax.nn.sigmoid(mixed)
    first = grad * gate * (1.0 + mixed * (1.0 - gate)) + dots * gate * (1.0 - gate)
    weighted = mm(first.astype(BF16), mix_t) * near.astype(F32)
    radial_grad = jnp.concatenate([weighted.astype(BF16)] + parts, axis=1)
    hidden_grad = mm(radial_grad, radt_ref[...])
    pre = pre.astype(F32)
    logistic = jax.nn.sigmoid(pre)
    pre_grad = (hidden_grad * logistic * (1.0 + pre * (1.0 - logistic))).astype(BF16)
    centred = centred_of(unit[:, 3:4], spacing, rbft_ref.shape[1])
    slope = jnp.exp(-0.5 * centred * centred) * centred
    basis_grad = mm(pre_grad, rbft_ref[...])
    dist_grad = jnp.sum(basis_grad * slope, axis=1, keepdims=True) * (-1.0 / spacing)
    pull = unit * dist_grad
    across = pull.T[0:8, :]
    top = across.astype(BF16)
    rest = (across - top.astype(F32)).astype(BF16)
    return pull, top, rest


def sum_of(refs, rows):
    total = refs[0][rows, :].astype(F32)
    for ref in refs[1:]:
        total += ref[rows, :].astype(F32)
    return total


def degree_parts(refs, rows):
    by_degree = {}
    refs = list(refs)
    for degrees in DEGREES:
        for degree in degrees:
            by_degree.setdefault(degree, []).append(refs.pop(0))
    return [sum_of(by_degree[degree], rows).astype(BF16) for degree in range(1, 5)]


PARTIALS = sum(len(degrees) for degrees in DEGREES)


def third_kernel(
    p0, p1, p2, p3, p4, own_ref, meta_ref, mix_ref, out_ref, nw_ref, oh_gh, d_gh, dt_gh, gate_gh,
    acc_own, radt_ref, rbft_ref, gs0_ref, en_0, en_a, new_0, new_a, pre_gh, unit_gh,
    m0_ref, nf0_ref, dot_a, *refs
):
    group = 1
    before, degrees = len(DEGREES[0]), DEGREES[group]
    gr_a, refs = refs[:before], refs[before:]
    radials, refs = dict(zip(degrees, refs)), refs[len(degrees) :]
    new_ref, energy_ref, src_ref, onto_ref, flow_ref, fmid_ref, fhigh_ref, gs_ref = refs[:8]
    table, sems, wm, wmt, wo, wot, nf_s, mx_s, acc_s, dot_c, en_s, fgh_s = refs[8:20]
    grads = dict(zip(degrees, refs[20:]))
    copies = fetch((p0, p1, p2, p3, p4), slice(0, GROUP_COLS[group]), table, sems)
    atoms = own_ref.shape[0]
    spacing = spacing_of(atoms, rbft_ref.shape[1])
    block_diagonal(KINDS[group], mix_ref, wm, wmt)
    block_diagonal(KINDS[group], out_ref, wo, wot)
    en_s[...] = en_0[...] + en_a[...]
    at = 0
    for part in (new_0, new_a):
        new_ref[:, at : at + part.shape[1]] = part[...]
        at += part.shape[1]
    steps = step_count(meta_ref)

    for copy in copies:
        copy.wait()
    ghost_pairs(
        group, own_ref, table, new_ref, 0, oh_gh, d_gh, dt_gh, gate_gh, radials, nw_ref,
        steps, wm, wmt, wo, wot, nf_s, mx_s, acc_own, acc_s, gs_ref, dot_c, grads, en_s,
    )
    energy_ref[...] = jnp.sum(en_s[...].T, axis=0, keepdims=True)

    fgh_s[...] = jnp.zeros_like(fgh_s)
    src_ref[...] = jnp.zeros_like(src_ref)
    onto_ref[...] = jnp.zeros_like(onto_ref)
    gs0_low = gs0_ref[...].astype(BF16)
    mix_t = flip(mix_ref[0])

    def ghost_finish(step):
        here, _ = ghost_rows(step)
        grad = mm(d_gh[here, :], gs0_low)
        pull, top, rest = finish(
            grad, m0_ref[here, :], nf0_ref[here, :], sum_of((dot_a, dot_c), here),
            degree_parts(gr_a + refs[20:], here), pre_gh[here, :], unit_gh[here, :], spacing,
            radt_ref, rbft_ref, mix_t,
        )
        pull_top = pull.astype(BF16)
        pull_rest = (pull - pull_top.astype(F32)).astype(BF16)
        spread = dt_gh[:, here]
        src_ref[...] += mm(spread, pull_top) + mm(spread, pull_rest)
        onehot = oh_gh[here, :]
        fgh_s[...] += mm(top, onehot) + mm(rest, onehot)

    over_ghost_steps(steps, ghost_finish)
    low, mid = flow_ref.shape[1], fmid_ref.shape[1]
    flow_ref[...] = fgh_s[:, 0:low]
    fmid_ref[...] = fgh_s[:, low : low + mid]
    fhigh_ref[...] = fgh_s[:, low + mid :]


def third_stage(pieces, feats, *rest):
    atoms, feat = feats.shape
    half = atoms * HALF
    ghosts = sum(piece.shape[0] for piece in pieces)
    sizes = (ghosts // 4, ghosts // 2, ghosts // 4)
    out_shape = (
        struct(atoms, feat, dtype=BF16),
        struct(1, atoms),
        struct(atoms, CH),
        struct(8, atoms),
    ) + tuple(struct(8, size) for size in sizes) + (
        struct(atoms, GROUP_COLS[1], dtype=BF16),
    )
    scratch = pair_scratch(atoms, half, ghosts, 1) + [
        pltpu.VMEM((half, CH), BF16),
        pltpu.VMEM((atoms, CH), F32),
        pltpu.VMEM((8, ghosts), F32),
    ]
    scratch += [pltpu.VMEM((half, CH), BF16)] * len(DEGREES[1])
    args = tuple(pieces) + (feats,) + rest
    return call(
        third_kernel, "third_group", out_shape, scratch, args,
        any_specs(len(pieces), len(args)), 28,
    )


def own_back_kernel(
    steps, oh_own, pre_own, unit_own, radt_ref, rbft_ref, mix_ref, gs0_ref,
    m0_ref, nf0_ref, dot_a, dot_c, *refs
):
    gr_own, (src_in, onto_in, src_out, onto_out) = refs[:PARTIALS], refs[PARTIALS:]
    atoms = oh_own.shape[1]
    spacing = spacing_of(atoms, rbft_ref.shape[1])
    grad = tiled(gs0_ref[...])
    mix_t = flip(mix_ref[0])
    src = src_in[...]
    onto = onto_in[...]
    for step in steps:
        rows = own_rows(step)
        pull, top, rest = finish(
            grad, m0_ref[rows, :], nf0_ref[rows, :], sum_of((dot_a, dot_c), rows),
            degree_parts(gr_own, rows), pre_own[rows, :], unit_own[rows, :], spacing, radt_ref,
            rbft_ref, mix_t,
        )
        src += over_slots(pull, atoms)
        onehot = oh_own[rows, :]
        onto += mm(top, onehot) + mm(rest, onehot)
    src_out[...] = src
    onto_out[...] = onto


def own_back_stage(steps, *args):
    atoms = args[0].shape[1]
    out_shape = (struct(atoms, CH), struct(8, atoms))
    kernel = functools.partial(own_back_kernel, tuple(steps))
    return call(kernel, "own_back", out_shape, [], args)


def ring(axis):
    peers = lax.axis_size(axis)
    up = [(i, (i + 1) % peers) for i in range(peers)]
    return up, [(j, i) for i, j in up]


def neighbours_of(block, axis, dim):
    up, down = ring(axis)
    length = block.shape[dim]
    if len(up) == 2 and length == 2:
        other = lax.ppermute(block, axis, up)
        return (
            lax.slice_in_dim(other, length - 1, length, axis=dim),
            lax.slice_in_dim(other, 0, 1, axis=dim),
        )
    before = lax.ppermute(lax.slice_in_dim(block, length - 1, length, axis=dim), axis, up)
    after = lax.ppermute(lax.slice_in_dim(block, 0, 1, axis=dim), axis, down)
    return before, after


def grown(block, axis, dim):
    before, after = neighbours_of(block, axis, dim)
    return jnp.concatenate([before, block, after], axis=dim)


def flat_rows(piece):
    return piece.reshape(-1, piece.shape[-1])


def fold_kernel(mid_ref, low_ref, high_ref, out_ref):
    lanes = mid_ref.shape[1]
    ext_y = iota(mid_ref.shape, 1) // 32 % 4
    out_ref[...] = (
        mid_ref[...]
        + jnp.where(ext_y == 1, pltpu.roll(low_ref[...], lanes - 64, 1), 0.0)
        + jnp.where(ext_y == 2, pltpu.roll(high_ref[...], 64, 1), 0.0)
    )


def forces_kernel(mid_ref, low_ref, high_ref, src_ref, onto_ref, home_ref, out_ref):
    values = mid_ref[...]
    lanes = values.shape[1]
    ext_z = iota(values.shape, 1) // 8 % 4
    values += jnp.where(ext_z == 1, pltpu.roll(low_ref[...], lanes - 16, 1), 0.0)
    values += jnp.where(ext_z == 2, pltpu.roll(high_ref[...], 16, 1), 0.0)
    first = values.astype(BF16)
    values -= first.astype(F32)
    second = values.astype(BF16)
    third = (values - second.astype(F32)).astype(BF16)
    home = home_ref[...]
    total = onto_ref[...] - src_ref[...].T[0:8, :]
    total += (mm_nt(first, home) + (mm_nt(second, home) + mm_nt(third, home)))
    for comp in range(3):
        out_ref[comp] = -total[comp : comp + 1, :]


def give_back_x(low, mid, high):
    up, down = ring("gx")
    from_low = lax.ppermute(high, "gx", up)
    from_high = lax.ppermute(low, "gx", down)
    return mid, jnp.concatenate([from_low, from_high], axis=1)


def give_back_y(mid):
    up, down = ring("gy")
    return mid, lax.ppermute(mid, "gy", up), lax.ppermute(mid, "gy", down)


def fold(*args):
    return call(fold_kernel, "fold", (struct(*args[0].shape),), [], args)[0]


def give_back_z(mid):
    up, down = ring("gz")
    from_low = lax.ppermute(mid, "gz", up)
    return mid, from_low, from_low if len(up) == 2 else lax.ppermute(mid, "gz", down)


def local(
    features,
    positions,
    neighbours,
    counts,
    cell_atoms,
    rbf_weight,
    radial_weight,
    mix_weight,
    out_weight,
    energy_weight,
    norm_weight,
):
    feats = features[0, 0, 0]
    places = jnp.swapaxes(positions[0, 0], 0, 1)
    lists = jnp.concatenate([neighbours[0, 0, 0].T, counts[0, 0], cell_atoms[0, 0]], axis=0)
    cells0, cells1, own_pos, meta = make_cells(feats, places, lists)
    hold = lax.optimization_barrier
    block0, block1 = (part.reshape(2, 2, 2, 8, part.shape[1]) for part in (cells0, cells1))
    z0 = neighbours_of(block0, "gz", 2)
    z1 = neighbours_of(block1, "gz", 2)
    y1_in = neighbours_of(block1, "gy", 1)
    z0, own_pos, meta = hold((z0, own_pos, meta))
    block0 = jnp.concatenate([z0[0], block0, z0[1]], axis=2)
    y0 = neighbours_of(block0, "gy", 1)
    oh_own, pre_own, unit_own, radt, rbft, home, *radial_own = own_stage(
        meta, own_pos, rbf_weight, radial_weight
    )
    z1, y1_in, oh_own = hold((z1, y1_in, oh_own))
    block1 = jnp.concatenate([z1[0], block1, z1[1]], axis=2)
    x1_in = neighbours_of(block1, "gx", 0)
    y0, z1, oh_own = hold((y0, z1, oh_own))
    middle = jnp.concatenate([y0[0], block0, y0[1]], axis=1)
    x0 = neighbours_of(middle, "gx", 0)
    y1_out = neighbours_of(jnp.concatenate(z1, axis=2), "gy", 1)
    x1_in, oh_own = hold((x1_in, oh_own))
    (m0_own, gate_own, nf0_own, acc0), (own_a,) = own_forward_stage(
        (0,), feats, mix_weight, oh_own, radial_own
    )
    _, (own_b,) = own_forward_stage((1,), feats, mix_weight, oh_own, radial_own, gate_own)
    x0, y1_out, acc0, acc_b = hold((x0, y1_out, acc0, own_b[2]))
    pieces0 = tuple(flat_rows(piece) for piece in (x0[0], middle, x0[1]))
    y1 = [
        jnp.concatenate([out[:, :, 0:1], inner, out[:, :, 1:2]], axis=2)
        for out, inner in zip(y1_out, y1_in)
    ]
    outer = jnp.concatenate(y1, axis=1)
    x1_out = neighbours_of(outer, "gx", 0)
    block1 = jnp.concatenate([y1[0], block1, y1[1]], axis=1)
    pieces1 = (x1_in[0], x1_out[0], block1, x1_in[1], x1_out[1])
    pieces1 = tuple(flat_rows(piece) for piece in pieces1)
    (
        new_0, oh_gh, d_gh, dt_gh, pre_gh, unit_gh, gs0, en_0, m0_gh, gate_gh, nf0_gh, *radial_gh,
    ) = start_stage(
        pieces0, feats, own_pos, meta, rbf_weight, radial_weight, mix_weight, out_weight,
        energy_weight[None], acc0,
    )
    shared = (feats, meta, mix_weight, out_weight, norm_weight, oh_gh, d_gh, dt_gh, gate_gh)
    new_a, en_a, _, (dot_gh_a, *gr_gh_a), (dot_own_a, *gr_own_a) = pairs_stage(
        0, 2 * CH, pieces0, shared, (gate_own, *own_a), radial_gh
    )
    new, energy, src, onto, low, mid, high, gs_b = third_stage(
        pieces1, *shared, acc_b, radt, rbft, gs0, en_0, en_a, new_0, new_a, pre_gh,
        unit_gh, m0_gh, nf0_gh, dot_gh_a, *gr_gh_a,
        *[radial_gh[degree - 1] for degree in DEGREES[1]],
    )
    mid, arrived = give_back_x(low, mid, high)
    dot_own_b, *gr_own_b = own_backward_stage(1, mix_weight, gs_b, gate_own, *own_b[:2])
    arrived, gs0, dot_own_b = hold((arrived, gs0, dot_own_b))
    mid, from_low, from_high = give_back_y(mid + arrived)
    back = (oh_own, pre_own, unit_own, radt, rbft, mix_weight, gs0, m0_own, nf0_own)
    back += (dot_own_a, dot_own_b, *gr_own_a, *gr_own_b)
    src, onto = own_back_stage(range(2), *back, src, onto)
    from_low, from_high, src = hold((from_low, from_high, src))
    folded = give_back_z(fold(mid, from_low, from_high))
    src, onto = own_back_stage(range(2, 4), *back, src, onto)
    args = (*folded, src, onto, home)
    out_shape = (struct(3, 1, src.shape[0]),)
    forces = call(forces_kernel, "forces", out_shape, [], args)[0]
    return (
        new[None, None, None],
        energy[None, None],
        jnp.swapaxes(forces, 0, 1)[None, None],
    )


def solution(mesh):
    split = P("gx", "gy", "gz", None, None)
    flat = P("gx", "gy", "gz", None)
    return jax.shard_map(
        local,
        mesh=mesh,
        in_specs=(split, split, split, flat, flat, P(), P(), P(), P(), P(), P()),
        out_specs=(split, flat, split),
        check_vma=False,
    )
```

```python
import functools
import math

import jax
import jax.numpy as jnp
from jax import lax
from jax.experimental import pallas as pl
from jax.experimental.pallas import tpu as pltpu
from jax.sharding import PartitionSpec as P

F32 = jnp.float32
BF16 = jnp.bfloat16
CH = 128
SLOTS = 32
HALF = 16
STEP = 256
OWN_STEPS = 4
GH_STEPS = 2
MIB = 1024 * 1024
SPACE = pltpu.VMEM
PAIR_DEGREES = (
    (1, 1), (1, 2), (2, 2), (2, 2),
    (3, 3), (3, 3), (3, 3), (3, 4),
    (4, 4), (4, 4), (4, 4), (4, 4),
)
GROUPS = ((0, 4), (4, 12))
KINDS = tuple(sorted({PAIR_DEGREES[pair] for pair in range(*group)}) for group in GROUPS)
DEGREES = tuple(sorted({d for both in kinds for d in both}) for kinds in KINDS)
GROUP_COLS = tuple(2 * CH * (end - begin) for begin, end in GROUPS)


def mm(a, b):
    return jnp.dot(a, b, preferred_element_type=F32)


def mm_nt(a, b):
    return lax.dot_general(a, b, (((1,), (1,)), ((), ())), preferred_element_type=F32)


def iota(shape, dim):
    return lax.broadcasted_iota(jnp.int32, shape, dim)


def flip(w):
    return w.astype(F32).T.astype(BF16)


def pair_cols(pair):
    return slice(CH + pair * 2 * CH, CH + (pair + 1) * 2 * CH)


def struct(*shape, dtype=F32):
    return jax.ShapeDtypeStruct(shape, dtype)


def call(kernel, name, out_shape, scratch, args, specs=None, limit=16, work=1024):
    return pl.pallas_call(
        kernel,
        out_shape=out_shape,
        in_specs=specs or [pl.BlockSpec(memory_space=SPACE)] * len(args),
        out_specs=tuple(pl.BlockSpec(memory_space=SPACE) for _ in out_shape),
        scratch_shapes=scratch,
        compiler_params=pltpu.CompilerParams(vmem_limit_bytes=limit * MIB),
        cost_estimate=pl.CostEstimate(flops=work, bytes_accessed=1024, transcendentals=0),
        name=name,
    )(*args)


def cells_kernel(
    feat_ref, pos_ref, lists_ref,
    out_ref, own_pos_ref, meta_ref, pick_ref, rows_ref, pos_rows,
):
    rows_ref[...] = jnp.zeros_like(rows_ref)
    pos_rows[...] = jnp.zeros_like(pos_rows)
    atoms = feat_ref.shape[0]
    rows_ref[0 : SLOTS + 2, :] = lists_ref[...].astype(F32)
    meta = rows_ref[...].T
    meta_ref[...] = meta
    for comp in range(3):
        places = pos_ref[comp]
        first = places.astype(BF16).astype(F32)
        second = (places - first).astype(BF16).astype(F32)
        pos_rows[comp : comp + 1, :] = first
        pos_rows[4 + comp : 5 + comp, :] = second
        pos_rows[8 + comp : 9 + comp, :] = places - first - second
    pieces = pos_rows[...].astype(BF16)
    lane = iota((atoms, atoms), 1).astype(F32)
    pick = (meta[:, SLOTS + 1 : SLOTS + 2] == lane).astype(F32).astype(BF16)
    same = (iota((atoms, atoms), 0) == iota((atoms, atoms), 1)).astype(F32).astype(BF16)
    own_pos_ref[...] = mm_nt(same, pieces).astype(BF16)
    out_ref[:, CH : 2 * CH] = mm_nt(pick, pieces).astype(BF16)
    pick_ref[...] = pick
    out_ref[:, 0:CH] = mm(pick, feat_ref[:, 0:CH]).astype(BF16)
    cut = pair_cols(GROUPS[1][0]).start
    out_ref[:, 2 * CH :] = mm(pick, feat_ref[:, CH:cut]).astype(BF16)


def rest_kernel(feat_ref, pick_ref, rest_ref):
    cut = pair_cols(GROUPS[1][0]).start
    rest_ref[...] = mm(pick_ref[...], feat_ref[:, cut:]).astype(BF16)


def make_cells(feats, places, lists):
    atoms = feats.shape[0]
    out_shape = (
        struct(atoms, 2 * CH + GROUP_COLS[0], dtype=BF16),
        struct(atoms, CH, dtype=BF16),
        struct(atoms, CH),
        struct(atoms, atoms, dtype=BF16),
    )
    args = (feats, places, lists)
    scratch = [pltpu.VMEM((CH, atoms), F32), pltpu.VMEM((CH, atoms), F32)]
    first, own_pos, meta, pick = call(cells_kernel, "cells", out_shape, scratch, args)
    out_shape = (struct(atoms, GROUP_COLS[1], dtype=BF16),)
    rest = call(rest_kernel, "cells_rest", out_shape, [], (feats, pick), work=1 << 32)[0]
    return first, rest, own_pos, meta


def spacing_of(atoms, nbasis):
    depth = atoms // 16
    return 2.0 * math.sqrt(32.0 + depth * depth) / (nbasis - 1)


def own_onehots(meta_ref, oh_own):
    atoms = meta_ref.shape[0]
    counts = meta_ref[:, SLOTS : SLOTS + 1]
    lane_atom = iota((atoms, atoms), 1).astype(F32)
    for slot in range(HALF):
        hit = jnp.logical_and(meta_ref[:, slot : slot + 1] == lane_atom, counts > slot)
        oh_own[slot * atoms : (slot + 1) * atoms, :] = hit.astype(F32).astype(BF16)


def geometry(near, here):
    diff = near - here
    rel = (diff + pltpu.roll(diff, CH - 4, 1)) + (
        pltpu.roll(diff, CH - 8, 1) + pltpu.roll(diff, CH - 12, 1)
    )
    lane = iota(rel.shape, 1)
    rel = jnp.where(lane < 3, rel, 0.0)
    square = jnp.sum(rel * rel, axis=1, keepdims=True)
    inverse = lax.rsqrt(jnp.where(square > 0.0, square, 1.0))
    dist = square * inverse
    return jnp.where(lane == 3, dist, rel * inverse), dist


def centred_of(dist, spacing, nbasis):
    return dist * (1.0 / spacing) - iota((dist.shape[0], nbasis), 1).astype(F32)


def radial_net(dist, spacing, rbf_ref, rad_ref):
    centred = centred_of(dist, spacing, rbf_ref.shape[0])
    basis = jnp.exp(-0.5 * centred * centred)
    pre = mm(basis.astype(BF16), rbf_ref[...])
    hidden = (pre * jax.nn.sigmoid(pre)).astype(BF16)
    return pre, mm(hidden, rad_ref[...]).astype(BF16)


def tiled(values, size=STEP):
    return jnp.concatenate([values] * (size // values.shape[0]), axis=0)


def live_ghosts(meta_ref):
    return jnp.maximum(meta_ref[:, SLOTS : SLOTS + 1] - HALF, 0.0)


def step_count(meta_ref):
    total = jnp.sum(live_ghosts(meta_ref)).astype(jnp.int32)
    rows = GH_STEPS * STEP
    return jnp.maximum((total + (rows - 1)) // rows, 1) * GH_STEPS


def own_rows(step, size=STEP):
    return pl.ds(step * size, size)


def ghost_rows(step, size=STEP):
    first = OWN_STEPS * STEP
    if isinstance(step, int):
        return pl.ds(step * size, size), pl.ds(first + step * size, size)
    base = pl.multiple_of(step * size, size)
    return pl.ds(base, size), pl.ds(pl.multiple_of(first + base, size), size)


def over_ghost_steps(steps, body, size=STEP):
    static = GH_STEPS * STEP // size
    for step in range(static):
        body(step)

    def again(step, carry):
        body(step)
        return carry

    lax.fori_loop(static, (steps * STEP + (size - 1)) // size, again, 0)


def block_diagonal(kinds, source, straight=None, across=None):
    zero = jnp.zeros((CH, CH), BF16)
    targets = [ref for ref in (straight, across) if ref is not None]
    for kind, both in enumerate(kinds):
        for ref in targets:
            ref[kind, 0:CH, CH:] = zero
            ref[kind, CH:, 0:CH] = zero
    for degree in sorted({d for both in kinds for d in both}):
        weight = source[degree]
        flipped = flip(weight) if across is not None else None
        for kind, both in enumerate(kinds):
            for side in range(2):
                if both[side] == degree:
                    part = slice(side * CH, side * CH + CH)
                    if straight is not None:
                        straight[kind, part, part] = weight
                    if across is not None:
                        across[kind, part, part] = flipped


def joined(pieces, cols):
    if len(pieces) == 3:
        return jnp.concatenate([piece[:, cols] for piece in pieces], axis=0)
    low_in, low_out, mid, high_in, high_out = pieces
    half = low_out.shape[0] // 2
    parts = [low_out[0:half, cols], low_in[:, cols], low_out[half:, cols], mid[:, cols]]
    parts += [high_out[0:half, cols], high_in[:, cols], high_out[half:, cols]]
    return jnp.concatenate(parts, axis=0)


def infos_of(group):
    infos = []
    for index, pair in enumerate(range(*GROUPS[group])):
        degrees = PAIR_DEGREES[pair]
        cols = slice(index * 2 * CH, (index + 1) * 2 * CH)
        infos.append((cols, degrees, KINDS[group].index(degrees)))
    return infos


def group_cols(group):
    begin, end = GROUPS[group]
    return slice(pair_cols(begin).start, pair_cols(end - 1).stop)


def twice(values):
    return jnp.concatenate([values, values], axis=1)


def forward(group, rows, onehot, feats, radials, gate_ref, wm, nf_ref, mx_ref, slots):
    near = mm(onehot, feats).astype(BF16)
    nf_ref[rows, :] = near
    gate = twice(gate_ref[rows, :])
    wide = gate.astype(F32) if slots else None
    messages = []
    for cols, degrees, kind in infos_of(group):
        radial = jnp.concatenate([radials[d][rows, :] for d in degrees], axis=1)
        mixed = mm(near[:, cols] * radial, wm[kind])
        low = mixed.astype(BF16)
        mx_ref[rows, cols] = low
        messages.append(mixed * wide if slots else low * gate)
    return messages


def backward(group, rows, grad, gate_ref, wmt, nf_ref, mx_ref, dot_ref, grad_refs):
    parts = {}
    dots = None
    gate = twice(gate_ref[rows, :])
    for cols, degrees, kind in infos_of(group):
        product = grad[:, cols] * mx_ref[rows, cols]
        dot = (product[:, 0:CH] + product[:, CH:]).astype(F32)
        dots = dot if dots is None else dots + dot
        weighted = mm(grad[:, cols] * gate, wmt[kind]) * nf_ref[rows, cols].astype(F32)
        for side in range(2):
            part = weighted[:, side * CH : (side + 1) * CH]
            degree = degrees[side]
            parts[degree] = parts[degree] + part if degree in parts else part
    dot_ref[rows, :] = dots.astype(dot_ref.dtype)
    for degree, part in parts.items():
        grad_refs[degree][rows, :] = part.astype(grad_refs[degree].dtype)


def over_slots(values, atoms):
    return jnp.sum(values.reshape(-1, atoms, values.shape[1]), axis=0)


def own_forward(group, own_ref, oh_own, radials, gate_ref, wm, nf_ref, mx_ref, acc_ref):
    atoms = own_ref.shape[0]
    feats = own_ref[:, group_cols(group)]
    for step in range(OWN_STEPS):
        rows = own_rows(step)
        messages = forward(
            group, rows, oh_own[rows, :], feats, radials, gate_ref, wm, nf_ref, mx_ref, True
        )
        for (cols, _, _), message in zip(infos_of(group), messages):
            part = over_slots(message, atoms)
            acc_ref[:, cols] = part if step == 0 else acc_ref[:, cols] + part


def own_backward(group, gs_ref, gate_ref, wmt, nf_ref, mx_ref, dot_ref, grad_refs):
    grad = tiled(gs_ref[...])
    for step in range(OWN_STEPS):
        backward(
            group, own_rows(step), grad, gate_ref, wmt, nf_ref, mx_ref, dot_ref, grad_refs
        )


def ghost_pairs(
    group, own_ref, pieces, skip, new_ref, new_base, oh_gh, d_gh, dt_gh, gate_ref, radials, nw_ref,
    steps, wm, wmt, wo, wot, nf_s, mx_s, acc_in, acc_s, gs_ref, dot_ref, grad_refs, en_ref,
):
    norm = 1.0 / math.sqrt(SLOTS)
    cols = slice(skip, skip + GROUP_COLS[group])
    acc_s[...] = acc_in[...]

    def ghost_forward(step):
        here, _ = ghost_rows(step)
        messages = forward(
            group, here, oh_gh[here, :], joined(pieces, cols), radials, gate_ref, wm, nf_s, mx_s,
            False,
        )
        acc_s[...] += mm(dt_gh[:, here], jnp.concatenate(messages, axis=1))

    over_ghost_steps(steps, ghost_forward)

    begin = group_cols(group).start
    for cols, degrees, kind in infos_of(group):
        summed_low = (acc_s[:, cols] * norm).astype(BF16)
        own = own_ref[:, begin + cols.start : begin + cols.stop]
        updated = own.astype(F32) + mm(summed_low, wo[kind])
        at = begin - new_base + cols.start
        new_ref[:, at : at + 2 * CH] = updated.astype(BF16)
        weight = jnp.concatenate(
            [nw_ref[d - 1 : d, :] * (1.0 / (2 * d + 1)) for d in degrees], axis=1
        )
        scale = weight * updated
        energy = scale * updated
        en_ref[...] += energy[:, 0:CH] + energy[:, CH:]
        gs_ref[:, cols] = (mm((2.0 * scale).astype(BF16), wot[kind]) * norm).astype(BF16)

    def ghost_backward(step):
        here, _ = ghost_rows(step)
        grad = mm(d_gh[here, :], gs_ref[...]).astype(BF16)
        backward(group, here, grad, gate_ref, wmt, nf_s, mx_s, dot_ref, grad_refs)

    over_ghost_steps(steps, ghost_backward)


def pair_scratch(atoms, half, group):
    count, width = len(KINDS[group]), GROUP_COLS[group]
    return (
        [pltpu.VMEM((count, 2 * CH, 2 * CH), BF16) for _ in range(4)]
        + [
            pltpu.VMEM((half, width), BF16),
            pltpu.VMEM((half, width), BF16),
            pltpu.VMEM((atoms, width), F32),
        ]
    )


def own_kernel(
    meta_ref, own_pos_ref, rbf_ref, rad_ref,
    oh_own, pre_ref, unit_ref, radt_ref, rbft_ref, home_ref, *radial_refs
):
    atoms = meta_ref.shape[0]
    nbasis = rbft_ref.shape[1]
    spacing = spacing_of(atoms, nbasis)
    own_onehots(meta_ref, oh_own)
    here = tiled(own_pos_ref[...].astype(F32))
    for step in range(OWN_STEPS):
        rows = own_rows(step)
        unit, dist = geometry(mm(oh_own[rows, :], own_pos_ref[...]), here)
        unit_ref[rows, :] = unit
        pre, radial = radial_net(dist, spacing, rbf_ref, rad_ref)
        pre_ref[rows, :] = pre.astype(BF16)
        for degree, ref in enumerate(radial_refs):
            ref[rows, :] = radial[:, degree * CH : (degree + 1) * CH]
    for degree in range(5):
        part = slice(degree * CH, (degree + 1) * CH)
        radt_ref[part, :] = flip(rad_ref[:, part])
    for index in range(nbasis // CH):
        part = slice(index * CH, (index + 1) * CH)
        rbft_ref[:, part] = flip(rbf_ref[part, :])
    lanes = home_ref.shape[1]
    lane = iota((atoms, lanes), 1)
    ext_x, ext_y, ext_z = lane // 128, lane // 32 % 4, lane // 8 % 4
    slot = ((2 * ext_x + ext_y - 1) * 2 + ext_z - 1) * 8 + lane % 8
    inside = jnp.logical_and(
        jnp.logical_or(ext_y == 1, ext_y == 2), jnp.logical_or(ext_z == 1, ext_z == 2)
    )
    to_slot = jnp.logical_and(iota((atoms, lanes), 0) == slot, inside)
    to_slot = to_slot.astype(F32).astype(BF16)
    order = meta_ref[:, SLOTS + 1 : SLOTS + 2]
    to_atom = (order == iota((atoms, atoms), 1).astype(F32)).astype(F32)
    home_ref[...] = mm(to_atom.T.astype(BF16), to_slot).astype(BF16)


def own_stage(meta, own_pos, rbf, rad):
    atoms = meta.shape[0]
    edges = atoms * HALF
    out_shape = (
        struct(edges, atoms, dtype=BF16),
        struct(edges, CH, dtype=BF16),
        struct(edges, CH),
        struct(5 * CH, CH, dtype=BF16),
        struct(CH, rbf.shape[0], dtype=BF16),
        struct(atoms, 256, dtype=BF16),
    ) + (struct(edges, CH, dtype=BF16),) * 5
    return call(own_kernel, "own_edges", out_shape, [], (meta, own_pos, rbf, rad))


def scalar_forward(rows, near, radial, mix_ref, m0_ref, gate_ref, nf0_ref):
    near = near.astype(BF16)
    nf0_ref[rows, :] = near
    mixed = mm(near * radial, mix_ref[0])
    m0_ref[rows, :] = mixed.astype(BF16)
    gate = jax.nn.sigmoid(mixed)
    gate_ref[rows, :] = gate.astype(BF16)
    return mixed * gate


def own_forward_kernel(groups, scalar, *refs):
    own_ref, mix_ref, oh_own, refs = *refs[:3], refs[3:]
    radial0, radials = refs[0], dict(enumerate(refs[1:5], start=1))
    refs = refs[5:]
    if scalar:
        m0_ref, gate_ref, nf0_ref, acc0_ref = refs[:4]
        refs = refs[4:]
        atoms = own_ref.shape[0]
        feats = own_ref[:, 0:CH]
        summed = None
        for step in range(OWN_STEPS):
            rows = own_rows(step)
            message = scalar_forward(
                rows, mm(oh_own[rows, :], feats), radial0[rows, :], mix_ref, m0_ref, gate_ref,
                nf0_ref,
            )
            part = over_slots(message, atoms)
            summed = part if summed is None else summed + part
        acc0_ref[...] = summed
    else:
        gate_ref, refs = refs[0], refs[1:]
    outs, weights = refs[: 3 * len(groups)], refs[3 * len(groups) :]
    for index, group in enumerate(groups):
        block_diagonal(KINDS[group], mix_ref, weights[index])
        nf_ref, mx_ref, acc_ref = outs[3 * index : 3 * index + 3]
        own_forward(
            group, own_ref, oh_own, radials, gate_ref, weights[index], nf_ref, mx_ref, acc_ref
        )


def own_forward_stage(groups, feats, mix, oh_own, radial_own, gate=None):
    atoms = feats.shape[0]
    half = atoms * HALF
    out_shape = ()
    if gate is None:
        out_shape += (struct(half, CH, dtype=BF16),) * 3 + (struct(atoms, CH),)
    for group in groups:
        width = GROUP_COLS[group]
        out_shape += (struct(half, width, dtype=BF16),) * 2 + (struct(atoms, width),)
    args = (feats, mix, oh_own, *radial_own) + (() if gate is None else (gate,))
    scratch = [pltpu.VMEM((len(KINDS[group]), 2 * CH, 2 * CH), BF16) for group in groups]
    name = "own_forward_" + "".join("abc"[group] for group in groups)
    kernel = functools.partial(own_forward_kernel, groups, gate is None)
    outs = call(kernel, name, out_shape, scratch, args)
    first = len(outs) - 3 * len(groups)
    return outs[:first], [outs[first + 3 * i : first + 3 * i + 3] for i in range(len(groups))]


def start_kernel(
    p0, p1, p2, own_ref, own_pos_ref, meta_ref, rbf_ref, rad_ref, mix_ref, out_ref, ew_ref,
    acc0_ref,
    new_ref, oh_gh, d_gh, dt_gh, pre_ref, unit_ref, gs0_ref, en_ref, m0_gh, gate_gh, nf0_gh,
    radial_gh1, radial_gh2, radial_gh3, radial_gh4,
    ghpos, acc_s,
):
    radial_gh = (None, radial_gh1, radial_gh2, radial_gh3, radial_gh4)
    pieces = (p0, p1, p2)
    atoms = own_ref.shape[0]
    ghosts = ghpos.shape[0]
    spacing = spacing_of(atoms, rbf_ref.shape[0])
    norm = 1.0 / math.sqrt(SLOTS)

    live = live_ghosts(meta_ref)
    sub_atom = iota((atoms, atoms), 0)
    lane_atom = iota((atoms, atoms), 1)
    live_b = jnp.broadcast_to(live, (atoms, atoms))
    end_row = jnp.sum(jnp.where(sub_atom <= lane_atom, live_b, 0.0), axis=0, keepdims=True)
    live_row = jnp.sum(jnp.where(sub_atom == lane_atom, live_b, 0.0), axis=0, keepdims=True)
    start_row = end_row - live_row
    row_b = jnp.broadcast_to(live_row, (atoms, atoms))
    end_col = jnp.sum(jnp.where(lane_atom <= sub_atom, row_b, 0.0), axis=1, keepdims=True)
    start_col = end_col - live
    total = jnp.sum(live)
    steps = step_count(meta_ref)
    ghost_row = meta_ref[:, HALF:SLOTS] - atoms
    high_part = jnp.floor(ghost_row * (1.0 / 16.0))
    row_high = high_part.astype(BF16)
    row_low = (ghost_row - 16.0 * high_part).astype(BF16)

    row = iota((ghosts, CH), 0)
    lane = iota((ghosts, CH), 1)
    zcells = atoms // 32
    per_y = (zcells + 2) * 8
    ext_x = row // (4 * per_y)
    ext_y = row // per_y % 4
    ext_z = row // 8 % (zcells + 2)

    def side_of(ext, last, size):
        return jnp.where(ext == 0, -size, jnp.where(ext == last, size, 0.0))

    shift = jnp.where(lane == 12, side_of(ext_x, 3, 4.0), 0.0)
    shift = jnp.where(lane == 13, side_of(ext_y, 3, 4.0), shift)
    shift = jnp.where(lane == 14, side_of(ext_z, zcells + 1, 2.0 * zcells), shift)
    own0 = own_ref[:, 0:CH]
    acc_s[...] = acc0_ref[...]
    ghpos[...] = (joined(pieces, slice(CH, 2 * CH)).astype(F32) + shift).astype(BF16)

    def ghost_start(step):
        here, _ = ghost_rows(step)
        base = step * STEP
        edge = (iota((STEP, atoms), 0) + base).astype(F32)
        mine = jnp.logical_and(edge >= start_row, edge < end_row).astype(F32)
        source = mine.astype(BF16)
        d_gh[here, :] = source
        edge_t = (iota((atoms, STEP), 1) + base).astype(F32)
        mine_t = jnp.logical_and(edge_t >= start_col, edge_t < end_col)
        spread = mine_t.astype(F32).astype(BF16)
        dt_gh[:, here] = spread
        edge_col = edge[:, 0:1]
        slot = edge_col - jnp.sum(mine * start_row, axis=1, keepdims=True)
        listed = mm(source, row_high) * 16.0 + mm(source, row_low)
        at_slot = iota((STEP, HALF), 1).astype(F32) == slot
        which = jnp.sum(jnp.where(at_slot, listed, 0.0), axis=1, keepdims=True)
        which = jnp.where(edge_col < total, which, -1.0)
        onehot = (iota((STEP, ghosts), 1).astype(F32) == which).astype(F32).astype(BF16)
        oh_gh[here, :] = onehot
        unit, dist = geometry(mm(onehot, ghpos[...]), mm(source, own_pos_ref[...]))
        unit_ref[here, :] = unit
        pre, radial = radial_net(dist, spacing, rbf_ref, rad_ref)
        pre_ref[here, :] = pre.astype(BF16)
        for degree in range(1, 5):
            radial_gh[degree][here, :] = radial[:, degree * CH : (degree + 1) * CH]
        message = scalar_forward(
            here, mm(onehot, joined(pieces, slice(0, CH))), radial[:, 0:CH], mix_ref, m0_gh, gate_gh, nf0_gh
        )
        acc_s[...] += mm(spread, message.astype(BF16))

    over_ghost_steps(steps, ghost_start)

    low0 = (acc_s[...] * norm).astype(BF16)
    updated0 = own0.astype(F32) + mm(low0, out_ref[0])
    new_ref[:, 0:CH] = updated0.astype(BF16)
    logistic = jax.nn.sigmoid(updated0)
    weight0 = ew_ref[...]
    en_ref[...] = weight0 * updated0 * logistic
    grad0 = (weight0 * logistic * (1.0 + updated0 * (1.0 - logistic))).astype(BF16)
    gs0_ref[...] = mm_nt(grad0, out_ref[0]) * norm


def start_stage(pieces, feats, *rest):
    atoms = feats.shape[0]
    half = atoms * HALF
    ghosts = sum(piece.shape[0] for piece in pieces)
    out_shape = (
        struct(atoms, CH, dtype=BF16),
        struct(half, ghosts, dtype=BF16),
        struct(half, atoms, dtype=BF16),
        struct(atoms, half, dtype=BF16),
        struct(half, CH, dtype=BF16),
        struct(half, CH),
        struct(atoms, CH),
        struct(atoms, CH),
    ) + (struct(half, CH, dtype=BF16),) * 7
    scratch = [
        pltpu.VMEM((ghosts, CH), BF16),
        pltpu.VMEM((atoms, CH), F32),
    ]
    args = tuple(pieces) + (feats,) + rest
    return call(
        start_kernel, "ghost_start", out_shape, scratch, args, limit=24
    )


def pairs_kernel(group, count, skip, *refs):
    pieces, refs = refs[:count], refs[count:]
    own_ref, meta_ref, mix_ref, out_ref, nw_ref, oh_gh, d_gh, dt_gh, gate_gh = refs[:9]
    gate_own, nf_own, mx_own, acc_own = refs[9:13]
    refs = refs[13:]
    degrees = DEGREES[group]
    radials, refs = dict(zip(degrees, refs)), refs[len(degrees) :]
    new_ref, en_ref, gs_ref, dot_gh = refs[:4]
    grads, refs = dict(zip(degrees, refs[4:])), refs[4 + len(degrees) :]
    if group == 0:
        dot_own, refs = refs[0], refs[1:]
        grads_own, refs = dict(zip(degrees, refs)), refs[len(degrees) :]
    wm, wmt, wo, wot, nf_s, mx_s, acc_s = refs
    block_diagonal(KINDS[group], mix_ref, wm, wmt)
    block_diagonal(KINDS[group], out_ref, wo, wot)
    en_ref[...] = jnp.zeros_like(en_ref)
    ghost_pairs(
        group, own_ref, pieces, skip, new_ref, group_cols(group).start, oh_gh, d_gh, dt_gh, gate_gh,
        radials, nw_ref, step_count(meta_ref), wm, wmt, wo, wot, nf_s, mx_s, acc_own, acc_s,
        gs_ref, dot_gh, grads, en_ref,
    )
    if group == 0:
        own_backward(group, gs_ref, gate_own, wmt, nf_own, mx_own, dot_own, grads_own)


def pairs_stage(group, skip, pieces, shared, own_parts, radial_gh):
    feats = shared[0]
    atoms = feats.shape[0]
    half = atoms * HALF
    ghosts = sum(piece.shape[0] for piece in pieces)
    degrees = DEGREES[group]
    sides = 2 if group == 0 else 1
    out_shape = (
        struct(atoms, GROUP_COLS[group], dtype=BF16),
        struct(atoms, CH),
        struct(atoms, GROUP_COLS[group], dtype=BF16),
    ) + (struct(half, CH, dtype=BF16),) * (sides * (1 + len(degrees)))
    args = tuple(pieces) + tuple(shared) + tuple(own_parts)
    args += tuple(radial_gh[degree - 1] for degree in degrees)
    new, energy, gs, *rest = call(
        functools.partial(pairs_kernel, group, len(pieces), skip), "pairs_" + "abc"[group],
        out_shape, pair_scratch(atoms, half, group), args, limit=24,
    )
    return new, energy, gs, rest[: 1 + len(degrees)], rest[1 + len(degrees) :]


def own_backward_kernel(group, mix_ref, gs_ref, gate_ref, nf_ref, mx_ref, *refs):
    dot_ref, grads, wmt = refs[0], dict(zip(DEGREES[group], refs[1:-1])), refs[-1]
    block_diagonal(KINDS[group], mix_ref, None, wmt)
    own_backward(group, gs_ref, gate_ref, wmt, nf_ref, mx_ref, dot_ref, grads)


def own_backward_stage(group, mix, gs, gate, nf, mx):
    half = nf.shape[0]
    out_shape = (struct(half, CH, dtype=BF16),) * (1 + len(DEGREES[group]))
    scratch = [pltpu.VMEM((len(KINDS[group]), 2 * CH, 2 * CH), BF16)]
    kernel = functools.partial(own_backward_kernel, group)
    name = "own_backward_" + "abc"[group]
    return call(kernel, name, out_shape, scratch, (mix, gs, gate, nf, mx))


def finish(
    grad, mixed, near, dots, parts, pre, unit, spacing, radt_ref, rbft_ref, mix_t
):
    mixed = mixed.astype(F32)
    gate = jax.nn.sigmoid(mixed)
    first = grad * gate * (1.0 + mixed * (1.0 - gate)) + dots * gate * (1.0 - gate)
    weighted = mm(first.astype(BF16), mix_t) * near.astype(F32)
    radial_grad = jnp.concatenate([weighted.astype(BF16)] + parts, axis=1)
    hidden_grad = mm(radial_grad, radt_ref[...])
    pre = pre.astype(F32)
    logistic = jax.nn.sigmoid(pre)
    pre_grad = (hidden_grad * logistic * (1.0 + pre * (1.0 - logistic))).astype(BF16)
    centred = centred_of(unit[:, 3:4], spacing, rbft_ref.shape[1])
    slope = jnp.exp(-0.5 * centred * centred) * centred
    basis_grad = mm(pre_grad, rbft_ref[...])
    dist_grad = jnp.sum(basis_grad * slope, axis=1, keepdims=True) * (-1.0 / spacing)
    pull = unit * dist_grad
    across = pull.T[0:8, :]
    top = across.astype(BF16)
    rest = (across - top.astype(F32)).astype(BF16)
    return pull, top, rest


def sum_of(refs, rows):
    total = refs[0][rows, :].astype(F32)
    for ref in refs[1:]:
        total += ref[rows, :].astype(F32)
    return total


def degree_parts(refs, rows):
    by_degree = {}
    refs = list(refs)
    for degrees in DEGREES:
        for degree in degrees:
            by_degree.setdefault(degree, []).append(refs.pop(0))
    return [sum_of(by_degree[degree], rows).astype(BF16) for degree in range(1, 5)]


PARTIALS = sum(len(degrees) for degrees in DEGREES)


def third_kernel(
    p0, p1, p2, p3, p4, own_ref, meta_ref, mix_ref, out_ref, nw_ref, oh_gh, d_gh, dt_gh, gate_gh,
    acc_own, radt_ref, rbft_ref, gs0_ref, en_0, en_a, new_0, new_a, pre_gh, unit_gh,
    m0_ref, nf0_ref, dot_a, *refs
):
    group = 1
    before, degrees = len(DEGREES[0]), DEGREES[group]
    gr_a, refs = refs[:before], refs[before:]
    radials, refs = dict(zip(degrees, refs)), refs[len(degrees) :]
    new_ref, energy_ref, src_ref, onto_ref, flow_ref, fmid_ref, fhigh_ref, gs_ref = refs[:8]
    wm, wmt, wo, wot, nf_s, mx_s, acc_s, dot_c, en_s, fgh_s = refs[8:18]
    grads = dict(zip(degrees, refs[18:]))
    pieces = (p0, p1, p2, p3, p4)
    atoms = own_ref.shape[0]
    spacing = spacing_of(atoms, rbft_ref.shape[1])
    block_diagonal(KINDS[group], mix_ref, wm, wmt)
    block_diagonal(KINDS[group], out_ref, wo, wot)
    en_s[...] = en_0[...] + en_a[...]
    at = 0
    for part in (new_0, new_a):
        new_ref[:, at : at + part.shape[1]] = part[...]
        at += part.shape[1]
    steps = step_count(meta_ref)

    ghost_pairs(
        group, own_ref, pieces, 0, new_ref, 0, oh_gh, d_gh, dt_gh, gate_gh, radials, nw_ref,
        steps, wm, wmt, wo, wot, nf_s, mx_s, acc_own, acc_s, gs_ref, dot_c, grads, en_s,
    )
    energy_ref[...] = jnp.sum(en_s[...].T, axis=0, keepdims=True)

    fgh_s[...] = jnp.zeros_like(fgh_s)
    src_ref[...] = jnp.zeros_like(src_ref)
    onto_ref[...] = jnp.zeros_like(onto_ref)
    gs0_low = gs0_ref[...].astype(BF16)
    mix_t = flip(mix_ref[0])

    def ghost_finish(step):
        here, _ = ghost_rows(step)
        grad = mm(d_gh[here, :], gs0_low)
        pull, top, rest = finish(
            grad, m0_ref[here, :], nf0_ref[here, :], sum_of((dot_a, dot_c), here),
            degree_parts(gr_a + refs[18:], here), pre_gh[here, :], unit_gh[here, :], spacing,
            radt_ref, rbft_ref, mix_t,
        )
        pull_top = pull.astype(BF16)
        pull_rest = (pull - pull_top.astype(F32)).astype(BF16)
        spread = dt_gh[:, here]
        src_ref[...] += mm(spread, pull_top) + mm(spread, pull_rest)
        onehot = oh_gh[here, :]
        fgh_s[...] += mm(top, onehot) + mm(rest, onehot)

    over_ghost_steps(steps, ghost_finish)
    low, mid = flow_ref.shape[1], fmid_ref.shape[1]
    flow_ref[...] = fgh_s[:, 0:low]
    fmid_ref[...] = fgh_s[:, low : low + mid]
    fhigh_ref[...] = fgh_s[:, low + mid :]


def third_stage(pieces, feats, *rest):
    atoms, feat = feats.shape
    half = atoms * HALF
    ghosts = sum(piece.shape[0] for piece in pieces)
    sizes = (ghosts // 4, ghosts // 2, ghosts // 4)
    out_shape = (
        struct(atoms, feat, dtype=BF16),
        struct(1, atoms),
        struct(atoms, CH),
        struct(8, atoms),
    ) + tuple(struct(8, size) for size in sizes) + (
        struct(atoms, GROUP_COLS[1], dtype=BF16),
    )
    scratch = pair_scratch(atoms, half, 1) + [
        pltpu.VMEM((half, CH), BF16),
        pltpu.VMEM((atoms, CH), F32),
        pltpu.VMEM((8, ghosts), F32),
    ]
    scratch += [pltpu.VMEM((half, CH), BF16)] * len(DEGREES[1])
    args = tuple(pieces) + (feats,) + rest
    return call(
        third_kernel, "third_group", out_shape, scratch, args, limit=28
    )


def own_back_kernel(
    steps, oh_own, pre_own, unit_own, radt_ref, rbft_ref, mix_ref, gs0_ref,
    m0_ref, nf0_ref, dot_a, dot_c, *refs
):
    gr_own, (src_in, onto_in, src_out, onto_out) = refs[:PARTIALS], refs[PARTIALS:]
    atoms = oh_own.shape[1]
    spacing = spacing_of(atoms, rbft_ref.shape[1])
    grad = tiled(gs0_ref[...])
    mix_t = flip(mix_ref[0])
    src = src_in[...]
    onto = onto_in[...]
    for step in steps:
        rows = own_rows(step)
        pull, top, rest = finish(
            grad, m0_ref[rows, :], nf0_ref[rows, :], sum_of((dot_a, dot_c), rows),
            degree_parts(gr_own, rows), pre_own[rows, :], unit_own[rows, :], spacing, radt_ref,
            rbft_ref, mix_t,
        )
        src += over_slots(pull, atoms)
        onehot = oh_own[rows, :]
        onto += mm(top, onehot) + mm(rest, onehot)
    src_out[...] = src
    onto_out[...] = onto


def own_back_stage(steps, *args):
    atoms = args[0].shape[1]
    out_shape = (struct(atoms, CH), struct(8, atoms))
    kernel = functools.partial(own_back_kernel, tuple(steps))
    return call(kernel, "own_back", out_shape, [], args)


def ring(axis):
    peers = lax.axis_size(axis)
    up = [(i, (i + 1) % peers) for i in range(peers)]
    return up, [(j, i) for i, j in up]


def neighbours_of(block, axis, dim):
    up, down = ring(axis)
    length = block.shape[dim]
    if len(up) == 2 and length == 2:
        other = lax.ppermute(block, axis, up)
        return (
            lax.slice_in_dim(other, length - 1, length, axis=dim),
            lax.slice_in_dim(other, 0, 1, axis=dim),
        )
    before = lax.ppermute(lax.slice_in_dim(block, length - 1, length, axis=dim), axis, up)
    after = lax.ppermute(lax.slice_in_dim(block, 0, 1, axis=dim), axis, down)
    return before, after


def grown(block, axis, dim):
    before, after = neighbours_of(block, axis, dim)
    return jnp.concatenate([before, block, after], axis=dim)


def flat_rows(piece):
    return piece.reshape(-1, piece.shape[-1])


def fold_kernel(mid_ref, low_ref, high_ref, out_ref):
    lanes = mid_ref.shape[1]
    ext_y = iota(mid_ref.shape, 1) // 32 % 4
    out_ref[...] = (
        mid_ref[...]
        + jnp.where(ext_y == 1, pltpu.roll(low_ref[...], lanes - 64, 1), 0.0)
        + jnp.where(ext_y == 2, pltpu.roll(high_ref[...], 64, 1), 0.0)
    )


def forces_kernel(mid_ref, low_ref, high_ref, src_ref, onto_ref, home_ref, out_ref):
    values = mid_ref[...]
    lanes = values.shape[1]
    ext_z = iota(values.shape, 1) // 8 % 4
    values += jnp.where(ext_z == 1, pltpu.roll(low_ref[...], lanes - 16, 1), 0.0)
    values += jnp.where(ext_z == 2, pltpu.roll(high_ref[...], 16, 1), 0.0)
    first = values.astype(BF16)
    values -= first.astype(F32)
    second = values.astype(BF16)
    third = (values - second.astype(F32)).astype(BF16)
    home = home_ref[...]
    total = onto_ref[...] - src_ref[...].T[0:8, :]
    total += (mm_nt(first, home) + (mm_nt(second, home) + mm_nt(third, home)))
    for comp in range(3):
        out_ref[comp] = -total[comp : comp + 1, :]


def give_back_x(low, mid, high):
    up, down = ring("gx")
    from_low = lax.ppermute(high, "gx", up)
    from_high = lax.ppermute(low, "gx", down)
    return mid, jnp.concatenate([from_low, from_high], axis=1)


def give_back_y(mid):
    up, down = ring("gy")
    return mid, lax.ppermute(mid, "gy", up), lax.ppermute(mid, "gy", down)


def fold(*args):
    return call(fold_kernel, "fold", (struct(*args[0].shape),), [], args)[0]


def give_back_z(mid):
    up, down = ring("gz")
    from_low = lax.ppermute(mid, "gz", up)
    return mid, from_low, from_low if len(up) == 2 else lax.ppermute(mid, "gz", down)


def local(
    features,
    positions,
    neighbours,
    counts,
    cell_atoms,
    rbf_weight,
    radial_weight,
    mix_weight,
    out_weight,
    energy_weight,
    norm_weight,
):
    feats = features[0, 0, 0]
    places = jnp.swapaxes(positions[0, 0], 0, 1)
    lists = jnp.concatenate([neighbours[0, 0, 0].T, counts[0, 0], cell_atoms[0, 0]], axis=0)
    cells0, cells1, own_pos, meta = make_cells(feats, places, lists)
    hold = lax.optimization_barrier
    block0, block1 = (part.reshape(2, 2, 2, 8, part.shape[1]) for part in (cells0, cells1))
    z0 = neighbours_of(block0, "gz", 2)
    z1 = neighbours_of(block1, "gz", 2)
    y1_in = neighbours_of(block1, "gy", 1)
    z0, own_pos, meta = hold((z0, own_pos, meta))
    block0 = jnp.concatenate([z0[0], block0, z0[1]], axis=2)
    y0 = neighbours_of(block0, "gy", 1)
    oh_own, pre_own, unit_own, radt, rbft, home, *radial_own = own_stage(
        meta, own_pos, rbf_weight, radial_weight
    )
    z1, y1_in, oh_own = hold((z1, y1_in, oh_own))
    block1 = jnp.concatenate([z1[0], block1, z1[1]], axis=2)
    x1_in = neighbours_of(block1, "gx", 0)
    (m0_own, gate_own, nf0_own, acc0), (own_a,) = own_forward_stage(
        (0,), feats, mix_weight, oh_own, radial_own
    )
    y0, z1, gate_own = hold((y0, z1, gate_own))
    middle = jnp.concatenate([y0[0], block0, y0[1]], axis=1)
    x0 = neighbours_of(middle, "gx", 0)
    y1_out = neighbours_of(jnp.concatenate(z1, axis=2), "gy", 1)
    x1_in, gate_own = hold((x1_in, gate_own))
    _, (own_b,) = own_forward_stage((1,), feats, mix_weight, oh_own, radial_own, gate_own)
    x0, y1_out, acc0, acc_b = hold((x0, y1_out, acc0, own_b[2]))
    pieces0 = tuple(flat_rows(piece) for piece in (x0[0], middle, x0[1]))
    y1 = [
        jnp.concatenate([out[:, :, 0:1], inner, out[:, :, 1:2]], axis=2)
        for out, inner in zip(y1_out, y1_in)
    ]
    outer = jnp.concatenate(y1, axis=1)
    x1_out = neighbours_of(outer, "gx", 0)
    block1 = jnp.concatenate([y1[0], block1, y1[1]], axis=1)
    pieces1 = (x1_in[0], x1_out[0], block1, x1_in[1], x1_out[1])
    pieces1 = tuple(flat_rows(piece) for piece in pieces1)
    (
        new_0, oh_gh, d_gh, dt_gh, pre_gh, unit_gh, gs0, en_0, m0_gh, gate_gh, nf0_gh, *radial_gh,
    ) = start_stage(
        pieces0, feats, own_pos, meta, rbf_weight, radial_weight, mix_weight, out_weight,
        energy_weight[None], acc0,
    )
    shared = (feats, meta, mix_weight, out_weight, norm_weight, oh_gh, d_gh, dt_gh, gate_gh)
    new_a, en_a, _, (dot_gh_a, *gr_gh_a), (dot_own_a, *gr_own_a) = pairs_stage(
        0, 2 * CH, pieces0, shared, (gate_own, *own_a), radial_gh
    )
    new, energy, src, onto, low, mid, high, gs_b = third_stage(
        pieces1, *shared, acc_b, radt, rbft, gs0, en_0, en_a, new_0, new_a, pre_gh,
        unit_gh, m0_gh, nf0_gh, dot_gh_a, *gr_gh_a,
        *[radial_gh[degree - 1] for degree in DEGREES[1]],
    )
    mid, arrived = give_back_x(low, mid, high)
    dot_own_b, *gr_own_b = own_backward_stage(1, mix_weight, gs_b, gate_own, *own_b[:2])
    arrived, gs0, dot_own_b = hold((arrived, gs0, dot_own_b))
    mid, from_low, from_high = give_back_y(mid + arrived)
    back = (oh_own, pre_own, unit_own, radt, rbft, mix_weight, gs0, m0_own, nf0_own)
    back += (dot_own_a, dot_own_b, *gr_own_a, *gr_own_b)
    src, onto = own_back_stage(range(2), *back, src, onto)
    from_low, from_high, src = hold((from_low, from_high, src))
    folded = give_back_z(fold(mid, from_low, from_high))
    src, onto = own_back_stage(range(2, 4), *back, src, onto)
    args = (*folded, src, onto, home)
    out_shape = (struct(3, 1, src.shape[0]),)
    forces = call(forces_kernel, "forces", out_shape, [], args)[0]
    return (
        new[None, None, None],
        energy[None, None],
        jnp.swapaxes(forces, 0, 1)[None, None],
    )


def solution(mesh):
    split = P("gx", "gy", "gz", None, None)
    flat = P("gx", "gy", "gz", None)
    return jax.shard_map(
        local,
        mesh=mesh,
        in_specs=(split, split, split, flat, flat, P(), P(), P(), P(), P(), P()),
        out_specs=(split, flat, split),
        check_vma=False,
    )
```

```python
import functools
import math

import jax
import jax.numpy as jnp
from jax import lax
from jax.experimental import pallas as pl
from jax.experimental.pallas import tpu as pltpu
from jax.sharding import PartitionSpec as P

F32 = jnp.float32
BF16 = jnp.bfloat16
CH = 128
SLOTS = 32
HALF = 16
STEP = 256
OWN_STEPS = 4
GH_STEPS = 2
MIB = 1024 * 1024
SPACE = pltpu.VMEM
PAIR_DEGREES = (
    (1, 1), (1, 2), (2, 2), (2, 2),
    (3, 3), (3, 3), (3, 3), (3, 4),
    (4, 4), (4, 4), (4, 4), (4, 4),
)
GROUPS = ((0, 4), (4, 12))
KINDS = tuple(sorted({PAIR_DEGREES[pair] for pair in range(*group)}) for group in GROUPS)
DEGREES = tuple(sorted({d for both in kinds for d in both}) for kinds in KINDS)
GROUP_COLS = tuple(2 * CH * (end - begin) for begin, end in GROUPS)


def mm(a, b):
    return jnp.dot(a, b, preferred_element_type=F32)


def mm_nt(a, b):
    return lax.dot_general(a, b, (((1,), (1,)), ((), ())), preferred_element_type=F32)


def iota(shape, dim):
    return lax.broadcasted_iota(jnp.int32, shape, dim)


def flip(w):
    return w.astype(F32).T.astype(BF16)


def pair_cols(pair):
    return slice(CH + pair * 2 * CH, CH + (pair + 1) * 2 * CH)


def struct(*shape, dtype=F32):
    return jax.ShapeDtypeStruct(shape, dtype)


def call(kernel, name, out_shape, scratch, args, specs=None, limit=16, work=1024):
    return pl.pallas_call(
        kernel,
        out_shape=out_shape,
        in_specs=specs or [pl.BlockSpec(memory_space=SPACE)] * len(args),
        out_specs=tuple(pl.BlockSpec(memory_space=SPACE) for _ in out_shape),
        scratch_shapes=scratch,
        compiler_params=pltpu.CompilerParams(vmem_limit_bytes=limit * MIB),
        cost_estimate=pl.CostEstimate(flops=work, bytes_accessed=1024, transcendentals=0),
        name=name,
    )(*args)


def cells_kernel(
    feat_ref, pos_ref, lists_ref,
    out_ref, own_pos_ref, meta_ref, pick_ref, rows_ref, pos_rows,
):
    rows_ref[...] = jnp.zeros_like(rows_ref)
    pos_rows[...] = jnp.zeros_like(pos_rows)
    atoms = feat_ref.shape[0]
    rows_ref[0 : SLOTS + 2, :] = lists_ref[...].astype(F32)
    meta = rows_ref[...].T
    meta_ref[...] = meta
    for comp in range(3):
        places = pos_ref[comp]
        first = places.astype(BF16).astype(F32)
        second = (places - first).astype(BF16).astype(F32)
        pos_rows[comp : comp + 1, :] = first
        pos_rows[4 + comp : 5 + comp, :] = second
        pos_rows[8 + comp : 9 + comp, :] = places - first - second
    pieces = pos_rows[...].astype(BF16)
    lane = iota((atoms, atoms), 1).astype(F32)
    pick = (meta[:, SLOTS + 1 : SLOTS + 2] == lane).astype(F32).astype(BF16)
    same = (iota((atoms, atoms), 0) == iota((atoms, atoms), 1)).astype(F32).astype(BF16)
    own_pos_ref[...] = mm_nt(same, pieces).astype(BF16)
    out_ref[:, CH : 2 * CH] = mm_nt(pick, pieces).astype(BF16)
    pick_ref[...] = pick
    out_ref[:, 0:CH] = mm(pick, feat_ref[:, 0:CH]).astype(BF16)
    cut = pair_cols(GROUPS[1][0]).start
    out_ref[:, 2 * CH :] = mm(pick, feat_ref[:, CH:cut]).astype(BF16)


def rest_kernel(feat_ref, pick_ref, rest_ref):
    cut = pair_cols(GROUPS[1][0]).start
    rest_ref[...] = mm(pick_ref[...], feat_ref[:, cut:]).astype(BF16)


def make_cells(feats, places, lists):
    atoms = feats.shape[0]
    out_shape = (
        struct(atoms, 2 * CH + GROUP_COLS[0], dtype=BF16),
        struct(atoms, CH, dtype=BF16),
        struct(atoms, CH),
        struct(atoms, atoms, dtype=BF16),
    )
    args = (feats, places, lists)
    scratch = [pltpu.VMEM((CH, atoms), F32), pltpu.VMEM((CH, atoms), F32)]
    first, own_pos, meta, pick = call(cells_kernel, "cells", out_shape, scratch, args)
    out_shape = (struct(atoms, GROUP_COLS[1], dtype=BF16),)
    rest = call(rest_kernel, "cells_rest", out_shape, [], (feats, pick), work=1 << 32)[0]
    return first, rest, own_pos, meta


def spacing_of(atoms, nbasis):
    depth = atoms // 16
    return 2.0 * math.sqrt(32.0 + depth * depth) / (nbasis - 1)


def own_onehots(meta_ref, oh_own):
    atoms = meta_ref.shape[0]
    counts = meta_ref[:, SLOTS : SLOTS + 1]
    lane_atom = iota((atoms, atoms), 1).astype(F32)
    for slot in range(HALF):
        hit = jnp.logical_and(meta_ref[:, slot : slot + 1] == lane_atom, counts > slot)
        oh_own[slot * atoms : (slot + 1) * atoms, :] = hit.astype(F32).astype(BF16)


def geometry(near, here):
    diff = near - here
    rel = (diff + pltpu.roll(diff, CH - 4, 1)) + (
        pltpu.roll(diff, CH - 8, 1) + pltpu.roll(diff, CH - 12, 1)
    )
    lane = iota(rel.shape, 1)
    rel = jnp.where(lane < 3, rel, 0.0)
    square = jnp.sum(rel * rel, axis=1, keepdims=True)
    inverse = lax.rsqrt(jnp.where(square > 0.0, square, 1.0))
    dist = square * inverse
    return jnp.where(lane == 3, dist, rel * inverse), dist


def centred_of(dist, spacing, nbasis):
    return dist * (1.0 / spacing) - iota((dist.shape[0], nbasis), 1).astype(F32)


def radial_net(dist, spacing, rbf_ref, rad_ref):
    centred = centred_of(dist, spacing, rbf_ref.shape[0])
    basis = jnp.exp(-0.5 * centred * centred)
    pre = mm(basis.astype(BF16), rbf_ref[...])
    hidden = (pre * jax.nn.sigmoid(pre)).astype(BF16)
    return pre, mm(hidden, rad_ref[...]).astype(BF16)


def tiled(values, size=STEP):
    return jnp.concatenate([values] * (size // values.shape[0]), axis=0)


def live_ghosts(meta_ref):
    return jnp.maximum(meta_ref[:, SLOTS : SLOTS + 1] - HALF, 0.0)


def step_count(meta_ref):
    total = jnp.sum(live_ghosts(meta_ref)).astype(jnp.int32)
    rows = GH_STEPS * STEP
    return jnp.maximum((total + (rows - 1)) // rows, 1) * GH_STEPS


def own_rows(step, size=STEP):
    return pl.ds(step * size, size)


def ghost_rows(step, size=STEP):
    first = OWN_STEPS * STEP
    if isinstance(step, int):
        return pl.ds(step * size, size), pl.ds(first + step * size, size)
    base = pl.multiple_of(step * size, size)
    return pl.ds(base, size), pl.ds(pl.multiple_of(first + base, size), size)


def over_ghost_steps(steps, body, size=STEP):
    static = GH_STEPS * STEP // size
    for step in range(static):
        body(step)

    def again(step, carry):
        body(step)
        return carry

    lax.fori_loop(static, (steps * STEP + (size - 1)) // size, again, 0)


def block_diagonal(kinds, source, straight=None, across=None):
    zero = jnp.zeros((CH, CH), BF16)
    targets = [ref for ref in (straight, across) if ref is not None]
    for kind, both in enumerate(kinds):
        for ref in targets:
            ref[kind, 0:CH, CH:] = zero
            ref[kind, CH:, 0:CH] = zero
    for degree in sorted({d for both in kinds for d in both}):
        weight = source[degree]
        flipped = flip(weight) if across is not None else None
        for kind, both in enumerate(kinds):
            for side in range(2):
                if both[side] == degree:
                    part = slice(side * CH, side * CH + CH)
                    if straight is not None:
                        straight[kind, part, part] = weight
                    if across is not None:
                        across[kind, part, part] = flipped


def joined(pieces, cols):
    if len(pieces) == 3:
        return jnp.concatenate([piece[:, cols] for piece in pieces], axis=0)
    low_in, low_out, mid, high_in, high_out = pieces
    half = low_out.shape[0] // 2
    parts = [low_out[0:half, cols], low_in[:, cols], low_out[half:, cols], mid[:, cols]]
    parts += [high_out[0:half, cols], high_in[:, cols], high_out[half:, cols]]
    return jnp.concatenate(parts, axis=0)


def infos_of(group):
    infos = []
    for index, pair in enumerate(range(*GROUPS[group])):
        degrees = PAIR_DEGREES[pair]
        cols = slice(index * 2 * CH, (index + 1) * 2 * CH)
        infos.append((cols, degrees, KINDS[group].index(degrees)))
    return infos


def group_cols(group):
    begin, end = GROUPS[group]
    return slice(pair_cols(begin).start, pair_cols(end - 1).stop)


def twice(values):
    return jnp.concatenate([values, values], axis=1)


def forward(group, rows, onehot, feats, radials, gate_ref, wm, nf_ref, mx_ref, slots):
    near = mm(onehot, feats).astype(BF16)
    nf_ref[rows, :] = near
    gate = twice(gate_ref[rows, :])
    wide = gate.astype(F32) if slots else None
    messages = []
    for cols, degrees, kind in infos_of(group):
        radial = jnp.concatenate([radials[d][rows, :] for d in degrees], axis=1)
        mixed = mm(near[:, cols] * radial, wm[kind])
        low = mixed.astype(BF16)
        mx_ref[rows, cols] = low
        messages.append(mixed * wide if slots else low * gate)
    return messages


def backward(group, rows, grad, gate_ref, wmt, nf_ref, mx_ref, dot_ref, grad_refs):
    parts = {}
    dots = None
    gate = twice(gate_ref[rows, :])
    for cols, degrees, kind in infos_of(group):
        product = grad[:, cols] * mx_ref[rows, cols]
        dot = (product[:, 0:CH] + product[:, CH:]).astype(F32)
        dots = dot if dots is None else dots + dot
        weighted = mm(grad[:, cols] * gate, wmt[kind]) * nf_ref[rows, cols].astype(F32)
        for side in range(2):
            part = weighted[:, side * CH : (side + 1) * CH]
            degree = degrees[side]
            parts[degree] = parts[degree] + part if degree in parts else part
    dot_ref[rows, :] = dots.astype(dot_ref.dtype)
    for degree, part in parts.items():
        grad_refs[degree][rows, :] = part.astype(grad_refs[degree].dtype)


def over_slots(values, atoms):
    return jnp.sum(values.reshape(-1, atoms, values.shape[1]), axis=0)


def own_forward(group, own_ref, oh_own, radials, gate_ref, wm, nf_ref, mx_ref, acc_ref):
    atoms = own_ref.shape[0]
    feats = own_ref[:, group_cols(group)]
    for step in range(OWN_STEPS):
        rows = own_rows(step)
        messages = forward(
            group, rows, oh_own[rows, :], feats, radials, gate_ref, wm, nf_ref, mx_ref, True
        )
        for (cols, _, _), message in zip(infos_of(group), messages):
            part = over_slots(message, atoms)
            acc_ref[:, cols] = part if step == 0 else acc_ref[:, cols] + part


def own_backward(group, gs_ref, gate_ref, wmt, nf_ref, mx_ref, dot_ref, grad_refs):
    grad = tiled(gs_ref[...])
    for step in range(OWN_STEPS):
        backward(
            group, own_rows(step), grad, gate_ref, wmt, nf_ref, mx_ref, dot_ref, grad_refs
        )


def ghost_pairs(
    group, own_ref, pieces, skip, new_ref, new_base, oh_gh, d_gh, dt_gh, gate_ref, radials, nw_ref,
    steps, wm, wmt, wo, wot, nf_s, mx_s, acc_in, acc_s, gs_ref, dot_ref, grad_refs, en_ref,
):
    norm = 1.0 / math.sqrt(SLOTS)
    cols = slice(skip, skip + GROUP_COLS[group])
    acc_s[...] = acc_in[...]

    def ghost_forward(step):
        here, _ = ghost_rows(step)
        messages = forward(
            group, here, oh_gh[here, :], joined(pieces, cols), radials, gate_ref, wm, nf_s, mx_s,
            False,
        )
        acc_s[...] += mm(dt_gh[:, here], jnp.concatenate(messages, axis=1))

    over_ghost_steps(steps, ghost_forward)

    begin = group_cols(group).start
    for cols, degrees, kind in infos_of(group):
        summed_low = (acc_s[:, cols] * norm).astype(BF16)
        own = own_ref[:, begin + cols.start : begin + cols.stop]
        updated = own.astype(F32) + mm(summed_low, wo[kind])
        at = begin - new_base + cols.start
        new_ref[:, at : at + 2 * CH] = updated.astype(BF16)
        weight = jnp.concatenate(
            [nw_ref[d - 1 : d, :] * (1.0 / (2 * d + 1)) for d in degrees], axis=1
        )
        scale = weight * updated
        energy = scale * updated
        en_ref[...] += energy[:, 0:CH] + energy[:, CH:]
        gs_ref[:, cols] = (mm((2.0 * scale).astype(BF16), wot[kind]) * norm).astype(BF16)

    def ghost_backward(step):
        here, _ = ghost_rows(step)
        grad = mm(d_gh[here, :], gs_ref[...]).astype(BF16)
        backward(group, here, grad, gate_ref, wmt, nf_s, mx_s, dot_ref, grad_refs)

    over_ghost_steps(steps, ghost_backward)


def pair_scratch(atoms, half, group):
    width = GROUP_COLS[group]
    return (
        [
            pltpu.VMEM((half, width), BF16),
            pltpu.VMEM((half, width), BF16),
            pltpu.VMEM((atoms, width), F32),
        ]
    )


def weights_kernel(mix_ref, out_ref, *refs):
    for group, kinds in enumerate(KINDS):
        wm, wmt, wo, wot = refs[4 * group : 4 * group + 4]
        block_diagonal(kinds, mix_ref, wm, wmt)
        block_diagonal(kinds, out_ref, wo, wot)


def weights_stage(mix, out):
    out_shape = ()
    for kinds in KINDS:
        out_shape += (struct(len(kinds), 2 * CH, 2 * CH, dtype=BF16),) * 4
    outs = call(weights_kernel, "weights", out_shape, [], (mix, out))
    return outs[:4], outs[4:]


def own_kernel(
    meta_ref, own_pos_ref, rbf_ref, rad_ref,
    oh_own, pre_ref, unit_ref, radt_ref, rbft_ref, home_ref, *radial_refs
):
    atoms = meta_ref.shape[0]
    nbasis = rbft_ref.shape[1]
    spacing = spacing_of(atoms, nbasis)
    own_onehots(meta_ref, oh_own)
    here = tiled(own_pos_ref[...].astype(F32))
    for step in range(OWN_STEPS):
        rows = own_rows(step)
        unit, dist = geometry(mm(oh_own[rows, :], own_pos_ref[...]), here)
        unit_ref[rows, :] = unit
        pre, radial = radial_net(dist, spacing, rbf_ref, rad_ref)
        pre_ref[rows, :] = pre.astype(BF16)
        for degree, ref in enumerate(radial_refs):
            ref[rows, :] = radial[:, degree * CH : (degree + 1) * CH]
    for degree in range(5):
        part = slice(degree * CH, (degree + 1) * CH)
        radt_ref[part, :] = flip(rad_ref[:, part])
    for index in range(nbasis // CH):
        part = slice(index * CH, (index + 1) * CH)
        rbft_ref[:, part] = flip(rbf_ref[part, :])
    lanes = home_ref.shape[1]
    lane = iota((atoms, lanes), 1)
    ext_x, ext_y, ext_z = lane // 128, lane // 32 % 4, lane // 8 % 4
    slot = ((2 * ext_x + ext_y - 1) * 2 + ext_z - 1) * 8 + lane % 8
    inside = jnp.logical_and(
        jnp.logical_or(ext_y == 1, ext_y == 2), jnp.logical_or(ext_z == 1, ext_z == 2)
    )
    to_slot = jnp.logical_and(iota((atoms, lanes), 0) == slot, inside)
    to_slot = to_slot.astype(F32).astype(BF16)
    order = meta_ref[:, SLOTS + 1 : SLOTS + 2]
    to_atom = (order == iota((atoms, atoms), 1).astype(F32)).astype(F32)
    home_ref[...] = mm(to_atom.T.astype(BF16), to_slot).astype(BF16)


def own_stage(meta, own_pos, rbf, rad):
    atoms = meta.shape[0]
    edges = atoms * HALF
    out_shape = (
        struct(edges, atoms, dtype=BF16),
        struct(edges, CH, dtype=BF16),
        struct(edges, CH),
        struct(5 * CH, CH, dtype=BF16),
        struct(CH, rbf.shape[0], dtype=BF16),
        struct(atoms, 256, dtype=BF16),
    ) + (struct(edges, CH, dtype=BF16),) * 5
    return call(own_kernel, "own_edges", out_shape, [], (meta, own_pos, rbf, rad))


def scalar_forward(rows, near, radial, mix_ref, m0_ref, gate_ref, nf0_ref):
    near = near.astype(BF16)
    nf0_ref[rows, :] = near
    mixed = mm(near * radial, mix_ref[0])
    m0_ref[rows, :] = mixed.astype(BF16)
    gate = jax.nn.sigmoid(mixed)
    gate_ref[rows, :] = gate.astype(BF16)
    return mixed * gate


def own_forward_kernel(groups, scalar, *refs):
    own_ref, mix_ref, oh_own, refs = *refs[:3], refs[3:]
    radial0, radials = refs[0], dict(enumerate(refs[1:5], start=1))
    refs = refs[5:]
    if scalar:
        m0_ref, gate_ref, nf0_ref, acc0_ref = refs[:4]
        refs = refs[4:]
        atoms = own_ref.shape[0]
        feats = own_ref[:, 0:CH]
        summed = None
        for step in range(OWN_STEPS):
            rows = own_rows(step)
            message = scalar_forward(
                rows, mm(oh_own[rows, :], feats), radial0[rows, :], mix_ref, m0_ref, gate_ref,
                nf0_ref,
            )
            part = over_slots(message, atoms)
            summed = part if summed is None else summed + part
        acc0_ref[...] = summed
    else:
        gate_ref, refs = refs[0], refs[1:]
    outs, weights = refs[: 3 * len(groups)], refs[3 * len(groups) :]
    for index, group in enumerate(groups):
        block_diagonal(KINDS[group], mix_ref, weights[index])
        nf_ref, mx_ref, acc_ref = outs[3 * index : 3 * index + 3]
        own_forward(
            group, own_ref, oh_own, radials, gate_ref, weights[index], nf_ref, mx_ref, acc_ref
        )


def own_forward_stage(groups, feats, mix, oh_own, radial_own, gate=None):
    atoms = feats.shape[0]
    half = atoms * HALF
    out_shape = ()
    if gate is None:
        out_shape += (struct(half, CH, dtype=BF16),) * 3 + (struct(atoms, CH),)
    for group in groups:
        width = GROUP_COLS[group]
        out_shape += (struct(half, width, dtype=BF16),) * 2 + (struct(atoms, width),)
    args = (feats, mix, oh_own, *radial_own) + (() if gate is None else (gate,))
    scratch = [pltpu.VMEM((len(KINDS[group]), 2 * CH, 2 * CH), BF16) for group in groups]
    name = "own_forward_" + "".join("abc"[group] for group in groups)
    kernel = functools.partial(own_forward_kernel, groups, gate is None)
    outs = call(kernel, name, out_shape, scratch, args)
    first = len(outs) - 3 * len(groups)
    return outs[:first], [outs[first + 3 * i : first + 3 * i + 3] for i in range(len(groups))]


def start_kernel(
    p0, p1, p2, own_ref, own_pos_ref, meta_ref, rbf_ref, rad_ref, mix_ref, out_ref, ew_ref,
    acc0_ref,
    new_ref, oh_gh, d_gh, dt_gh, pre_ref, unit_ref, gs0_ref, en_ref, m0_gh, gate_gh, nf0_gh,
    radial_gh1, radial_gh2, radial_gh3, radial_gh4,
    ghpos, acc_s,
):
    radial_gh = (None, radial_gh1, radial_gh2, radial_gh3, radial_gh4)
    pieces = (p0, p1, p2)
    atoms = own_ref.shape[0]
    ghosts = ghpos.shape[0]
    spacing = spacing_of(atoms, rbf_ref.shape[0])
    norm = 1.0 / math.sqrt(SLOTS)

    live = live_ghosts(meta_ref)
    sub_atom = iota((atoms, atoms), 0)
    lane_atom = iota((atoms, atoms), 1)
    live_b = jnp.broadcast_to(live, (atoms, atoms))
    end_row = jnp.sum(jnp.where(sub_atom <= lane_atom, live_b, 0.0), axis=0, keepdims=True)
    live_row = jnp.sum(jnp.where(sub_atom == lane_atom, live_b, 0.0), axis=0, keepdims=True)
    start_row = end_row - live_row
    row_b = jnp.broadcast_to(live_row, (atoms, atoms))
    end_col = jnp.sum(jnp.where(lane_atom <= sub_atom, row_b, 0.0), axis=1, keepdims=True)
    start_col = end_col - live
    total = jnp.sum(live)
    steps = step_count(meta_ref)
    ghost_row = meta_ref[:, HALF:SLOTS] - atoms
    high_part = jnp.floor(ghost_row * (1.0 / 16.0))
    row_high = high_part.astype(BF16)
    row_low = (ghost_row - 16.0 * high_part).astype(BF16)

    row = iota((ghosts, CH), 0)
    lane = iota((ghosts, CH), 1)
    zcells = atoms // 32
    per_y = (zcells + 2) * 8
    ext_x = row // (4 * per_y)
    ext_y = row // per_y % 4
    ext_z = row // 8 % (zcells + 2)

    def side_of(ext, last, size):
        return jnp.where(ext == 0, -size, jnp.where(ext == last, size, 0.0))

    shift = jnp.where(lane == 12, side_of(ext_x, 3, 4.0), 0.0)
    shift = jnp.where(lane == 13, side_of(ext_y, 3, 4.0), shift)
    shift = jnp.where(lane == 14, side_of(ext_z, zcells + 1, 2.0 * zcells), shift)
    own0 = own_ref[:, 0:CH]
    acc_s[...] = acc0_ref[...]
    ghpos[...] = (joined(pieces, slice(CH, 2 * CH)).astype(F32) + shift).astype(BF16)

    def ghost_start(step):
        here, _ = ghost_rows(step)
        base = step * STEP
        edge = (iota((STEP, atoms), 0) + base).astype(F32)
        mine = jnp.logical_and(edge >= start_row, edge < end_row).astype(F32)
        source = mine.astype(BF16)
        d_gh[here, :] = source
        edge_t = (iota((atoms, STEP), 1) + base).astype(F32)
        mine_t = jnp.logical_and(edge_t >= start_col, edge_t < end_col)
        spread = mine_t.astype(F32).astype(BF16)
        dt_gh[:, here] = spread
        edge_col = edge[:, 0:1]
        slot = edge_col - jnp.sum(mine * start_row, axis=1, keepdims=True)
        listed = mm(source, row_high) * 16.0 + mm(source, row_low)
        at_slot = iota((STEP, HALF), 1).astype(F32) == slot
        which = jnp.sum(jnp.where(at_slot, listed, 0.0), axis=1, keepdims=True)
        which = jnp.where(edge_col < total, which, -1.0)
        onehot = (iota((STEP, ghosts), 1).astype(F32) == which).astype(F32).astype(BF16)
        oh_gh[here, :] = onehot
        unit, dist = geometry(mm(onehot, ghpos[...]), mm(source, own_pos_ref[...]))
        unit_ref[here, :] = unit
        pre, radial = radial_net(dist, spacing, rbf_ref, rad_ref)
        pre_ref[here, :] = pre.astype(BF16)
        for degree in range(1, 5):
            radial_gh[degree][here, :] = radial[:, degree * CH : (degree + 1) * CH]
        message = scalar_forward(
            here, mm(onehot, joined(pieces, slice(0, CH))), radial[:, 0:CH], mix_ref, m0_gh, gate_gh, nf0_gh
        )
        acc_s[...] += mm(spread, message.astype(BF16))

    over_ghost_steps(steps, ghost_start)

    low0 = (acc_s[...] * norm).astype(BF16)
    updated0 = own0.astype(F32) + mm(low0, out_ref[0])
    new_ref[:, 0:CH] = updated0.astype(BF16)
    logistic = jax.nn.sigmoid(updated0)
    weight0 = ew_ref[...]
    en_ref[...] = weight0 * updated0 * logistic
    grad0 = (weight0 * logistic * (1.0 + updated0 * (1.0 - logistic))).astype(BF16)
    gs0_ref[...] = mm_nt(grad0, out_ref[0]) * norm


def start_stage(pieces, feats, *rest):
    atoms = feats.shape[0]
    half = atoms * HALF
    ghosts = sum(piece.shape[0] for piece in pieces)
    out_shape = (
        struct(atoms, CH, dtype=BF16),
        struct(half, ghosts, dtype=BF16),
        struct(half, atoms, dtype=BF16),
        struct(atoms, half, dtype=BF16),
        struct(half, CH, dtype=BF16),
        struct(half, CH),
        struct(atoms, CH),
        struct(atoms, CH),
    ) + (struct(half, CH, dtype=BF16),) * 7
    scratch = [
        pltpu.VMEM((ghosts, CH), BF16),
        pltpu.VMEM((atoms, CH), F32),
    ]
    args = tuple(pieces) + (feats,) + rest
    return call(
        start_kernel, "ghost_start", out_shape, scratch, args, limit=24
    )


def pairs_kernel(group, count, skip, *refs):
    pieces, refs = refs[:count], refs[count:]
    own_ref, meta_ref, mix_ref, out_ref, nw_ref, oh_gh, d_gh, dt_gh, gate_gh = refs[:9]
    gate_own, nf_own, mx_own, acc_own = refs[9:13]
    refs = refs[13:]
    degrees = DEGREES[group]
    radials, refs = dict(zip(degrees, refs)), refs[len(degrees) :]
    (wm, wmt, wo, wot), refs = refs[:4], refs[4:]
    new_ref, en_ref, gs_ref, dot_gh = refs[:4]
    grads, refs = dict(zip(degrees, refs[4:])), refs[4 + len(degrees) :]
    if group == 0:
        dot_own, refs = refs[0], refs[1:]
        grads_own, refs = dict(zip(degrees, refs)), refs[len(degrees) :]
    nf_s, mx_s, acc_s = refs
    en_ref[...] = jnp.zeros_like(en_ref)
    ghost_pairs(
        group, own_ref, pieces, skip, new_ref, group_cols(group).start, oh_gh, d_gh, dt_gh, gate_gh,
        radials, nw_ref, step_count(meta_ref), wm, wmt, wo, wot, nf_s, mx_s, acc_own, acc_s,
        gs_ref, dot_gh, grads, en_ref,
    )
    if group == 0:
        own_backward(group, gs_ref, gate_own, wmt, nf_own, mx_own, dot_own, grads_own)


def pairs_stage(group, skip, pieces, shared, own_parts, radial_gh, weights):
    feats = shared[0]
    atoms = feats.shape[0]
    half = atoms * HALF
    ghosts = sum(piece.shape[0] for piece in pieces)
    degrees = DEGREES[group]
    sides = 2 if group == 0 else 1
    out_shape = (
        struct(atoms, GROUP_COLS[group], dtype=BF16),
        struct(atoms, CH),
        struct(atoms, GROUP_COLS[group], dtype=BF16),
    ) + (struct(half, CH, dtype=BF16),) * (sides * (1 + len(degrees)))
    args = tuple(pieces) + tuple(shared) + tuple(own_parts)
    args += tuple(radial_gh[degree - 1] for degree in degrees) + tuple(weights)
    new, energy, gs, *rest = call(
        functools.partial(pairs_kernel, group, len(pieces), skip), "pairs_" + "abc"[group],
        out_shape, pair_scratch(atoms, half, group), args, limit=24,
    )
    return new, energy, gs, rest[: 1 + len(degrees)], rest[1 + len(degrees) :]


def own_backward_kernel(group, wmt, gs_ref, gate_ref, nf_ref, mx_ref, *refs):
    dot_ref, grads = refs[0], dict(zip(DEGREES[group], refs[1:]))
    own_backward(group, gs_ref, gate_ref, wmt, nf_ref, mx_ref, dot_ref, grads)


def own_backward_stage(group, wmt, gs, gate, nf, mx):
    half = nf.shape[0]
    out_shape = (struct(half, CH, dtype=BF16),) * (1 + len(DEGREES[group]))
    kernel = functools.partial(own_backward_kernel, group)
    name = "own_backward_" + "abc"[group]
    return call(kernel, name, out_shape, [], (wmt, gs, gate, nf, mx))


def finish(
    grad, mixed, near, dots, parts, pre, unit, spacing, radt_ref, rbft_ref, mix_t
):
    mixed = mixed.astype(F32)
    gate = jax.nn.sigmoid(mixed)
    first = grad * gate * (1.0 + mixed * (1.0 - gate)) + dots * gate * (1.0 - gate)
    weighted = mm(first.astype(BF16), mix_t) * near.astype(F32)
    radial_grad = jnp.concatenate([weighted.astype(BF16)] + parts, axis=1)
    hidden_grad = mm(radial_grad, radt_ref[...])
    pre = pre.astype(F32)
    logistic = jax.nn.sigmoid(pre)
    pre_grad = (hidden_grad * logistic * (1.0 + pre * (1.0 - logistic))).astype(BF16)
    centred = centred_of(unit[:, 3:4], spacing, rbft_ref.shape[1])
    slope = jnp.exp(-0.5 * centred * centred) * centred
    basis_grad = mm(pre_grad, rbft_ref[...])
    dist_grad = jnp.sum(basis_grad * slope, axis=1, keepdims=True) * (-1.0 / spacing)
    pull = unit * dist_grad
    across = pull.T[0:8, :]
    top = across.astype(BF16)
    rest = (across - top.astype(F32)).astype(BF16)
    return pull, top, rest


def sum_of(refs, rows):
    total = refs[0][rows, :].astype(F32)
    for ref in refs[1:]:
        total += ref[rows, :].astype(F32)
    return total


def degree_parts(refs, rows):
    by_degree = {}
    refs = list(refs)
    for degrees in DEGREES:
        for degree in degrees:
            by_degree.setdefault(degree, []).append(refs.pop(0))
    return [sum_of(by_degree[degree], rows).astype(BF16) for degree in range(1, 5)]


PARTIALS = sum(len(degrees) for degrees in DEGREES)


def third_kernel(
    p0, p1, p2, p3, p4, own_ref, meta_ref, mix_ref, out_ref, nw_ref, oh_gh, d_gh, dt_gh, gate_gh,
    acc_own, radt_ref, rbft_ref, gs0_ref, en_0, en_a, new_0, new_a, pre_gh, unit_gh,
    m0_ref, nf0_ref, dot_a, *refs
):
    group = 1
    before, degrees = len(DEGREES[0]), DEGREES[group]
    gr_a, refs = refs[:before], refs[before:]
    radials, refs = dict(zip(degrees, refs)), refs[len(degrees) :]
    (wm, wmt, wo, wot), refs = refs[:4], refs[4:]
    new_ref, energy_ref, src_ref, onto_ref, flow_ref, fmid_ref, fhigh_ref, gs_ref = refs[:8]
    nf_s, mx_s, acc_s, dot_c, en_s, fgh_s = refs[8:14]
    grads = dict(zip(degrees, refs[14:]))
    pieces = (p0, p1, p2, p3, p4)
    atoms = own_ref.shape[0]
    spacing = spacing_of(atoms, rbft_ref.shape[1])
    en_s[...] = en_0[...] + en_a[...]
    at = 0
    for part in (new_0, new_a):
        new_ref[:, at : at + part.shape[1]] = part[...]
        at += part.shape[1]
    steps = step_count(meta_ref)

    ghost_pairs(
        group, own_ref, pieces, 0, new_ref, 0, oh_gh, d_gh, dt_gh, gate_gh, radials, nw_ref,
        steps, wm, wmt, wo, wot, nf_s, mx_s, acc_own, acc_s, gs_ref, dot_c, grads, en_s,
    )
    energy_ref[...] = jnp.sum(en_s[...].T, axis=0, keepdims=True)

    fgh_s[...] = jnp.zeros_like(fgh_s)
    src_ref[...] = jnp.zeros_like(src_ref)
    onto_ref[...] = jnp.zeros_like(onto_ref)
    gs0_low = gs0_ref[...].astype(BF16)
    mix_t = flip(mix_ref[0])

    def ghost_finish(step):
        here, _ = ghost_rows(step)
        grad = mm(d_gh[here, :], gs0_low)
        pull, top, rest = finish(
            grad, m0_ref[here, :], nf0_ref[here, :], sum_of((dot_a, dot_c), here),
            degree_parts(gr_a + refs[14:], here), pre_gh[here, :], unit_gh[here, :], spacing,
            radt_ref, rbft_ref, mix_t,
        )
        pull_top = pull.astype(BF16)
        pull_rest = (pull - pull_top.astype(F32)).astype(BF16)
        spread = dt_gh[:, here]
        src_ref[...] += mm(spread, pull_top) + mm(spread, pull_rest)
        onehot = oh_gh[here, :]
        fgh_s[...] += mm(top, onehot) + mm(rest, onehot)

    over_ghost_steps(steps, ghost_finish)
    low, mid = flow_ref.shape[1], fmid_ref.shape[1]
    flow_ref[...] = fgh_s[:, 0:low]
    fmid_ref[...] = fgh_s[:, low : low + mid]
    fhigh_ref[...] = fgh_s[:, low + mid :]


def third_stage(pieces, feats, *rest):
    atoms, feat = feats.shape
    half = atoms * HALF
    ghosts = sum(piece.shape[0] for piece in pieces)
    sizes = (ghosts // 4, ghosts // 2, ghosts // 4)
    out_shape = (
        struct(atoms, feat, dtype=BF16),
        struct(1, atoms),
        struct(atoms, CH),
        struct(8, atoms),
    ) + tuple(struct(8, size) for size in sizes) + (
        struct(atoms, GROUP_COLS[1], dtype=BF16),
    )
    scratch = pair_scratch(atoms, half, 1) + [
        pltpu.VMEM((half, CH), BF16),
        pltpu.VMEM((atoms, CH), F32),
        pltpu.VMEM((8, ghosts), F32),
    ]
    scratch += [pltpu.VMEM((half, CH), BF16)] * len(DEGREES[1])
    args = tuple(pieces) + (feats,) + rest
    return call(
        third_kernel, "third_group", out_shape, scratch, args, limit=28
    )


def own_back_kernel(
    steps, oh_own, pre_own, unit_own, radt_ref, rbft_ref, mix_ref, gs0_ref,
    m0_ref, nf0_ref, dot_a, dot_c, *refs
):
    gr_own, (src_in, onto_in, src_out, onto_out) = refs[:PARTIALS], refs[PARTIALS:]
    atoms = oh_own.shape[1]
    spacing = spacing_of(atoms, rbft_ref.shape[1])
    grad = tiled(gs0_ref[...])
    mix_t = flip(mix_ref[0])
    src = src_in[...]
    onto = onto_in[...]
    for step in steps:
        rows = own_rows(step)
        pull, top, rest = finish(
            grad, m0_ref[rows, :], nf0_ref[rows, :], sum_of((dot_a, dot_c), rows),
            degree_parts(gr_own, rows), pre_own[rows, :], unit_own[rows, :], spacing, radt_ref,
            rbft_ref, mix_t,
        )
        src += over_slots(pull, atoms)
        onehot = oh_own[rows, :]
        onto += mm(top, onehot) + mm(rest, onehot)
    src_out[...] = src
    onto_out[...] = onto


def own_back_stage(steps, *args):
    atoms = args[0].shape[1]
    out_shape = (struct(atoms, CH), struct(8, atoms))
    kernel = functools.partial(own_back_kernel, tuple(steps))
    return call(kernel, "own_back", out_shape, [], args)


def ring(axis):
    peers = lax.axis_size(axis)
    up = [(i, (i + 1) % peers) for i in range(peers)]
    return up, [(j, i) for i, j in up]


def neighbours_of(block, axis, dim):
    up, down = ring(axis)
    length = block.shape[dim]
    if len(up) == 2 and length == 2:
        other = lax.ppermute(block, axis, up)
        return (
            lax.slice_in_dim(other, length - 1, length, axis=dim),
            lax.slice_in_dim(other, 0, 1, axis=dim),
        )
    before = lax.ppermute(lax.slice_in_dim(block, length - 1, length, axis=dim), axis, up)
    after = lax.ppermute(lax.slice_in_dim(block, 0, 1, axis=dim), axis, down)
    return before, after


def grown(block, axis, dim):
    before, after = neighbours_of(block, axis, dim)
    return jnp.concatenate([before, block, after], axis=dim)


def flat_rows(piece):
    return piece.reshape(-1, piece.shape[-1])


def fold_kernel(mid_ref, low_ref, high_ref, out_ref):
    lanes = mid_ref.shape[1]
    ext_y = iota(mid_ref.shape, 1) // 32 % 4
    out_ref[...] = (
        mid_ref[...]
        + jnp.where(ext_y == 1, pltpu.roll(low_ref[...], lanes - 64, 1), 0.0)
        + jnp.where(ext_y == 2, pltpu.roll(high_ref[...], 64, 1), 0.0)
    )


def forces_kernel(mid_ref, low_ref, high_ref, src_ref, onto_ref, home_ref, out_ref):
    values = mid_ref[...]
    lanes = values.shape[1]
    ext_z = iota(values.shape, 1) // 8 % 4
    values += jnp.where(ext_z == 1, pltpu.roll(low_ref[...], lanes - 16, 1), 0.0)
    values += jnp.where(ext_z == 2, pltpu.roll(high_ref[...], 16, 1), 0.0)
    first = values.astype(BF16)
    values -= first.astype(F32)
    second = values.astype(BF16)
    third = (values - second.astype(F32)).astype(BF16)
    home = home_ref[...]
    total = onto_ref[...] - src_ref[...].T[0:8, :]
    total += (mm_nt(first, home) + (mm_nt(second, home) + mm_nt(third, home)))
    for comp in range(3):
        out_ref[comp] = -total[comp : comp + 1, :]


def give_back_x(low, mid, high):
    up, down = ring("gx")
    from_low = lax.ppermute(high, "gx", up)
    from_high = lax.ppermute(low, "gx", down)
    return mid, jnp.concatenate([from_low, from_high], axis=1)


def give_back_y(mid):
    up, down = ring("gy")
    return mid, lax.ppermute(mid, "gy", up), lax.ppermute(mid, "gy", down)


def fold(*args):
    return call(fold_kernel, "fold", (struct(*args[0].shape),), [], args)[0]


def give_back_z(mid):
    up, down = ring("gz")
    from_low = lax.ppermute(mid, "gz", up)
    return mid, from_low, from_low if len(up) == 2 else lax.ppermute(mid, "gz", down)


def local(
    features,
    positions,
    neighbours,
    counts,
    cell_atoms,
    rbf_weight,
    radial_weight,
    mix_weight,
    out_weight,
    energy_weight,
    norm_weight,
):
    feats = features[0, 0, 0]
    places = jnp.swapaxes(positions[0, 0], 0, 1)
    lists = jnp.concatenate([neighbours[0, 0, 0].T, counts[0, 0], cell_atoms[0, 0]], axis=0)
    cells0, cells1, own_pos, meta = make_cells(feats, places, lists)
    hold = lax.optimization_barrier
    block0, block1 = (part.reshape(2, 2, 2, 8, part.shape[1]) for part in (cells0, cells1))
    z0 = neighbours_of(block0, "gz", 2)
    z1 = neighbours_of(block1, "gz", 2)
    y1_in = neighbours_of(block1, "gy", 1)
    z0, own_pos, meta = hold((z0, own_pos, meta))
    block0 = jnp.concatenate([z0[0], block0, z0[1]], axis=2)
    y0 = neighbours_of(block0, "gy", 1)
    oh_own, pre_own, unit_own, radt, rbft, home, *radial_own = own_stage(
        meta, own_pos, rbf_weight, radial_weight
    )
    z1, y1_in, oh_own = hold((z1, y1_in, oh_own))
    block1 = jnp.concatenate([z1[0], block1, z1[1]], axis=2)
    x1_in = neighbours_of(block1, "gx", 0)
    (m0_own, gate_own, nf0_own, acc0), (own_a,) = own_forward_stage(
        (0,), feats, mix_weight, oh_own, radial_own
    )
    y0, z1, gate_own = hold((y0, z1, gate_own))
    middle = jnp.concatenate([y0[0], block0, y0[1]], axis=1)
    x0 = neighbours_of(middle, "gx", 0)
    y1_out = neighbours_of(jnp.concatenate(z1, axis=2), "gy", 1)
    weights_a, weights_b = weights_stage(mix_weight, out_weight)
    x1_in, gate_own, weights_a = hold((x1_in, gate_own, weights_a))
    _, (own_b,) = own_forward_stage((1,), feats, mix_weight, oh_own, radial_own, gate_own)
    x0, y1_out, acc0, acc_b = hold((x0, y1_out, acc0, own_b[2]))
    pieces0 = tuple(flat_rows(piece) for piece in (x0[0], middle, x0[1]))
    y1 = [
        jnp.concatenate([out[:, :, 0:1], inner, out[:, :, 1:2]], axis=2)
        for out, inner in zip(y1_out, y1_in)
    ]
    outer = jnp.concatenate(y1, axis=1)
    x1_out = neighbours_of(outer, "gx", 0)
    block1 = jnp.concatenate([y1[0], block1, y1[1]], axis=1)
    pieces1 = (x1_in[0], x1_out[0], block1, x1_in[1], x1_out[1])
    pieces1 = tuple(flat_rows(piece) for piece in pieces1)
    (
        new_0, oh_gh, d_gh, dt_gh, pre_gh, unit_gh, gs0, en_0, m0_gh, gate_gh, nf0_gh, *radial_gh,
    ) = start_stage(
        pieces0, feats, own_pos, meta, rbf_weight, radial_weight, mix_weight, out_weight,
        energy_weight[None], acc0,
    )
    shared = (feats, meta, mix_weight, out_weight, norm_weight, oh_gh, d_gh, dt_gh, gate_gh)
    new_a, en_a, _, (dot_gh_a, *gr_gh_a), (dot_own_a, *gr_own_a) = pairs_stage(
        0, 2 * CH, pieces0, shared, (gate_own, *own_a), radial_gh, weights_a
    )
    new, energy, src, onto, low, mid, high, gs_b = third_stage(
        pieces1, *shared, acc_b, radt, rbft, gs0, en_0, en_a, new_0, new_a, pre_gh,
        unit_gh, m0_gh, nf0_gh, dot_gh_a, *gr_gh_a,
        *[radial_gh[degree - 1] for degree in DEGREES[1]], *weights_b,
    )
    mid, arrived = give_back_x(low, mid, high)
    dot_own_b, *gr_own_b = own_backward_stage(1, weights_b[1], gs_b, gate_own, *own_b[:2])
    arrived, gs0, dot_own_b = hold((arrived, gs0, dot_own_b))
    mid, from_low, from_high = give_back_y(mid + arrived)
    back = (oh_own, pre_own, unit_own, radt, rbft, mix_weight, gs0, m0_own, nf0_own)
    back += (dot_own_a, dot_own_b, *gr_own_a, *gr_own_b)
    src, onto = own_back_stage(range(2), *back, src, onto)
    from_low, from_high, src = hold((from_low, from_high, src))
    folded = give_back_z(fold(mid, from_low, from_high))
    src, onto = own_back_stage(range(2, 4), *back, src, onto)
    args = (*folded, src, onto, home)
    out_shape = (struct(3, 1, src.shape[0]),)
    forces = call(forces_kernel, "forces", out_shape, [], args)[0]
    return (
        new[None, None, None],
        energy[None, None],
        jnp.swapaxes(forces, 0, 1)[None, None],
    )


def solution(mesh):
    split = P("gx", "gy", "gz", None, None)
    flat = P("gx", "gy", "gz", None)
    return jax.shard_map(
        local,
        mesh=mesh,
        in_specs=(split, split, split, flat, flat, P(), P(), P(), P(), P(), P()),
        out_specs=(split, flat, split),
        check_vma=False,
    )
```

```python
import functools
import math

import jax
import jax.numpy as jnp
from jax import lax
from jax.experimental import pallas as pl
from jax.experimental.pallas import tpu as pltpu
from jax.sharding import PartitionSpec as P

F32 = jnp.float32
BF16 = jnp.bfloat16
CH = 128
SLOTS = 32
HALF = 16
STEP = 256
OWN_STEPS = 4
GH_STEPS = 2
MIB = 1024 * 1024
SPACE = pltpu.VMEM
PAIR_DEGREES = (
    (1, 1), (1, 2), (2, 2), (2, 2),
    (3, 3), (3, 3), (3, 3), (3, 4),
    (4, 4), (4, 4), (4, 4), (4, 4),
)
GROUPS = ((0, 4), (4, 12))
KINDS = tuple(sorted({PAIR_DEGREES[pair] for pair in range(*group)}) for group in GROUPS)
DEGREES = tuple(sorted({d for both in kinds for d in both}) for kinds in KINDS)
GROUP_COLS = tuple(2 * CH * (end - begin) for begin, end in GROUPS)


def mm(a, b):
    return jnp.dot(a, b, preferred_element_type=F32)


def mm_nt(a, b):
    return lax.dot_general(a, b, (((1,), (1,)), ((), ())), preferred_element_type=F32)


def iota(shape, dim):
    return lax.broadcasted_iota(jnp.int32, shape, dim)


def flip(w):
    return w.astype(F32).T.astype(BF16)


def pair_cols(pair):
    return slice(CH + pair * 2 * CH, CH + (pair + 1) * 2 * CH)


def struct(*shape, dtype=F32):
    return jax.ShapeDtypeStruct(shape, dtype)


def call(kernel, name, out_shape, scratch, args, specs=None, limit=16, work=1024):
    return pl.pallas_call(
        kernel,
        out_shape=out_shape,
        in_specs=specs or [pl.BlockSpec(memory_space=SPACE)] * len(args),
        out_specs=tuple(pl.BlockSpec(memory_space=SPACE) for _ in out_shape),
        scratch_shapes=scratch,
        compiler_params=pltpu.CompilerParams(vmem_limit_bytes=limit * MIB),
        cost_estimate=pl.CostEstimate(flops=work, bytes_accessed=1024, transcendentals=0),
        name=name,
    )(*args)


def cells_kernel(
    feat_ref, pos_ref, lists_ref,
    out_ref, own_pos_ref, meta_ref, pick_ref, rows_ref, pos_rows,
):
    rows_ref[...] = jnp.zeros_like(rows_ref)
    pos_rows[...] = jnp.zeros_like(pos_rows)
    atoms = feat_ref.shape[0]
    rows_ref[0 : SLOTS + 2, :] = lists_ref[...].astype(F32)
    meta = rows_ref[...].T
    meta_ref[...] = meta
    for comp in range(3):
        places = pos_ref[comp]
        first = places.astype(BF16).astype(F32)
        second = (places - first).astype(BF16).astype(F32)
        pos_rows[comp : comp + 1, :] = first
        pos_rows[4 + comp : 5 + comp, :] = second
        pos_rows[8 + comp : 9 + comp, :] = places - first - second
    pieces = pos_rows[...].astype(BF16)
    lane = iota((atoms, atoms), 1).astype(F32)
    pick = (meta[:, SLOTS + 1 : SLOTS + 2] == lane).astype(F32).astype(BF16)
    same = (iota((atoms, atoms), 0) == iota((atoms, atoms), 1)).astype(F32).astype(BF16)
    own_pos_ref[...] = mm_nt(same, pieces).astype(BF16)
    out_ref[:, CH : 2 * CH] = mm_nt(pick, pieces).astype(BF16)
    pick_ref[...] = pick
    out_ref[:, 0:CH] = mm(pick, feat_ref[:, 0:CH]).astype(BF16)
    cut = pair_cols(GROUPS[1][0]).start
    out_ref[:, 2 * CH :] = mm(pick, feat_ref[:, CH:cut]).astype(BF16)


def rest_kernel(feat_ref, pick_ref, rest_ref):
    cut = pair_cols(GROUPS[1][0]).start
    rest_ref[...] = mm(pick_ref[...], feat_ref[:, cut:]).astype(BF16)


def make_cells(feats, places, lists):
    atoms = feats.shape[0]
    out_shape = (
        struct(atoms, 2 * CH + GROUP_COLS[0], dtype=BF16),
        struct(atoms, CH, dtype=BF16),
        struct(atoms, CH),
        struct(atoms, atoms, dtype=BF16),
    )
    args = (feats, places, lists)
    scratch = [pltpu.VMEM((CH, atoms), F32), pltpu.VMEM((CH, atoms), F32)]
    first, own_pos, meta, pick = call(cells_kernel, "cells", out_shape, scratch, args)
    out_shape = (struct(atoms, GROUP_COLS[1], dtype=BF16),)
    rest = call(rest_kernel, "cells_rest", out_shape, [], (feats, pick), work=1 << 32)[0]
    return first, rest, own_pos, meta


def spacing_of(atoms, nbasis):
    depth = atoms // 16
    return 2.0 * math.sqrt(32.0 + depth * depth) / (nbasis - 1)


def own_onehots(meta_ref, oh_own):
    atoms = meta_ref.shape[0]
    counts = meta_ref[:, SLOTS : SLOTS + 1]
    lane_atom = iota((atoms, atoms), 1).astype(F32)
    for slot in range(HALF):
        hit = jnp.logical_and(meta_ref[:, slot : slot + 1] == lane_atom, counts > slot)
        oh_own[slot * atoms : (slot + 1) * atoms, :] = hit.astype(F32).astype(BF16)


def geometry(near, here):
    diff = near - here
    rel = (diff + pltpu.roll(diff, CH - 4, 1)) + (
        pltpu.roll(diff, CH - 8, 1) + pltpu.roll(diff, CH - 12, 1)
    )
    lane = iota(rel.shape, 1)
    rel = jnp.where(lane < 3, rel, 0.0)
    square = jnp.sum(rel * rel, axis=1, keepdims=True)
    inverse = lax.rsqrt(jnp.where(square > 0.0, square, 1.0))
    dist = square * inverse
    return jnp.where(lane == 3, dist, rel * inverse), dist


def centred_of(dist, spacing, nbasis):
    return dist * (1.0 / spacing) - iota((dist.shape[0], nbasis), 1).astype(F32)


def radial_net(dist, spacing, rbf_ref, rad_ref):
    centred = centred_of(dist, spacing, rbf_ref.shape[0])
    basis = jnp.exp(-0.5 * centred * centred)
    pre = mm(basis.astype(BF16), rbf_ref[...])
    hidden = (pre * jax.nn.sigmoid(pre)).astype(BF16)
    return pre, mm(hidden, rad_ref[...]).astype(BF16), basis * centred


def tiled(values, size=STEP):
    return jnp.concatenate([values] * (size // values.shape[0]), axis=0)


def live_ghosts(meta_ref):
    return jnp.maximum(meta_ref[:, SLOTS : SLOTS + 1] - HALF, 0.0)


def step_count(meta_ref):
    total = jnp.sum(live_ghosts(meta_ref)).astype(jnp.int32)
    rows = GH_STEPS * STEP
    return jnp.maximum((total + (rows - 1)) // rows, 1) * GH_STEPS


def own_rows(step, size=STEP):
    return pl.ds(step * size, size)


def ghost_rows(step, size=STEP):
    first = OWN_STEPS * STEP
    if isinstance(step, int):
        return pl.ds(step * size, size), pl.ds(first + step * size, size)
    base = pl.multiple_of(step * size, size)
    return pl.ds(base, size), pl.ds(pl.multiple_of(first + base, size), size)


def over_ghost_steps(steps, body, size=STEP):
    static = GH_STEPS * STEP // size
    for step in range(static):
        body(step)

    def again(step, carry):
        body(step)
        return carry

    lax.fori_loop(static, (steps * STEP + (size - 1)) // size, again, 0)


def block_diagonal(kinds, source, straight=None, across=None):
    zero = jnp.zeros((CH, CH), BF16)
    targets = [ref for ref in (straight, across) if ref is not None]
    for kind, both in enumerate(kinds):
        for ref in targets:
            ref[kind, 0:CH, CH:] = zero
            ref[kind, CH:, 0:CH] = zero
    for degree in sorted({d for both in kinds for d in both}):
        weight = source[degree]
        flipped = flip(weight) if across is not None else None
        for kind, both in enumerate(kinds):
            for side in range(2):
                if both[side] == degree:
                    part = slice(side * CH, side * CH + CH)
                    if straight is not None:
                        straight[kind, part, part] = weight
                    if across is not None:
                        across[kind, part, part] = flipped


def joined(pieces, cols):
    if len(pieces) == 3:
        return jnp.concatenate([piece[:, cols] for piece in pieces], axis=0)
    low_in, low_out, mid, high_in, high_out = pieces
    half = low_out.shape[0] // 2
    parts = [low_out[0:half, cols], low_in[:, cols], low_out[half:, cols], mid[:, cols]]
    parts += [high_out[0:half, cols], high_in[:, cols], high_out[half:, cols]]
    return jnp.concatenate(parts, axis=0)


def infos_of(group):
    infos = []
    for index, pair in enumerate(range(*GROUPS[group])):
        degrees = PAIR_DEGREES[pair]
        cols = slice(index * 2 * CH, (index + 1) * 2 * CH)
        infos.append((cols, degrees, KINDS[group].index(degrees)))
    return infos


def group_cols(group):
    begin, end = GROUPS[group]
    return slice(pair_cols(begin).start, pair_cols(end - 1).stop)


def twice(values):
    return jnp.concatenate([values, values], axis=1)


def forward(group, rows, onehot, feats, radials, gate_ref, wm, nf_ref, mx_ref, slots):
    near = mm(onehot, feats).astype(BF16)
    nf_ref[rows, :] = near
    gate = twice(gate_ref[rows, :])
    wide = gate.astype(F32) if slots else None
    messages = []
    for cols, degrees, kind in infos_of(group):
        radial = jnp.concatenate([radials[d][rows, :] for d in degrees], axis=1)
        mixed = mm(near[:, cols] * radial, wm[kind])
        low = mixed.astype(BF16)
        mx_ref[rows, cols] = low
        messages.append(mixed * wide if slots else low * gate)
    return messages


def backward(group, rows, grad, gate_ref, wmt, nf_ref, mx_ref, dot_ref, grad_refs):
    parts = {}
    dots = None
    gate = twice(gate_ref[rows, :])
    for cols, degrees, kind in infos_of(group):
        product = grad[:, cols] * mx_ref[rows, cols]
        dot = (product[:, 0:CH] + product[:, CH:]).astype(F32)
        dots = dot if dots is None else dots + dot
        weighted = mm(grad[:, cols] * gate, wmt[kind]) * nf_ref[rows, cols].astype(F32)
        for side in range(2):
            part = weighted[:, side * CH : (side + 1) * CH]
            degree = degrees[side]
            parts[degree] = parts[degree] + part if degree in parts else part
    dot_ref[rows, :] = dots.astype(dot_ref.dtype)
    for degree, part in parts.items():
        grad_refs[degree][rows, :] = part.astype(grad_refs[degree].dtype)


def over_slots(values, atoms):
    return jnp.sum(values.reshape(-1, atoms, values.shape[1]), axis=0)


def own_forward(group, own_ref, oh_own, radials, gate_ref, wm, nf_ref, mx_ref, acc_ref):
    atoms = own_ref.shape[0]
    feats = own_ref[:, group_cols(group)]
    for step in range(OWN_STEPS):
        rows = own_rows(step)
        messages = forward(
            group, rows, oh_own[rows, :], feats, radials, gate_ref, wm, nf_ref, mx_ref, True
        )
        for (cols, _, _), message in zip(infos_of(group), messages):
            part = over_slots(message, atoms)
            acc_ref[:, cols] = part if step == 0 else acc_ref[:, cols] + part


def own_backward(group, gs_ref, gate_ref, wmt, nf_ref, mx_ref, dot_ref, grad_refs):
    grad = tiled(gs_ref[...])
    for step in range(OWN_STEPS):
        backward(
            group, own_rows(step), grad, gate_ref, wmt, nf_ref, mx_ref, dot_ref, grad_refs
        )


def ghost_pairs(
    group, own_ref, pieces, skip, new_ref, new_base, oh_gh, d_gh, dt_gh, gate_ref, radials, nw_ref,
    steps, wm, wmt, wo, wot, nf_s, mx_s, acc_in, acc_s, gs_ref, dot_ref, grad_refs, en_ref,
):
    norm = 1.0 / math.sqrt(SLOTS)
    cols = slice(skip, skip + GROUP_COLS[group])
    acc_s[...] = acc_in[...]

    def ghost_forward(step):
        here, _ = ghost_rows(step)
        messages = forward(
            group, here, oh_gh[here, :], joined(pieces, cols), radials, gate_ref, wm, nf_s, mx_s,
            False,
        )
        acc_s[...] += mm(dt_gh[:, here], jnp.concatenate(messages, axis=1))

    over_ghost_steps(steps, ghost_forward)

    begin = group_cols(group).start
    for cols, degrees, kind in infos_of(group):
        summed_low = (acc_s[:, cols] * norm).astype(BF16)
        own = own_ref[:, begin + cols.start : begin + cols.stop]
        updated = own.astype(F32) + mm(summed_low, wo[kind])
        at = begin - new_base + cols.start
        new_ref[:, at : at + 2 * CH] = updated.astype(BF16)
        weight = jnp.concatenate(
            [nw_ref[d - 1 : d, :] * (1.0 / (2 * d + 1)) for d in degrees], axis=1
        )
        scale = weight * updated
        energy = scale * updated
        en_ref[...] += energy[:, 0:CH] + energy[:, CH:]
        gs_ref[:, cols] = (mm((2.0 * scale).astype(BF16), wot[kind]) * norm).astype(BF16)

    def ghost_backward(step):
        here, _ = ghost_rows(step)
        grad = mm(d_gh[here, :], gs_ref[...]).astype(BF16)
        backward(group, here, grad, gate_ref, wmt, nf_s, mx_s, dot_ref, grad_refs)

    over_ghost_steps(steps, ghost_backward)


def pair_scratch(atoms, half, group):
    count, width = len(KINDS[group]), GROUP_COLS[group]
    return (
        [pltpu.VMEM((count, 2 * CH, 2 * CH), BF16) for _ in range(4)]
        + [
            pltpu.VMEM((half, width), BF16),
            pltpu.VMEM((half, width), BF16),
            pltpu.VMEM((atoms, width), F32),
        ]
    )


def own_kernel(
    meta_ref, own_pos_ref, rbf_ref, rad_ref,
    oh_own, pre_ref, unit_ref, radt_ref, rbft_ref, home_ref, slope_ref, *radial_refs
):
    atoms = meta_ref.shape[0]
    nbasis = rbft_ref.shape[1]
    spacing = spacing_of(atoms, nbasis)
    own_onehots(meta_ref, oh_own)
    here = tiled(own_pos_ref[...].astype(F32))
    for step in range(OWN_STEPS):
        rows = own_rows(step)
        unit, dist = geometry(mm(oh_own[rows, :], own_pos_ref[...]), here)
        unit_ref[rows, :] = unit
        pre, radial, slope = radial_net(dist, spacing, rbf_ref, rad_ref)
        slope_ref[rows, :] = slope.astype(BF16)
        pre_ref[rows, :] = pre.astype(BF16)
        for degree, ref in enumerate(radial_refs):
            ref[rows, :] = radial[:, degree * CH : (degree + 1) * CH]
    for degree in range(5):
        part = slice(degree * CH, (degree + 1) * CH)
        radt_ref[part, :] = flip(rad_ref[:, part])
    for index in range(nbasis // CH):
        part = slice(index * CH, (index + 1) * CH)
        rbft_ref[:, part] = flip(rbf_ref[part, :])
    lanes = home_ref.shape[1]
    lane = iota((atoms, lanes), 1)
    ext_x, ext_y, ext_z = lane // 128, lane // 32 % 4, lane // 8 % 4
    slot = ((2 * ext_x + ext_y - 1) * 2 + ext_z - 1) * 8 + lane % 8
    inside = jnp.logical_and(
        jnp.logical_or(ext_y == 1, ext_y == 2), jnp.logical_or(ext_z == 1, ext_z == 2)
    )
    to_slot = jnp.logical_and(iota((atoms, lanes), 0) == slot, inside)
    to_slot = to_slot.astype(F32).astype(BF16)
    order = meta_ref[:, SLOTS + 1 : SLOTS + 2]
    to_atom = (order == iota((atoms, atoms), 1).astype(F32)).astype(F32)
    home_ref[...] = mm(to_atom.T.astype(BF16), to_slot).astype(BF16)


def own_stage(meta, own_pos, rbf, rad):
    atoms = meta.shape[0]
    edges = atoms * HALF
    out_shape = (
        struct(edges, atoms, dtype=BF16),
        struct(edges, CH, dtype=BF16),
        struct(edges, CH),
        struct(5 * CH, CH, dtype=BF16),
        struct(CH, rbf.shape[0], dtype=BF16),
        struct(atoms, 256, dtype=BF16),
        struct(edges, rbf.shape[0], dtype=BF16),
    ) + (struct(edges, CH, dtype=BF16),) * 5
    return call(own_kernel, "own_edges", out_shape, [], (meta, own_pos, rbf, rad))


def scalar_forward(rows, near, radial, mix_ref, m0_ref, gate_ref, nf0_ref):
    near = near.astype(BF16)
    nf0_ref[rows, :] = near
    mixed = mm(near * radial, mix_ref[0])
    m0_ref[rows, :] = mixed.astype(BF16)
    gate = jax.nn.sigmoid(mixed)
    gate_ref[rows, :] = gate.astype(BF16)
    return mixed * gate


def own_forward_kernel(groups, scalar, *refs):
    own_ref, mix_ref, oh_own, refs = *refs[:3], refs[3:]
    radial0, radials = refs[0], dict(enumerate(refs[1:5], start=1))
    refs = refs[5:]
    if scalar:
        m0_ref, gate_ref, nf0_ref, acc0_ref = refs[:4]
        refs = refs[4:]
        atoms = own_ref.shape[0]
        feats = own_ref[:, 0:CH]
        summed = None
        for step in range(OWN_STEPS):
            rows = own_rows(step)
            message = scalar_forward(
                rows, mm(oh_own[rows, :], feats), radial0[rows, :], mix_ref, m0_ref, gate_ref,
                nf0_ref,
            )
            part = over_slots(message, atoms)
            summed = part if summed is None else summed + part
        acc0_ref[...] = summed
    else:
        gate_ref, refs = refs[0], refs[1:]
    outs, weights = refs[: 3 * len(groups)], refs[3 * len(groups) :]
    for index, group in enumerate(groups):
        block_diagonal(KINDS[group], mix_ref, weights[index])
        nf_ref, mx_ref, acc_ref = outs[3 * index : 3 * index + 3]
        own_forward(
            group, own_ref, oh_own, radials, gate_ref, weights[index], nf_ref, mx_ref, acc_ref
        )


def own_forward_stage(groups, feats, mix, oh_own, radial_own, gate=None):
    atoms = feats.shape[0]
    half = atoms * HALF
    out_shape = ()
    if gate is None:
        out_shape += (struct(half, CH, dtype=BF16),) * 3 + (struct(atoms, CH),)
    for group in groups:
        width = GROUP_COLS[group]
        out_shape += (struct(half, width, dtype=BF16),) * 2 + (struct(atoms, width),)
    args = (feats, mix, oh_own, *radial_own) + (() if gate is None else (gate,))
    scratch = [pltpu.VMEM((len(KINDS[group]), 2 * CH, 2 * CH), BF16) for group in groups]
    name = "own_forward_" + "".join("abc"[group] for group in groups)
    kernel = functools.partial(own_forward_kernel, groups, gate is None)
    outs = call(kernel, name, out_shape, scratch, args)
    first = len(outs) - 3 * len(groups)
    return outs[:first], [outs[first + 3 * i : first + 3 * i + 3] for i in range(len(groups))]


def start_kernel(
    p0, p1, p2, own_ref, own_pos_ref, meta_ref, rbf_ref, rad_ref, mix_ref, out_ref, ew_ref,
    acc0_ref,
    new_ref, oh_gh, d_gh, dt_gh, pre_ref, unit_ref, gs0_ref, en_ref, m0_gh, gate_gh, nf0_gh,
    radial_gh1, radial_gh2, radial_gh3, radial_gh4,
    ghpos, acc_s,
):
    radial_gh = (None, radial_gh1, radial_gh2, radial_gh3, radial_gh4)
    pieces = (p0, p1, p2)
    atoms = own_ref.shape[0]
    ghosts = ghpos.shape[0]
    spacing = spacing_of(atoms, rbf_ref.shape[0])
    norm = 1.0 / math.sqrt(SLOTS)

    live = live_ghosts(meta_ref)
    sub_atom = iota((atoms, atoms), 0)
    lane_atom = iota((atoms, atoms), 1)
    live_b = jnp.broadcast_to(live, (atoms, atoms))
    end_row = jnp.sum(jnp.where(sub_atom <= lane_atom, live_b, 0.0), axis=0, keepdims=True)
    live_row = jnp.sum(jnp.where(sub_atom == lane_atom, live_b, 0.0), axis=0, keepdims=True)
    start_row = end_row - live_row
    row_b = jnp.broadcast_to(live_row, (atoms, atoms))
    end_col = jnp.sum(jnp.where(lane_atom <= sub_atom, row_b, 0.0), axis=1, keepdims=True)
    start_col = end_col - live
    total = jnp.sum(live)
    steps = step_count(meta_ref)
    ghost_row = meta_ref[:, HALF:SLOTS] - atoms
    high_part = jnp.floor(ghost_row * (1.0 / 16.0))
    row_high = high_part.astype(BF16)
    row_low = (ghost_row - 16.0 * high_part).astype(BF16)

    row = iota((ghosts, CH), 0)
    lane = iota((ghosts, CH), 1)
    zcells = atoms // 32
    per_y = (zcells + 2) * 8
    ext_x = row // (4 * per_y)
    ext_y = row // per_y % 4
    ext_z = row // 8 % (zcells + 2)

    def side_of(ext, last, size):
        return jnp.where(ext == 0, -size, jnp.where(ext == last, size, 0.0))

    shift = jnp.where(lane == 12, side_of(ext_x, 3, 4.0), 0.0)
    shift = jnp.where(lane == 13, side_of(ext_y, 3, 4.0), shift)
    shift = jnp.where(lane == 14, side_of(ext_z, zcells + 1, 2.0 * zcells), shift)
    own0 = own_ref[:, 0:CH]
    acc_s[...] = acc0_ref[...]
    ghpos[...] = (joined(pieces, slice(CH, 2 * CH)).astype(F32) + shift).astype(BF16)

    def ghost_start(step):
        here, _ = ghost_rows(step)
        base = step * STEP
        edge = (iota((STEP, atoms), 0) + base).astype(F32)
        mine = jnp.logical_and(edge >= start_row, edge < end_row).astype(F32)
        source = mine.astype(BF16)
        d_gh[here, :] = source
        edge_t = (iota((atoms, STEP), 1) + base).astype(F32)
        mine_t = jnp.logical_and(edge_t >= start_col, edge_t < end_col)
        spread = mine_t.astype(F32).astype(BF16)
        dt_gh[:, here] = spread
        edge_col = edge[:, 0:1]
        slot = edge_col - jnp.sum(mine * start_row, axis=1, keepdims=True)
        listed = mm(source, row_high) * 16.0 + mm(source, row_low)
        at_slot = iota((STEP, HALF), 1).astype(F32) == slot
        which = jnp.sum(jnp.where(at_slot, listed, 0.0), axis=1, keepdims=True)
        which = jnp.where(edge_col < total, which, -1.0)
        onehot = (iota((STEP, ghosts), 1).astype(F32) == which).astype(F32).astype(BF16)
        oh_gh[here, :] = onehot
        unit, dist = geometry(mm(onehot, ghpos[...]), mm(source, own_pos_ref[...]))
        unit_ref[here, :] = unit
        pre, radial, _ = radial_net(dist, spacing, rbf_ref, rad_ref)
        pre_ref[here, :] = pre.astype(BF16)
        for degree in range(1, 5):
            radial_gh[degree][here, :] = radial[:, degree * CH : (degree + 1) * CH]
        message = scalar_forward(
            here, mm(onehot, joined(pieces, slice(0, CH))), radial[:, 0:CH], mix_ref, m0_gh, gate_gh, nf0_gh
        )
        acc_s[...] += mm(spread, message.astype(BF16))

    over_ghost_steps(steps, ghost_start)

    low0 = (acc_s[...] * norm).astype(BF16)
    updated0 = own0.astype(F32) + mm(low0, out_ref[0])
    new_ref[:, 0:CH] = updated0.astype(BF16)
    logistic = jax.nn.sigmoid(updated0)
    weight0 = ew_ref[...]
    en_ref[...] = weight0 * updated0 * logistic
    grad0 = (weight0 * logistic * (1.0 + updated0 * (1.0 - logistic))).astype(BF16)
    gs0_ref[...] = mm_nt(grad0, out_ref[0]) * norm


def start_stage(pieces, feats, *rest):
    atoms = feats.shape[0]
    half = atoms * HALF
    ghosts = sum(piece.shape[0] for piece in pieces)
    out_shape = (
        struct(atoms, CH, dtype=BF16),
        struct(half, ghosts, dtype=BF16),
        struct(half, atoms, dtype=BF16),
        struct(atoms, half, dtype=BF16),
        struct(half, CH, dtype=BF16),
        struct(half, CH),
        struct(atoms, CH),
        struct(atoms, CH),
    ) + (struct(half, CH, dtype=BF16),) * 7
    scratch = [
        pltpu.VMEM((ghosts, CH), BF16),
        pltpu.VMEM((atoms, CH), F32),
    ]
    args = tuple(pieces) + (feats,) + rest
    return call(
        start_kernel, "ghost_start", out_shape, scratch, args, limit=24
    )


def pairs_kernel(group, count, skip, *refs):
    pieces, refs = refs[:count], refs[count:]
    own_ref, meta_ref, mix_ref, out_ref, nw_ref, oh_gh, d_gh, dt_gh, gate_gh = refs[:9]
    gate_own, nf_own, mx_own, acc_own = refs[9:13]
    refs = refs[13:]
    degrees = DEGREES[group]
    radials, refs = dict(zip(degrees, refs)), refs[len(degrees) :]
    new_ref, en_ref, gs_ref, dot_gh = refs[:4]
    grads, refs = dict(zip(degrees, refs[4:])), refs[4 + len(degrees) :]
    if group == 0:
        dot_own, refs = refs[0], refs[1:]
        grads_own, refs = dict(zip(degrees, refs)), refs[len(degrees) :]
    wm, wmt, wo, wot, nf_s, mx_s, acc_s = refs
    block_diagonal(KINDS[group], mix_ref, wm, wmt)
    block_diagonal(KINDS[group], out_ref, wo, wot)
    en_ref[...] = jnp.zeros_like(en_ref)
    ghost_pairs(
        group, own_ref, pieces, skip, new_ref, group_cols(group).start, oh_gh, d_gh, dt_gh, gate_gh,
        radials, nw_ref, step_count(meta_ref), wm, wmt, wo, wot, nf_s, mx_s, acc_own, acc_s,
        gs_ref, dot_gh, grads, en_ref,
    )
    if group == 0:
        own_backward(group, gs_ref, gate_own, wmt, nf_own, mx_own, dot_own, grads_own)


def pairs_stage(group, skip, pieces, shared, own_parts, radial_gh):
    feats = shared[0]
    atoms = feats.shape[0]
    half = atoms * HALF
    ghosts = sum(piece.shape[0] for piece in pieces)
    degrees = DEGREES[group]
    sides = 2 if group == 0 else 1
    out_shape = (
        struct(atoms, GROUP_COLS[group], dtype=BF16),
        struct(atoms, CH),
        struct(atoms, GROUP_COLS[group], dtype=BF16),
    ) + (struct(half, CH, dtype=BF16),) * (sides * (1 + len(degrees)))
    args = tuple(pieces) + tuple(shared) + tuple(own_parts)
    args += tuple(radial_gh[degree - 1] for degree in degrees)
    new, energy, gs, *rest = call(
        functools.partial(pairs_kernel, group, len(pieces), skip), "pairs_" + "abc"[group],
        out_shape, pair_scratch(atoms, half, group), args, limit=24,
    )
    return new, energy, gs, rest[: 1 + len(degrees)], rest[1 + len(degrees) :]


def own_backward_kernel(group, mix_ref, gs_ref, gate_ref, nf_ref, mx_ref, *refs):
    dot_ref, grads, wmt = refs[0], dict(zip(DEGREES[group], refs[1:-1])), refs[-1]
    block_diagonal(KINDS[group], mix_ref, None, wmt)
    own_backward(group, gs_ref, gate_ref, wmt, nf_ref, mx_ref, dot_ref, grads)


def own_backward_stage(group, mix, gs, gate, nf, mx):
    half = nf.shape[0]
    out_shape = (struct(half, CH, dtype=BF16),) * (1 + len(DEGREES[group]))
    scratch = [pltpu.VMEM((len(KINDS[group]), 2 * CH, 2 * CH), BF16)]
    kernel = functools.partial(own_backward_kernel, group)
    name = "own_backward_" + "abc"[group]
    return call(kernel, name, out_shape, scratch, (mix, gs, gate, nf, mx))


def finish(
    grad, mixed, near, dots, parts, pre, unit, spacing, radt_ref, rbft_ref, mix_t,
    slope=None,
):
    mixed = mixed.astype(F32)
    gate = jax.nn.sigmoid(mixed)
    first = grad * gate * (1.0 + mixed * (1.0 - gate)) + dots * gate * (1.0 - gate)
    weighted = mm(first.astype(BF16), mix_t) * near.astype(F32)
    radial_grad = jnp.concatenate([weighted.astype(BF16)] + parts, axis=1)
    hidden_grad = mm(radial_grad, radt_ref[...])
    pre = pre.astype(F32)
    logistic = jax.nn.sigmoid(pre)
    pre_grad = (hidden_grad * logistic * (1.0 + pre * (1.0 - logistic))).astype(BF16)
    if slope is None:
        centred = centred_of(unit[:, 3:4], spacing, rbft_ref.shape[1])
        slope = jnp.exp(-0.5 * centred * centred) * centred
    basis_grad = mm(pre_grad, rbft_ref[...])
    dist_grad = jnp.sum(basis_grad * slope, axis=1, keepdims=True) * (-1.0 / spacing)
    pull = unit * dist_grad
    across = pull.T[0:8, :]
    top = across.astype(BF16)
    rest = (across - top.astype(F32)).astype(BF16)
    return pull, top, rest


def sum_of(refs, rows):
    total = refs[0][rows, :].astype(F32)
    for ref in refs[1:]:
        total += ref[rows, :].astype(F32)
    return total


def degree_parts(refs, rows):
    by_degree = {}
    refs = list(refs)
    for degrees in DEGREES:
        for degree in degrees:
            by_degree.setdefault(degree, []).append(refs.pop(0))
    return [sum_of(by_degree[degree], rows).astype(BF16) for degree in range(1, 5)]


PARTIALS = sum(len(degrees) for degrees in DEGREES)


def third_kernel(
    p0, p1, p2, p3, p4, own_ref, meta_ref, mix_ref, out_ref, nw_ref, oh_gh, d_gh, dt_gh, gate_gh,
    acc_own, radt_ref, rbft_ref, gs0_ref, en_0, en_a, new_0, new_a, pre_gh, unit_gh,
    m0_ref, nf0_ref, dot_a, *refs
):
    group = 1
    before, degrees = len(DEGREES[0]), DEGREES[group]
    gr_a, refs = refs[:before], refs[before:]
    radials, refs = dict(zip(degrees, refs)), refs[len(degrees) :]
    new_ref, energy_ref, src_ref, onto_ref, flow_ref, fmid_ref, fhigh_ref, gs_ref = refs[:8]
    wm, wmt, wo, wot, nf_s, mx_s, acc_s, dot_c, en_s, fgh_s = refs[8:18]
    grads = dict(zip(degrees, refs[18:]))
    pieces = (p0, p1, p2, p3, p4)
    atoms = own_ref.shape[0]
    spacing = spacing_of(atoms, rbft_ref.shape[1])
    block_diagonal(KINDS[group], mix_ref, wm, wmt)
    block_diagonal(KINDS[group], out_ref, wo, wot)
    en_s[...] = en_0[...] + en_a[...]
    at = 0
    for part in (new_0, new_a):
        new_ref[:, at : at + part.shape[1]] = part[...]
        at += part.shape[1]
    steps = step_count(meta_ref)

    ghost_pairs(
        group, own_ref, pieces, 0, new_ref, 0, oh_gh, d_gh, dt_gh, gate_gh, radials, nw_ref,
        steps, wm, wmt, wo, wot, nf_s, mx_s, acc_own, acc_s, gs_ref, dot_c, grads, en_s,
    )
    energy_ref[...] = jnp.sum(en_s[...].T, axis=0, keepdims=True)

    fgh_s[...] = jnp.zeros_like(fgh_s)
    src_ref[...] = jnp.zeros_like(src_ref)
    onto_ref[...] = jnp.zeros_like(onto_ref)
    gs0_low = gs0_ref[...].astype(BF16)
    mix_t = flip(mix_ref[0])

    def ghost_finish(step):
        here, _ = ghost_rows(step)
        grad = mm(d_gh[here, :], gs0_low)
        pull, top, rest = finish(
            grad, m0_ref[here, :], nf0_ref[here, :], sum_of((dot_a, dot_c), here),
            degree_parts(gr_a + refs[18:], here), pre_gh[here, :], unit_gh[here, :], spacing,
            radt_ref, rbft_ref, mix_t,
        )
        pull_top = pull.astype(BF16)
        pull_rest = (pull - pull_top.astype(F32)).astype(BF16)
        spread = dt_gh[:, here]
        src_ref[...] += mm(spread, pull_top) + mm(spread, pull_rest)
        onehot = oh_gh[here, :]
        fgh_s[...] += mm(top, onehot) + mm(rest, onehot)

    over_ghost_steps(steps, ghost_finish)
    low, mid = flow_ref.shape[1], fmid_ref.shape[1]
    flow_ref[...] = fgh_s[:, 0:low]
    fmid_ref[...] = fgh_s[:, low : low + mid]
    fhigh_ref[...] = fgh_s[:, low + mid :]


def third_stage(pieces, feats, *rest):
    atoms, feat = feats.shape
    half = atoms * HALF
    ghosts = sum(piece.shape[0] for piece in pieces)
    sizes = (ghosts // 4, ghosts // 2, ghosts // 4)
    out_shape = (
        struct(atoms, feat, dtype=BF16),
        struct(1, atoms),
        struct(atoms, CH),
        struct(8, atoms),
    ) + tuple(struct(8, size) for size in sizes) + (
        struct(atoms, GROUP_COLS[1], dtype=BF16),
    )
    scratch = pair_scratch(atoms, half, 1) + [
        pltpu.VMEM((half, CH), BF16),
        pltpu.VMEM((atoms, CH), F32),
        pltpu.VMEM((8, ghosts), F32),
    ]
    scratch += [pltpu.VMEM((half, CH), BF16)] * len(DEGREES[1])
    args = tuple(pieces) + (feats,) + rest
    return call(
        third_kernel, "third_group", out_shape, scratch, args, limit=28
    )


def own_back_kernel(
    steps, oh_own, pre_own, unit_own, slope_ref, radt_ref, rbft_ref, mix_ref, gs0_ref,
    m0_ref, nf0_ref, dot_a, dot_c, *refs
):
    gr_own, (src_in, onto_in, src_out, onto_out) = refs[:PARTIALS], refs[PARTIALS:]
    atoms = oh_own.shape[1]
    spacing = spacing_of(atoms, rbft_ref.shape[1])
    grad = tiled(gs0_ref[...])
    mix_t = flip(mix_ref[0])
    src = src_in[...]
    onto = onto_in[...]
    for step in steps:
        rows = own_rows(step)
        pull, top, rest = finish(
            grad, m0_ref[rows, :], nf0_ref[rows, :], sum_of((dot_a, dot_c), rows),
            degree_parts(gr_own, rows), pre_own[rows, :], unit_own[rows, :], spacing, radt_ref,
            rbft_ref, mix_t, slope_ref[rows, :].astype(F32),
        )
        src += over_slots(pull, atoms)
        onehot = oh_own[rows, :]
        onto += mm(top, onehot) + mm(rest, onehot)
    src_out[...] = src
    onto_out[...] = onto


def own_back_stage(steps, *args):
    atoms = args[0].shape[1]
    out_shape = (struct(atoms, CH), struct(8, atoms))
    kernel = functools.partial(own_back_kernel, tuple(steps))
    return call(kernel, "own_back", out_shape, [], args)


def ring(axis):
    peers = lax.axis_size(axis)
    up = [(i, (i + 1) % peers) for i in range(peers)]
    return up, [(j, i) for i, j in up]


def neighbours_of(block, axis, dim):
    up, down = ring(axis)
    length = block.shape[dim]
    if len(up) == 2 and length == 2:
        other = lax.ppermute(block, axis, up)
        return (
            lax.slice_in_dim(other, length - 1, length, axis=dim),
            lax.slice_in_dim(other, 0, 1, axis=dim),
        )
    before = lax.ppermute(lax.slice_in_dim(block, length - 1, length, axis=dim), axis, up)
    after = lax.ppermute(lax.slice_in_dim(block, 0, 1, axis=dim), axis, down)
    return before, after


def grown(block, axis, dim):
    before, after = neighbours_of(block, axis, dim)
    return jnp.concatenate([before, block, after], axis=dim)


def flat_rows(piece):
    return piece.reshape(-1, piece.shape[-1])


def fold_kernel(mid_ref, low_ref, high_ref, out_ref):
    lanes = mid_ref.shape[1]
    ext_y = iota(mid_ref.shape, 1) // 32 % 4
    out_ref[...] = (
        mid_ref[...]
        + jnp.where(ext_y == 1, pltpu.roll(low_ref[...], lanes - 64, 1), 0.0)
        + jnp.where(ext_y == 2, pltpu.roll(high_ref[...], 64, 1), 0.0)
    )


def forces_kernel(mid_ref, low_ref, high_ref, src_ref, onto_ref, home_ref, out_ref):
    values = mid_ref[...]
    lanes = values.shape[1]
    ext_z = iota(values.shape, 1) // 8 % 4
    values += jnp.where(ext_z == 1, pltpu.roll(low_ref[...], lanes - 16, 1), 0.0)
    values += jnp.where(ext_z == 2, pltpu.roll(high_ref[...], 16, 1), 0.0)
    first = values.astype(BF16)
    values -= first.astype(F32)
    second = values.astype(BF16)
    third = (values - second.astype(F32)).astype(BF16)
    home = home_ref[...]
    total = onto_ref[...] - src_ref[...].T[0:8, :]
    total += (mm_nt(first, home) + (mm_nt(second, home) + mm_nt(third, home)))
    for comp in range(3):
        out_ref[comp] = -total[comp : comp + 1, :]


def give_back_x(low, mid, high):
    up, down = ring("gx")
    from_low = lax.ppermute(high, "gx", up)
    from_high = lax.ppermute(low, "gx", down)
    return mid, jnp.concatenate([from_low, from_high], axis=1)


def give_back_y(mid):
    up, down = ring("gy")
    return mid, lax.ppermute(mid, "gy", up), lax.ppermute(mid, "gy", down)


def fold(*args):
    return call(fold_kernel, "fold", (struct(*args[0].shape),), [], args)[0]


def give_back_z(mid):
    up, down = ring("gz")
    from_low = lax.ppermute(mid, "gz", up)
    return mid, from_low, from_low if len(up) == 2 else lax.ppermute(mid, "gz", down)


def local(
    features,
    positions,
    neighbours,
    counts,
    cell_atoms,
    rbf_weight,
    radial_weight,
    mix_weight,
    out_weight,
    energy_weight,
    norm_weight,
):
    feats = features[0, 0, 0]
    places = jnp.swapaxes(positions[0, 0], 0, 1)
    lists = jnp.concatenate([neighbours[0, 0, 0].T, counts[0, 0], cell_atoms[0, 0]], axis=0)
    cells0, cells1, own_pos, meta = make_cells(feats, places, lists)
    hold = lax.optimization_barrier
    block0, block1 = (part.reshape(2, 2, 2, 8, part.shape[1]) for part in (cells0, cells1))
    z0 = neighbours_of(block0, "gz", 2)
    z1 = neighbours_of(block1, "gz", 2)
    y1_in = neighbours_of(block1, "gy", 1)
    z0, own_pos, meta = hold((z0, own_pos, meta))
    block0 = jnp.concatenate([z0[0], block0, z0[1]], axis=2)
    y0 = neighbours_of(block0, "gy", 1)
    oh_own, pre_own, unit_own, radt, rbft, home, slope, *radial_own = own_stage(
        meta, own_pos, rbf_weight, radial_weight
    )
    z1, y1_in, oh_own = hold((z1, y1_in, oh_own))
    block1 = jnp.concatenate([z1[0], block1, z1[1]], axis=2)
    x1_in = neighbours_of(block1, "gx", 0)
    (m0_own, gate_own, nf0_own, acc0), (own_a,) = own_forward_stage(
        (0,), feats, mix_weight, oh_own, radial_own
    )
    y0, z1, gate_own = hold((y0, z1, gate_own))
    middle = jnp.concatenate([y0[0], block0, y0[1]], axis=1)
    x0 = neighbours_of(middle, "gx", 0)
    y1_out = neighbours_of(jnp.concatenate(z1, axis=2), "gy", 1)
    x1_in, gate_own = hold((x1_in, gate_own))
    _, (own_b,) = own_forward_stage((1,), feats, mix_weight, oh_own, radial_own, gate_own)
    x0, y1_out, acc0, acc_b = hold((x0, y1_out, acc0, own_b[2]))
    pieces0 = tuple(flat_rows(piece) for piece in (x0[0], middle, x0[1]))
    y1 = [
        jnp.concatenate([out[:, :, 0:1], inner, out[:, :, 1:2]], axis=2)
        for out, inner in zip(y1_out, y1_in)
    ]
    outer = jnp.concatenate(y1, axis=1)
    x1_out = neighbours_of(outer, "gx", 0)
    block1 = jnp.concatenate([y1[0], block1, y1[1]], axis=1)
    pieces1 = (x1_in[0], x1_out[0], block1, x1_in[1], x1_out[1])
    pieces1 = tuple(flat_rows(piece) for piece in pieces1)
    (
        new_0, oh_gh, d_gh, dt_gh, pre_gh, unit_gh, gs0, en_0, m0_gh, gate_gh, nf0_gh, *radial_gh,
    ) = start_stage(
        pieces0, feats, own_pos, meta, rbf_weight, radial_weight, mix_weight, out_weight,
        energy_weight[None], acc0,
    )
    shared = (feats, meta, mix_weight, out_weight, norm_weight, oh_gh, d_gh, dt_gh, gate_gh)
    new_a, en_a, _, (dot_gh_a, *gr_gh_a), (dot_own_a, *gr_own_a) = pairs_stage(
        0, 2 * CH, pieces0, shared, (gate_own, *own_a), radial_gh
    )
    new, energy, src, onto, low, mid, high, gs_b = third_stage(
        pieces1, *shared, acc_b, radt, rbft, gs0, en_0, en_a, new_0, new_a, pre_gh,
        unit_gh, m0_gh, nf0_gh, dot_gh_a, *gr_gh_a,
        *[radial_gh[degree - 1] for degree in DEGREES[1]],
    )
    mid, arrived = give_back_x(low, mid, high)
    dot_own_b, *gr_own_b = own_backward_stage(1, mix_weight, gs_b, gate_own, *own_b[:2])
    arrived, gs0, dot_own_b = hold((arrived, gs0, dot_own_b))
    mid, from_low, from_high = give_back_y(mid + arrived)
    back = (oh_own, pre_own, unit_own, slope, radt, rbft, mix_weight, gs0, m0_own, nf0_own)
    back += (dot_own_a, dot_own_b, *gr_own_a, *gr_own_b)
    src, onto = own_back_stage(range(2), *back, src, onto)
    from_low, from_high, src = hold((from_low, from_high, src))
    folded = give_back_z(fold(mid, from_low, from_high))
    src, onto = own_back_stage(range(2, 4), *back, src, onto)
    args = (*folded, src, onto, home)
    out_shape = (struct(3, 1, src.shape[0]),)
    forces = call(forces_kernel, "forces", out_shape, [], args)[0]
    return (
        new[None, None, None],
        energy[None, None],
        jnp.swapaxes(forces, 0, 1)[None, None],
    )


def solution(mesh):
    split = P("gx", "gy", "gz", None, None)
    flat = P("gx", "gy", "gz", None)
    return jax.shard_map(
        local,
        mesh=mesh,
        in_specs=(split, split, split, flat, flat, P(), P(), P(), P(), P(), P()),
        out_specs=(split, flat, split),
        check_vma=False,
    )
```
